32 devices in a mesh: lon: 8 (over z, x), lat: 4 (over y, core).
Axes of the slice: x: 2, y: 2, z: 4, core: 2. Of those that a mesh axis runs over, the one named last changes fastest.
Arguments:
- tokens: bfloat16 [4, 24, 192, 192], P(None, 'lat', 'lon'), may hold values from -6 to 6
- cotangent: bfloat16 [4, 24, 192, 192], P(None, 'lat', 'lon'), may hold values from -6 to 6
- land_sea: int32 [24, 192], P('lat', 'lon'), may hold values 0 or 1
- land_vector: float32 [192], replicated, may hold values from -4 to 4
- triple_weight: bfloat16 [192, 576], replicated, may hold values from -0.4375 to 0.4375
- project_weight: bfloat16 [192, 192], replicated, may hold values from -0.4375 to 0.4375
- up_weight: bfloat16 [192, 768], replicated, may hold values from -0.4375 to 0.4375
- down_weight: bfloat16 [768, 192], replicated, may hold values from -0.21875 to 0.21875
- earth_bias: float32 [4, 2, 6, 144, 23], P('lat'), may hold values from -5 to 5
Outputs:
- grad_tokens: bfloat16 [4, 24, 192, 192], P(None, 'lat', 'lon')
- grad_triple: float32 [192, 576], replicated
- grad_project: float32 [192, 192], replicated
- grad_up: float32 [192, 768], replicated
- grad_down: float32 [768, 192], replicated
- grad_land: float32 [192], replicated
The draws below stay inside these ranges and needn't reach their ends.
All inputs are finite; a program needn't handle non-finite values. No bound on the sum of `land_sea` on one device may be relied on, other than what follows from the above.
Results may differ from the reference program's by a relative error of at most 0.013.
Values may be sent and summed in bfloat16 or wider, within the bound.
No kernel may reach another device: no remote copies, remote signals or barrier semaphores. Data moves between devices by JAX's collectives and lax.ppermute only.
A program may use at most 128 MiB of HBM per device.

```python
import math
import jax
import jax.numpy as jnp
from jax import lax

C = 192
HEADS = 6
FF = 768
Z = 4
WZ = 2
WH = 6
WW = 12
ZW = 2
LAT = 24
LON = 192
LWG = 4
PAIRS = 144
RELW = 23


def with_ends(result, rng, smallest, high):
    longest = result.shape.index(max(result.shape))
    spots = []
    for shift in (0, 1):
        where = [jax.random.randint(jax.random.fold_in(rng, axis), (), 0, length) for axis, length in enumerate(result.shape)]
        where[longest] = (where[longest] + shift) % result.shape[longest]
        spots.append(tuple(where))
    return result.at[spots[0]].set(smallest).at[spots[1]].set(high)


def level_of(own_key, dims, split, least, largest):
    level, own = 1.0, jax.random.fold_in(own_key, 6)
    for axis_at, blocks in split:
        heights = jnp.exp(jax.random.uniform(jax.random.fold_in(own, axis_at), (blocks,), jnp.float32, least / len(split), largest / len(split)))
        level = level * jnp.repeat(heights, dims[axis_at] // blocks).reshape([-1 if axis == axis_at else 1 for axis in range(len(dims))])
    return level


def bell_draw(own_key, dims, width, most, split=(), held_as=jnp.bfloat16):
    array = jax.random.normal(own_key, dims, jnp.float32) * width
    if len(split) > 0:
        array = level_of(own_key, dims, split, -0.22, 0.18) * array
    return jnp.clip(array, min=-most, max=most).astype(held_as)


def setup_inputs(seed: int = 0) -> dict:
    keys = jax.random.split(jax.random.key(seed), 10)
    tokens = bell_draw(keys[0], (Z, LAT, LON, C), 1.0, 6.0, ((1, 4), (2, 8)))
    cotangent = bell_draw(keys[1], (Z, LAT, LON, C), 1.0, 6.0, ((1, 4), (2, 8)))
    land_sea = with_ends((jax.random.randint(keys[2], (LAT, LON), 0, 10) < 3).astype(jnp.int32), jax.random.fold_in(keys[2], 1), 0, 1)
    land_vector = bell_draw(keys[3], (C,), 1.0, 4.0, (), jnp.float32)
    triple_weight = bell_draw(keys[4], (C, 3 * C), C ** -0.5, 0.4375)
    project_weight = bell_draw(keys[5], (C, C), C ** -0.5, 0.4375)
    up_weight = bell_draw(keys[6], (C, FF), C ** -0.5, 0.4375)
    down_weight = bell_draw(keys[7], (FF, C), FF ** -0.5, 0.21875)
    earth_bias = bell_draw(keys[8], (LWG, ZW, HEADS, PAIRS, RELW), 1.0, 5.0, ((0, 4),), jnp.float32)
    return dict(tokens=tokens, cotangent=cotangent, land_sea=land_sea, land_vector=land_vector, triple_weight=triple_weight, project_weight=project_weight, up_weight=up_weight, down_weight=down_weight, earth_bias=earth_bias)


mask_fill = -10000.0
norm_eps = 1e-05
root_half = 0.7071067811865476
inv_root_tau = 0.3989422804014327

def product(pattern, left_op, right_op):
    return jnp.einsum(pattern, left_op.astype(jnp.float32), right_op.astype(jnp.float32))

def layer_norm(values_in):
    average = lax.optimization_barrier(jnp.mean(values_in, -1, keepdims=True))
    centred = values_in - average
    variance = lax.optimization_barrier(jnp.mean(centred * centred, -1, keepdims=True))
    spread = lax.rsqrt(variance + norm_eps)
    return (centred * spread, spread)

def norm_back(upstream, unit_vals, spread):
    first_mean = lax.optimization_barrier(jnp.mean(upstream, -1, keepdims=True))
    second_mean = lax.optimization_barrier(jnp.mean(upstream * unit_vals, -1, keepdims=True))
    return spread * (upstream - first_mean - unit_vals * second_mean)

def gelu_exact(values_in):
    return 0.5 * values_in * (1.0 + lax.erf(values_in * root_half))

def gelu_slope(values_in):
    return 0.5 * (1.0 + lax.erf(values_in * root_half)) + values_in * inv_root_tau * jnp.exp(-0.5 * values_in * values_in)

def expand_bias(table):
    width_w = (table.shape[-1] + 1) // 2
    places = jnp.arange(width_w, dtype=jnp.int32)
    offsets = places[:, None] - places[None, :] + width_w - 1
    onehot = (offsets[:, :, None] == jnp.arange(2 * width_w - 1, dtype=jnp.int32)[None, None, :]).astype(jnp.float32)
    expanded = jnp.einsum('...pr,uvr->...puv', table, onehot, precision=lax.Precision.HIGHEST)
    pair_side = math.isqrt(table.shape[-2])
    leading = table.shape[:-2]
    expanded = expanded.reshape(leading + (pair_side, pair_side, width_w, width_w))
    expanded = jnp.moveaxis(expanded, -2, -3)
    return expanded.reshape(leading + (pair_side * width_w, pair_side * width_w))

def make_bias(table, first_window):
    lat_windows = table.shape[0]
    level_windows = table.shape[1]
    expanded = jnp.transpose(expand_bias(table), (1, 0, 2, 3, 4))
    token_ids = jnp.arange(WZ * WH * WW, dtype=jnp.int32)
    level_pos = token_ids // (WH * WW)
    row_pos = token_ids // WW % WH
    level_flag = ((jnp.arange(level_windows, dtype=jnp.int32)[:, None, None] == 0) & (level_pos[None, None, :] < WZ // 2)).astype(jnp.int32)
    lat_index = first_window + jnp.arange(lat_windows, dtype=jnp.int32)
    pole_flag = ((lat_index[None, :, None] == 0) & (row_pos[None, None, :] < WH // 2)).astype(jnp.int32)
    region = level_flag * 2 + pole_flag
    blocked = jnp.where(region[..., :, None] == region[..., None, :], 0.0, mask_fill).astype(jnp.float32)
    return expanded + blocked[:, :, None]

def to_windows(field):
    levels, lat_rows, lon_cols, features = field.shape
    shaped = field.reshape(levels // WZ, WZ, lat_rows // WH, WH, lon_cols // WW, WW, features)
    shaped = shaped.transpose(0, 2, 4, 1, 3, 5, 6)
    return shaped.reshape(levels // WZ, lat_rows // WH, lon_cols // WW, WZ * WH * WW, features)

def from_windows(windows):
    level_w, lat_w, lon_w, token_count, features = windows.shape
    shaped = windows.reshape(level_w, lat_w, lon_w, WZ, WH, WW, features)
    shaped = shaped.transpose(0, 3, 1, 4, 2, 5, 6)
    return shaped.reshape(level_w * WZ, lat_w * WH, lon_w * WW, features)

def split_packed(window_block, bias_block, triple_weight):
    groups, members, token_count, features = window_block.shape
    head_count = bias_block.shape[-3]
    head_size = features // head_count
    packed = product('prtc,cf->prtf', window_block, triple_weight).astype(jnp.bfloat16)
    packed = packed.reshape(groups, members, token_count, 3, head_count, head_size)
    return (packed[:, :, :, 0], packed[:, :, :, 1], packed[:, :, :, 2], head_size)

def softmax_of(query, key_part, bias_block, head_size):
    scores = product('prqhd,prkhd->prhqk', query, key_part) * head_size ** (-0.5) + bias_block
    raised = jnp.exp(scores)
    return raised / lax.optimization_barrier(jnp.sum(raised, -1, keepdims=True))

def attend(window_block, bias_block, triple_weight, project_weight):
    groups, members, token_count, features = window_block.shape
    query, key_part, value_part, head_size = split_packed(window_block, bias_block, triple_weight)
    probs = softmax_of(query, key_part, bias_block, head_size)
    probs_b = probs.astype(jnp.bfloat16)
    mixed_heads = product('prhqk,prkhd->prqhd', probs_b, value_part).astype(jnp.bfloat16)
    mixed_heads = mixed_heads.reshape(groups, members, token_count, features)
    return product('prtc,cf->prtf', mixed_heads, project_weight).astype(jnp.bfloat16)

def attend_back(window_block, grad_block, bias_block, triple_weight, project_weight):
    groups, members, token_count, features = window_block.shape
    query, key_part, value_part, head_size = split_packed(window_block, bias_block, triple_weight)
    probs = softmax_of(query, key_part, bias_block, head_size)
    probs_b = probs.astype(jnp.bfloat16)
    mixed_heads = product('prhqk,prkhd->prqhd', probs_b, value_part).astype(jnp.bfloat16)
    mixed_flat = mixed_heads.reshape(groups, members, token_count, features)
    grad_project = product('prtc,prtf->cf', mixed_flat, grad_block)
    grad_mixed = product('prtf,cf->prtc', grad_block, project_weight).astype(jnp.bfloat16)
    grad_mixed = grad_mixed.reshape(mixed_heads.shape)
    grad_probs = product('prqhd,prkhd->prhqk', grad_mixed, value_part)
    grad_value = product('prhqk,prqhd->prkhd', probs_b, grad_mixed)
    grad_scores = probs * (grad_probs - lax.optimization_barrier(jnp.sum(grad_probs * probs, -1, keepdims=True)))
    grad_scaled = (grad_scores * head_size ** (-0.5)).astype(jnp.bfloat16)
    grad_query = product('prhqk,prkhd->prqhd', grad_scaled, key_part)
    grad_key = product('prhqk,prqhd->prkhd', grad_scaled, query)
    grad_packed = jnp.stack([grad_query, grad_key, grad_value], axis=3).astype(jnp.bfloat16)
    grad_packed = grad_packed.reshape(groups, members, token_count, 3 * features)
    grad_triple = product('prtc,prtf->cf', window_block, grad_packed)
    grad_window = product('prtf,cf->prtc', grad_packed, triple_weight).astype(jnp.bfloat16)
    return (grad_window, grad_triple, grad_project)

def mlp_back(summed_rows, cot_rows, up_weight, down_weight):
    unit2, spread2 = layer_norm(summed_rows)
    normed2 = unit2.astype(jnp.bfloat16)
    pre_act = product('mc,cf->mf', normed2, up_weight)
    activated = gelu_exact(pre_act).astype(jnp.bfloat16)
    hidden_grad = (product('mc,fc->mf', cot_rows, down_weight) * gelu_slope(pre_act)).astype(jnp.bfloat16)
    grad_down = product('mf,mc->fc', activated, cot_rows)
    grad_up = product('mc,mf->cf', normed2, hidden_grad)
    back_in = product('mf,cf->mc', hidden_grad, up_weight)
    grad_summed = cot_rows.astype(jnp.float32) + norm_back(back_in, unit2, spread2)
    return (grad_summed, grad_up, grad_down)

def reference(tokens, cotangent, land_sea, land_vector, triple_weight, project_weight, up_weight, down_weight, earth_bias):
    features = tokens.shape[-1]
    land_mask = land_sea.astype(jnp.float32)
    embedded = (tokens.astype(jnp.float32) + land_mask[None, :, :, None] * land_vector).astype(jnp.bfloat16)
    residual = embedded.astype(jnp.float32)
    unit_one, spread_one = layer_norm(residual)
    normed = unit_one.astype(jnp.bfloat16)
    shifted = jnp.roll(normed, (WZ // 2, WH // 2, WW // 2), axis=(0, 1, 2))
    biases = make_bias(earth_bias, 0)
    windows = to_windows(shifted)
    level_w, lat_w, lon_w, token_count, _ = windows.shape
    head_count = biases.shape[2]
    flat_windows = windows.reshape(level_w * lat_w, 1, lon_w, token_count, features)
    flat_biases = biases.reshape(level_w * lat_w, 1, 1, head_count, token_count, token_count)

    def forward_step(element):
        return attend(element[0], element[1], triple_weight, project_weight)
    branch = lax.map(forward_step, (flat_windows, flat_biases))
    branch = from_windows(branch.reshape(windows.shape))
    attended = jnp.roll(branch, (-(WZ // 2), -(WH // 2), -(WW // 2)), axis=(0, 1, 2))
    summed = residual + attended.astype(jnp.float32)

    def level_step(totals, element):
        summed_level, cot_level = element
        grad_mix, grad_up_part, grad_down_part = mlp_back(summed_level.reshape(-1, features), cot_level.reshape(-1, features), up_weight, down_weight)
        return ((totals[0] + grad_up_part, totals[1] + grad_down_part), grad_mix.reshape(summed_level.shape))
    mlp_init = (jnp.zeros(up_weight.shape, jnp.float32), jnp.zeros(down_weight.shape, jnp.float32))
    mlp_totals, grad_summed = lax.scan(level_step, mlp_init, (summed, cotangent))
    grad_attended = grad_summed.astype(jnp.bfloat16)
    grad_branch = jnp.roll(grad_attended, (WZ // 2, WH // 2, WW // 2), axis=(0, 1, 2))
    flat_grads = to_windows(grad_branch).reshape(flat_windows.shape)

    def backward_step(totals, element):
        grad_window, grad_triple_part, grad_project_part = attend_back(element[0], element[1], element[2], triple_weight, project_weight)
        return ((totals[0] + grad_triple_part, totals[1] + grad_project_part), grad_window)
    attn_init = (jnp.zeros(triple_weight.shape, jnp.float32), jnp.zeros(project_weight.shape, jnp.float32))
    attn_totals, grad_windows = lax.scan(backward_step, attn_init, (flat_windows, flat_grads, flat_biases))
    grad_shifted = from_windows(grad_windows.reshape(windows.shape))
    grad_normed = jnp.roll(grad_shifted, (-(WZ // 2), -(WH // 2), -(WW // 2)), axis=(0, 1, 2))
    grad_embedded = grad_summed + norm_back(grad_normed.astype(jnp.float32), unit_one, spread_one)
    grad_tokens = grad_embedded.astype(jnp.bfloat16)
    grad_land = product('zilc,il->c', grad_tokens, land_sea)
    return (grad_tokens, attn_totals[0], attn_totals[1], mlp_totals[0], mlp_totals[1], grad_land)
```

```python
import functools
import math

import jax
import jax.numpy as jnp
import numpy as np
from jax import lax
from jax.experimental import pallas as pl
from jax.experimental.pallas import tpu as pltpu
from jax.sharding import PartitionSpec as P

Z = 4
WZ = 2
WH = 6
WW = 12
C = 192
HEADS = 6
HEAD = 32
FF = 768
HZ, HH, HW = WZ // 2, WH // 2, WW // 2
TOK = WZ * WH * WW
PLACES = WZ * WH
RELW = 2 * WW - 1
STRIP = -(-RELW * PLACES // 128) * 128

mask_fill = -10000.0
norm_eps = 1e-05
log2e = 1.4426950408889634
root_half = 0.7071067811865476
inv_root_tau = 0.3989422804014327
score_scale = HEAD**-0.5

f32 = jnp.float32
bf16 = jnp.bfloat16
MIB = 1 << 20


def mm(a, b):
    return lax.dot_general(a, b, (((1,), (0,)), ((), ())), preferred_element_type=f32)


def mm_nt(a, b):
    return lax.dot_general(a, b, (((1,), (1,)), ((), ())), preferred_element_type=f32)


def mm_tn(a, b):
    return lax.dot_general(a, b, (((0,), (0,)), ((), ())), preferred_element_type=f32)


def unit_norm(values):
    average = jnp.mean(values, -1, keepdims=True)
    centred = values - average
    variance = jnp.mean(centred * centred, -1, keepdims=True)
    spread = lax.rsqrt(variance + norm_eps)
    return centred * spread, spread


def norm_back(upstream, unit, spread):
    first = jnp.mean(upstream, -1, keepdims=True)
    second = jnp.mean(upstream * unit, -1, keepdims=True)
    return spread * (upstream - first - unit * second)


def piece_rows(rows, cols):
    home = np.arange(Z * rows * cols).reshape(Z, rows, cols)
    top, low = slice(0, rows - HH), slice(rows - HH, rows)
    west, east = slice(0, cols - HW), slice(cols - HW, cols)
    parts = [home[:, top, west], home[:, low, west], home[:, top, east], home[:, low, east]]
    return [part.reshape(-1) for part in parts]


def window_rows(rows, cols):
    sizes = [part.size for part in piece_rows(rows, cols)]
    starts = np.cumsum([0] + sizes)
    own, north, side, corner = [np.arange(starts[k], starts[k + 1]) for k in range(4)]
    frame = np.zeros((Z, rows, cols), np.int64)
    frame[:, HH:, HW:] = own.reshape(Z, rows - HH, cols - HW)
    frame[:, :HH, HW:] = north.reshape(Z, HH, cols - HW)
    frame[:, HH:, :HW] = side.reshape(Z, rows - HH, HW)
    frame[:, :HH, :HW] = corner.reshape(Z, HH, HW)
    frame = np.roll(frame, HZ, axis=0)
    frame = frame.reshape(Z // WZ, WZ, rows // WH, WH, cols // WW, WW)
    return frame.transpose(0, 2, 4, 5, 1, 3).reshape(-1)


def one_hot(places):
    table = np.zeros((places.size, places.size), np.float32)
    table[np.arange(places.size), places] = 1.0
    return table


def vmem(count):
    return [pl.BlockSpec(memory_space=pltpu.VMEM)] * count


smem = pl.BlockSpec(memory_space=pltpu.SMEM)


def shape(dims, dtype):
    return jax.ShapeDtypeStruct(dims, dtype)


def cost(flops, moved):
    return pl.CostEstimate(flops=flops, bytes_accessed=moved, transcendentals=0)


def land_column(land_ref, rows, cols):
    eye = (
        lax.broadcasted_iota(jnp.int32, (cols, cols), 0)
        == lax.broadcasted_iota(jnp.int32, (cols, cols), 1)
    ).astype(f32)
    land = land_ref[...].astype(f32)
    parts = [jnp.sum(eye * land[i : i + 1, :], -1, keepdims=True) for i in range(rows)]
    return jnp.concatenate(parts, axis=0)


def pack_kernel(rows, cols, tokens_ref, cot_ref, land_ref, vec_ref, perm_ref, *outs):
    column = land_column(land_ref, rows, cols)
    added = column * vec_ref[...]
    added = jnp.concatenate([added] * Z, axis=0)
    embedded = (tokens_ref[...].astype(f32) + added).astype(bf16)
    left = mm(perm_ref[...], embedded)
    right = mm(perm_ref[...], cot_ref[...])
    packed = jnp.concatenate([left, right], axis=1)
    start = 0
    for out in outs:
        out[...] = packed[start : start + out.shape[0]].astype(bf16)
        start += out.shape[0]


def pack(tokens, cotangent, land_sea, vector, rows, cols):
    parts = piece_rows(rows, cols)
    perm = jnp.asarray(one_hot(np.concatenate(parts)), bf16)
    count = Z * rows * cols
    return pl.pallas_call(
        functools.partial(pack_kernel, rows, cols),
        out_shape=[shape((part.size, 2 * C), bf16) for part in parts],
        in_specs=vmem(5),
        out_specs=vmem(4),
        compiler_params=pltpu.CompilerParams(vmem_limit_bytes=32 * MIB),
        cost_estimate=cost(4 * count * count * C, 4 * MIB),
        name="pack",
    )(tokens.reshape(count, C), cotangent.reshape(count, C), land_sea, vector.reshape(1, C), perm)


def bias_kernel(groups, pole_ref, table_ref, spread_ref, place_ref, rowlab_ref, lanelab_ref, out_ref, *wide_refs):
    table = table_ref[...]
    high = table.astype(bf16)
    rest = table - high.astype(f32)
    middle = rest.astype(bf16)
    low = (rest - middle.astype(f32)).astype(bf16)
    onehot = spread_ref[...]
    wide = mm(high, onehot) + mm(middle, onehot) + mm(low, onehot)
    strips = groups * PLACES
    parts = []
    for n in range(STRIP // 128):
        lanes = slice(n * 128, (n + 1) * 128)
        wide_ref = wide_refs[n]
        wide_ref[...] = wide[:, lanes]
        place = place_ref[:, lanes]
        part = jnp.zeros((strips, 128), f32)
        for p in range(PLACES):
            part = jnp.where(place == p, wide_ref[pl.ds(p, strips, stride=PLACES), :], part)
        parts.append(part)
    strip = jnp.concatenate(parts, axis=1)
    pole = pole_ref[0].astype(f32)
    rowlab = rowlab_ref[...]
    lanelab = lanelab_ref[...]
    differs = jnp.maximum(
        rowlab[:, 2:3] * jnp.abs(rowlab[:, 0:1] - lanelab[0:1, :]),
        pole * jnp.abs(rowlab[:, 1:2] - lanelab[1:2, :]),
    )
    strip = (strip + mask_fill * differs) * log2e
    for w in range(WW):
        start = (WW - 1 - w) * PLACES
        part = strip[:, start : start + TOK]
        for g in range(groups):
            out_ref[g, w * PLACES : (w + 1) * PLACES, :] = part[g * PLACES : (g + 1) * PLACES, :]


def expand_bias(table, pole):
    levels = table.shape[1]
    groups = levels * HEADS
    flat = table.reshape(groups * PLACES * PLACES, RELW)
    onehot = np.zeros((RELW, STRIP), np.float32)
    for r in range(RELW):
        onehot[RELW - 1 - r, r * PLACES : (r + 1) * PLACES] = 1.0
    place = (np.arange(STRIP) % PLACES).astype(np.int32)[None]
    level_label = (np.arange(PLACES) // WH < HZ).astype(np.float32)
    lat_label = (np.arange(PLACES) % WH < HH).astype(np.float32)
    rowlab = np.zeros((groups, PLACES, 3), np.float32)
    rowlab[:, :, 0] = level_label
    rowlab[:, :, 1] = lat_label
    rowlab[:HEADS, :, 2] = 1.0
    lanelab = np.zeros((2, STRIP), np.float32)
    lanelab[:, : RELW * PLACES] = np.stack([np.tile(level_label, RELW), np.tile(lat_label, RELW)])
    return pl.pallas_call(
        functools.partial(bias_kernel, groups),
        out_shape=shape((groups, TOK, TOK), f32),
        in_specs=[smem] + vmem(5),
        out_specs=vmem(1)[0],
        scratch_shapes=[pltpu.VMEM((groups * PLACES * PLACES, 128), f32)] * (STRIP // 128),
        compiler_params=pltpu.CompilerParams(vmem_limit_bytes=32 * MIB),
        cost_estimate=cost(10**9, 8 * MIB),
        name="bias",
    )(pole, flat, jnp.asarray(onehot, bf16), jnp.asarray(place), jnp.asarray(rowlab.reshape(-1, 3)), jnp.asarray(lanelab))


def head_masks(count):
    lane = lax.broadcasted_iota(jnp.int32, (count, C), 1)
    return [((lane >= h * HEAD) & (lane < (h + 1) * HEAD)).astype(f32) for h in range(HEADS)]


def stacked(values, masks):
    return jnp.concatenate([values * mask for mask in masks], axis=0)


def head_sum(values, masks):
    total = values[:TOK] * masks[0]
    for h in range(1, HEADS):
        total = total + values[h * TOK : (h + 1) * TOK] * masks[h]
    return total


def relative_chunks(rank, scratch, outs, part_rows):
    stretches = scratch.shape[0] // C
    for d, out in enumerate(outs):
        who = jnp.bitwise_xor(rank, d)
        pieces = []
        for s in range(stretches):
            start = pl.multiple_of(s * C + who * part_rows, 8)
            pieces.append(scratch[pl.ds(start, part_rows), :])
        whole = pieces[0] if stretches == 1 else jnp.concatenate(pieces, axis=0)
        out[...] = whole.astype(out.dtype)


def forward_kernel(
    windows, lon_windows, rank_ref,
    own_ref, north_ref, side_ref, corner_ref, perm_ref, bias_ref, triple_ref, project_ref, up_ref, down_ref,
    q_ref, k_ref, v_ref, p_ref, mixed_ref, normed_ref, unit_ref, spread_ref, gsum_ref, *rest,
):
    chunks, (branch_ref, cot_ref, emb_ref, total_ref) = rest[:-4], rest[-4:]
    pieces = [ref[...].astype(f32) for ref in (own_ref, north_ref, side_ref, corner_ref)]
    pieces = jnp.concatenate(pieces, axis=0).astype(bf16)
    ordered = mm(perm_ref[...], pieces)
    emb = ordered[:, :C]
    emb_ref[...] = emb
    cot_ref[...] = ordered[:, C:].astype(bf16)
    unit, spread = unit_norm(emb)
    unit_ref[...] = unit
    spread_ref[...] = spread
    normed = unit.astype(bf16)
    normed_ref[...] = normed
    packed = mm(normed, triple_ref[...])
    q_ref[...] = packed[:, :C].astype(bf16)
    k_ref[...] = packed[:, C : 2 * C].astype(bf16)
    v_ref[...] = packed[:, 2 * C :].astype(bf16)
    masks = head_masks(TOK)
    masks_b = [mask.astype(bf16) for mask in masks]

    def window_step(w, carry):
        rows = pl.ds(pl.multiple_of(w * TOK, TOK), TOK)
        level = w // lon_windows
        scores = mm_nt(stacked(q_ref[rows, :], masks_b), k_ref[rows, :])
        bias = bias_ref[pl.ds(level * HEADS, HEADS)].reshape(HEADS * TOK, TOK)
        raised = jnp.exp2(scores * (score_scale * log2e) + bias)
        probs = raised * (1.0 / jnp.sum(raised, -1, keepdims=True))
        probs_b = probs.astype(bf16)
        p_ref[pl.ds(w * HEADS, HEADS)] = probs_b.reshape(HEADS, TOK, TOK)
        mixed = head_sum(mm(probs_b, v_ref[rows, :]), masks).astype(bf16)
        mixed_ref[rows, :] = mixed
        branch_ref[rows, :] = mm(mixed, project_ref[...])
        return carry

    lax.fori_loop(0, windows, window_step, 0)

    attended = branch_ref[...].astype(bf16).astype(f32)
    unit2, spread2 = unit_norm(emb_ref[...] + attended)
    normed2 = unit2.astype(bf16)
    cot = cot_ref[...]
    back = jnp.zeros(unit2.shape, f32)
    block = 256
    for start in range(0, FF, block):
        cols = slice(start, start + block)
        up_part = up_ref[:, cols]
        pre = mm(normed2, up_part)
        upstream = mm_nt(cot, down_ref[cols, :])
        phi = 0.5 * (1.0 + lax.erf(pre * root_half))
        activated = (pre * phi).astype(bf16)
        slope = phi + pre * inv_root_tau * jnp.exp2(pre * pre * (-0.5 * log2e))
        hidden = (upstream * slope).astype(bf16)
        total_ref[0:C, cols] = mm_tn(normed2, hidden)
        total_ref[C : 2 * C, cols] = mm_tn(cot, activated)
        back = back + mm_nt(hidden, up_part)
    gsum_ref[...] = cot.astype(f32) + norm_back(back, unit2, spread2)
    relative_chunks(rank_ref[0], total_ref, chunks, C // len(chunks))


def forward(rank, pieces, perm, bias, triple, project, up, down, group, lon_windows):
    count = perm.shape[0]
    windows = count // TOK
    out_shape = [
        shape((count, C), bf16),
        shape((count, C), bf16),
        shape((count, C), bf16),
        shape((windows * HEADS, TOK, TOK), bf16),
        shape((count, C), bf16),
        shape((count, C), bf16),
        shape((count, C), f32),
        shape((count, 1), f32),
        shape((count, C), f32),
    ] + [shape((2 * C // group, FF), bf16)] * group
    return pl.pallas_call(
        functools.partial(forward_kernel, windows, lon_windows),
        out_shape=out_shape,
        in_specs=[smem] + vmem(10),
        out_specs=vmem(len(out_shape)),
        scratch_shapes=[
            pltpu.VMEM((count, C), f32),
            pltpu.VMEM((count, C), bf16),
            pltpu.VMEM((count, C), f32),
            pltpu.VMEM((2 * C, FF), f32),
        ],
        compiler_params=pltpu.CompilerParams(vmem_limit_bytes=48 * MIB),
        cost_estimate=cost(3 * 10**9, 16 * MIB),
        name="forward",
    )(rank, *pieces, perm, bias, triple, project, up, down)


def backward_kernel(
    windows, sizes, rank_ref,
    q_ref, k_ref, v_ref, p_ref, mixed_ref, normed_ref, unit_ref, spread_ref, gsum_ref, perm_ref, triple_ref, project_ref,
    *rest,
):
    outs, chunks = rest[: len(sizes)], rest[len(sizes) : -4]
    gq_ref, gk_ref, gv_ref, total_ref = rest[-4:]
    masks = head_masks(TOK)
    masks_b = [mask.astype(bf16) for mask in masks]

    def window_step(w, carry):
        rows = pl.ds(pl.multiple_of(w * TOK, TOK), TOK)
        grad = gsum_ref[rows, :].astype(bf16)
        grad_mixed = mm_nt(grad, project_ref[...])
        grad_mixed_b = grad_mixed.astype(bf16)
        probs_b = p_ref[pl.ds(w * HEADS, HEADS)].reshape(HEADS * TOK, TOK)
        probs = probs_b.astype(f32)
        grad_probs = mm_nt(stacked(grad_mixed_b, masks_b), v_ref[rows, :])
        inner = jnp.sum(grad_probs * probs, -1, keepdims=True)
        scaled = (probs * (grad_probs - inner) * score_scale).astype(bf16)
        grad_q = head_sum(mm(scaled, k_ref[rows, :]), masks)
        grad_mixed_t = grad_mixed_b.astype(f32).T.astype(bf16)
        query_t = q_ref[rows, :].astype(f32).T.astype(bf16)
        grad_k, grad_v = [], []
        for h in range(HEADS):
            spot = slice(h * HEAD, (h + 1) * HEAD)
            span = slice(h * TOK, (h + 1) * TOK)
            grad_k.append(mm(query_t[spot], scaled[span]))
            grad_v.append(mm(grad_mixed_t[spot], probs_b[span]))
        gq_ref[rows, :] = grad_q.astype(bf16)
        gk_ref[rows, :] = jnp.concatenate(grad_k, axis=0).T.astype(bf16)
        gv_ref[rows, :] = jnp.concatenate(grad_v, axis=0).T.astype(bf16)
        return carry

    lax.fori_loop(0, windows, window_step, 0)

    grad_packed = [gq_ref[...], gk_ref[...], gv_ref[...]]
    normed = normed_ref[...]
    triple = triple_ref[...]
    grad_normed = jnp.zeros(unit_ref.shape, f32)
    parts = []
    for n, grad in enumerate(grad_packed):
        grad_normed = grad_normed + mm_nt(grad, triple[:, n * C : (n + 1) * C])
        parts.append(mm_tn(normed, grad))
    parts.append(mm_tn(mixed_ref[...], gsum_ref[...].astype(bf16)))
    total_ref[...] = jnp.concatenate(parts, axis=1)
    grad_normed = grad_normed.astype(bf16).astype(f32)
    grad_tokens = gsum_ref[...] + norm_back(grad_normed, unit_ref[...], spread_ref[...])
    pieces = mm(perm_ref[...], grad_tokens.astype(bf16))
    start = 0
    for out in outs:
        out[...] = pieces[start : start + out.shape[0]].astype(bf16)
        start += out.shape[0]
    relative_chunks(rank_ref[0], total_ref, chunks, C // len(chunks))


def backward(rank, saved, perm, triple, project, sizes, group):
    count = perm.shape[0]
    windows = count // TOK
    out_shape = [shape((size, C), bf16) for size in sizes] + [shape((C // group, FF), bf16)] * group
    return pl.pallas_call(
        functools.partial(backward_kernel, windows, sizes),
        out_shape=out_shape,
        in_specs=[smem] + vmem(12),
        out_specs=vmem(len(out_shape)),
        scratch_shapes=[pltpu.VMEM((count, C), bf16)] * 3 + [pltpu.VMEM((C, FF), f32)],
        compiler_params=pltpu.CompilerParams(vmem_limit_bytes=48 * MIB),
        cost_estimate=cost(3 * 10**9, 16 * MIB),
        name="backward",
    )(rank, *saved, perm, triple, project)


def home_kernel(rows, cols, own_ref, north_ref, side_ref, corner_ref, perm_ref, land_ref, out_ref, sum_ref):
    pieces = [ref[...].astype(f32) for ref in (own_ref, north_ref, side_ref, corner_ref)]
    pieces = jnp.concatenate(pieces, axis=0).astype(bf16)
    grads = mm(perm_ref[...], pieces)
    out_ref[...] = grads.astype(bf16)
    column = land_column(land_ref, rows, cols)
    column = jnp.concatenate([column] * Z, axis=0)
    sum_ref[...] = jnp.broadcast_to(jnp.sum(grads * column, 0, keepdims=True), sum_ref.shape)


def to_home(pieces, land_sea, rows, cols):
    count = Z * rows * cols
    perm = jnp.asarray(one_hot(np.concatenate(piece_rows(rows, cols))).T, bf16)
    return pl.pallas_call(
        functools.partial(home_kernel, rows, cols),
        out_shape=[shape((count, C), bf16), shape((8, C), f32)],
        in_specs=vmem(6),
        out_specs=vmem(2),
        compiler_params=pltpu.CompilerParams(vmem_limit_bytes=32 * MIB),
        cost_estimate=cost(2 * count * count * C, 4 * MIB),
        name="to_home",
    )(*pieces, perm, land_sea)


def add_kernel(lists, *refs):
    ins, outs = refs[: sum(lists)], refs[sum(lists) :]
    start = 0
    for count, out in zip(lists, outs):
        total = ins[start][...].astype(f32)
        for ref in ins[start + 1 : start + count]:
            total = total + ref[...].astype(f32)
        out[...] = total.astype(out.dtype)
        start += count


def add_up(*groups):
    lists = [len(group) for group in groups]
    return pl.pallas_call(
        functools.partial(add_kernel, lists),
        out_shape=[shape(group[0].shape, group[0].dtype) for group in groups],
        in_specs=vmem(sum(lists)),
        out_specs=vmem(len(groups)),
        compiler_params=pltpu.CompilerParams(vmem_limit_bytes=32 * MIB),
        cost_estimate=cost(10**6, 2 * MIB),
        name="add_up",
    )(*[array for group in groups for array in group])


def finish_kernel(group, rank_ref, *refs):
    attn, mlp, land = refs[:group], refs[group : 2 * group], refs[2 * group : 3 * group]
    triple_ref, project_ref, up_ref, down_ref, land_ref, wide_ref, tall_ref = refs[3 * group :]
    part = C // group
    total = land[0][...]
    for ref in land[1:]:
        total = total + ref[...]
    land_ref[...] = total[0:1]
    for d in range(group):
        who = jnp.bitwise_xor(rank_ref[0], d)
        rows = pl.ds(pl.multiple_of(who * part, 8), part)
        wide_ref[rows, :] = attn[d][...].astype(f32)
        both = mlp[d][...].astype(f32)
        up_ref[rows, :] = both[:part]
        tall_ref[rows, :] = both[part:]
    triple_ref[...] = wide_ref[:, : 3 * C]
    project_ref[...] = wide_ref[:, 3 * C :]
    down_ref[...] = tall_ref[...].T


def finish(rank, attn, mlp, land):
    group = len(attn)
    return pl.pallas_call(
        functools.partial(finish_kernel, group),
        out_shape=[shape((C, 3 * C), f32), shape((C, C), f32), shape((C, FF), f32), shape((FF, C), f32), shape((1, C), f32)],
        in_specs=[smem] + vmem(3 * group),
        out_specs=vmem(5),
        scratch_shapes=[pltpu.VMEM((C, FF), f32)] * 2,
        compiler_params=pltpu.CompilerParams(vmem_limit_bytes=32 * MIB),
        cost_estimate=cost(10**6, 8 * MIB),
        name="finish",
    )(rank, *attn, *mlp, *land)


AXES = ("lon", "lat")


def send(value, lon_count, lat_count, move):
    pairs = []
    for lon in range(lon_count):
        for lat in range(lat_count):
            to_lon, to_lat = move(lon, lat)
            pairs.append((lon * lat_count + lat, (to_lon % lon_count) * lat_count + to_lat % lat_count))
    return lax.ppermute(value, AXES, pairs)


def near_move(distance):
    return lambda lon, lat: (lon ^ (distance // 4), lat ^ (distance % 4))


def far_move(distance):
    return lambda lon, lat: (lon ^ (2 * distance), lat)


def body(
    lon_count, lat_count,
    tokens, cotangent, land_sea, land_vector, triple_weight, project_weight, up_weight, down_weight, earth_bias,
):
    levels, rows, cols, features = tokens.shape
    shift = functools.partial(send, lon_count=lon_count, lat_count=lat_count)
    lon_at, lat_at = lax.axis_index("lon"), lax.axis_index("lat")
    group = 2 * lat_count
    rank = (lat_at + lat_count * (lon_at % 2)).astype(jnp.int32).reshape(1)
    pole = (lat_at == 0).astype(jnp.int32).reshape(1)
    lon_windows = cols // WW

    own, north, side, corner = pack(tokens, cotangent, land_sea, land_vector, rows, cols)
    north = shift(north, move=lambda lon, lat: (lon, lat + 1))
    side = shift(side, move=lambda lon, lat: (lon + 1, lat))
    corner = shift(corner, move=lambda lon, lat: (lon + 1, lat + 1))
    bias = expand_bias(earth_bias, pole)

    places = one_hot(window_rows(rows, cols))
    sizes = [part.size for part in piece_rows(rows, cols)]
    results = forward(
        rank, (own, north, side, corner), jnp.asarray(places, bf16), bias,
        triple_weight, project_weight, up_weight, down_weight, group, lon_windows,
    )
    saved, mlp_parts = results[:9], results[9:]
    mlp_parts = [mlp_parts[0]] + [shift(mlp_parts[d], move=near_move(d)) for d in range(1, group)]

    results = backward(rank, saved, jnp.asarray(places.T, bf16), triple_weight, project_weight, sizes, group)
    (own, north, side, corner), attn_parts = results[:4], results[4:]
    north = shift(north, move=lambda lon, lat: (lon, lat - 1))
    side = shift(side, move=lambda lon, lat: (lon - 1, lat))
    corner = shift(corner, move=lambda lon, lat: (lon - 1, lat - 1))
    attn_parts = [attn_parts[0]] + [shift(attn_parts[d], move=near_move(d)) for d in range(1, group)]

    grad_tokens, land = to_home((own, north, side, corner), land_sea, rows, cols)
    attn, mlp = add_up(attn_parts, mlp_parts)
    reach = 1
    while reach < lon_count // 2:
        steps = min(4, lon_count // 2 // reach)
        moves = [far_move(reach * d) for d in range(1, steps)]
        attn, mlp, land = add_up(
            *[[value] + [shift(value, move=move) for move in moves] for value in (attn, mlp, land)]
        )
        reach *= steps
    moves = [near_move(d) for d in range(1, group)]
    attn, mlp, land = [[value] + [shift(value, move=move) for move in moves] for value in (attn, mlp, land)]
    triple, project, up, down, land = finish(rank, attn, mlp, land)
    return grad_tokens.reshape(tokens.shape), triple, project, up, down, land.reshape(features)


def solution(mesh):
    return jax.shard_map(
        functools.partial(body, mesh.shape["lon"], mesh.shape["lat"]),
        mesh=mesh,
        in_specs=(
            P(None, "lat", "lon", None),
            P(None, "lat", "lon", None),
            P("lat", "lon"),
            P(),
            P(),
            P(),
            P(),
            P(),
            P("lat", None, None, None, None),
        ),
        out_specs=(P(None, "lat", "lon", None), P(), P(), P(), P(), P()),
        check_vma=False,
    )
```

```python
import functools
import math

import jax
import jax.numpy as jnp
import numpy as np
from jax import lax
from jax.experimental import pallas as pl
from jax.experimental.pallas import tpu as pltpu
from jax.sharding import PartitionSpec as P

Z = 4
WZ = 2
WH = 6
WW = 12
C = 192
HEADS = 6
HEAD = 32
FF = 768
HZ, HH, HW = WZ // 2, WH // 2, WW // 2
TOK = WZ * WH * WW
PLACES = WZ * WH
RELW = 2 * WW - 1
STRIP = -(-RELW * PLACES // 128) * 128

mask_fill = -10000.0
norm_eps = 1e-05
log2e = 1.4426950408889634
root_half = 0.7071067811865476
inv_root_tau = 0.3989422804014327
score_scale = HEAD**-0.5

f32 = jnp.float32
bf16 = jnp.bfloat16
MIB = 1 << 20

QUADS = 4
PART = C // (2 * QUADS)
CHUNK = 3 * PART
FULL = CHUNK + 8


def mm(a, b):
    return lax.dot_general(a, b, (((1,), (0,)), ((), ())), preferred_element_type=f32)


def mm_nt(a, b):
    return lax.dot_general(a, b, (((1,), (1,)), ((), ())), preferred_element_type=f32)


def mm_tn(a, b):
    return lax.dot_general(a, b, (((0,), (0,)), ((), ())), preferred_element_type=f32)


def unit_norm(values):
    average = jnp.mean(values, -1, keepdims=True)
    centred = values - average
    variance = jnp.mean(centred * centred, -1, keepdims=True)
    spread = lax.rsqrt(variance + norm_eps)
    return centred * spread, spread


def norm_back(upstream, unit, spread):
    first = jnp.mean(upstream, -1, keepdims=True)
    second = jnp.mean(upstream * unit, -1, keepdims=True)
    return spread * (upstream - first - unit * second)


def piece_rows(rows, cols):
    home = np.arange(Z * rows * cols).reshape(Z, rows, cols)
    top, low = slice(0, rows - HH), slice(rows - HH, rows)
    west, east = slice(0, cols - HW), slice(cols - HW, cols)
    parts = [home[:, top, west], home[:, low, west], home[:, top, east], home[:, low, east]]
    return [part.reshape(-1) for part in parts]


def window_rows(rows, cols):
    sizes = [part.size for part in piece_rows(rows, cols)]
    starts = np.cumsum([0] + sizes)
    own, north, side, corner = [np.arange(starts[k], starts[k + 1]) for k in range(4)]
    frame = np.zeros((Z, rows, cols), np.int64)
    frame[:, HH:, HW:] = own.reshape(Z, rows - HH, cols - HW)
    frame[:, :HH, HW:] = north.reshape(Z, HH, cols - HW)
    frame[:, HH:, :HW] = side.reshape(Z, rows - HH, HW)
    frame[:, :HH, :HW] = corner.reshape(Z, HH, HW)
    frame = np.roll(frame, HZ, axis=0)
    frame = frame.reshape(Z // WZ, WZ, rows // WH, WH, cols // WW, WW)
    return frame.transpose(0, 2, 4, 5, 1, 3).reshape(-1)


def spots(places):
    return jnp.asarray(np.argsort(places).astype(np.int32)[None])


def one_hot(spot_ref):
    count = spot_ref.shape[1]
    rows = lax.broadcasted_iota(jnp.int32, (count, count), 0)
    return (rows == spot_ref[...]).astype(f32).astype(bf16)


def vmem(count):
    return [pl.BlockSpec(memory_space=pltpu.VMEM)] * count


smem = pl.BlockSpec(memory_space=pltpu.SMEM)


def shape(dims, dtype):
    return jax.ShapeDtypeStruct(dims, dtype)


def cost(flops, moved):
    return pl.CostEstimate(flops=flops, bytes_accessed=moved, transcendentals=0)


def land_column(land_ref, rows, cols):
    eye = (
        lax.broadcasted_iota(jnp.int32, (cols, cols), 0)
        == lax.broadcasted_iota(jnp.int32, (cols, cols), 1)
    ).astype(f32)
    land = land_ref[...].astype(f32)
    parts = [jnp.sum(eye * land[i : i + 1, :], -1, keepdims=True) for i in range(rows)]
    return jnp.concatenate(parts, axis=0)


def pack_kernel(rows, cols, tokens_ref, cot_ref, land_ref, vec_ref, perm_ref, *outs):
    column = land_column(land_ref, rows, cols)
    added = column * vec_ref[...]
    added = jnp.concatenate([added] * Z, axis=0)
    embedded = (tokens_ref[...].astype(f32) + added).astype(bf16)
    perm = one_hot(perm_ref)
    left = mm(perm, embedded)
    right = mm(perm, cot_ref[...])
    packed = jnp.concatenate([left, right], axis=1)
    start = 0
    for out in outs:
        out[...] = packed[start : start + out.shape[0]].astype(bf16)
        start += out.shape[0]


def pack(tokens, cotangent, land_sea, vector, rows, cols):
    parts = piece_rows(rows, cols)
    perm = spots(np.concatenate(parts))
    count = Z * rows * cols
    return pl.pallas_call(
        functools.partial(pack_kernel, rows, cols),
        out_shape=[shape((part.size, 2 * C), bf16) for part in parts],
        in_specs=vmem(5),
        out_specs=vmem(4),
        cost_estimate=cost(4 * count * count * C, 4 * MIB),
        name="pack",
    )(tokens.reshape(count, C), cotangent.reshape(count, C), land_sea, vector.reshape(1, C), perm)


def bias_kernel(groups, pole_ref, table_ref, spread_ref, place_ref, rowlab_ref, lanelab_ref, out_ref, *wide_refs):
    table = table_ref[...]
    high = table.astype(bf16)
    rest = table - high.astype(f32)
    middle = rest.astype(bf16)
    low = (rest - middle.astype(f32)).astype(bf16)
    onehot = spread_ref[...]
    wide = mm(high, onehot) + mm(middle, onehot) + mm(low, onehot)
    strips = groups * PLACES
    parts = []
    for n in range(STRIP // 128):
        lanes = slice(n * 128, (n + 1) * 128)
        wide_ref = wide_refs[n]
        wide_ref[...] = wide[:, lanes]
        place = place_ref[:, lanes]
        part = jnp.zeros((strips, 128), f32)
        for p in range(PLACES):
            part = jnp.where(place == p, wide_ref[pl.ds(p, strips, stride=PLACES), :], part)
        parts.append(part)
    strip = jnp.concatenate(parts, axis=1)
    pole = pole_ref[0].astype(f32)
    rowlab = rowlab_ref[...]
    lanelab = lanelab_ref[...]
    differs = jnp.maximum(
        rowlab[:, 2:3] * jnp.abs(rowlab[:, 0:1] - lanelab[0:1, :]),
        pole * jnp.abs(rowlab[:, 1:2] - lanelab[1:2, :]),
    )
    strip = (strip + mask_fill * differs) * log2e
    for w in range(WW):
        start = (WW - 1 - w) * PLACES
        part = strip[:, start : start + TOK]
        for g in range(groups):
            out_ref[g, w * PLACES : (w + 1) * PLACES, :] = part[g * PLACES : (g + 1) * PLACES, :]


def expand_bias(table, pole):
    levels = table.shape[1]
    groups = levels * HEADS
    flat = table.reshape(groups * PLACES * PLACES, RELW)
    onehot = np.zeros((RELW, STRIP), np.float32)
    for r in range(RELW):
        onehot[RELW - 1 - r, r * PLACES : (r + 1) * PLACES] = 1.0
    place = (np.arange(STRIP) % PLACES).astype(np.int32)[None]
    level_label = (np.arange(PLACES) // WH < HZ).astype(np.float32)
    lat_label = (np.arange(PLACES) % WH < HH).astype(np.float32)
    rowlab = np.zeros((groups, PLACES, 3), np.float32)
    rowlab[:, :, 0] = level_label
    rowlab[:, :, 1] = lat_label
    rowlab[:HEADS, :, 2] = 1.0
    lanelab = np.zeros((2, STRIP), np.float32)
    lanelab[:, : RELW * PLACES] = np.stack([np.tile(level_label, RELW), np.tile(lat_label, RELW)])
    return pl.pallas_call(
        functools.partial(bias_kernel, groups),
        out_shape=shape((groups, TOK, TOK), f32),
        in_specs=[smem] + vmem(5),
        out_specs=vmem(1)[0],
        scratch_shapes=[pltpu.VMEM((groups * PLACES * PLACES, 128), f32)] * (STRIP // 128),
        compiler_params=pltpu.CompilerParams(vmem_limit_bytes=32 * MIB),
        cost_estimate=cost(10**9, 8 * MIB),
        name="bias",
    )(pole, flat, jnp.asarray(onehot, bf16), jnp.asarray(place), jnp.asarray(rowlab.reshape(-1, 3)), jnp.asarray(lanelab))


def head_masks(count):
    lane = lax.broadcasted_iota(jnp.int32, (count, C), 1)
    return [((lane >= h * HEAD) & (lane < (h + 1) * HEAD)).astype(f32) for h in range(HEADS)]


def stacked(values, masks):
    return jnp.concatenate([values * mask for mask in masks], axis=0)


def head_sum(values, masks):
    total = values[:TOK] * masks[0]
    for h in range(1, HEADS):
        total = total + values[h * TOK : (h + 1) * TOK] * masks[h]
    return total


def forward_kernel(
    windows, lon_windows,
    own_ref, north_ref, side_ref, corner_ref, perm_ref, bias_ref, triple_ref, project_ref, up_ref, down_ref,
    q_ref, k_ref, v_ref, p_ref, mixed_ref, normed_ref, unit_ref, spread_ref, gsum_ref, total_ref,
    branch_ref, cot_ref, emb_ref,
):
    pieces = [ref[...].astype(f32) for ref in (own_ref, north_ref, side_ref, corner_ref)]
    pieces = jnp.concatenate(pieces, axis=0).astype(bf16)
    ordered = mm(one_hot(perm_ref), pieces)
    emb = ordered[:, :C]
    emb_ref[...] = emb
    cot_ref[...] = ordered[:, C:].astype(bf16)
    unit, spread = unit_norm(emb)
    unit_ref[...] = unit
    spread_ref[...] = spread
    normed = unit.astype(bf16)
    normed_ref[...] = normed
    packed = mm(normed, triple_ref[...])
    q_ref[...] = packed[:, :C].astype(bf16)
    k_ref[...] = packed[:, C : 2 * C].astype(bf16)
    v_ref[...] = packed[:, 2 * C :].astype(bf16)
    masks = head_masks(TOK)
    masks_b = [mask.astype(bf16) for mask in masks]

    def window_step(w, carry):
        rows = pl.ds(pl.multiple_of(w * TOK, TOK), TOK)
        level = w // lon_windows
        scores = mm_nt(stacked(q_ref[rows, :], masks_b), k_ref[rows, :])
        bias = bias_ref[pl.ds(level * HEADS, HEADS)].reshape(HEADS * TOK, TOK)
        raised = jnp.exp2(scores * (score_scale * log2e) + bias)
        probs = raised * (1.0 / jnp.sum(raised, -1, keepdims=True))
        probs_b = probs.astype(bf16)
        p_ref[pl.ds(w * HEADS, HEADS)] = probs_b.reshape(HEADS, TOK, TOK)
        mixed = head_sum(mm(probs_b, v_ref[rows, :]), masks).astype(bf16)
        mixed_ref[rows, :] = mixed
        branch_ref[rows, :] = mm(mixed, project_ref[...])
        return carry

    lax.fori_loop(0, windows, window_step, 0)

    attended = branch_ref[...].astype(bf16).astype(f32)
    unit2, spread2 = unit_norm(emb_ref[...] + attended)
    normed2 = unit2.astype(bf16)
    cot = cot_ref[...]
    back = jnp.zeros(unit2.shape, f32)
    block = 256
    for start in range(0, FF, block):
        cols = slice(start, start + block)
        up_part = up_ref[:, cols]
        pre = mm(normed2, up_part)
        upstream = mm(cot, down_ref[:, cols])
        phi = 0.5 * (1.0 + lax.erf(pre * root_half))
        activated = (pre * phi).astype(bf16)
        slope = phi + pre * inv_root_tau * jnp.exp2(pre * pre * (-0.5 * log2e))
        hidden = (upstream * slope).astype(bf16)
        total_ref[0:C, cols] = mm_tn(normed2, hidden)
        total_ref[C : 2 * C, cols] = mm_tn(cot, activated)
        back = back + mm_nt(hidden, up_part)
    gsum_ref[...] = cot.astype(f32) + norm_back(back, unit2, spread2)


def forward(pieces, perm, bias, triple, project, up, down, lon_windows):
    count = perm.shape[1]
    windows = count // TOK
    out_shape = [
        shape((count, C), bf16),
        shape((count, C), bf16),
        shape((count, C), bf16),
        shape((windows * HEADS, TOK, TOK), bf16),
        shape((count, C), bf16),
        shape((count, C), bf16),
        shape((count, C), f32),
        shape((count, 1), f32),
        shape((count, C), f32),
        shape((2 * C, FF), f32),
    ]
    return pl.pallas_call(
        functools.partial(forward_kernel, windows, lon_windows),
        out_shape=out_shape,
        in_specs=vmem(10),
        out_specs=vmem(len(out_shape)),
        scratch_shapes=[pltpu.VMEM((count, C), f32), pltpu.VMEM((count, C), bf16), pltpu.VMEM((count, C), f32)],
        compiler_params=pltpu.CompilerParams(vmem_limit_bytes=28 * MIB),
        cost_estimate=cost(3 * 10**9, 16 * MIB),
        name="forward",
    )(*pieces, perm, bias, triple, project, up, down)


def backward_kernel(
    windows, sizes, rank_ref,
    q_ref, k_ref, v_ref, p_ref, mixed_ref, normed_ref, unit_ref, spread_ref, gsum_ref, mlp_ref, perm_ref, triple_ref,
    project_ref, *rest,
):
    outs = rest[: len(sizes)]
    keep_ref, send_ref, gq_ref, gk_ref, gv_ref, total_ref = rest[len(sizes) :]
    masks = head_masks(TOK)
    masks_b = [mask.astype(bf16) for mask in masks]

    def window_step(w, carry):
        rows = pl.ds(pl.multiple_of(w * TOK, TOK), TOK)
        grad = gsum_ref[rows, :].astype(bf16)
        grad_mixed = mm_nt(grad, project_ref[...])
        grad_mixed_b = grad_mixed.astype(bf16)
        probs_b = p_ref[pl.ds(w * HEADS, HEADS)].reshape(HEADS * TOK, TOK)
        probs = probs_b.astype(f32)
        grad_probs = mm_nt(stacked(grad_mixed_b, masks_b), v_ref[rows, :])
        inner = jnp.sum(grad_probs * probs, -1, keepdims=True)
        scaled = (probs * (grad_probs - inner) * score_scale).astype(bf16)
        grad_q = head_sum(mm(scaled, k_ref[rows, :]), masks)
        grad_mixed_t = grad_mixed_b.astype(f32).T.astype(bf16)
        query_t = q_ref[rows, :].astype(f32).T.astype(bf16)
        grad_k, grad_v = [], []
        for h in range(HEADS):
            spot = slice(h * HEAD, (h + 1) * HEAD)
            span = slice(h * TOK, (h + 1) * TOK)
            grad_k.append(mm(query_t[spot], scaled[span]))
            grad_v.append(mm(grad_mixed_t[spot], probs_b[span]))
        gq_ref[rows, :] = grad_q.astype(bf16)
        gk_ref[rows, :] = jnp.concatenate(grad_k, axis=0).T.astype(bf16)
        gv_ref[rows, :] = jnp.concatenate(grad_v, axis=0).T.astype(bf16)
        return carry

    lax.fori_loop(0, windows, window_step, 0)

    grad_packed = [gq_ref[...], gk_ref[...], gv_ref[...]]
    normed = normed_ref[...]
    triple = triple_ref[...]
    grad_normed = jnp.zeros(unit_ref.shape, f32)
    parts = []
    for n, grad in enumerate(grad_packed):
        grad_normed = grad_normed + mm_nt(grad, triple[:, n * C : (n + 1) * C])
        parts.append(mm_tn(normed, grad))
    parts.append(mm_tn(mixed_ref[...], gsum_ref[...].astype(bf16)))
    total_ref[...] = jnp.concatenate(parts, axis=1)
    grad_normed = grad_normed.astype(bf16).astype(f32)
    grad_tokens = gsum_ref[...] + norm_back(grad_normed, unit_ref[...], spread_ref[...])
    pieces = mm(one_hot(perm_ref), grad_tokens.astype(bf16))
    start = 0
    for out in outs:
        out[...] = pieces[start : start + out.shape[0]].astype(bf16)
        start += out.shape[0]
    core, chip = rank_ref[0], rank_ref[1]
    for out, side in ((keep_ref, core), (send_ref, 1 - core)):
        parts = []
        for e in range(QUADS):
            start = pl.multiple_of((side * QUADS + jnp.bitwise_xor(chip, e)) * PART, PART)
            rows, low_rows = pl.ds(start, PART), pl.ds(pl.multiple_of(C + start, PART), PART)
            parts += [mlp_ref[rows, :], mlp_ref[low_rows, :], total_ref[rows, :]]
        out[...] = jnp.concatenate(parts, axis=0).astype(out.dtype)


def backward(rank, saved, perm, triple, project, sizes):
    count = perm.shape[1]
    windows = count // TOK
    out_shape = [shape((size, C), bf16) for size in sizes] + [
        shape((QUADS * CHUNK, FF), dtype) for dtype in (f32, bf16)
    ]
    return pl.pallas_call(
        functools.partial(backward_kernel, windows, sizes),
        out_shape=out_shape,
        in_specs=[smem] + vmem(13),
        out_specs=vmem(len(out_shape)),
        scratch_shapes=[pltpu.VMEM((count, C), bf16)] * 3 + [pltpu.VMEM((C, FF), f32)],
        compiler_params=pltpu.CompilerParams(vmem_limit_bytes=28 * MIB),
        cost_estimate=cost(3 * 10**9, 16 * MIB),
        name="backward",
    )(rank, *saved, perm, triple, project)


def home_kernel(rows, cols, own_ref, north_ref, side_ref, corner_ref, perm_ref, land_ref, out_ref, sum_ref):
    pieces = [ref[...].astype(f32) for ref in (own_ref, north_ref, side_ref, corner_ref)]
    pieces = jnp.concatenate(pieces, axis=0).astype(bf16)
    grads = mm(one_hot(perm_ref), pieces)
    out_ref[...] = grads.astype(bf16)
    column = land_column(land_ref, rows, cols)
    column = jnp.concatenate([column] * Z, axis=0)
    sum_ref[...] = jnp.sum(grads * column, 0, keepdims=True)


def to_home(pieces, land_sea, rows, cols):
    count = Z * rows * cols
    perm = spots(np.argsort(np.concatenate(piece_rows(rows, cols))))
    return pl.pallas_call(
        functools.partial(home_kernel, rows, cols),
        out_shape=[shape((count, C), bf16), shape((1, C), f32)],
        in_specs=vmem(6),
        out_specs=vmem(2),
        compiler_params=pltpu.CompilerParams(vmem_limit_bytes=32 * MIB),
        cost_estimate=cost(2 * count * count * C, 4 * MIB),
        name="to_home",
    )(*pieces, perm, land_sea)


def core_add_kernel(keep_ref, got_ref, own_ref, *outs):
    total = keep_ref[...] + got_ref[...].astype(f32)
    own_ref[...] = total[:CHUNK]
    for e, out in enumerate(outs, 1):
        out[...] = total[e * CHUNK : (e + 1) * CHUNK].astype(bf16)


def coded(total):
    high = total.astype(bf16).astype(f32)
    row = total[CHUNK : CHUNK + 1] - high[CHUNK : CHUNK + 1]
    zeros = jnp.zeros((FULL - CHUNK - 2, FF), f32)
    return jnp.concatenate([high[:CHUNK], high[CHUNK : CHUNK + 1], row, zeros], axis=0).astype(bf16)


def decoded(values):
    wide = values.astype(f32)
    row = wide[CHUNK : CHUNK + 1] + wide[CHUNK + 1 : CHUNK + 2]
    zeros = jnp.zeros((FULL - CHUNK - 1, FF), f32)
    return jnp.concatenate([wide[:CHUNK], row, zeros], axis=0)


def chip_add_kernel(own_ref, *refs):
    gots, (land_ref, send_ref) = refs[:-2], refs[-2:]
    total = own_ref[...]
    for ref in gots:
        total = total + ref[...].astype(f32)
    land = jnp.concatenate([land_ref[...], jnp.zeros((1, FF - C), f32)], axis=1)
    total = jnp.concatenate([total, land, jnp.zeros((FULL - CHUNK - 1, FF), f32)], axis=0)
    send_ref[...] = coded(total)


def far_add_kernel(sent_ref, got_ref, out_ref):
    out_ref[...] = coded(decoded(sent_ref[...]) + decoded(got_ref[...]))


def join_kernel(*refs):
    refs[-1][...] = jnp.concatenate([ref[...] for ref in refs[:-1]], axis=0)


def small_call(kernel, out_shape, args, name):
    return pl.pallas_call(
        kernel,
        out_shape=out_shape,
        in_specs=vmem(len(args)),
        out_specs=vmem(len(out_shape)),
        compiler_params=pltpu.CompilerParams(vmem_limit_bytes=16 * MIB),
        cost_estimate=cost(10**6, 2 * MIB),
        name=name,
    )(*args)


def finish_kernel(rank_ref, *refs):
    near, (far_ref, triple_ref, project_ref, up_ref, down_ref, land_ref, wide_ref, lands_ref) = refs[:QUADS], refs[QUADS:]
    core, chip = rank_ref[0], rank_ref[1]
    for side in range(2):
        for e in range(QUADS):
            chunk = near[e][...] if side == 0 else far_ref[e * FULL : (e + 1) * FULL, :]
            chunk = chunk.astype(f32)
            block = jnp.bitwise_xor(core, side) * QUADS + jnp.bitwise_xor(chip, e)
            rows = pl.ds(pl.multiple_of(block * PART, PART), PART)
            up_ref[rows, :] = chunk[:PART]
            down_ref[rows, :] = chunk[PART : 2 * PART]
            wide_ref[rows, :] = chunk[2 * PART : CHUNK]
            lands_ref[pl.ds(pl.multiple_of(block * 8, 8), 8), :] = chunk[CHUNK:, :C]
    triple_ref[...] = wide_ref[:, : 3 * C]
    project_ref[...] = wide_ref[:, 3 * C :]
    land_ref[...] = jnp.sum(lands_ref[...], 0, keepdims=True)


def finish(rank, near, far):
    return pl.pallas_call(
        finish_kernel,
        out_shape=[shape((C, 3 * C), f32), shape((C, C), f32), shape((C, FF), f32), shape((C, FF), f32), shape((1, C), f32)],
        in_specs=[smem] + vmem(QUADS + 1),
        out_specs=vmem(5),
        scratch_shapes=[pltpu.VMEM((C, FF), f32), pltpu.VMEM((2 * QUADS * 8, C), f32)],
        compiler_params=pltpu.CompilerParams(vmem_limit_bytes=16 * MIB),
        cost_estimate=cost(10**6, 8 * MIB),
        name="finish",
    )(rank, *near, far)


def reduce_all(keep, sent, land, rank, shift, lon_count):
    chip_move = lambda e: lambda lon, lat: (lon ^ (e & 1), lat ^ (2 * (e >> 1)))
    core_move = lambda lon, lat: (lon, lat ^ 1)
    got = shift(sent, move=core_move)
    part = [shape((CHUNK, FF), f32)] + [shape((CHUNK, FF), bf16)] * (QUADS - 1)
    own, *parts = small_call(core_add_kernel, part, (keep, got), "core_add")
    gots = [shift(value, move=chip_move(e)) for e, value in enumerate(parts, 1)]
    full = [shape((FULL, FF), bf16)]
    (chunk,) = small_call(chip_add_kernel, full, (own, *gots, land), "chip_add")
    reach = 2
    while reach < lon_count:
        got = shift(chunk, move=lambda lon, lat, reach=reach: (lon ^ reach, lat))
        reach *= 2
        (chunk,) = small_call(far_add_kernel, full, (chunk, got), "far_add")
    near = [chunk] + [shift(chunk, move=chip_move(e)) for e in range(1, QUADS)]
    (joined,) = small_call(join_kernel, [shape((QUADS * FULL, FF), bf16)], near, "join")
    return finish(rank, near, shift(joined, move=core_move))


AXES = ("lon", "lat")


def send(value, lon_count, lat_count, move):
    pairs = []
    for lon in range(lon_count):
        for lat in range(lat_count):
            to_lon, to_lat = move(lon, lat)
            pairs.append((lon * lat_count + lat, (to_lon % lon_count) * lat_count + to_lat % lat_count))
    return lax.ppermute(value, AXES, pairs)


def body(
    lon_count, lat_count,
    tokens, cotangent, land_sea, land_vector, triple_weight, project_weight, up_weight, down_weight, earth_bias,
):
    levels, rows, cols, features = tokens.shape
    shift = functools.partial(send, lon_count=lon_count, lat_count=lat_count)
    lon_at, lat_at = lax.axis_index("lon"), lax.axis_index("lat")
    rank = jnp.stack([lat_at % 2, 2 * (lat_at // 2) + lon_at % 2]).astype(jnp.int32)
    pole = (lat_at == 0).astype(jnp.int32).reshape(1)
    lon_windows = cols // WW

    own, north, side, corner = pack(tokens, cotangent, land_sea, land_vector, rows, cols)
    north = shift(north, move=lambda lon, lat: (lon, lat + 1))
    side = shift(side, move=lambda lon, lat: (lon + 1, lat))
    corner = shift(corner, move=lambda lon, lat: (lon + 1, lat + 1))
    bias = expand_bias(earth_bias, pole)

    places = window_rows(rows, cols)
    sizes = [part.size for part in piece_rows(rows, cols)]
    saved = forward(
        (own, north, side, corner), spots(places), bias,
        triple_weight, project_weight, up_weight, down_weight.T, lon_windows,
    )
    own, north, side, corner, keep, sent = backward(
        rank, saved, spots(np.argsort(places)), triple_weight, project_weight, sizes
    )
    north = shift(north, move=lambda lon, lat: (lon, lat - 1))
    side = shift(side, move=lambda lon, lat: (lon - 1, lat))
    corner = shift(corner, move=lambda lon, lat: (lon - 1, lat - 1))
    grad_tokens, land = to_home((own, north, side, corner), land_sea, rows, cols)
    triple, project, up, down, land = reduce_all(keep, sent, land, rank, shift, lon_count)
    return grad_tokens.reshape(tokens.shape), triple, project, up, down.T, land.reshape(features)


def solution(mesh):
    return jax.shard_map(
        functools.partial(body, mesh.shape["lon"], mesh.shape["lat"]),
        mesh=mesh,
        in_specs=(
            P(None, "lat", "lon", None),
            P(None, "lat", "lon", None),
            P("lat", "lon"),
            P(),
            P(),
            P(),
            P(),
            P(),
            P("lat", None, None, None, None),
        ),
        out_specs=(P(None, "lat", "lon", None), P(), P(), P(), P(), P()),
        check_vma=False,
    )
```

```python
import functools
import math

import jax
import jax.numpy as jnp
import numpy as np
from jax import lax
from jax.experimental import pallas as pl
from jax.experimental.pallas import tpu as pltpu
from jax.sharding import PartitionSpec as P

Z = 4
WZ = 2
WH = 6
WW = 12
C = 192
HEADS = 6
HEAD = 32
FF = 768
HZ, HH, HW = WZ // 2, WH // 2, WW // 2
TOK = WZ * WH * WW
PLACES = WZ * WH
RELW = 2 * WW - 1
STRIP = -(-RELW * PLACES // 128) * 128

mask_fill = -10000.0
norm_eps = 1e-05
log2e = 1.4426950408889634
root_half = 0.7071067811865476
inv_root_tau = 0.3989422804014327
score_scale = HEAD**-0.5

f32 = jnp.float32
bf16 = jnp.bfloat16
MIB = 1 << 20

QUADS = 4
PART = C // (2 * QUADS)
EXTRA = 8


def mm(a, b):
    return lax.dot_general(a, b, (((1,), (0,)), ((), ())), preferred_element_type=f32)


def mm_nt(a, b):
    return lax.dot_general(a, b, (((1,), (1,)), ((), ())), preferred_element_type=f32)


def mm_tn(a, b):
    return lax.dot_general(a, b, (((0,), (0,)), ((), ())), preferred_element_type=f32)


def unit_norm(values):
    average = jnp.mean(values, -1, keepdims=True)
    centred = values - average
    variance = jnp.mean(centred * centred, -1, keepdims=True)
    spread = lax.rsqrt(variance + norm_eps)
    return centred * spread, spread


def norm_back(upstream, unit, spread):
    first = jnp.mean(upstream, -1, keepdims=True)
    second = jnp.mean(upstream * unit, -1, keepdims=True)
    return spread * (upstream - first - unit * second)


def piece_rows(rows, cols):
    home = np.arange(Z * rows * cols).reshape(Z, rows, cols)
    top, low = slice(0, rows - HH), slice(rows - HH, rows)
    west, east = slice(0, cols - HW), slice(cols - HW, cols)
    parts = [home[:, top, west], home[:, low, west], home[:, top, east], home[:, low, east]]
    return [part.reshape(-1) for part in parts]


def window_rows(rows, cols):
    sizes = [part.size for part in piece_rows(rows, cols)]
    starts = np.cumsum([0] + sizes)
    own, north, side, corner = [np.arange(starts[k], starts[k + 1]) for k in range(4)]
    frame = np.zeros((Z, rows, cols), np.int64)
    frame[:, HH:, HW:] = own.reshape(Z, rows - HH, cols - HW)
    frame[:, :HH, HW:] = north.reshape(Z, HH, cols - HW)
    frame[:, HH:, :HW] = side.reshape(Z, rows - HH, HW)
    frame[:, :HH, :HW] = corner.reshape(Z, HH, HW)
    frame = np.roll(frame, HZ, axis=0)
    frame = frame.reshape(Z // WZ, WZ, rows // WH, WH, cols // WW, WW)
    return frame.transpose(0, 2, 4, 5, 1, 3).reshape(-1)


def spots(places):
    return jnp.asarray(np.argsort(places).astype(np.int32)[None])


def one_hot(spot_ref):
    count = spot_ref.shape[1]
    rows = lax.broadcasted_iota(jnp.int32, (count, count), 0)
    return (rows == spot_ref[...]).astype(f32).astype(bf16)


def vmem(count):
    return [pl.BlockSpec(memory_space=pltpu.VMEM)] * count


smem = pl.BlockSpec(memory_space=pltpu.SMEM)


def shape(dims, dtype):
    return jax.ShapeDtypeStruct(dims, dtype)


def cost(flops, moved):
    return pl.CostEstimate(flops=flops, bytes_accessed=moved, transcendentals=0)


def land_column(land_ref, rows, cols):
    eye = (
        lax.broadcasted_iota(jnp.int32, (cols, cols), 0)
        == lax.broadcasted_iota(jnp.int32, (cols, cols), 1)
    ).astype(f32)
    land = land_ref[...].astype(f32)
    parts = [jnp.sum(eye * land[i : i + 1, :], -1, keepdims=True) for i in range(rows)]
    return jnp.concatenate(parts, axis=0)


def pack_kernel(rows, cols, tokens_ref, cot_ref, land_ref, vec_ref, perm_ref, *outs):
    column = land_column(land_ref, rows, cols)
    added = column * vec_ref[...]
    added = jnp.concatenate([added] * Z, axis=0)
    embedded = (tokens_ref[...].astype(f32) + added).astype(bf16)
    perm = one_hot(perm_ref)
    left = mm(perm, embedded)
    right = mm(perm, cot_ref[...])
    packed = jnp.concatenate([left, right], axis=1)
    column = jnp.concatenate([column] * Z, axis=0)
    flags = mm(perm, jnp.broadcast_to(column, (column.shape[0], 128)).astype(bf16))
    start = 0
    for out in outs:
        count = out.shape[0] - EXTRA
        eye = lax.broadcasted_iota(jnp.int32, (count, count), 0) == lax.broadcasted_iota(jnp.int32, (count, count), 1)
        row = jnp.sum(jnp.where(eye, flags[start : start + count, 0:1], 0.0), 0, keepdims=True)
        row = jnp.concatenate([row, jnp.zeros((1, 2 * C - count), f32)], axis=1)
        row = jnp.broadcast_to(row, (EXTRA, 2 * C))
        out[...] = jnp.concatenate([packed[start : start + count], row], axis=0).astype(bf16)
        start += count


def pack(tokens, cotangent, land_sea, vector, rows, cols):
    parts = piece_rows(rows, cols)
    perm = spots(np.concatenate(parts))
    count = Z * rows * cols
    return pl.pallas_call(
        functools.partial(pack_kernel, rows, cols),
        out_shape=[shape((part.size + EXTRA, 2 * C), bf16) for part in parts],
        in_specs=vmem(5),
        out_specs=vmem(4),
        cost_estimate=cost(4 * count * count * C, 4 * MIB),
        name="pack",
    )(tokens.reshape(count, C), cotangent.reshape(count, C), land_sea, vector.reshape(1, C), perm)


def bias_kernel(groups, pole_ref, table_ref, spread_ref, place_ref, rowlab_ref, lanelab_ref, out_ref, *wide_refs):
    table = table_ref[...]
    high = table.astype(bf16)
    rest = table - high.astype(f32)
    middle = rest.astype(bf16)
    low = (rest - middle.astype(f32)).astype(bf16)
    onehot = spread_ref[...]
    wide = mm(high, onehot) + mm(middle, onehot) + mm(low, onehot)
    strips = groups * PLACES
    parts = []
    for n in range(STRIP // 128):
        lanes = slice(n * 128, (n + 1) * 128)
        wide_ref = wide_refs[n]
        wide_ref[...] = wide[:, lanes]
        place = place_ref[:, lanes]
        part = jnp.zeros((strips, 128), f32)
        for p in range(PLACES):
            part = jnp.where(place == p, wide_ref[pl.ds(p, strips, stride=PLACES), :], part)
        parts.append(part)
    strip = jnp.concatenate(parts, axis=1)
    pole = pole_ref[0].astype(f32)
    rowlab = rowlab_ref[...]
    lanelab = lanelab_ref[...]
    differs = jnp.maximum(
        rowlab[:, 2:3] * jnp.abs(rowlab[:, 0:1] - lanelab[0:1, :]),
        pole * jnp.abs(rowlab[:, 1:2] - lanelab[1:2, :]),
    )
    strip = (strip + mask_fill * differs) * log2e
    for w in range(WW):
        start = (WW - 1 - w) * PLACES
        part = strip[:, start : start + TOK]
        for g in range(groups):
            out_ref[g, w * PLACES : (w + 1) * PLACES, :] = part[g * PLACES : (g + 1) * PLACES, :]


def expand_bias(table, pole):
    levels = table.shape[1]
    groups = levels * HEADS
    flat = table.reshape(groups * PLACES * PLACES, RELW)
    onehot = np.zeros((RELW, STRIP), np.float32)
    for r in range(RELW):
        onehot[RELW - 1 - r, r * PLACES : (r + 1) * PLACES] = 1.0
    place = (np.arange(STRIP) % PLACES).astype(np.int32)[None]
    level_label = (np.arange(PLACES) // WH < HZ).astype(np.float32)
    lat_label = (np.arange(PLACES) % WH < HH).astype(np.float32)
    rowlab = np.zeros((groups, PLACES, 3), np.float32)
    rowlab[:, :, 0] = level_label
    rowlab[:, :, 1] = lat_label
    rowlab[:HEADS, :, 2] = 1.0
    lanelab = np.zeros((2, STRIP), np.float32)
    lanelab[:, : RELW * PLACES] = np.stack([np.tile(level_label, RELW), np.tile(lat_label, RELW)])
    return pl.pallas_call(
        functools.partial(bias_kernel, groups),
        out_shape=shape((groups, TOK, TOK), f32),
        in_specs=[smem] + vmem(5),
        out_specs=vmem(1)[0],
        scratch_shapes=[pltpu.VMEM((groups * PLACES * PLACES, 128), f32)] * (STRIP // 128),
        compiler_params=pltpu.CompilerParams(vmem_limit_bytes=32 * MIB),
        cost_estimate=cost(10**9, 8 * MIB),
        name="bias",
    )(pole, flat, jnp.asarray(onehot, bf16), jnp.asarray(place), jnp.asarray(rowlab.reshape(-1, 3)), jnp.asarray(lanelab))


def head_masks(count):
    lane = lax.broadcasted_iota(jnp.int32, (count, C), 1)
    return [((lane >= h * HEAD) & (lane < (h + 1) * HEAD)).astype(f32) for h in range(HEADS)]


def stacked(values, masks):
    return jnp.concatenate([values * mask for mask in masks], axis=0)


def head_sum(values, masks):
    total = values[:TOK] * masks[0]
    for h in range(1, HEADS):
        total = total + values[h * TOK : (h + 1) * TOK] * masks[h]
    return total


def split_parts(rank_ref, total_ref, keep_ref, send_ref):
    core, chip = rank_ref[0], rank_ref[1]
    for out, side in ((keep_ref, core), (send_ref, 1 - core)):
        parts = []
        for e in range(QUADS):
            start = (side * QUADS + jnp.bitwise_xor(chip, e)) * PART
            for base in range(0, total_ref.shape[0], C):
                parts.append(total_ref[pl.ds(pl.multiple_of(base + start, 8), PART), :])
        out[...] = jnp.concatenate(parts, axis=0).astype(out.dtype)


def forward_kernel(
    windows, lon_windows, rank_ref,
    own_ref, north_ref, side_ref, corner_ref, perm_ref, bias_ref, triple_ref, project_ref, up_ref, down_ref,
    q_ref, k_ref, v_ref, p_ref, mixed_ref, normed_ref, unit_ref, spread_ref, gsum_ref, keep_ref, send_ref,
    branch_ref, cot_ref, emb_ref, total_ref,
):
    pieces = [ref[...].astype(f32)[:-EXTRA] for ref in (own_ref, north_ref, side_ref, corner_ref)]
    pieces = jnp.concatenate(pieces, axis=0).astype(bf16)
    ordered = mm(one_hot(perm_ref), pieces)
    emb = ordered[:, :C]
    emb_ref[...] = emb
    cot_ref[...] = ordered[:, C:].astype(bf16)
    unit, spread = unit_norm(emb)
    unit_ref[...] = unit
    spread_ref[...] = spread
    normed = unit.astype(bf16)
    normed_ref[...] = normed
    packed = mm(normed, triple_ref[...])
    q_ref[...] = packed[:, :C].astype(bf16)
    k_ref[...] = packed[:, C : 2 * C].astype(bf16)
    v_ref[...] = packed[:, 2 * C :].astype(bf16)
    masks = head_masks(TOK)
    masks_b = [mask.astype(bf16) for mask in masks]

    def window_step(w, carry):
        rows = pl.ds(pl.multiple_of(w * TOK, TOK), TOK)
        level = w // lon_windows
        scores = mm_nt(stacked(q_ref[rows, :], masks_b), k_ref[rows, :])
        bias = bias_ref[pl.ds(level * HEADS, HEADS)].reshape(HEADS * TOK, TOK)
        raised = jnp.exp2(scores * (score_scale * log2e) + bias)
        probs = raised * (1.0 / jnp.sum(raised, -1, keepdims=True))
        probs_b = probs.astype(bf16)
        p_ref[pl.ds(w * HEADS, HEADS)] = probs_b.reshape(HEADS, TOK, TOK)
        mixed = head_sum(mm(probs_b, v_ref[rows, :]), masks).astype(bf16)
        mixed_ref[rows, :] = mixed
        branch_ref[rows, :] = mm(mixed, project_ref[...])
        return carry

    lax.fori_loop(0, windows, window_step, 0)

    attended = branch_ref[...].astype(bf16).astype(f32)
    unit2, spread2 = unit_norm(emb_ref[...] + attended)
    normed2 = unit2.astype(bf16)
    cot = cot_ref[...]
    back = jnp.zeros(unit2.shape, f32)
    block = 256
    for start in range(0, FF, block):
        cols = slice(start, start + block)
        up_part = up_ref[:, cols]
        pre = mm(normed2, up_part)
        upstream = mm(cot, down_ref[:, cols])
        phi = 0.5 * (1.0 + lax.erf(pre * root_half))
        activated = (pre * phi).astype(bf16)
        slope = phi + pre * inv_root_tau * jnp.exp2(pre * pre * (-0.5 * log2e))
        hidden = (upstream * slope).astype(bf16)
        total_ref[0:C, cols] = mm_tn(normed2, hidden)
        total_ref[C : 2 * C, cols] = mm_tn(cot, activated)
        back = back + mm_nt(hidden, up_part)
    gsum_ref[...] = cot.astype(f32) + norm_back(back, unit2, spread2)
    split_parts(rank_ref, total_ref, keep_ref, send_ref)


def forward(rank, pieces, perm, bias, triple, project, up, down, lon_windows):
    count = perm.shape[1]
    windows = count // TOK
    out_shape = [
        shape((count, C), bf16),
        shape((count, C), bf16),
        shape((count, C), bf16),
        shape((windows * HEADS, TOK, TOK), bf16),
        shape((count, C), bf16),
        shape((count, C), bf16),
        shape((count, C), f32),
        shape((count, 1), f32),
        shape((count, C), f32),
        shape((QUADS * 2 * PART, FF), f32),
        shape((QUADS * 2 * PART, FF), bf16),
    ]
    return pl.pallas_call(
        functools.partial(forward_kernel, windows, lon_windows),
        out_shape=out_shape,
        in_specs=[smem] + vmem(10),
        out_specs=vmem(len(out_shape)),
        scratch_shapes=[pltpu.VMEM((count, C), f32), pltpu.VMEM((count, C), bf16), pltpu.VMEM((count, C), f32), pltpu.VMEM((2 * C, FF), f32)],
        compiler_params=pltpu.CompilerParams(vmem_limit_bytes=28 * MIB),
        cost_estimate=cost(3 * 10**9, 16 * MIB),
        name="forward",
    )(rank, *pieces, perm, bias, triple, project, up, down)


def windows_back_kernel(windows, q_ref, k_ref, v_ref, p_ref, gsum_ref, project_ref, gq_ref, gk_ref, gv_ref):
    masks = head_masks(TOK)
    masks_b = [mask.astype(bf16) for mask in masks]

    def window_step(w, carry):
        rows = pl.ds(pl.multiple_of(w * TOK, TOK), TOK)
        grad = gsum_ref[rows, :].astype(bf16)
        grad_mixed = mm_nt(grad, project_ref[...])
        grad_mixed_b = grad_mixed.astype(bf16)
        probs_b = p_ref[pl.ds(w * HEADS, HEADS)].reshape(HEADS * TOK, TOK)
        probs = probs_b.astype(f32)
        grad_probs = mm_nt(stacked(grad_mixed_b, masks_b), v_ref[rows, :])
        inner = jnp.sum(grad_probs * probs, -1, keepdims=True)
        scaled = (probs * (grad_probs - inner) * score_scale).astype(bf16)
        grad_q = head_sum(mm(scaled, k_ref[rows, :]), masks)
        grad_mixed_t = grad_mixed_b.astype(f32).T.astype(bf16)
        query_t = q_ref[rows, :].astype(f32).T.astype(bf16)
        grad_k, grad_v = [], []
        for h in range(HEADS):
            spot = slice(h * HEAD, (h + 1) * HEAD)
            span = slice(h * TOK, (h + 1) * TOK)
            grad_k.append(mm(query_t[spot], scaled[span]))
            grad_v.append(mm(grad_mixed_t[spot], probs_b[span]))
        gq_ref[rows, :] = grad_q.astype(bf16)
        gk_ref[rows, :] = jnp.concatenate(grad_k, axis=0).T.astype(bf16)
        gv_ref[rows, :] = jnp.concatenate(grad_v, axis=0).T.astype(bf16)
        return carry

    lax.fori_loop(0, windows, window_step, 0)


def windows_back(q, k, v, p, gsum, project):
    count = q.shape[0]
    return pl.pallas_call(
        functools.partial(windows_back_kernel, count // TOK),
        out_shape=[shape((count, C), bf16)] * 3,
        in_specs=vmem(6),
        out_specs=vmem(3),
        compiler_params=pltpu.CompilerParams(vmem_limit_bytes=28 * MIB),
        cost_estimate=cost(3 * 10**9, 16 * MIB),
        name="windows_back",
    )(q, k, v, p, gsum, project)


def halved(rows):
    return -(-rows // 16) * 8


def tokens_back_kernel(
    sizes, rank_ref, gq_ref, gk_ref, gv_ref, mixed_ref, normed_ref, unit_ref, spread_ref, gsum_ref, perm_ref, triple_ref,
    *rest,
):
    flag_refs, rest = rest[: len(sizes)], rest[len(sizes) :]
    outs, (land_ref, keep_ref, send_ref, total_ref) = rest[: len(sizes)], rest[len(sizes) :]
    normed = normed_ref[...]
    triple = triple_ref[...]
    grad_normed = jnp.zeros(unit_ref.shape, f32)
    parts = []
    for n, ref in enumerate((gq_ref, gk_ref, gv_ref)):
        grad = ref[...]
        grad_normed = grad_normed + mm_nt(grad, triple[:, n * C : (n + 1) * C])
        parts.append(mm_tn(normed, grad))
    parts.append(mm_tn(mixed_ref[...], gsum_ref[...].astype(bf16)))
    total_ref[...] = jnp.concatenate(parts, axis=1)
    grad_normed = grad_normed.astype(bf16).astype(f32)
    grad_tokens = gsum_ref[...] + norm_back(grad_normed, unit_ref[...], spread_ref[...])
    pieces = mm(one_hot(perm_ref), grad_tokens.astype(bf16))
    land = jnp.zeros((EXTRA, C), f32)
    start = 0
    for size, out, flag_ref in zip(sizes, outs, flag_refs):
        piece = pieces[start : start + size]
        flags = flag_ref[size - 8 : size + 8, :].astype(f32)[8:, :size]
        land = land + mm(flags.astype(bf16), piece.astype(bf16))
        half = halved(size)
        second = jnp.concatenate([piece[half:], jnp.zeros((2 * half - size, C), f32)], axis=0)
        out[...] = jnp.concatenate([piece[:half], second], axis=1).astype(bf16)
        start += size
    land_ref[...] = land[0:1]
    split_parts(rank_ref, total_ref, keep_ref, send_ref)


def tokens_back(rank, grads, mixed, normed, unit, spread, gsum, perm, triple, pieces, sizes):
    out_shape = [shape((halved(size), 2 * C), bf16) for size in sizes] + [
        shape((1, C), f32),
        shape((QUADS * PART, FF), f32),
        shape((QUADS * PART, FF), bf16),
    ]
    return pl.pallas_call(
        functools.partial(tokens_back_kernel, sizes),
        out_shape=out_shape,
        in_specs=[smem] + vmem(10 + len(pieces)),
        out_specs=vmem(len(out_shape)),
        scratch_shapes=[pltpu.VMEM((C, FF), f32)],
        compiler_params=pltpu.CompilerParams(vmem_limit_bytes=28 * MIB),
        cost_estimate=cost(2 * 10**9, 8 * MIB),
        name="tokens_back",
    )(rank, *grads, mixed, normed, unit, spread, gsum, perm, triple, *pieces)


def home_kernel(sizes, own_ref, north_ref, side_ref, corner_ref, perm_ref, out_ref):
    pieces = []
    for size, ref in zip(sizes, (own_ref, north_ref, side_ref, corner_ref)):
        wide = ref[...].astype(f32)
        pieces += [wide[:, :C], wide[: size - wide.shape[0], C:]]
    pieces = jnp.concatenate(pieces, axis=0).astype(bf16)
    out_ref[...] = mm(one_hot(perm_ref), pieces).astype(bf16)


def to_home(pieces, sizes, rows, cols):
    count = Z * rows * cols
    perm = spots(np.argsort(np.concatenate(piece_rows(rows, cols))))
    return pl.pallas_call(
        functools.partial(home_kernel, sizes),
        out_shape=shape((count, C), bf16),
        in_specs=vmem(5),
        out_specs=vmem(1)[0],
        compiler_params=pltpu.CompilerParams(vmem_limit_bytes=32 * MIB),
        cost_estimate=cost(2 * count * count * C, 4 * MIB),
        name="to_home",
    )(*pieces, perm)


def core_add_kernel(keep_ref, got_ref, own_ref, *outs):
    total = keep_ref[...] + got_ref[...].astype(f32)
    chunk = own_ref.shape[0]
    own_ref[...] = total[:chunk]
    for e, out in enumerate(outs, 1):
        out[...] = total[e * chunk : (e + 1) * chunk].astype(bf16)


def coded(total, extra):
    if not extra:
        return total.astype(bf16)
    at = total.shape[0] - EXTRA
    high = total.astype(bf16).astype(f32)
    rest = total[at : at + 1] - high[at : at + 1]
    zeros = jnp.zeros((EXTRA - 2, FF), f32)
    return jnp.concatenate([high[:at], high[at : at + 1], rest, zeros], axis=0).astype(bf16)


def decoded(values, extra):
    wide = values.astype(f32)
    if not extra:
        return wide
    at = wide.shape[0] - EXTRA
    row = wide[at : at + 1] + wide[at + 1 : at + 2]
    return jnp.concatenate([wide[:at], row, jnp.zeros((EXTRA - 1, FF), f32)], axis=0)


def chip_add_kernel(extra, own_ref, *refs):
    gots, send_ref = refs[:-1], refs[-1]
    if extra:
        gots, land_ref = gots[:-1], gots[-1]
    total = own_ref[...]
    for ref in gots:
        total = total + ref[...].astype(f32)
    if extra:
        land = jnp.concatenate([land_ref[...], jnp.zeros((1, FF - C), f32)], axis=1)
        total = jnp.concatenate([total, land, jnp.zeros((EXTRA - 1, FF), f32)], axis=0)
    send_ref[...] = coded(total, extra)


def far_add_kernel(extra, sent_ref, got_ref, out_ref):
    out_ref[...] = coded(decoded(sent_ref[...], extra) + decoded(got_ref[...], extra), extra)


def join_kernel(*refs):
    refs[-1][...] = jnp.concatenate([ref[...] for ref in refs[:-1]], axis=0)


def small_call(kernel, out_shape, args, name):
    return pl.pallas_call(
        kernel,
        out_shape=out_shape,
        in_specs=vmem(len(args)),
        out_specs=vmem(len(out_shape)),
        compiler_params=pltpu.CompilerParams(vmem_limit_bytes=16 * MIB),
        cost_estimate=cost(10**6, 2 * MIB),
        name=name,
    )(*args)


def blocks(rank_ref, near, far_ref):
    core, chip = rank_ref[0], rank_ref[1]
    rows = far_ref.shape[0] // QUADS
    for side in range(2):
        for e in range(QUADS):
            chunk = near[e][...] if side == 0 else far_ref[e * rows : (e + 1) * rows, :]
            yield jnp.bitwise_xor(core, side) * QUADS + jnp.bitwise_xor(chip, e), chunk.astype(f32)


def finish_mlp_kernel(rank_ref, *refs):
    near, (far_ref, up_ref, down_ref) = refs[:QUADS], refs[QUADS:]
    for block, chunk in blocks(rank_ref, near, far_ref):
        rows = pl.ds(pl.multiple_of(block * PART, PART), PART)
        up_ref[rows, :] = chunk[:PART]
        down_ref[rows, :] = chunk[PART:]


def finish_attn_kernel(rank_ref, *refs):
    near, (far_ref, triple_ref, project_ref, land_ref, wide_ref, lands_ref) = refs[:QUADS], refs[QUADS:]
    for block, chunk in blocks(rank_ref, near, far_ref):
        wide_ref[pl.ds(pl.multiple_of(block * PART, PART), PART), :] = chunk[:PART]
        lands_ref[pl.ds(pl.multiple_of(block * EXTRA, EXTRA), EXTRA), :] = chunk[PART:, :C]
    triple_ref[...] = wide_ref[:, : 3 * C]
    project_ref[...] = wide_ref[:, 3 * C :]
    land_ref[...] = jnp.sum(lands_ref[...], 0, keepdims=True)


def finish(kernel, out_shape, scratch, rank, near, far, name):
    return pl.pallas_call(
        kernel,
        out_shape=out_shape,
        in_specs=[smem] + vmem(QUADS + 1),
        out_specs=vmem(len(out_shape)),
        scratch_shapes=scratch,
        compiler_params=pltpu.CompilerParams(vmem_limit_bytes=16 * MIB),
        cost_estimate=cost(10**6, 4 * MIB),
        name=name,
    )(rank, *near, far)


def reduce_all(keep, sent, land, shift, lon_count):
    chip_move = lambda e: lambda lon, lat: (lon ^ (e & 1), lat ^ (2 * (e >> 1)))
    core_move = lambda lon, lat: (lon, lat ^ 1)
    extra = len(land)
    chunk_rows = keep.shape[0] // QUADS
    full_rows = chunk_rows + EXTRA * extra
    full = [shape((full_rows, FF), bf16)]
    part = [shape((chunk_rows, FF), f32)] + [shape((chunk_rows, FF), bf16)] * (QUADS - 1)
    got = shift(sent, move=core_move)
    own, *parts = small_call(core_add_kernel, part, (keep, got), "core_add")
    gots = [shift(value, move=chip_move(e)) for e, value in enumerate(parts, 1)]
    (chunk,) = small_call(functools.partial(chip_add_kernel, extra), full, (own, *gots, *land), "chip_add")
    reach = 2
    while reach < lon_count:
        got = shift(chunk, move=lambda lon, lat, reach=reach: (lon ^ reach, lat))
        reach *= 2
        (chunk,) = small_call(functools.partial(far_add_kernel, extra), full, (chunk, got), "far_add")
    near = [chunk] + [shift(chunk, move=chip_move(e)) for e in range(1, QUADS)]
    (joined,) = small_call(join_kernel, [shape((QUADS * full_rows, FF), bf16)], near, "join")
    return near, shift(joined, move=core_move)


AXES = ("lon", "lat")


def send(value, lon_count, lat_count, move):
    pairs = []
    for lon in range(lon_count):
        for lat in range(lat_count):
            to_lon, to_lat = move(lon, lat)
            pairs.append((lon * lat_count + lat, (to_lon % lon_count) * lat_count + to_lat % lat_count))
    return lax.ppermute(value, AXES, pairs)


def body(
    lon_count, lat_count,
    tokens, cotangent, land_sea, land_vector, triple_weight, project_weight, up_weight, down_weight, earth_bias,
):
    levels, rows, cols, features = tokens.shape
    shift = functools.partial(send, lon_count=lon_count, lat_count=lat_count)
    lon_at, lat_at = lax.axis_index("lon"), lax.axis_index("lat")
    rank = jnp.stack([lat_at % 2, 2 * (lat_at // 2) + lon_at % 2]).astype(jnp.int32)
    pole = (lat_at == 0).astype(jnp.int32).reshape(1)
    lon_windows = cols // WW

    own, north, side, corner = pack(tokens, cotangent, land_sea, land_vector, rows, cols)
    north = shift(north, move=lambda lon, lat: (lon, lat + 1))
    side = shift(side, move=lambda lon, lat: (lon + 1, lat))
    corner = shift(corner, move=lambda lon, lat: (lon + 1, lat + 1))
    bias = expand_bias(earth_bias, pole)

    places = window_rows(rows, cols)
    sizes = [part.size for part in piece_rows(rows, cols)]
    pieces = (own, north, side, corner)
    q, k, v, p, mixed, normed, unit, spread, gsum, keep, sent = forward(
        rank, pieces, spots(places), bias, triple_weight, project_weight, up_weight, down_weight.T, lon_windows
    )
    near, far = reduce_all(keep, sent, (), shift, lon_count)
    up, down = finish(finish_mlp_kernel, [shape((C, FF), f32)] * 2, [], rank, near, far, "finish_mlp")

    grads = windows_back(q, k, v, p, gsum, project_weight)
    own, north, side, corner, land, keep, sent = tokens_back(
        rank, grads, mixed, normed, unit, spread, gsum, spots(np.argsort(places)), triple_weight, pieces, sizes
    )
    near, far = reduce_all(keep, sent, (land,), shift, lon_count)
    triple, project, land = finish(
        finish_attn_kernel,
        [shape((C, 3 * C), f32), shape((C, C), f32), shape((1, C), f32)],
        [pltpu.VMEM((C, FF), f32), pltpu.VMEM((2 * QUADS * EXTRA, C), f32)],
        rank, near, far, "finish_attn",
    )
    north = shift(north, move=lambda lon, lat: (lon, lat - 1))
    side = shift(side, move=lambda lon, lat: (lon - 1, lat))
    corner = shift(corner, move=lambda lon, lat: (lon - 1, lat - 1))
    grad_tokens = to_home((own, north, side, corner), sizes, rows, cols)
    return grad_tokens.reshape(tokens.shape), triple, project, up, down.T, land.reshape(features)


def solution(mesh):
    return jax.shard_map(
        functools.partial(body, mesh.shape["lon"], mesh.shape["lat"]),
        mesh=mesh,
        in_specs=(
            P(None, "lat", "lon", None),
            P(None, "lat", "lon", None),
            P("lat", "lon"),
            P(),
            P(),
            P(),
            P(),
            P(),
            P("lat", None, None, None, None),
        ),
        out_specs=(P(None, "lat", "lon", None), P(), P(), P(), P(), P()),
        check_vma=False,
    )
```

```python
import functools
import math

import jax
import jax.numpy as jnp
import numpy as np
from jax import lax
from jax.experimental import pallas as pl
from jax.experimental.pallas import tpu as pltpu
from jax.sharding import PartitionSpec as P

Z = 4
WZ = 2
WH = 6
WW = 12
C = 192
HEADS = 6
HEAD = 32
FF = 768
HZ, HH, HW = WZ // 2, WH // 2, WW // 2
TOK = WZ * WH * WW
PLACES = WZ * WH
RELW = 2 * WW - 1
STRIP = -(-RELW * PLACES // 128) * 128

mask_fill = -10000.0
norm_eps = 1e-05
log2e = 1.4426950408889634
root_half = 0.7071067811865476
inv_root_tau = 0.3989422804014327
score_scale = HEAD**-0.5

f32 = jnp.float32
bf16 = jnp.bfloat16
MIB = 1 << 20

QUADS = 4
PART = C // (2 * QUADS)
CHUNK = 3 * PART
EXTRA = 8
FULL = CHUNK + EXTRA
HALF = FULL // 2


def mm(a, b):
    return lax.dot_general(a, b, (((1,), (0,)), ((), ())), preferred_element_type=f32)


def mm_nt(a, b):
    return lax.dot_general(a, b, (((1,), (1,)), ((), ())), preferred_element_type=f32)


def mm_tn(a, b):
    return lax.dot_general(a, b, (((0,), (0,)), ((), ())), preferred_element_type=f32)


def unit_norm(values):
    average = jnp.mean(values, -1, keepdims=True)
    centred = values - average
    variance = jnp.mean(centred * centred, -1, keepdims=True)
    spread = lax.rsqrt(variance + norm_eps)
    return centred * spread, spread


def norm_back(upstream, unit, spread):
    first = jnp.mean(upstream, -1, keepdims=True)
    second = jnp.mean(upstream * unit, -1, keepdims=True)
    return spread * (upstream - first - unit * second)


def piece_rows(rows, cols):
    home = np.arange(Z * rows * cols).reshape(Z, rows, cols)
    top, low = slice(0, rows - HH), slice(rows - HH, rows)
    west, east = slice(0, cols - HW), slice(cols - HW, cols)
    parts = [home[:, top, west], home[:, low, west], home[:, top, east], home[:, low, east]]
    return [part.reshape(-1) for part in parts]


def window_rows(rows, cols):
    sizes = [part.size for part in piece_rows(rows, cols)]
    starts = np.cumsum([0] + sizes)
    own, north, side, corner = [np.arange(starts[k], starts[k + 1]) for k in range(4)]
    frame = np.zeros((Z, rows, cols), np.int64)
    frame[:, HH:, HW:] = own.reshape(Z, rows - HH, cols - HW)
    frame[:, :HH, HW:] = north.reshape(Z, HH, cols - HW)
    frame[:, HH:, :HW] = side.reshape(Z, rows - HH, HW)
    frame[:, :HH, :HW] = corner.reshape(Z, HH, HW)
    frame = np.roll(frame, HZ, axis=0)
    frame = frame.reshape(Z // WZ, WZ, rows // WH, WH, cols // WW, WW)
    return frame.transpose(0, 2, 4, 5, 1, 3).reshape(-1)


def spots(places):
    return jnp.asarray(np.argsort(places).astype(np.int32)[None])


def one_hot(spot_ref):
    count = spot_ref.shape[1]
    rows = lax.broadcasted_iota(jnp.int32, (count, count), 0)
    return (rows == spot_ref[...]).astype(f32).astype(bf16)


def vmem(count):
    return [pl.BlockSpec(memory_space=pltpu.VMEM)] * count


smem = pl.BlockSpec(memory_space=pltpu.SMEM)


def shape(dims, dtype):
    return jax.ShapeDtypeStruct(dims, dtype)


def cost(flops, moved):
    return pl.CostEstimate(flops=flops, bytes_accessed=moved, transcendentals=0)


def land_column(land_ref, rows, cols):
    eye = (
        lax.broadcasted_iota(jnp.int32, (cols, cols), 0)
        == lax.broadcasted_iota(jnp.int32, (cols, cols), 1)
    ).astype(f32)
    land = land_ref[...].astype(f32)
    parts = [jnp.sum(eye * land[i : i + 1, :], -1, keepdims=True) for i in range(rows)]
    return jnp.concatenate(parts, axis=0)


def pack_kernel(rows, cols, tokens_ref, cot_ref, land_ref, vec_ref, perm_ref, *outs):
    column = land_column(land_ref, rows, cols)
    added = column * vec_ref[...]
    added = jnp.concatenate([added] * Z, axis=0)
    embedded = (tokens_ref[...].astype(f32) + added).astype(bf16)
    perm = one_hot(perm_ref)
    left = mm(perm, embedded)
    right = mm(perm, cot_ref[...])
    packed = jnp.concatenate([left, right], axis=1)
    column = jnp.concatenate([column] * Z, axis=0)
    flags = mm(perm, jnp.broadcast_to(column, (column.shape[0], 128)).astype(bf16))
    start = 0
    for out in outs:
        count = out.shape[0] - EXTRA
        eye = lax.broadcasted_iota(jnp.int32, (count, count), 0) == lax.broadcasted_iota(jnp.int32, (count, count), 1)
        row = jnp.sum(jnp.where(eye, flags[start : start + count, 0:1], 0.0), 0, keepdims=True)
        row = jnp.concatenate([row, jnp.zeros((1, 2 * C - count), f32)], axis=1)
        row = jnp.broadcast_to(row, (EXTRA, 2 * C))
        out[...] = jnp.concatenate([packed[start : start + count], row], axis=0).astype(bf16)
        start += count


def pack(tokens, cotangent, land_sea, vector, rows, cols):
    parts = piece_rows(rows, cols)
    perm = spots(np.concatenate(parts))
    count = Z * rows * cols
    return pl.pallas_call(
        functools.partial(pack_kernel, rows, cols),
        out_shape=[shape((part.size + EXTRA, 2 * C), bf16) for part in parts],
        in_specs=vmem(5),
        out_specs=vmem(4),
        cost_estimate=cost(4 * count * count * C, 4 * MIB),
        name="pack",
    )(tokens.reshape(count, C), cotangent.reshape(count, C), land_sea, vector.reshape(1, C), perm)


def bias_kernel(groups, pole_ref, table_ref, spread_ref, place_ref, rowlab_ref, lanelab_ref, out_ref, *wide_refs):
    table = table_ref[...]
    high = table.astype(bf16)
    rest = table - high.astype(f32)
    middle = rest.astype(bf16)
    low = (rest - middle.astype(f32)).astype(bf16)
    onehot = spread_ref[...]
    wide = mm(high, onehot) + mm(middle, onehot) + mm(low, onehot)
    strips = groups * PLACES
    parts = []
    for n in range(STRIP // 128):
        lanes = slice(n * 128, (n + 1) * 128)
        wide_ref = wide_refs[n]
        wide_ref[...] = wide[:, lanes]
        place = place_ref[:, lanes]
        part = jnp.zeros((strips, 128), f32)
        for p in range(PLACES):
            part = jnp.where(place == p, wide_ref[pl.ds(p, strips, stride=PLACES), :], part)
        parts.append(part)
    strip = jnp.concatenate(parts, axis=1)
    pole = pole_ref[0].astype(f32)
    rowlab = rowlab_ref[...]
    lanelab = lanelab_ref[...]
    differs = jnp.maximum(
        rowlab[:, 2:3] * jnp.abs(rowlab[:, 0:1] - lanelab[0:1, :]),
        pole * jnp.abs(rowlab[:, 1:2] - lanelab[1:2, :]),
    )
    strip = (strip + mask_fill * differs) * log2e
    for w in range(WW):
        start = (WW - 1 - w) * PLACES
        part = strip[:, start : start + TOK]
        for g in range(groups):
            out_ref[g, w * PLACES : (w + 1) * PLACES, :] = part[g * PLACES : (g + 1) * PLACES, :]


def expand_bias(table, pole):
    levels = table.shape[1]
    groups = levels * HEADS
    flat = table.reshape(groups * PLACES * PLACES, RELW)
    onehot = np.zeros((RELW, STRIP), np.float32)
    for r in range(RELW):
        onehot[RELW - 1 - r, r * PLACES : (r + 1) * PLACES] = 1.0
    place = (np.arange(STRIP) % PLACES).astype(np.int32)[None]
    level_label = (np.arange(PLACES) // WH < HZ).astype(np.float32)
    lat_label = (np.arange(PLACES) % WH < HH).astype(np.float32)
    rowlab = np.zeros((groups, PLACES, 3), np.float32)
    rowlab[:, :, 0] = level_label
    rowlab[:, :, 1] = lat_label
    rowlab[:HEADS, :, 2] = 1.0
    lanelab = np.zeros((2, STRIP), np.float32)
    lanelab[:, : RELW * PLACES] = np.stack([np.tile(level_label, RELW), np.tile(lat_label, RELW)])
    return pl.pallas_call(
        functools.partial(bias_kernel, groups),
        out_shape=shape((groups, TOK, TOK), f32),
        in_specs=[smem] + vmem(5),
        out_specs=vmem(1)[0],
        scratch_shapes=[pltpu.VMEM((groups * PLACES * PLACES, 128), f32)] * (STRIP // 128),
        compiler_params=pltpu.CompilerParams(vmem_limit_bytes=32 * MIB),
        cost_estimate=cost(10**9, 8 * MIB),
        name="bias",
    )(pole, flat, jnp.asarray(onehot, bf16), jnp.asarray(place), jnp.asarray(rowlab.reshape(-1, 3)), jnp.asarray(lanelab))


def head_masks(count):
    lane = lax.broadcasted_iota(jnp.int32, (count, C), 1)
    return [((lane >= h * HEAD) & (lane < (h + 1) * HEAD)).astype(f32) for h in range(HEADS)]


def stacked(values, masks):
    return jnp.concatenate([values * mask for mask in masks], axis=0)


def head_sum(values, masks):
    total = values[:TOK] * masks[0]
    for h in range(1, HEADS):
        total = total + values[h * TOK : (h + 1) * TOK] * masks[h]
    return total


def block_of(core, chip, g):
    first, second = g >> 1, g & 1
    flip = jnp.where(core == 0, first + 2 * second, 2 * first + second)
    return core * QUADS + jnp.bitwise_xor(chip, flip)


def chunk_rows(block):
    return pl.ds(pl.multiple_of(block * PART, PART), PART)


def split_parts(rank_ref, total_refs, keep_ref, send_ref):
    core, chip = rank_ref[0], rank_ref[1]
    for out, side in ((keep_ref, core), (send_ref, 1 - core)):
        parts = []
        for g in range(QUADS):
            rows = chunk_rows(block_of(side, chip, g))
            parts += [ref[rows, :] for ref in total_refs]
        out[...] = jnp.concatenate(parts, axis=0).astype(out.dtype)


def forward_kernel(
    windows, lon_windows,
    own_ref, north_ref, side_ref, corner_ref, perm_ref, bias_ref, triple_ref, project_ref, up_ref, down_ref,
    q_ref, k_ref, v_ref, p_ref, mixed_ref, normed_ref, unit_ref, spread_ref, gsum_ref, up_grad_ref, down_grad_ref,
    branch_ref, cot_ref, emb_ref,
):
    pieces = [ref[...].astype(f32)[:-EXTRA] for ref in (own_ref, north_ref, side_ref, corner_ref)]
    pieces = jnp.concatenate(pieces, axis=0).astype(bf16)
    ordered = mm(one_hot(perm_ref), pieces)
    emb = ordered[:, :C]
    emb_ref[...] = emb
    cot_ref[...] = ordered[:, C:].astype(bf16)
    unit, spread = unit_norm(emb)
    unit_ref[...] = unit
    spread_ref[...] = spread
    normed = unit.astype(bf16)
    normed_ref[...] = normed
    packed = mm(normed, triple_ref[...])
    q_ref[...] = packed[:, :C].astype(bf16)
    k_ref[...] = packed[:, C : 2 * C].astype(bf16)
    v_ref[...] = packed[:, 2 * C :].astype(bf16)
    masks = head_masks(TOK)
    masks_b = [mask.astype(bf16) for mask in masks]

    def window_step(w, carry):
        rows = pl.ds(pl.multiple_of(w * TOK, TOK), TOK)
        level = w // lon_windows
        scores = mm_nt(stacked(q_ref[rows, :], masks_b), k_ref[rows, :])
        bias = bias_ref[pl.ds(level * HEADS, HEADS)].reshape(HEADS * TOK, TOK)
        raised = jnp.exp2(scores * (score_scale * log2e) + bias)
        probs = raised * (1.0 / jnp.sum(raised, -1, keepdims=True))
        probs_b = probs.astype(bf16)
        p_ref[pl.ds(w * HEADS, HEADS)] = probs_b.reshape(HEADS, TOK, TOK)
        mixed = head_sum(mm(probs_b, v_ref[rows, :]), masks).astype(bf16)
        mixed_ref[rows, :] = mixed
        branch_ref[rows, :] = mm(mixed, project_ref[...])
        return carry

    lax.fori_loop(0, windows, window_step, 0)

    attended = branch_ref[...].astype(bf16).astype(f32)
    unit2, spread2 = unit_norm(emb_ref[...] + attended)
    normed2 = unit2.astype(bf16)
    cot = cot_ref[...]
    back = jnp.zeros(unit2.shape, f32)
    block = 256
    for start in range(0, FF, block):
        cols = slice(start, start + block)
        up_part = up_ref[:, cols]
        pre = mm(normed2, up_part)
        upstream = mm(cot, down_ref[:, cols])
        phi = 0.5 * (1.0 + lax.erf(pre * root_half))
        activated = (pre * phi).astype(bf16)
        slope = phi + pre * inv_root_tau * jnp.exp2(pre * pre * (-0.5 * log2e))
        hidden = (upstream * slope).astype(bf16)
        up_grad_ref[:, cols] = mm_tn(normed2, hidden)
        down_grad_ref[:, cols] = mm_tn(cot, activated)
        back = back + mm_nt(hidden, up_part)
    gsum_ref[...] = cot.astype(f32) + norm_back(back, unit2, spread2)


def forward(pieces, perm, bias, triple, project, up, down, lon_windows):
    count = perm.shape[1]
    windows = count // TOK
    out_shape = [
        shape((count, C), bf16),
        shape((count, C), bf16),
        shape((count, C), bf16),
        shape((windows * HEADS, TOK, TOK), bf16),
        shape((count, C), bf16),
        shape((count, C), bf16),
        shape((count, C), f32),
        shape((count, 1), f32),
        shape((count, C), f32),
        shape((C, FF), f32),
        shape((C, FF), f32),
    ]
    return pl.pallas_call(
        functools.partial(forward_kernel, windows, lon_windows),
        out_shape=out_shape,
        in_specs=vmem(10),
        out_specs=vmem(len(out_shape)),
        scratch_shapes=[pltpu.VMEM((count, C), f32), pltpu.VMEM((count, C), bf16), pltpu.VMEM((count, C), f32)],
        compiler_params=pltpu.CompilerParams(vmem_limit_bytes=28 * MIB),
        cost_estimate=cost(3 * 10**9, 16 * MIB),
        name="forward",
    )(*pieces, perm, bias, triple, project, up, down)


def windows_back_kernel(windows, q_ref, k_ref, v_ref, p_ref, gsum_ref, project_ref, gq_ref, gk_ref, gv_ref):
    masks = head_masks(TOK)
    masks_b = [mask.astype(bf16) for mask in masks]

    def window_step(w, carry):
        rows = pl.ds(pl.multiple_of(w * TOK, TOK), TOK)
        grad = gsum_ref[rows, :].astype(bf16)
        grad_mixed = mm_nt(grad, project_ref[...])
        grad_mixed_b = grad_mixed.astype(bf16)
        probs_b = p_ref[pl.ds(w * HEADS, HEADS)].reshape(HEADS * TOK, TOK)
        probs = probs_b.astype(f32)
        grad_probs = mm_nt(stacked(grad_mixed_b, masks_b), v_ref[rows, :])
        inner = jnp.sum(grad_probs * probs, -1, keepdims=True)
        scaled = (probs * (grad_probs - inner) * score_scale).astype(bf16)
        grad_q = head_sum(mm(scaled, k_ref[rows, :]), masks)
        grad_mixed_t = grad_mixed_b.astype(f32).T.astype(bf16)
        query_t = q_ref[rows, :].astype(f32).T.astype(bf16)
        grad_k, grad_v = [], []
        for h in range(HEADS):
            spot = slice(h * HEAD, (h + 1) * HEAD)
            span = slice(h * TOK, (h + 1) * TOK)
            grad_k.append(mm(query_t[spot], scaled[span]))
            grad_v.append(mm(grad_mixed_t[spot], probs_b[span]))
        gq_ref[rows, :] = grad_q.astype(bf16)
        gk_ref[rows, :] = jnp.concatenate(grad_k, axis=0).T.astype(bf16)
        gv_ref[rows, :] = jnp.concatenate(grad_v, axis=0).T.astype(bf16)
        return carry

    lax.fori_loop(0, windows, window_step, 0)


def windows_back(q, k, v, p, gsum, project):
    count = q.shape[0]
    return pl.pallas_call(
        functools.partial(windows_back_kernel, count // TOK),
        out_shape=[shape((count, C), bf16)] * 3,
        in_specs=vmem(6),
        out_specs=vmem(3),
        compiler_params=pltpu.CompilerParams(vmem_limit_bytes=28 * MIB),
        cost_estimate=cost(3 * 10**9, 16 * MIB),
        name="windows_back",
    )(q, k, v, p, gsum, project)


def halved(rows):
    return -(-rows // 16) * 8


def tokens_back_kernel(
    sizes, rank_ref, gq_ref, gk_ref, gv_ref, mixed_ref, normed_ref, unit_ref, spread_ref, gsum_ref, perm_ref, triple_ref,
    up_grad_ref, down_grad_ref, *rest,
):
    flag_refs, rest = rest[: len(sizes)], rest[len(sizes) :]
    outs, (land_ref, keep_ref, send_ref, total_ref) = rest[: len(sizes)], rest[len(sizes) :]
    normed = normed_ref[...]
    triple = triple_ref[...]
    grad_normed = jnp.zeros(unit_ref.shape, f32)
    parts = []
    for n, ref in enumerate((gq_ref, gk_ref, gv_ref)):
        grad = ref[...]
        grad_normed = grad_normed + mm_nt(grad, triple[:, n * C : (n + 1) * C])
        parts.append(mm_tn(normed, grad))
    parts.append(mm_tn(mixed_ref[...], gsum_ref[...].astype(bf16)))
    total_ref[...] = jnp.concatenate(parts, axis=1)
    grad_normed = grad_normed.astype(bf16).astype(f32)
    grad_tokens = gsum_ref[...] + norm_back(grad_normed, unit_ref[...], spread_ref[...])
    pieces = mm(one_hot(perm_ref), grad_tokens.astype(bf16))
    land = jnp.zeros((EXTRA, C), f32)
    start = 0
    for size, out, flag_ref in zip(sizes, outs, flag_refs):
        piece = pieces[start : start + size]
        flags = flag_ref[size - 8 : size + 8, :].astype(f32)[8:, :size]
        land = land + mm(flags.astype(bf16), piece.astype(bf16))
        half = halved(size)
        second = jnp.concatenate([piece[half:], jnp.zeros((2 * half - size, C), f32)], axis=0)
        out[...] = jnp.concatenate([piece[:half], second], axis=1).astype(bf16)
        start += size
    land_ref[...] = land[0:1]
    split_parts(rank_ref, (up_grad_ref, down_grad_ref, total_ref), keep_ref, send_ref)


def tokens_back(rank, grads, mixed, normed, unit, spread, gsum, perm, triple, up_grad, down_grad, pieces, sizes):
    out_shape = [shape((halved(size), 2 * C), bf16) for size in sizes] + [
        shape((1, C), f32),
        shape((QUADS * CHUNK, FF), f32),
        shape((QUADS * CHUNK, FF), bf16),
    ]
    return pl.pallas_call(
        functools.partial(tokens_back_kernel, sizes),
        out_shape=out_shape,
        in_specs=[smem] + vmem(12 + len(pieces)),
        out_specs=vmem(len(out_shape)),
        scratch_shapes=[pltpu.VMEM((C, FF), f32)],
        compiler_params=pltpu.CompilerParams(vmem_limit_bytes=28 * MIB),
        cost_estimate=cost(2 * 10**9, 8 * MIB),
        name="tokens_back",
    )(rank, *grads, mixed, normed, unit, spread, gsum, perm, triple, up_grad, down_grad, *pieces)


def home_kernel(sizes, own_ref, north_ref, side_ref, corner_ref, perm_ref, out_ref):
    pieces = []
    for size, ref in zip(sizes, (own_ref, north_ref, side_ref, corner_ref)):
        wide = ref[...].astype(f32)
        pieces += [wide[:, :C], wide[: size - wide.shape[0], C:]]
    pieces = jnp.concatenate(pieces, axis=0).astype(bf16)
    out_ref[...] = mm(one_hot(perm_ref), pieces).astype(bf16)


def to_home(pieces, sizes, rows, cols):
    count = Z * rows * cols
    perm = spots(np.argsort(np.concatenate(piece_rows(rows, cols))))
    return pl.pallas_call(
        functools.partial(home_kernel, sizes),
        out_shape=shape((count, C), bf16),
        in_specs=vmem(5),
        out_specs=vmem(1)[0],
        compiler_params=pltpu.CompilerParams(vmem_limit_bytes=32 * MIB),
        cost_estimate=cost(2 * count * count * C, 4 * MIB),
        name="to_home",
    )(*pieces, perm)


def halve_kernel(keep_ref, got_ref, own_ref, send_ref):
    total = keep_ref[...] + got_ref[...].astype(f32)
    half = own_ref.shape[0]
    own_ref[...] = total[:half]
    send_ref[...] = total[half:].astype(bf16)


def deep_halve_kernel(rank_ref, keep_ref, got_ref, land_ref, own_ref, send_ref, total_ref):
    land = jnp.concatenate([land_ref[...], jnp.zeros((1, FF - C), f32)], axis=1)
    land = jnp.concatenate([land, jnp.zeros((EXTRA - 1, FF), f32)], axis=0)
    total_ref[...] = jnp.concatenate([keep_ref[...] + got_ref[...].astype(f32), land], axis=0)
    deep = rank_ref[2]
    own_ref[...] = total_ref[pl.ds(pl.multiple_of(deep * HALF, 8), HALF), :]
    send_ref[...] = total_ref[pl.ds(pl.multiple_of((1 - deep) * HALF, 8), HALF), :].astype(bf16)


def add_kernel(one_ref, two_ref, out_ref):
    out_ref[...] = (one_ref[...].astype(f32) + two_ref[...].astype(f32)).astype(bf16)


def add_after_kernel(one_ref, two_ref, *refs):
    add_kernel(one_ref, two_ref, refs[-1])


def deep_join_kernel(rank_ref, own_ref, got_ref, out_ref):
    own, got = own_ref[...].astype(f32), got_ref[...].astype(f32)
    swap = rank_ref[2] == 1
    both = [jnp.where(swap, got, own), jnp.where(swap, own, got)]
    out_ref[...] = jnp.concatenate(both, axis=0).astype(bf16)


def join_kernel(own_ref, got_ref, out_ref):
    out_ref[...] = jnp.concatenate([own_ref[...], got_ref[...]], axis=0)


def small_call(kernel, out_shape, args, name, rank=(), after=(), scratch=()):
    return pl.pallas_call(
        kernel,
        out_shape=out_shape,
        in_specs=[smem] * len(rank) + vmem(len(args)) + [pl.BlockSpec(memory_space=pl.ANY)] * len(after),
        out_specs=vmem(len(out_shape)),
        scratch_shapes=scratch,
        compiler_params=pltpu.CompilerParams(vmem_limit_bytes=16 * MIB),
        cost_estimate=cost(10**6, 2 * MIB),
        name=name,
    )(*rank, *args, *after)


def finish_kernel(
    rank_ref, own_ref, got_ref, triple_ref, project_ref, up_ref, down_ref, land_ref, wide_ref, lands_ref
):
    core, chip = rank_ref[0], rank_ref[1]
    for side, ref in ((core, own_ref), (1 - core, got_ref)):
        for g in range(QUADS):
            chunk = ref[g * FULL : (g + 1) * FULL, :].astype(f32)
            block = block_of(side, chip, g)
            rows = chunk_rows(block)
            up_ref[rows, :] = chunk[:PART]
            down_ref[rows, :] = chunk[PART : 2 * PART]
            wide_ref[rows, :] = chunk[2 * PART : CHUNK]
            lands_ref[pl.ds(pl.multiple_of(block * EXTRA, EXTRA), EXTRA), :] = chunk[CHUNK:, :C]
    triple_ref[...] = wide_ref[:, : 3 * C]
    project_ref[...] = wide_ref[:, 3 * C :]
    land_ref[...] = jnp.sum(lands_ref[...], 0, keepdims=True)


def finish(rank, own, got):
    out_shape = [shape((C, 3 * C), f32), shape((C, C), f32), shape((C, FF), f32), shape((C, FF), f32), shape((1, C), f32)]
    scratch = [pltpu.VMEM((C, FF), f32), pltpu.VMEM((2 * QUADS * EXTRA, C), f32)]
    return small_call(finish_kernel, out_shape, (own, got), "finish", (rank,), scratch=scratch)


def reduce_all(keep, sent, land, rank, shift, lon_count, after):
    core_move = lambda lon, lat: (lon, lat ^ 1)
    first_move = lambda lon, lat: (lon, lat ^ 2) if lat & 1 else (lon ^ 1, lat)
    second_move = lambda lon, lat: (lon ^ 1, lat) if lat & 1 else (lon, lat ^ 2)
    deep_move = lambda lon, lat: (lon ^ 2, lat)

    def both(rows):
        return [shape((rows, FF), f32), shape((rows, FF), bf16)]

    def one(rows):
        return [shape((rows, FF), bf16)]

    got = shift(sent, move=core_move)
    keep, sent = small_call(halve_kernel, both(2 * CHUNK), (keep, got), "core_add")
    got = shift(sent, move=first_move)
    keep, sent = small_call(halve_kernel, both(CHUNK), (keep, got), "first_add")
    got = shift(sent, move=second_move)
    scratch = [pltpu.VMEM((FULL, FF), f32)]
    keep, sent = small_call(deep_halve_kernel, both(HALF), (keep, got, land), "second_add", (rank,), scratch=scratch)
    got = shift(sent, move=deep_move)
    (total,) = small_call(add_kernel, one(HALF), (keep, got), "deep_add")
    reach = 4
    while reach < lon_count:
        got = shift(total, move=lambda lon, lat, reach=reach: (lon ^ reach, lat))
        reach *= 2
        waits = () if reach < lon_count else after
        (total,) = small_call(add_after_kernel, one(HALF), (total, got), "far_add", after=waits)
    got = shift(total, move=deep_move)
    (total,) = small_call(deep_join_kernel, one(FULL), (total, got), "deep_join", (rank,))
    got = shift(total, move=second_move)
    (total,) = small_call(join_kernel, one(2 * FULL), (total, got), "second_join")
    got = shift(total, move=first_move)
    (total,) = small_call(join_kernel, one(4 * FULL), (total, got), "first_join")
    return finish(rank, total, shift(total, move=core_move))


AXES = ("lon", "lat")


def send(value, lon_count, lat_count, move):
    pairs = []
    for lon in range(lon_count):
        for lat in range(lat_count):
            to_lon, to_lat = move(lon, lat)
            pairs.append((lon * lat_count + lat, (to_lon % lon_count) * lat_count + to_lat % lat_count))
    return lax.ppermute(value, AXES, pairs)


def body(
    lon_count, lat_count,
    tokens, cotangent, land_sea, land_vector, triple_weight, project_weight, up_weight, down_weight, earth_bias,
):
    levels, rows, cols, features = tokens.shape
    shift = functools.partial(send, lon_count=lon_count, lat_count=lat_count)
    lon_at, lat_at = lax.axis_index("lon"), lax.axis_index("lat")
    rank = jnp.stack([lat_at % 2, 2 * (lat_at // 2) + lon_at % 2, lon_at // 2 % 2]).astype(jnp.int32)
    pole = (lat_at == 0).astype(jnp.int32).reshape(1)
    lon_windows = cols // WW

    own, north, side, corner = pack(tokens, cotangent, land_sea, land_vector, rows, cols)
    north = shift(north, move=lambda lon, lat: (lon, lat + 1))
    side = shift(side, move=lambda lon, lat: (lon + 1, lat))
    corner = shift(corner, move=lambda lon, lat: (lon + 1, lat + 1))
    bias = expand_bias(earth_bias, pole)

    places = window_rows(rows, cols)
    sizes = [part.size for part in piece_rows(rows, cols)]
    pieces = (own, north, side, corner)
    q, k, v, p, mixed, normed, unit, spread, gsum, up, down = forward(
        pieces, spots(places), bias, triple_weight, project_weight, up_weight, down_weight.T, lon_windows
    )
    grads = windows_back(q, k, v, p, gsum, project_weight)
    own, north, side, corner, land, keep, sent = tokens_back(
        rank, grads, mixed, normed, unit, spread, gsum, spots(np.argsort(places)), triple_weight, up, down, pieces, sizes
    )
    north = shift(north, move=lambda lon, lat: (lon, lat - 1))
    side = shift(side, move=lambda lon, lat: (lon - 1, lat))
    corner = shift(corner, move=lambda lon, lat: (lon - 1, lat - 1))
    after = (north, side, corner)
    triple, project, up, down, land = reduce_all(keep, sent, land, rank, shift, lon_count, after)
    grad_tokens = to_home((own, north, side, corner), sizes, rows, cols)
    return grad_tokens.reshape(tokens.shape), triple, project, up, down.T, land.reshape(features)


def solution(mesh):
    return jax.shard_map(
        functools.partial(body, mesh.shape["lon"], mesh.shape["lat"]),
        mesh=mesh,
        in_specs=(
            P(None, "lat", "lon", None),
            P(None, "lat", "lon", None),
            P("lat", "lon"),
            P(),
            P(),
            P(),
            P(),
            P(),
            P("lat", None, None, None, None),
        ),
        out_specs=(P(None, "lat", "lon", None), P(), P(), P(), P(), P()),
        check_vma=False,
    )
```

```python
import functools
import math

import jax
import jax.numpy as jnp
import numpy as np
from jax import lax
from jax.experimental import pallas as pl
from jax.experimental.pallas import tpu as pltpu
from jax.sharding import PartitionSpec as P

Z = 4
WZ = 2
WH = 6
WW = 12
C = 192
HEADS = 6
HEAD = 32
FF = 768
HZ, HH, HW = WZ // 2, WH // 2, WW // 2
TOK = WZ * WH * WW
PLACES = WZ * WH
RELW = 2 * WW - 1
STRIP = -(-RELW * PLACES // 128) * 128

mask_fill = -10000.0
norm_eps = 1e-05
log2e = 1.4426950408889634
root_half = 0.7071067811865476
inv_root_tau = 0.3989422804014327
score_scale = HEAD**-0.5

f32 = jnp.float32
bf16 = jnp.bfloat16
MIB = 1 << 20

QUADS = 4
PART = C // (2 * QUADS)
CHUNK = 3 * PART
EXTRA = 8
FULL = CHUNK + EXTRA
HALF = FULL // 2


def mm(a, b):
    return lax.dot_general(a, b, (((1,), (0,)), ((), ())), preferred_element_type=f32)


def mm_nt(a, b):
    return lax.dot_general(a, b, (((1,), (1,)), ((), ())), preferred_element_type=f32)


def mm_tn(a, b):
    return lax.dot_general(a, b, (((0,), (0,)), ((), ())), preferred_element_type=f32)


def unit_norm(values):
    average = jnp.mean(values, -1, keepdims=True)
    centred = values - average
    variance = jnp.mean(centred * centred, -1, keepdims=True)
    spread = lax.rsqrt(variance + norm_eps)
    return centred * spread, spread


def norm_back(upstream, unit, spread):
    first = jnp.mean(upstream, -1, keepdims=True)
    second = jnp.mean(upstream * unit, -1, keepdims=True)
    return spread * (upstream - first - unit * second)


def piece_rows(rows, cols):
    home = np.arange(Z * rows * cols).reshape(Z, rows, cols)
    top, low = slice(0, rows - HH), slice(rows - HH, rows)
    west, east = slice(0, cols - HW), slice(cols - HW, cols)
    parts = [home[:, top, west], home[:, low, west], home[:, top, east], home[:, low, east]]
    return [part.reshape(-1) for part in parts]


def window_rows(rows, cols):
    sizes = [part.size for part in piece_rows(rows, cols)]
    starts = np.cumsum([0] + sizes)
    own, north, side, corner = [np.arange(starts[k], starts[k + 1]) for k in range(4)]
    frame = np.zeros((Z, rows, cols), np.int64)
    frame[:, HH:, HW:] = own.reshape(Z, rows - HH, cols - HW)
    frame[:, :HH, HW:] = north.reshape(Z, HH, cols - HW)
    frame[:, HH:, :HW] = side.reshape(Z, rows - HH, HW)
    frame[:, :HH, :HW] = corner.reshape(Z, HH, HW)
    frame = np.roll(frame, HZ, axis=0)
    frame = frame.reshape(Z // WZ, WZ, rows // WH, WH, cols // WW, WW)
    return frame.transpose(0, 2, 4, 5, 1, 3).reshape(-1)


def spots(places):
    return jnp.asarray(np.argsort(places).astype(np.int32)[None])


def one_hot(spot_ref):
    count = spot_ref.shape[1]
    rows = lax.broadcasted_iota(jnp.int32, (count, count), 0)
    return (rows == spot_ref[...]).astype(f32).astype(bf16)


def vmem(count):
    return [pl.BlockSpec(memory_space=pltpu.VMEM)] * count


smem = pl.BlockSpec(memory_space=pltpu.SMEM)


def shape(dims, dtype):
    return jax.ShapeDtypeStruct(dims, dtype)


def cost(flops, moved):
    return pl.CostEstimate(flops=flops, bytes_accessed=moved, transcendentals=0)


def land_column(land_ref, rows, cols):
    eye = (
        lax.broadcasted_iota(jnp.int32, (cols, cols), 0)
        == lax.broadcasted_iota(jnp.int32, (cols, cols), 1)
    ).astype(f32)
    land = land_ref[...].astype(f32)
    parts = [jnp.sum(eye * land[i : i + 1, :], -1, keepdims=True) for i in range(rows)]
    return jnp.concatenate(parts, axis=0)


def pack_kernel(rows, cols, *refs):
    sources, outs, (tokens_ref, cot_ref, land_ref, vec_ref, perm_ref, sems) = refs[:5], refs[5:-6], refs[-6:]
    copies = [
        pltpu.make_async_copy(source, target, sems.at[n])
        for n, (source, target) in enumerate(zip(sources, (tokens_ref, cot_ref, land_ref, vec_ref, perm_ref)))
    ]
    for copy in copies:
        copy.start()
    for copy in copies:
        copy.wait()
    column = land_column(land_ref, rows, cols)
    added = column * vec_ref[...]
    added = jnp.concatenate([added] * Z, axis=0)
    embedded = (tokens_ref[...].astype(f32) + added).astype(bf16)
    perm = one_hot(perm_ref)
    left = mm(perm, embedded)
    right = mm(perm, cot_ref[...])
    packed = jnp.concatenate([left, right], axis=1)
    column = jnp.concatenate([column] * Z, axis=0)
    flags = mm(perm, jnp.broadcast_to(column, (column.shape[0], 128)).astype(bf16))
    start = 0
    for out in outs:
        count = out.shape[0] - EXTRA
        eye = lax.broadcasted_iota(jnp.int32, (count, count), 0) == lax.broadcasted_iota(jnp.int32, (count, count), 1)
        row = jnp.sum(jnp.where(eye, flags[start : start + count, 0:1], 0.0), 0, keepdims=True)
        row = jnp.concatenate([row, jnp.zeros((1, 2 * C - count), f32)], axis=1)
        row = jnp.broadcast_to(row, (EXTRA, 2 * C))
        out[...] = jnp.concatenate([packed[start : start + count], row], axis=0).astype(bf16)
        start += count


def pack(tokens, cotangent, land_sea, vector, rows, cols):
    parts = piece_rows(rows, cols)
    perm = spots(np.concatenate(parts))
    count = Z * rows * cols
    return pl.pallas_call(
        functools.partial(pack_kernel, rows, cols),
        out_shape=[shape((part.size + EXTRA, 2 * C), bf16) for part in parts],
        in_specs=[pl.BlockSpec(memory_space=pltpu.HBM)] * 5,
        out_specs=vmem(4),
        scratch_shapes=[
            pltpu.VMEM((count, C), bf16),
            pltpu.VMEM((count, C), bf16),
            pltpu.VMEM((rows, cols), jnp.int32),
            pltpu.VMEM((1, C), f32),
            pltpu.VMEM((1, count), jnp.int32),
            pltpu.SemaphoreType.DMA((5,)),
        ],
        compiler_params=pltpu.CompilerParams(vmem_limit_bytes=16 * MIB),
        cost_estimate=cost(4 * count * count * C, 4 * MIB),
        name="pack",
    )(tokens.reshape(count, C), cotangent.reshape(count, C), land_sea, vector.reshape(1, C), perm)


def bias_kernel(groups, pole_ref, table_ref, spread_ref, place_ref, rowlab_ref, lanelab_ref, out_ref, *wide_refs):
    table = table_ref[...]
    high = table.astype(bf16)
    rest = table - high.astype(f32)
    middle = rest.astype(bf16)
    low = (rest - middle.astype(f32)).astype(bf16)
    onehot = spread_ref[...]
    wide = mm(high, onehot) + mm(middle, onehot) + mm(low, onehot)
    strips = groups * PLACES
    parts = []
    for n in range(STRIP // 128):
        lanes = slice(n * 128, (n + 1) * 128)
        wide_ref = wide_refs[n]
        wide_ref[...] = wide[:, lanes]
        place = place_ref[:, lanes]
        part = jnp.zeros((strips, 128), f32)
        for p in range(PLACES):
            part = jnp.where(place == p, wide_ref[pl.ds(p, strips, stride=PLACES), :], part)
        parts.append(part)
    strip = jnp.concatenate(parts, axis=1)
    pole = pole_ref[0].astype(f32)
    rowlab = rowlab_ref[...]
    lanelab = lanelab_ref[...]
    differs = jnp.maximum(
        rowlab[:, 2:3] * jnp.abs(rowlab[:, 0:1] - lanelab[0:1, :]),
        pole * jnp.abs(rowlab[:, 1:2] - lanelab[1:2, :]),
    )
    strip = (strip + mask_fill * differs) * log2e
    for w in range(WW):
        start = (WW - 1 - w) * PLACES
        part = strip[:, start : start + TOK]
        for g in range(groups):
            out_ref[g, w * PLACES : (w + 1) * PLACES, :] = part[g * PLACES : (g + 1) * PLACES, :]


def expand_bias(table, pole):
    levels = table.shape[1]
    groups = levels * HEADS
    flat = table.reshape(groups * PLACES * PLACES, RELW)
    onehot = np.zeros((RELW, STRIP), np.float32)
    for r in range(RELW):
        onehot[RELW - 1 - r, r * PLACES : (r + 1) * PLACES] = 1.0
    place = (np.arange(STRIP) % PLACES).astype(np.int32)[None]
    level_label = (np.arange(PLACES) // WH < HZ).astype(np.float32)
    lat_label = (np.arange(PLACES) % WH < HH).astype(np.float32)
    rowlab = np.zeros((groups, PLACES, 3), np.float32)
    rowlab[:, :, 0] = level_label
    rowlab[:, :, 1] = lat_label
    rowlab[:HEADS, :, 2] = 1.0
    lanelab = np.zeros((2, STRIP), np.float32)
    lanelab[:, : RELW * PLACES] = np.stack([np.tile(level_label, RELW), np.tile(lat_label, RELW)])
    return pl.pallas_call(
        functools.partial(bias_kernel, groups),
        out_shape=shape((groups, TOK, TOK), f32),
        in_specs=[smem] + vmem(5),
        out_specs=vmem(1)[0],
        scratch_shapes=[pltpu.VMEM((groups * PLACES * PLACES, 128), f32)] * (STRIP // 128),
        compiler_params=pltpu.CompilerParams(vmem_limit_bytes=32 * MIB),
        cost_estimate=cost(10**9, 8 * MIB),
        name="bias",
    )(pole, flat, jnp.asarray(onehot, bf16), jnp.asarray(place), jnp.asarray(rowlab.reshape(-1, 3)), jnp.asarray(lanelab))


def head_masks(count):
    lane = lax.broadcasted_iota(jnp.int32, (count, C), 1)
    return [((lane >= h * HEAD) & (lane < (h + 1) * HEAD)).astype(f32) for h in range(HEADS)]


def stacked(values, masks):
    return jnp.concatenate([values * mask for mask in masks], axis=0)


def head_sum(values, masks):
    total = values[:TOK] * masks[0]
    for h in range(1, HEADS):
        total = total + values[h * TOK : (h + 1) * TOK] * masks[h]
    return total


def block_of(core, chip, g):
    return core * QUADS + jnp.bitwise_xor(chip, g)


def chunk_rows(block):
    return pl.ds(pl.multiple_of(block * PART, PART), PART)


def split_parts(rank_ref, total_refs, keep_ref, send_ref):
    core, chip = rank_ref[0], rank_ref[1]
    for out, side in ((keep_ref, core), (send_ref, 1 - core)):
        parts = []
        for g in range(QUADS):
            rows = chunk_rows(block_of(side, chip, g))
            parts += [ref[rows, :] for ref in total_refs]
        out[...] = jnp.concatenate(parts, axis=0).astype(out.dtype)


def forward_kernel(
    windows, lon_windows,
    own_ref, north_ref, side_ref, corner_ref, perm_ref, bias_ref, triple_ref, project_ref, up_ref, down_ref,
    q_ref, k_ref, v_ref, p_ref, mixed_ref, normed_ref, unit_ref, spread_ref, gsum_ref, up_grad_ref, down_grad_ref,
    branch_ref, cot_ref, emb_ref,
):
    pieces = [ref[...].astype(f32)[:-EXTRA] for ref in (own_ref, north_ref, side_ref, corner_ref)]
    pieces = jnp.concatenate(pieces, axis=0).astype(bf16)
    ordered = mm(one_hot(perm_ref), pieces)
    emb = ordered[:, :C]
    emb_ref[...] = emb
    cot_ref[...] = ordered[:, C:].astype(bf16)
    unit, spread = unit_norm(emb)
    unit_ref[...] = unit
    spread_ref[...] = spread
    normed = unit.astype(bf16)
    normed_ref[...] = normed
    packed = mm(normed, triple_ref[...])
    q_ref[...] = packed[:, :C].astype(bf16)
    k_ref[...] = packed[:, C : 2 * C].astype(bf16)
    v_ref[...] = packed[:, 2 * C :].astype(bf16)
    masks = head_masks(TOK)
    masks_b = [mask.astype(bf16) for mask in masks]

    def window_step(w, carry):
        rows = pl.ds(pl.multiple_of(w * TOK, TOK), TOK)
        level = w // lon_windows
        scores = mm_nt(stacked(q_ref[rows, :], masks_b), k_ref[rows, :])
        bias = bias_ref[pl.ds(level * HEADS, HEADS)].reshape(HEADS * TOK, TOK)
        raised = jnp.exp2(scores * (score_scale * log2e) + bias)
        probs = raised * (1.0 / jnp.sum(raised, -1, keepdims=True))
        probs_b = probs.astype(bf16)
        p_ref[pl.ds(w * HEADS, HEADS)] = probs_b.reshape(HEADS, TOK, TOK)
        mixed = head_sum(mm(probs_b, v_ref[rows, :]), masks).astype(bf16)
        mixed_ref[rows, :] = mixed
        branch_ref[rows, :] = mm(mixed, project_ref[...])
        return carry

    lax.fori_loop(0, windows, window_step, 0, unroll=True)

    attended = branch_ref[...].astype(bf16).astype(f32)
    unit2, spread2 = unit_norm(emb_ref[...] + attended)
    normed2 = unit2.astype(bf16)
    cot = cot_ref[...]
    back = jnp.zeros(unit2.shape, f32)
    block = 256
    for start in range(0, FF, block):
        cols = slice(start, start + block)
        up_part = up_ref[:, cols]
        pre = mm(normed2, up_part)
        upstream = mm(cot, down_ref[:, cols])
        phi = 0.5 * (1.0 + lax.erf(pre * root_half))
        activated = (pre * phi).astype(bf16)
        slope = phi + pre * inv_root_tau * jnp.exp2(pre * pre * (-0.5 * log2e))
        hidden = (upstream * slope).astype(bf16)
        up_grad_ref[:, cols] = mm_tn(normed2, hidden)
        down_grad_ref[:, cols] = mm_tn(cot, activated)
        back = back + mm_nt(hidden, up_part)
    gsum_ref[...] = cot.astype(f32) + norm_back(back, unit2, spread2)


def forward(pieces, perm, bias, triple, project, up, down, lon_windows):
    count = perm.shape[1]
    windows = count // TOK
    out_shape = [
        shape((count, C), bf16),
        shape((count, C), bf16),
        shape((count, C), bf16),
        shape((windows * HEADS, TOK, TOK), bf16),
        shape((count, C), bf16),
        shape((count, C), bf16),
        shape((count, C), f32),
        shape((count, 1), f32),
        shape((count, C), f32),
        shape((C, FF), f32),
        shape((C, FF), f32),
    ]
    return pl.pallas_call(
        functools.partial(forward_kernel, windows, lon_windows),
        out_shape=out_shape,
        in_specs=vmem(10),
        out_specs=vmem(len(out_shape)),
        scratch_shapes=[pltpu.VMEM((count, C), f32), pltpu.VMEM((count, C), bf16), pltpu.VMEM((count, C), f32)],
        compiler_params=pltpu.CompilerParams(vmem_limit_bytes=28 * MIB),
        cost_estimate=cost(3 * 10**9, 16 * MIB),
        name="forward",
    )(*pieces, perm, bias, triple, project, up, down)


def windows_back_kernel(windows, q_ref, k_ref, v_ref, p_ref, gsum_ref, project_ref, gq_ref, gk_ref, gv_ref):
    masks = head_masks(TOK)
    masks_b = [mask.astype(bf16) for mask in masks]

    def window_step(w, carry):
        rows = pl.ds(pl.multiple_of(w * TOK, TOK), TOK)
        grad = gsum_ref[rows, :].astype(bf16)
        grad_mixed = mm_nt(grad, project_ref[...])
        grad_mixed_b = grad_mixed.astype(bf16)
        probs_b = p_ref[pl.ds(w * HEADS, HEADS)].reshape(HEADS * TOK, TOK)
        probs = probs_b.astype(f32)
        grad_probs = mm_nt(stacked(grad_mixed_b, masks_b), v_ref[rows, :])
        inner = jnp.sum(grad_probs * probs, -1, keepdims=True)
        scaled = (probs * (grad_probs - inner) * score_scale).astype(bf16)
        grad_q = head_sum(mm(scaled, k_ref[rows, :]), masks)
        grad_mixed_t = grad_mixed_b.astype(f32).T.astype(bf16)
        query_t = q_ref[rows, :].astype(f32).T.astype(bf16)
        grad_k, grad_v = [], []
        for h in range(HEADS):
            spot = slice(h * HEAD, (h + 1) * HEAD)
            span = slice(h * TOK, (h + 1) * TOK)
            grad_k.append(mm(query_t[spot], scaled[span]))
            grad_v.append(mm(grad_mixed_t[spot], probs_b[span]))
        gq_ref[rows, :] = grad_q.astype(bf16)
        gk_ref[rows, :] = jnp.concatenate(grad_k, axis=0).T.astype(bf16)
        gv_ref[rows, :] = jnp.concatenate(grad_v, axis=0).T.astype(bf16)
        return carry

    lax.fori_loop(0, windows, window_step, 0, unroll=True)


def windows_back(q, k, v, p, gsum, project):
    count = q.shape[0]
    return pl.pallas_call(
        functools.partial(windows_back_kernel, count // TOK),
        out_shape=[shape((count, C), bf16)] * 3,
        in_specs=vmem(6),
        out_specs=vmem(3),
        compiler_params=pltpu.CompilerParams(vmem_limit_bytes=28 * MIB),
        cost_estimate=cost(3 * 10**9, 16 * MIB),
        name="windows_back",
    )(q, k, v, p, gsum, project)


def halved(rows):
    return -(-rows // 16) * 8


def tokens_back_kernel(
    sizes, rank_ref, gq_ref, gk_ref, gv_ref, mixed_ref, normed_ref, unit_ref, spread_ref, gsum_ref, perm_ref, triple_ref,
    up_grad_ref, down_grad_ref, *rest,
):
    flag_refs, rest = rest[: len(sizes)], rest[len(sizes) :]
    outs, (land_ref, keep_ref, send_ref, total_ref) = rest[: len(sizes)], rest[len(sizes) :]
    normed = normed_ref[...]
    triple = triple_ref[...]
    grad_normed = jnp.zeros(unit_ref.shape, f32)
    parts = []
    for n, ref in enumerate((gq_ref, gk_ref, gv_ref)):
        grad = ref[...]
        grad_normed = grad_normed + mm_nt(grad, triple[:, n * C : (n + 1) * C])
        parts.append(mm_tn(normed, grad))
    parts.append(mm_tn(mixed_ref[...], gsum_ref[...].astype(bf16)))
    total_ref[...] = jnp.concatenate(parts, axis=1)
    grad_normed = grad_normed.astype(bf16).astype(f32)
    grad_tokens = gsum_ref[...] + norm_back(grad_normed, unit_ref[...], spread_ref[...])
    pieces = mm(one_hot(perm_ref), grad_tokens.astype(bf16))
    land = jnp.zeros((EXTRA, C), f32)
    start = 0
    for size, out, flag_ref in zip(sizes, outs, flag_refs):
        piece = pieces[start : start + size]
        flags = flag_ref[size - 8 : size + 8, :].astype(f32)[8:, :size]
        land = land + mm(flags.astype(bf16), piece.astype(bf16))
        half = halved(size)
        second = jnp.concatenate([piece[half:], jnp.zeros((2 * half - size, C), f32)], axis=0)
        out[...] = jnp.concatenate([piece[:half], second], axis=1).astype(bf16)
        start += size
    land_ref[...] = land[0:1]
    split_parts(rank_ref, (up_grad_ref, down_grad_ref, total_ref), keep_ref, send_ref)


def tokens_back(rank, grads, mixed, normed, unit, spread, gsum, perm, triple, up_grad, down_grad, pieces, sizes):
    out_shape = [shape((halved(size), 2 * C), bf16) for size in sizes] + [
        shape((1, C), f32),
        shape((QUADS * CHUNK, FF), f32),
        shape((QUADS * CHUNK, FF), bf16),
    ]
    return pl.pallas_call(
        functools.partial(tokens_back_kernel, sizes),
        out_shape=out_shape,
        in_specs=[smem] + vmem(12 + len(pieces)),
        out_specs=vmem(len(out_shape)),
        scratch_shapes=[pltpu.VMEM((C, FF), f32)],
        compiler_params=pltpu.CompilerParams(vmem_limit_bytes=28 * MIB),
        cost_estimate=cost(2 * 10**9, 8 * MIB),
        name="tokens_back",
    )(rank, *grads, mixed, normed, unit, spread, gsum, perm, triple, up_grad, down_grad, *pieces)


def home_kernel(sizes, own_ref, north_ref, side_ref, corner_ref, perm_ref, out_ref):
    pieces = []
    for size, ref in zip(sizes, (own_ref, north_ref, side_ref, corner_ref)):
        wide = ref[...].astype(f32)
        pieces += [wide[:, :C], wide[: size - wide.shape[0], C:]]
    pieces = jnp.concatenate(pieces, axis=0).astype(bf16)
    out_ref[...] = mm(one_hot(perm_ref), pieces).astype(bf16)


def to_home(pieces, sizes, rows, cols):
    count = Z * rows * cols
    perm = spots(np.argsort(np.concatenate(piece_rows(rows, cols))))
    return pl.pallas_call(
        functools.partial(home_kernel, sizes),
        out_shape=shape((count, C), bf16),
        in_specs=vmem(5),
        out_specs=vmem(1)[0],
        compiler_params=pltpu.CompilerParams(vmem_limit_bytes=32 * MIB),
        cost_estimate=cost(2 * count * count * C, 4 * MIB),
        name="to_home",
    )(*pieces, perm)


def core_add_kernel(keep_ref, got_ref, own_ref, *outs):
    total = keep_ref[...] + got_ref[...].astype(f32)
    own_ref[...] = total[:CHUNK]
    for e, out in enumerate(outs, 1):
        out[...] = total[e * CHUNK : (e + 1) * CHUNK].astype(bf16)


def core_add_after_kernel(keep_ref, got_ref, *rest):
    core_add_kernel(keep_ref, got_ref, *rest[-QUADS:])


def chip_add_kernel(rank_ref, keep_ref, *refs):
    gots, (land_ref, own_ref, send_ref, total_ref) = refs[:-4], refs[-4:]
    total = keep_ref[...]
    for ref in gots:
        total = total + ref[...].astype(f32)
    land = jnp.concatenate([land_ref[...], jnp.zeros((1, FF - C), f32)], axis=1)
    land = jnp.concatenate([land, jnp.zeros((EXTRA - 1, FF), f32)], axis=0)
    total_ref[...] = jnp.concatenate([total, land], axis=0)
    deep = rank_ref[2]
    own_ref[...] = total_ref[pl.ds(pl.multiple_of(deep * HALF, 8), HALF), :]
    send_ref[...] = total_ref[pl.ds(pl.multiple_of((1 - deep) * HALF, 8), HALF), :].astype(bf16)


def add_kernel(one_ref, two_ref, out_ref):
    out_ref[...] = (one_ref[...].astype(f32) + two_ref[...].astype(f32)).astype(bf16)


def deep_join_kernel(rank_ref, own_ref, got_ref, out_ref):
    own, got = own_ref[...].astype(f32), got_ref[...].astype(f32)
    swap = rank_ref[2] == 1
    both = [jnp.where(swap, got, own), jnp.where(swap, own, got)]
    out_ref[...] = jnp.concatenate(both, axis=0).astype(bf16)


def join_kernel(*refs):
    refs[-1][...] = jnp.concatenate([ref[...] for ref in refs[:-1]], axis=0)


def small_call(kernel, out_shape, args, name, rank=(), after=(), scratch=()):
    return pl.pallas_call(
        kernel,
        out_shape=out_shape,
        in_specs=[smem] * len(rank) + vmem(len(args)) + [pl.BlockSpec(memory_space=pl.ANY)] * len(after),
        out_specs=vmem(len(out_shape)),
        scratch_shapes=scratch,
        compiler_params=pltpu.CompilerParams(vmem_limit_bytes=16 * MIB),
        cost_estimate=cost(10**6, 2 * MIB),
        name=name,
    )(*rank, *args, *after)


def finish_kernel(
    rank_ref, own_ref, got_ref, triple_ref, project_ref, up_ref, down_ref, land_ref, wide_ref, lands_ref
):
    core, chip = rank_ref[0], rank_ref[1]
    for side, ref in ((core, own_ref), (1 - core, got_ref)):
        for g in range(QUADS):
            chunk = ref[g * FULL : (g + 1) * FULL, :].astype(f32)
            block = block_of(side, chip, g)
            rows = chunk_rows(block)
            up_ref[rows, :] = chunk[:PART]
            down_ref[rows, :] = chunk[PART : 2 * PART]
            wide_ref[rows, :] = chunk[2 * PART : CHUNK]
            lands_ref[pl.ds(pl.multiple_of(block * EXTRA, EXTRA), EXTRA), :] = chunk[CHUNK:, :C]
    triple_ref[...] = wide_ref[:, : 3 * C]
    project_ref[...] = wide_ref[:, 3 * C :]
    land_ref[...] = jnp.sum(lands_ref[...], 0, keepdims=True)


def finish(rank, own, got):
    out_shape = [shape((C, 3 * C), f32), shape((C, C), f32), shape((C, FF), f32), shape((C, FF), f32), shape((1, C), f32)]
    scratch = [pltpu.VMEM((C, FF), f32), pltpu.VMEM((2 * QUADS * EXTRA, C), f32)]
    return small_call(finish_kernel, out_shape, (own, got), "finish", (rank,), scratch=scratch)


def reduce_all(keep, sent, land, rank, shift, lon_count, after):
    core_move = lambda lon, lat: (lon, lat ^ 1)
    chip_move = lambda e: lambda lon, lat: (lon ^ (e & 1), lat ^ (2 * (e >> 1)))
    deep_move = lambda lon, lat: (lon ^ 2, lat)

    def one(rows):
        return [shape((rows, FF), bf16)]

    got = shift(sent, move=core_move)
    parts = [shape((CHUNK, FF), f32)] + one(CHUNK) * (QUADS - 1)
    own, *parts = small_call(core_add_after_kernel, parts, (keep, got), "core_add", after=after)
    gots = [shift(value, move=chip_move(e)) for e, value in enumerate(parts, 1)]
    scratch = [pltpu.VMEM((FULL, FF), f32)]
    halves = [shape((HALF, FF), f32)] + one(HALF)
    keep, sent = small_call(chip_add_kernel, halves, (own, *gots, land), "chip_add", (rank,), scratch=scratch)
    got = shift(sent, move=deep_move)
    (total,) = small_call(add_kernel, one(HALF), (keep, got), "deep_add")
    reach = 4
    while reach < lon_count:
        got = shift(total, move=lambda lon, lat, reach=reach: (lon ^ reach, lat))
        reach *= 2
        (total,) = small_call(add_kernel, one(HALF), (total, got), "far_add")
    got = shift(total, move=deep_move)
    (total,) = small_call(deep_join_kernel, one(FULL), (total, got), "deep_join", (rank,))
    near = [total] + [shift(total, move=chip_move(e)) for e in range(1, QUADS)]
    (total,) = small_call(join_kernel, one(QUADS * FULL), near, "join")
    return finish(rank, total, shift(total, move=core_move))


AXES = ("lon", "lat")


def send(value, lon_count, lat_count, move):
    pairs = []
    for lon in range(lon_count):
        for lat in range(lat_count):
            to_lon, to_lat = move(lon, lat)
            pairs.append((lon * lat_count + lat, (to_lon % lon_count) * lat_count + to_lat % lat_count))
    return lax.ppermute(value, AXES, pairs)


def body(
    lon_count, lat_count,
    tokens, cotangent, land_sea, land_vector, triple_weight, project_weight, up_weight, down_weight, earth_bias,
):
    levels, rows, cols, features = tokens.shape
    shift = functools.partial(send, lon_count=lon_count, lat_count=lat_count)
    lon_at, lat_at = lax.axis_index("lon"), lax.axis_index("lat")
    rank = jnp.stack([lat_at % 2, 2 * (lat_at // 2) + lon_at % 2, lon_at // 2 % 2]).astype(jnp.int32)
    pole = (lat_at == 0).astype(jnp.int32).reshape(1)
    lon_windows = cols // WW

    own, north, side, corner = pack(tokens, cotangent, land_sea, land_vector, rows, cols)
    north = shift(north, move=lambda lon, lat: (lon, lat + 1))
    side = shift(side, move=lambda lon, lat: (lon + 1, lat))
    corner = shift(corner, move=lambda lon, lat: (lon + 1, lat + 1))
    bias = expand_bias(earth_bias, pole)

    places = window_rows(rows, cols)
    sizes = [part.size for part in piece_rows(rows, cols)]
    pieces = (own, north, side, corner)
    q, k, v, p, mixed, normed, unit, spread, gsum, up, down = forward(
        pieces, spots(places), bias, triple_weight, project_weight, up_weight, down_weight.T, lon_windows
    )
    grads = windows_back(q, k, v, p, gsum, project_weight)
    own, north, side, corner, land, keep, sent = tokens_back(
        rank, grads, mixed, normed, unit, spread, gsum, spots(np.argsort(places)), triple_weight, up, down, pieces, sizes
    )
    north = shift(north, move=lambda lon, lat: (lon, lat - 1))
    side = shift(side, move=lambda lon, lat: (lon - 1, lat))
    corner = shift(corner, move=lambda lon, lat: (lon - 1, lat - 1))
    after = (north, side, corner)
    triple, project, up, down, land = reduce_all(keep, sent, land, rank, shift, lon_count, after)
    grad_tokens = to_home((own, north, side, corner), sizes, rows, cols)
    return grad_tokens.reshape(tokens.shape), triple, project, up, down.T, land.reshape(features)


def solution(mesh):
    return jax.shard_map(
        functools.partial(body, mesh.shape["lon"], mesh.shape["lat"]),
        mesh=mesh,
        in_specs=(
            P(None, "lat", "lon", None),
            P(None, "lat", "lon", None),
            P("lat", "lon"),
            P(),
            P(),
            P(),
            P(),
            P(),
            P("lat", None, None, None, None),
        ),
        out_specs=(P(None, "lat", "lon", None), P(), P(), P(), P(), P()),
        check_vma=False,
    )
```

```python
import functools
import math

import jax
import jax.numpy as jnp
import numpy as np
from jax import lax
from jax.experimental import pallas as pl
from jax.experimental.pallas import tpu as pltpu
from jax.sharding import PartitionSpec as P

Z = 4
WZ = 2
WH = 6
WW = 12
C = 192
HEADS = 6
HEAD = 32
FF = 768
HZ, HH, HW = WZ // 2, WH // 2, WW // 2
TOK = WZ * WH * WW
PLACES = WZ * WH
RELW = 2 * WW - 1
STRIP = -(-RELW * PLACES // 128) * 128

mask_fill = -10000.0
norm_eps = 1e-05
log2e = 1.4426950408889634
root_half = 0.7071067811865476
inv_root_tau = 0.3989422804014327
score_scale = HEAD**-0.5

f32 = jnp.float32
bf16 = jnp.bfloat16
MIB = 1 << 20

QUADS = 4
PART = C // (2 * QUADS)
CHUNK = 3 * PART
EXTRA = 8
FULL = CHUNK + EXTRA
HALF = FULL // 2


def mm(a, b):
    return lax.dot_general(a, b, (((1,), (0,)), ((), ())), preferred_element_type=f32)


def mm_nt(a, b):
    return lax.dot_general(a, b, (((1,), (1,)), ((), ())), preferred_element_type=f32)


def mm_tn(a, b):
    return lax.dot_general(a, b, (((0,), (0,)), ((), ())), preferred_element_type=f32)


def unit_norm(values):
    average = jnp.mean(values, -1, keepdims=True)
    centred = values - average
    variance = jnp.mean(centred * centred, -1, keepdims=True)
    spread = lax.rsqrt(variance + norm_eps)
    return centred * spread, spread


def norm_back(upstream, unit, spread):
    first = jnp.mean(upstream, -1, keepdims=True)
    second = jnp.mean(upstream * unit, -1, keepdims=True)
    return spread * (upstream - first - unit * second)


def piece_rows(rows, cols):
    home = np.arange(Z * rows * cols).reshape(Z, rows, cols)
    top, low = slice(0, rows - HH), slice(rows - HH, rows)
    west, east = slice(0, cols - HW), slice(cols - HW, cols)
    parts = [home[:, top, west], home[:, low, west], home[:, top, east], home[:, low, east]]
    return [part.reshape(-1) for part in parts]


def window_rows(rows, cols):
    sizes = [part.size for part in piece_rows(rows, cols)]
    starts = np.cumsum([0] + sizes)
    own, north, side, corner = [np.arange(starts[k], starts[k + 1]) for k in range(4)]
    frame = np.zeros((Z, rows, cols), np.int64)
    frame[:, HH:, HW:] = own.reshape(Z, rows - HH, cols - HW)
    frame[:, :HH, HW:] = north.reshape(Z, HH, cols - HW)
    frame[:, HH:, :HW] = side.reshape(Z, rows - HH, HW)
    frame[:, :HH, :HW] = corner.reshape(Z, HH, HW)
    frame = np.roll(frame, HZ, axis=0)
    frame = frame.reshape(Z // WZ, WZ, rows // WH, WH, cols // WW, WW)
    return frame.transpose(0, 2, 4, 5, 1, 3).reshape(-1)


def spots(places):
    return jnp.asarray(np.argsort(places).astype(np.int32)[None])


def one_hot(spot_ref):
    count = spot_ref.shape[1]
    rows = lax.broadcasted_iota(jnp.int32, (count, count), 0)
    return (rows == spot_ref[...]).astype(f32).astype(bf16)


def vmem(count):
    return [pl.BlockSpec(memory_space=pltpu.VMEM)] * count


def shape(dims, dtype):
    return jax.ShapeDtypeStruct(dims, dtype)


def cost(flops, moved):
    return pl.CostEstimate(flops=flops, bytes_accessed=moved, transcendentals=0)


def land_column(land_ref, rows, cols):
    eye = (
        lax.broadcasted_iota(jnp.int32, (cols, cols), 0)
        == lax.broadcasted_iota(jnp.int32, (cols, cols), 1)
    ).astype(f32)
    land = land_ref[...].astype(f32)
    parts = [jnp.sum(eye * land[i : i + 1, :], -1, keepdims=True) for i in range(rows)]
    return jnp.concatenate(parts, axis=0)


def pack_kernel(rows, cols, *refs):
    sources, outs, (tokens_ref, cot_ref, land_ref, vec_ref, perm_ref, sems) = refs[:5], refs[5:-6], refs[-6:]
    copies = [
        pltpu.make_async_copy(source, target, sems.at[n])
        for n, (source, target) in enumerate(zip(sources, (tokens_ref, cot_ref, land_ref, vec_ref, perm_ref)))
    ]
    for copy in copies:
        copy.start()
    for copy in copies:
        copy.wait()
    column = land_column(land_ref, rows, cols)
    added = column * vec_ref[...]
    added = jnp.concatenate([added] * Z, axis=0)
    embedded = (tokens_ref[...].astype(f32) + added).astype(bf16)
    perm = one_hot(perm_ref)
    left = mm(perm, embedded)
    right = mm(perm, cot_ref[...])
    packed = jnp.concatenate([left, right], axis=1)
    column = jnp.concatenate([column] * Z, axis=0)
    flags = mm(perm, jnp.broadcast_to(column, (column.shape[0], 128)).astype(bf16))
    start = 0
    for out in outs:
        count = out.shape[0] - EXTRA
        eye = lax.broadcasted_iota(jnp.int32, (count, count), 0) == lax.broadcasted_iota(jnp.int32, (count, count), 1)
        row = jnp.sum(jnp.where(eye, flags[start : start + count, 0:1], 0.0), 0, keepdims=True)
        row = jnp.concatenate([row, jnp.zeros((1, 2 * C - count), f32)], axis=1)
        row = jnp.broadcast_to(row, (EXTRA, 2 * C))
        out[...] = jnp.concatenate([packed[start : start + count], row], axis=0).astype(bf16)
        start += count


def pack(tokens, cotangent, land_sea, vector, rows, cols):
    parts = piece_rows(rows, cols)
    perm = spots(np.concatenate(parts))
    count = Z * rows * cols
    return pl.pallas_call(
        functools.partial(pack_kernel, rows, cols),
        out_shape=[shape((part.size + EXTRA, 2 * C), bf16) for part in parts],
        in_specs=[pl.BlockSpec(memory_space=pltpu.HBM)] * 5,
        out_specs=vmem(4),
        scratch_shapes=[
            pltpu.VMEM((count, C), bf16),
            pltpu.VMEM((count, C), bf16),
            pltpu.VMEM((rows, cols), jnp.int32),
            pltpu.VMEM((1, C), f32),
            pltpu.VMEM((1, count), jnp.int32),
            pltpu.SemaphoreType.DMA((5,)),
        ],
        cost_estimate=cost(4 * count * count * C, 4 * MIB),
        name="pack",
    )(tokens.reshape(count, C), cotangent.reshape(count, C), land_sea, vector.reshape(1, C), perm)


def bias_kernel(levels, table_ref, spread_ref, place_ref, rowlab_ref, lanelab_ref, out_ref, *wide_refs):
    groups = levels * HEADS
    pairs = PLACES * PLACES
    onehot = spread_ref[...]
    for level in range(levels):
        table = table_ref[:, level, :].T
        high = table.astype(bf16)
        rest = table - high.astype(f32)
        wide = mm(high, onehot) + mm(rest.astype(bf16), onehot)
        for head in range(HEADS):
            for n, wide_ref in enumerate(wide_refs):
                start = head * STRIP + n * 128
                wide_ref[(level * HEADS + head) * pairs : (level * HEADS + head + 1) * pairs, :] = wide[:, start : start + 128]
    strips = groups * PLACES
    parts = []
    for n, wide_ref in enumerate(wide_refs):
        place = place_ref[:, n * 128 : (n + 1) * 128]
        part = jnp.zeros((strips, 128), f32)
        for p in range(PLACES):
            part = jnp.where(place == p, wide_ref[pl.ds(p, strips, stride=PLACES), :], part)
        parts.append(part)
    strip = jnp.concatenate(parts, axis=1)
    pole = (lax.axis_index("lat") == 0).astype(f32)
    rowlab = rowlab_ref[...]
    lanelab = lanelab_ref[...]
    differs = jnp.maximum(
        rowlab[:, 2:3] * jnp.abs(rowlab[:, 0:1] - lanelab[0:1, :]),
        pole * jnp.abs(rowlab[:, 1:2] - lanelab[1:2, :]),
    )
    strip = (strip + mask_fill * differs) * log2e
    for w in range(WW):
        start = (WW - 1 - w) * PLACES
        part = strip[:, start : start + TOK]
        for g in range(groups):
            out_ref[g, w * PLACES : (w + 1) * PLACES, :] = part[g * PLACES : (g + 1) * PLACES, :]


def expand_bias(table):
    levels = table.shape[1]
    groups = levels * HEADS
    pairs = PLACES * PLACES
    flat = table[0].transpose(1, 3, 0, 2).reshape(HEADS * RELW, levels, pairs)
    onehot = np.zeros((HEADS, RELW, HEADS, STRIP), np.float32)
    for h in range(HEADS):
        for r in range(RELW):
            onehot[h, RELW - 1 - r, h, r * PLACES : (r + 1) * PLACES] = 1.0
    onehot = onehot.reshape(HEADS * RELW, HEADS * STRIP)
    place = (np.arange(STRIP) % PLACES).astype(np.int32)[None]
    level_label = (np.arange(PLACES) // WH < HZ).astype(np.float32)
    lat_label = (np.arange(PLACES) % WH < HH).astype(np.float32)
    rowlab = np.zeros((groups, PLACES, 3), np.float32)
    rowlab[:, :, 0] = level_label
    rowlab[:, :, 1] = lat_label
    rowlab[:HEADS, :, 2] = 1.0
    lanelab = np.zeros((2, STRIP), np.float32)
    lanelab[:, : RELW * PLACES] = np.stack([np.tile(level_label, RELW), np.tile(lat_label, RELW)])
    return pl.pallas_call(
        functools.partial(bias_kernel, levels),
        out_shape=shape((groups, TOK, TOK), f32),
        in_specs=vmem(5),
        out_specs=vmem(1)[0],
        scratch_shapes=[pltpu.VMEM((groups * pairs, 128), f32)] * (STRIP // 128),
        compiler_params=pltpu.CompilerParams(vmem_limit_bytes=28 * MIB),
        cost_estimate=cost(10**9, 8 * MIB),
        name="bias",
    )(flat, jnp.asarray(onehot, bf16), jnp.asarray(place), jnp.asarray(rowlab.reshape(-1, 3)), jnp.asarray(lanelab))


def head_masks(count):
    lane = lax.broadcasted_iota(jnp.int32, (count, C), 1)
    return [((lane >= h * HEAD) & (lane < (h + 1) * HEAD)).astype(f32) for h in range(HEADS)]


def stacked(values, masks):
    return jnp.concatenate([values * mask for mask in masks], axis=0)


def head_sum(values, masks):
    total = values[:TOK] * masks[0]
    for h in range(1, HEADS):
        total = total + values[h * TOK : (h + 1) * TOK] * masks[h]
    return total


def block_of(core, chip, g):
    return core * QUADS + jnp.bitwise_xor(chip, g)


def position():
    lon, lat = lax.axis_index("lon"), lax.axis_index("lat")
    return lat & 1, (lat >> 1) * 2 + (lon & 1), lon >> 1


def chunk_rows(block):
    return pl.ds(pl.multiple_of(block * PART, PART), PART)


def split_parts(total_refs, keep_ref, send_ref):
    core, chip, _ = position()
    for out, side in ((keep_ref, core), (send_ref, 1 - core)):
        parts = []
        for g in range(QUADS):
            rows = chunk_rows(block_of(side, chip, g))
            parts += [ref[rows, :] for ref in total_refs]
        out[...] = jnp.concatenate(parts, axis=0).astype(out.dtype)


def forward_kernel(
    windows, lon_windows,
    own_ref, north_ref, side_ref, corner_ref, perm_ref, bias_ref, triple_ref, project_ref, up_ref, down_ref,
    q_ref, k_ref, v_ref, p_ref, mixed_ref, normed_ref, unit_ref, spread_ref, gsum_ref, up_grad_ref, down_grad_ref,
    branch_ref, cot_ref, emb_ref,
):
    pieces = [ref[...].astype(f32)[:-EXTRA] for ref in (own_ref, north_ref, side_ref, corner_ref)]
    pieces = jnp.concatenate(pieces, axis=0).astype(bf16)
    ordered = mm(one_hot(perm_ref), pieces)
    emb = ordered[:, :C]
    emb_ref[...] = emb
    cot_ref[...] = ordered[:, C:].astype(bf16)
    unit, spread = unit_norm(emb)
    unit_ref[...] = unit
    spread_ref[...] = spread
    normed = unit.astype(bf16)
    normed_ref[...] = normed
    packed = mm(normed, triple_ref[...])
    q_ref[...] = packed[:, :C].astype(bf16)
    k_ref[...] = packed[:, C : 2 * C].astype(bf16)
    v_ref[...] = packed[:, 2 * C :].astype(bf16)
    masks = head_masks(TOK)
    masks_b = [mask.astype(bf16) for mask in masks]

    def window_step(w, carry):
        rows = pl.ds(pl.multiple_of(w * TOK, TOK), TOK)
        level = w // lon_windows
        scores = mm_nt(stacked(q_ref[rows, :], masks_b), k_ref[rows, :])
        bias = bias_ref[pl.ds(level * HEADS, HEADS)].reshape(HEADS * TOK, TOK)
        raised = jnp.exp2(scores * (score_scale * log2e) + bias)
        probs = raised * (1.0 / jnp.sum(raised, -1, keepdims=True))
        probs_b = probs.astype(bf16)
        p_ref[pl.ds(w * HEADS, HEADS)] = probs_b.reshape(HEADS, TOK, TOK)
        mixed = head_sum(mm(probs_b, v_ref[rows, :]), masks).astype(bf16)
        mixed_ref[rows, :] = mixed
        branch_ref[rows, :] = mm(mixed, project_ref[...])
        return carry

    lax.fori_loop(0, windows, window_step, 0, unroll=True)

    attended = branch_ref[...].astype(bf16).astype(f32)
    unit2, spread2 = unit_norm(emb_ref[...] + attended)
    normed2 = unit2.astype(bf16)
    cot = cot_ref[...]
    back = jnp.zeros(unit2.shape, f32)
    block = 256
    for start in range(0, FF, block):
        cols = slice(start, start + block)
        up_part = up_ref[:, cols]
        pre = mm(normed2, up_part)
        upstream = mm(cot, down_ref[:, cols])
        phi = 0.5 * (1.0 + lax.erf(pre * root_half))
        activated = (pre * phi).astype(bf16)
        slope = phi + pre * inv_root_tau * jnp.exp2(pre * pre * (-0.5 * log2e))
        hidden = (upstream * slope).astype(bf16)
        up_grad_ref[:, cols] = mm_tn(normed2, hidden)
        down_grad_ref[:, cols] = mm_tn(cot, activated)
        back = back + mm_nt(hidden, up_part)
    gsum_ref[...] = cot.astype(f32) + norm_back(back, unit2, spread2)


def forward(pieces, perm, bias, triple, project, up, down, lon_windows):
    count = perm.shape[1]
    windows = count // TOK
    out_shape = [
        shape((count, C), bf16),
        shape((count, C), bf16),
        shape((count, C), bf16),
        shape((windows * HEADS, TOK, TOK), bf16),
        shape((count, C), bf16),
        shape((count, C), bf16),
        shape((count, C), f32),
        shape((count, 1), f32),
        shape((count, C), f32),
        shape((C, FF), f32),
        shape((C, FF), f32),
    ]
    return pl.pallas_call(
        functools.partial(forward_kernel, windows, lon_windows),
        out_shape=out_shape,
        in_specs=vmem(10),
        out_specs=vmem(len(out_shape)),
        scratch_shapes=[pltpu.VMEM((count, C), f32), pltpu.VMEM((count, C), bf16), pltpu.VMEM((count, C), f32)],
        compiler_params=pltpu.CompilerParams(vmem_limit_bytes=28 * MIB),
        cost_estimate=cost(3 * 10**9, 16 * MIB),
        name="forward",
    )(*pieces, perm, bias, triple, project, up, down)


def windows_back_kernel(windows, q_ref, k_ref, v_ref, p_ref, gsum_ref, project_ref, gq_ref, gk_ref, gv_ref):
    masks = head_masks(TOK)
    masks_b = [mask.astype(bf16) for mask in masks]

    def window_step(w, carry):
        rows = pl.ds(pl.multiple_of(w * TOK, TOK), TOK)
        grad = gsum_ref[rows, :].astype(bf16)
        grad_mixed = mm_nt(grad, project_ref[...])
        grad_mixed_b = grad_mixed.astype(bf16)
        probs_b = p_ref[pl.ds(w * HEADS, HEADS)].reshape(HEADS * TOK, TOK)
        probs = probs_b.astype(f32)
        grad_probs = mm_nt(stacked(grad_mixed_b, masks_b), v_ref[rows, :])
        inner = jnp.sum(grad_probs * probs, -1, keepdims=True)
        scaled = (probs * (grad_probs - inner) * score_scale).astype(bf16)
        grad_q = head_sum(mm(scaled, k_ref[rows, :]), masks)
        grad_mixed_t = grad_mixed_b.astype(f32).T.astype(bf16)
        query_t = q_ref[rows, :].astype(f32).T.astype(bf16)
        grad_k, grad_v = [], []
        for h in range(HEADS):
            spot = slice(h * HEAD, (h + 1) * HEAD)
            span = slice(h * TOK, (h + 1) * TOK)
            grad_k.append(mm(query_t[spot], scaled[span]))
            grad_v.append(mm(grad_mixed_t[spot], probs_b[span]))
        gq_ref[rows, :] = grad_q.astype(bf16)
        gk_ref[rows, :] = jnp.concatenate(grad_k, axis=0).T.astype(bf16)
        gv_ref[rows, :] = jnp.concatenate(grad_v, axis=0).T.astype(bf16)
        return carry

    lax.fori_loop(0, windows, window_step, 0, unroll=True)


def windows_back(q, k, v, p, gsum, project):
    count = q.shape[0]
    return pl.pallas_call(
        functools.partial(windows_back_kernel, count // TOK),
        out_shape=[shape((count, C), bf16)] * 3,
        in_specs=vmem(6),
        out_specs=vmem(3),
        compiler_params=pltpu.CompilerParams(vmem_limit_bytes=28 * MIB),
        cost_estimate=cost(3 * 10**9, 16 * MIB),
        name="windows_back",
    )(q, k, v, p, gsum, project)


def halved(rows):
    return -(-rows // 16) * 8


def tokens_back_kernel(
    sizes, gq_ref, gk_ref, gv_ref, mixed_ref, normed_ref, unit_ref, spread_ref, gsum_ref, perm_ref, triple_ref,
    up_grad_ref, down_grad_ref, *rest,
):
    flag_refs, rest = rest[: len(sizes)], rest[len(sizes) :]
    outs, (land_ref, keep_ref, send_ref, total_ref) = rest[: len(sizes)], rest[len(sizes) :]
    normed = normed_ref[...]
    triple = triple_ref[...]
    grad_normed = jnp.zeros(unit_ref.shape, f32)
    parts = []
    for n, ref in enumerate((gq_ref, gk_ref, gv_ref)):
        grad = ref[...]
        grad_normed = grad_normed + mm_nt(grad, triple[:, n * C : (n + 1) * C])
        parts.append(mm_tn(normed, grad))
    parts.append(mm_tn(mixed_ref[...], gsum_ref[...].astype(bf16)))
    total_ref[...] = jnp.concatenate(parts, axis=1)
    grad_normed = grad_normed.astype(bf16).astype(f32)
    grad_tokens = gsum_ref[...] + norm_back(grad_normed, unit_ref[...], spread_ref[...])
    pieces = mm(one_hot(perm_ref), grad_tokens.astype(bf16))
    land = jnp.zeros((EXTRA, C), f32)
    start = 0
    for size, out, flag_ref in zip(sizes, outs, flag_refs):
        piece = pieces[start : start + size]
        flags = flag_ref[size - 8 : size + 8, :].astype(f32)[8:, :size]
        land = land + mm(flags.astype(bf16), piece.astype(bf16))
        half = halved(size)
        second = jnp.concatenate([piece[half:], jnp.zeros((2 * half - size, C), f32)], axis=0)
        out[...] = jnp.concatenate([piece[:half], second], axis=1).astype(bf16)
        start += size
    land_ref[...] = land[0:1]
    split_parts((up_grad_ref, down_grad_ref, total_ref), keep_ref, send_ref)


def tokens_back(grads, mixed, normed, unit, spread, gsum, perm, triple, up_grad, down_grad, pieces, sizes):
    out_shape = [shape((halved(size), 2 * C), bf16) for size in sizes] + [
        shape((1, C), f32),
        shape((QUADS * CHUNK, FF), f32),
        shape((QUADS * CHUNK, FF), bf16),
    ]
    return pl.pallas_call(
        functools.partial(tokens_back_kernel, sizes),
        out_shape=out_shape,
        in_specs=vmem(12 + len(pieces)),
        out_specs=vmem(len(out_shape)),
        scratch_shapes=[pltpu.VMEM((C, FF), f32)],
        compiler_params=pltpu.CompilerParams(vmem_limit_bytes=28 * MIB),
        cost_estimate=cost(2 * 10**9, 8 * MIB),
        name="tokens_back",
    )(*grads, mixed, normed, unit, spread, gsum, perm, triple, up_grad, down_grad, *pieces)


def home_kernel(sizes, own_ref, north_ref, side_ref, corner_ref, perm_ref, out_ref):
    pieces = []
    for size, ref in zip(sizes, (own_ref, north_ref, side_ref, corner_ref)):
        wide = ref[...].astype(f32)
        pieces += [wide[:, :C], wide[: size - wide.shape[0], C:]]
    pieces = jnp.concatenate(pieces, axis=0).astype(bf16)
    out_ref[...] = mm(one_hot(perm_ref), pieces).astype(bf16)


def to_home(pieces, sizes, rows, cols):
    count = Z * rows * cols
    perm = spots(np.argsort(np.concatenate(piece_rows(rows, cols))))
    return pl.pallas_call(
        functools.partial(home_kernel, sizes),
        out_shape=shape((count, C), bf16),
        in_specs=vmem(5),
        out_specs=vmem(1)[0],
        compiler_params=pltpu.CompilerParams(vmem_limit_bytes=32 * MIB),
        cost_estimate=cost(2 * count * count * C, 4 * MIB),
        name="to_home",
    )(*pieces, perm)


def core_add_kernel(keep_ref, got_ref, own_ref, *outs):
    total = keep_ref[...] + got_ref[...].astype(f32)
    own_ref[...] = total[:CHUNK]
    for e, out in enumerate(outs, 1):
        out[...] = total[e * CHUNK : (e + 1) * CHUNK].astype(bf16)


def core_add_after_kernel(keep_ref, got_ref, *rest):
    core_add_kernel(keep_ref, got_ref, *rest[-QUADS:])


def chip_add_kernel(keep_ref, *refs):
    gots, (land_ref, own_ref, send_ref, total_ref) = refs[:-4], refs[-4:]
    total = keep_ref[...]
    for ref in gots:
        total = total + ref[...].astype(f32)
    land = jnp.concatenate([land_ref[...], jnp.zeros((1, FF - C), f32)], axis=1)
    land = jnp.concatenate([land, jnp.zeros((EXTRA - 1, FF), f32)], axis=0)
    total_ref[...] = jnp.concatenate([total, land], axis=0)
    deep = position()[2] & 1
    own_ref[...] = total_ref[pl.ds(pl.multiple_of(deep * HALF, 8), HALF), :]
    send_ref[...] = total_ref[pl.ds(pl.multiple_of((1 - deep) * HALF, 8), HALF), :].astype(bf16)


def add_kernel(one_ref, two_ref, out_ref):
    out_ref[...] = (one_ref[...].astype(f32) + two_ref[...].astype(f32)).astype(bf16)


def deep_join_kernel(own_ref, got_ref, out_ref):
    own, got = own_ref[...].astype(f32), got_ref[...].astype(f32)
    swap = position()[2] & 1 == 1
    both = [jnp.where(swap, got, own), jnp.where(swap, own, got)]
    out_ref[...] = jnp.concatenate(both, axis=0).astype(bf16)


def join_kernel(*refs):
    refs[-1][...] = jnp.concatenate([ref[...] for ref in refs[:-1]], axis=0)


def small_call(kernel, out_shape, args, name, after=(), scratch=()):
    return pl.pallas_call(
        kernel,
        out_shape=out_shape,
        in_specs=vmem(len(args)) + [pl.BlockSpec(memory_space=pl.ANY)] * len(after),
        out_specs=vmem(len(out_shape)),
        scratch_shapes=scratch,
        compiler_params=pltpu.CompilerParams(vmem_limit_bytes=16 * MIB),
        cost_estimate=cost(10**6, 2 * MIB),
        name=name,
    )(*args, *after)


def finish_kernel(far, chunks_ref, *refs):
    if far:
        refs = refs[5:]
    outs, (up_ref, down_ref, triple_ref, project_ref, lands_ref, sems) = refs[:5], refs[5:]
    core, chip, _ = position()
    side = 1 - core if far else core
    for g in range(QUADS):
        chunk = chunks_ref[g * FULL : (g + 1) * FULL, :].astype(f32)
        block = jnp.bitwise_xor(chip, g)
        rows = chunk_rows(block)
        up_ref[rows, :] = chunk[:PART]
        down_ref[rows, :] = chunk[PART : 2 * PART]
        triple_ref[rows, :] = chunk[2 * PART : CHUNK, : 3 * C]
        project_ref[rows, :] = chunk[2 * PART : CHUNK, 3 * C :]
        lands_ref[pl.ds(pl.multiple_of(block * EXTRA, EXTRA), EXTRA), :] = chunk[CHUNK:, :C]
    starts = [side * QUADS * PART] * 4 + [side * QUADS * EXTRA]
    copies = []
    for n, (source, out, start) in enumerate(zip((triple_ref, project_ref, up_ref, down_ref, lands_ref), outs, starts)):
        target = out.at[pl.ds(pl.multiple_of(start, 8), source.shape[0]), :]
        copies.append(pltpu.make_async_copy(source, target, sems.at[n]))
    for copy in copies:
        copy.start()
    for copy in copies:
        copy.wait()


def finish(chunks, before=()):
    rows = QUADS * PART
    widths = (3 * C, C, FF, FF)
    hbm = pl.BlockSpec(memory_space=pltpu.HBM)
    return pl.pallas_call(
        functools.partial(finish_kernel, bool(before)),
        out_shape=[shape((C, width), f32) for width in widths] + [shape((2 * QUADS * EXTRA, C), f32)],
        in_specs=vmem(1) + [hbm] * len(before),
        out_specs=[hbm] * 5,
        scratch_shapes=[
            pltpu.VMEM((rows, FF), f32),
            pltpu.VMEM((rows, FF), f32),
            pltpu.VMEM((rows, 3 * C), f32),
            pltpu.VMEM((rows, C), f32),
            pltpu.VMEM((QUADS * EXTRA, C), f32),
            pltpu.SemaphoreType.DMA((5,)),
        ],
        input_output_aliases={1 + n: n for n in range(len(before))},
        compiler_params=pltpu.CompilerParams(vmem_limit_bytes=16 * MIB),
        cost_estimate=cost(10**6, 2 * MIB),
        name="finish_far" if before else "finish_own",
    )(chunks, *before)


def reduce_all(keep, sent, land, shift, lon_count, after):
    core_move = lambda lon, lat: (lon, lat ^ 1)
    chip_move = lambda e: lambda lon, lat: (lon ^ (e & 1), lat ^ (2 * (e >> 1)))
    deep_move = lambda lon, lat: (lon ^ 2, lat)

    def one(rows):
        return [shape((rows, FF), bf16)]

    got = shift(sent, move=core_move)
    parts = [shape((CHUNK, FF), f32)] + one(CHUNK) * (QUADS - 1)
    own, *parts = small_call(core_add_after_kernel, parts, (keep, got), "core_add", after=after)
    gots = [shift(value, move=chip_move(e)) for e, value in enumerate(parts, 1)]
    scratch = [pltpu.VMEM((FULL, FF), f32)]
    halves = [shape((HALF, FF), f32)] + one(HALF)
    keep, sent = small_call(chip_add_kernel, halves, (own, *gots, land), "chip_add", scratch=scratch)
    got = shift(sent, move=deep_move)
    (total,) = small_call(add_kernel, one(HALF), (keep, got), "deep_add")
    reach = 4
    while reach < lon_count:
        got = shift(total, move=lambda lon, lat, reach=reach: (lon ^ reach, lat))
        reach *= 2
        (total,) = small_call(add_kernel, one(HALF), (total, got), "far_add")
    got = shift(total, move=deep_move)
    (total,) = small_call(deep_join_kernel, one(FULL), (total, got), "deep_join")
    near = [total] + [shift(total, move=chip_move(e)) for e in range(1, QUADS)]
    (total,) = small_call(join_kernel, one(QUADS * FULL), near, "join")
    got = shift(total, move=core_move)
    *weights, lands = finish(got, finish(total))
    return (*weights, jnp.sum(lands, axis=0))


AXES = ("lon", "lat")


def send(value, lon_count, lat_count, move):
    pairs = []
    for lon in range(lon_count):
        for lat in range(lat_count):
            to_lon, to_lat = move(lon, lat)
            pairs.append((lon * lat_count + lat, (to_lon % lon_count) * lat_count + to_lat % lat_count))
    return lax.ppermute(value, AXES, pairs)


def body(
    lon_count, lat_count,
    tokens, cotangent, land_sea, land_vector, triple_weight, project_weight, up_weight, down_weight, earth_bias,
):
    levels, rows, cols, features = tokens.shape
    shift = functools.partial(send, lon_count=lon_count, lat_count=lat_count)
    lon_windows = cols // WW

    own, north, side, corner = pack(tokens, cotangent, land_sea, land_vector, rows, cols)
    north = shift(north, move=lambda lon, lat: (lon, lat + 1))
    side = shift(side, move=lambda lon, lat: (lon + 1, lat))
    corner = shift(corner, move=lambda lon, lat: (lon + 1, lat + 1))
    bias = expand_bias(earth_bias)

    places = window_rows(rows, cols)
    sizes = [part.size for part in piece_rows(rows, cols)]
    pieces = (own, north, side, corner)
    q, k, v, p, mixed, normed, unit, spread, gsum, up, down = forward(
        pieces, spots(places), bias, triple_weight, project_weight, up_weight, down_weight.T, lon_windows
    )
    grads = windows_back(q, k, v, p, gsum, project_weight)
    own, north, side, corner, land, keep, sent = tokens_back(
        grads, mixed, normed, unit, spread, gsum, spots(np.argsort(places)), triple_weight, up, down, pieces, sizes
    )
    north = shift(north, move=lambda lon, lat: (lon, lat - 1))
    side = shift(side, move=lambda lon, lat: (lon - 1, lat))
    corner = shift(corner, move=lambda lon, lat: (lon - 1, lat - 1))
    after = (north, side, corner)
    triple, project, up, down, land = reduce_all(keep, sent, land, shift, lon_count, after)
    grad_tokens = to_home((own, north, side, corner), sizes, rows, cols)
    return grad_tokens.reshape(tokens.shape), triple, project, up, down.T, land


def solution(mesh):
    return jax.shard_map(
        functools.partial(body, mesh.shape["lon"], mesh.shape["lat"]),
        mesh=mesh,
        in_specs=(
            P(None, "lat", "lon", None),
            P(None, "lat", "lon", None),
            P("lat", "lon"),
            P(),
            P(),
            P(),
            P(),
            P(),
            P("lat", None, None, None, None),
        ),
        out_specs=(P(None, "lat", "lon", None), P(), P(), P(), P(), P()),
        check_vma=False,
    )
```

```python
import functools
import math

import jax
import jax.numpy as jnp
import numpy as np
from jax import lax
from jax.experimental import pallas as pl
from jax.experimental.pallas import tpu as pltpu
from jax.sharding import PartitionSpec as P

Z = 4
WZ = 2
WH = 6
WW = 12
C = 192
HEADS = 6
HEAD = 32
FF = 768
HZ, HH, HW = WZ // 2, WH // 2, WW // 2
TOK = WZ * WH * WW
PLACES = WZ * WH
RELW = 2 * WW - 1
STRIP = -(-RELW * PLACES // 128) * 128

mask_fill = -10000.0
norm_eps = 1e-05
log2e = 1.4426950408889634
root_half = 0.7071067811865476
inv_root_tau = 0.3989422804014327
score_scale = HEAD**-0.5

f32 = jnp.float32
bf16 = jnp.bfloat16
MIB = 1 << 20

QUADS = 4
PART = C // (2 * QUADS)
CHUNK = 3 * PART
EXTRA = 8
FULL = CHUNK + EXTRA
HALF = FULL // 2


def mm(a, b):
    return lax.dot_general(a, b, (((1,), (0,)), ((), ())), preferred_element_type=f32)


def mm_nt(a, b):
    return lax.dot_general(a, b, (((1,), (1,)), ((), ())), preferred_element_type=f32)


def mm_tn(a, b):
    return lax.dot_general(a, b, (((0,), (0,)), ((), ())), preferred_element_type=f32)


def unit_norm(values):
    average = jnp.mean(values, -1, keepdims=True)
    centred = values - average
    variance = jnp.mean(centred * centred, -1, keepdims=True)
    spread = lax.rsqrt(variance + norm_eps)
    return centred * spread, spread


def norm_back(upstream, unit, spread):
    first = jnp.mean(upstream, -1, keepdims=True)
    second = jnp.mean(upstream * unit, -1, keepdims=True)
    return spread * (upstream - first - unit * second)


def piece_rows(rows, cols):
    home = np.arange(Z * rows * cols).reshape(Z, rows, cols)
    top, low = slice(0, rows - HH), slice(rows - HH, rows)
    west, east = slice(0, cols - HW), slice(cols - HW, cols)
    parts = [home[:, top, west], home[:, low, west], home[:, top, east], home[:, low, east]]
    return [part.reshape(-1) for part in parts]


def window_rows(rows, cols):
    sizes = [part.size for part in piece_rows(rows, cols)]
    starts = np.cumsum([0] + sizes)
    own, north, side, corner = [np.arange(starts[k], starts[k + 1]) for k in range(4)]
    frame = np.zeros((Z, rows, cols), np.int64)
    frame[:, HH:, HW:] = own.reshape(Z, rows - HH, cols - HW)
    frame[:, :HH, HW:] = north.reshape(Z, HH, cols - HW)
    frame[:, HH:, :HW] = side.reshape(Z, rows - HH, HW)
    frame[:, :HH, :HW] = corner.reshape(Z, HH, HW)
    frame = np.roll(frame, HZ, axis=0)
    frame = frame.reshape(Z // WZ, WZ, rows // WH, WH, cols // WW, WW)
    return frame.transpose(0, 2, 4, 5, 1, 3).reshape(-1)


def spots(places):
    return jnp.asarray(np.argsort(places).astype(np.int32)[None])


def one_hot(spot_ref):
    count = spot_ref.shape[1]
    rows = lax.broadcasted_iota(jnp.int32, (count, count), 0)
    return (rows == spot_ref[...]).astype(f32).astype(bf16)


def vmem(count):
    return [pl.BlockSpec(memory_space=pltpu.VMEM)] * count


def shape(dims, dtype):
    return jax.ShapeDtypeStruct(dims, dtype)


def cost(flops, moved):
    return pl.CostEstimate(flops=flops, bytes_accessed=moved, transcendentals=0)


def land_column(land_ref, rows, cols):
    eye = (
        lax.broadcasted_iota(jnp.int32, (cols, cols), 0)
        == lax.broadcasted_iota(jnp.int32, (cols, cols), 1)
    ).astype(f32)
    land = land_ref[...].astype(f32)
    parts = [jnp.sum(eye * land[i : i + 1, :], -1, keepdims=True) for i in range(rows)]
    return jnp.concatenate(parts, axis=0)


def pack_kernel(rows, cols, *refs):
    sources, outs, (tokens_ref, cot_ref, land_ref, vec_ref, perm_ref, sems) = refs[:5], refs[5:-6], refs[-6:]
    copies = [
        pltpu.make_async_copy(source, target, sems.at[n])
        for n, (source, target) in enumerate(zip(sources, (tokens_ref, cot_ref, land_ref, vec_ref, perm_ref)))
    ]
    for copy in copies:
        copy.start()
    for copy in copies:
        copy.wait()
    column = land_column(land_ref, rows, cols)
    added = column * vec_ref[...]
    added = jnp.concatenate([added] * Z, axis=0)
    embedded = (tokens_ref[...].astype(f32) + added).astype(bf16)
    perm = one_hot(perm_ref)
    left = mm(perm, embedded)
    right = mm(perm, cot_ref[...])
    packed = jnp.concatenate([left, right], axis=1)
    column = jnp.concatenate([column] * Z, axis=0)
    flags = mm(perm, jnp.broadcast_to(column, (column.shape[0], 128)).astype(bf16))
    start = 0
    for out in outs:
        count = out.shape[0] - EXTRA
        eye = lax.broadcasted_iota(jnp.int32, (count, count), 0) == lax.broadcasted_iota(jnp.int32, (count, count), 1)
        row = jnp.sum(jnp.where(eye, flags[start : start + count, 0:1], 0.0), 0, keepdims=True)
        row = jnp.concatenate([row, jnp.zeros((1, 2 * C - count), f32)], axis=1)
        row = jnp.broadcast_to(row, (EXTRA, 2 * C))
        out[...] = jnp.concatenate([packed[start : start + count], row], axis=0).astype(bf16)
        start += count


def pack(tokens, cotangent, land_sea, vector, rows, cols):
    parts = piece_rows(rows, cols)
    perm = spots(np.concatenate(parts))
    count = Z * rows * cols
    return pl.pallas_call(
        functools.partial(pack_kernel, rows, cols),
        out_shape=[shape((part.size + EXTRA, 2 * C), bf16) for part in parts],
        in_specs=[pl.BlockSpec(memory_space=pltpu.HBM)] * 5,
        out_specs=vmem(4),
        scratch_shapes=[
            pltpu.VMEM((count, C), bf16),
            pltpu.VMEM((count, C), bf16),
            pltpu.VMEM((rows, cols), jnp.int32),
            pltpu.VMEM((1, C), f32),
            pltpu.VMEM((1, count), jnp.int32),
            pltpu.SemaphoreType.DMA((5,)),
        ],
        cost_estimate=cost(4 * count * count * C, 4 * MIB),
        name="pack",
    )(tokens.reshape(count, C), cotangent.reshape(count, C), land_sea, vector.reshape(1, C), perm)


def floor_div(values, divisor):
    return (values * (65536 // divisor + 1)) >> 16


def bias_kernel(levels, table_ref, out_ref, *wide_refs):
    groups = levels * HEADS
    pairs = PLACES * PLACES
    row = lax.broadcasted_iota(jnp.int32, (HEADS * RELW, HEADS * STRIP), 0)
    lane = lax.broadcasted_iota(jnp.int32, (HEADS * RELW, HEADS * STRIP), 1)
    head = floor_div(row, RELW)
    ahead = lane - (head * STRIP + (RELW - 1 - (row - head * RELW)) * PLACES)
    onehot = ((ahead >= 0) & (ahead < PLACES)).astype(f32).astype(bf16)
    for level in range(levels):
        table = table_ref[:, level, :].T
        high = table.astype(bf16)
        rest = table - high.astype(f32)
        wide = mm(high, onehot) + mm(rest.astype(bf16), onehot)
        for head in range(HEADS):
            for n, wide_ref in enumerate(wide_refs):
                start = head * STRIP + n * 128
                wide_ref[(level * HEADS + head) * pairs : (level * HEADS + head + 1) * pairs, :] = wide[:, start : start + 128]
    strips = groups * PLACES
    parts = []
    for n, wide_ref in enumerate(wide_refs):
        place = lax.broadcasted_iota(jnp.int32, (strips, 128), 1) + n * 128
        place = place - floor_div(place, PLACES) * PLACES
        part = jnp.zeros((strips, 128), f32)
        for p in range(PLACES):
            part = jnp.where(place == p, wide_ref[pl.ds(p, strips, stride=PLACES), :], part)
        parts.append(part)
    strip = jnp.concatenate(parts, axis=1)
    row = lax.broadcasted_iota(jnp.int32, (strips, STRIP), 0)
    lane = lax.broadcasted_iota(jnp.int32, (strips, STRIP), 1)
    own, other = row - floor_div(row, PLACES) * PLACES, lane - floor_div(lane, PLACES) * PLACES
    low_own, low_other = (own < HZ * WH).astype(jnp.int32), (other < HZ * WH).astype(jnp.int32)
    first_level = (row < HEADS * PLACES).astype(jnp.int32)
    own_lat, other_lat = own + WH * low_own, other + WH * low_other
    north_own, north_other = (own_lat < WH + HH).astype(jnp.int32), (other_lat < WH + HH).astype(jnp.int32)
    pole = (lax.axis_index("y") + lax.axis_index("core") == 0).astype(jnp.int32)
    differs = first_level * (low_own ^ low_other) + pole * (north_own ^ north_other)
    strip = jnp.where(differs > 0, strip + mask_fill, strip) * log2e
    for w in range(WW):
        start = (WW - 1 - w) * PLACES
        part = strip[:, start : start + TOK]
        for g in range(groups):
            out_ref[g, w * PLACES : (w + 1) * PLACES, :] = part[g * PLACES : (g + 1) * PLACES, :]


def expand_bias(table):
    levels = table.shape[1]
    groups = levels * HEADS
    pairs = PLACES * PLACES
    flat = table[0].transpose(1, 3, 0, 2).reshape(HEADS * RELW, levels, pairs)
    return pl.pallas_call(
        functools.partial(bias_kernel, levels),
        out_shape=shape((groups, TOK, TOK), f32),
        in_specs=vmem(1),
        out_specs=vmem(1)[0],
        scratch_shapes=[pltpu.VMEM((groups * pairs, 128), f32)] * (STRIP // 128),
        compiler_params=pltpu.CompilerParams(vmem_limit_bytes=28 * MIB),
        cost_estimate=cost(10**9, 8 * MIB),
        name="bias",
    )(flat)


def head_masks(count):
    lane = lax.broadcasted_iota(jnp.int32, (count, C), 1)
    return [((lane >= h * HEAD) & (lane < (h + 1) * HEAD)).astype(f32) for h in range(HEADS)]


def stacked(values, masks):
    return jnp.concatenate([values * mask for mask in masks], axis=0)


def head_sum(values, masks):
    total = values[:TOK] * masks[0]
    for h in range(1, HEADS):
        total = total + values[h * TOK : (h + 1) * TOK] * masks[h]
    return total


def position():
    return lax.axis_index("core"), lax.axis_index("y") * 2 + lax.axis_index("x"), lax.axis_index("deep")


def chunk_rows(block):
    return pl.ds(pl.multiple_of(block * PART, PART), PART)


def split_parts(total_refs, keep_ref, send_ref):
    core = position()[0]
    for out, side in ((keep_ref, core), (send_ref, 1 - core)):
        parts = []
        for g in range(QUADS):
            rows = chunk_rows(side * QUADS + g)
            parts += [ref[rows, :] for ref in total_refs]
        out[...] = jnp.concatenate(parts, axis=0).astype(out.dtype)


def forward_kernel(
    windows, lon_windows,
    own_ref, north_ref, side_ref, corner_ref, perm_ref, bias_ref, triple_ref, project_ref, up_ref, down_ref,
    q_ref, k_ref, v_ref, p_ref, mixed_ref, normed_ref, unit_ref, spread_ref, gsum_ref, up_grad_ref, down_grad_ref,
    branch_ref, cot_ref, emb_ref,
):
    pieces = [ref[...].astype(f32)[:-EXTRA] for ref in (own_ref, north_ref, side_ref, corner_ref)]
    pieces = jnp.concatenate(pieces, axis=0).astype(bf16)
    ordered = mm(one_hot(perm_ref), pieces)
    emb = ordered[:, :C]
    emb_ref[...] = emb
    cot_ref[...] = ordered[:, C:].astype(bf16)
    unit, spread = unit_norm(emb)
    unit_ref[...] = unit
    spread_ref[...] = spread
    normed = unit.astype(bf16)
    normed_ref[...] = normed
    packed = mm(normed, triple_ref[...])
    q_ref[...] = packed[:, :C].astype(bf16)
    k_ref[...] = packed[:, C : 2 * C].astype(bf16)
    v_ref[...] = packed[:, 2 * C :].astype(bf16)
    masks = head_masks(TOK)
    masks_b = [mask.astype(bf16) for mask in masks]

    def window_step(w, carry):
        rows = pl.ds(pl.multiple_of(w * TOK, TOK), TOK)
        level = w // lon_windows
        scores = mm_nt(stacked(q_ref[rows, :], masks_b), k_ref[rows, :])
        bias = bias_ref[pl.ds(level * HEADS, HEADS)].reshape(HEADS * TOK, TOK)
        raised = jnp.exp2(scores * (score_scale * log2e) + bias)
        probs = raised * (1.0 / jnp.sum(raised, -1, keepdims=True))
        probs_b = probs.astype(bf16)
        p_ref[pl.ds(w * HEADS, HEADS)] = probs_b.reshape(HEADS, TOK, TOK)
        mixed = head_sum(mm(probs_b, v_ref[rows, :]), masks).astype(bf16)
        mixed_ref[rows, :] = mixed
        branch_ref[rows, :] = mm(mixed, project_ref[...])
        return carry

    lax.fori_loop(0, windows, window_step, 0, unroll=True)

    attended = branch_ref[...].astype(bf16).astype(f32)
    unit2, spread2 = unit_norm(emb_ref[...] + attended)
    normed2 = unit2.astype(bf16)
    cot = cot_ref[...]
    back = jnp.zeros(unit2.shape, f32)
    block = 256
    for start in range(0, FF, block):
        cols = slice(start, start + block)
        up_part = up_ref[:, cols]
        pre = mm(normed2, up_part)
        upstream = mm(cot, down_ref[:, cols])
        phi = 0.5 * (1.0 + lax.erf(pre * root_half))
        activated = (pre * phi).astype(bf16)
        slope = phi + pre * inv_root_tau * jnp.exp2(pre * pre * (-0.5 * log2e))
        hidden = (upstream * slope).astype(bf16)
        up_grad_ref[:, cols] = mm_tn(normed2, hidden)
        down_grad_ref[:, cols] = mm_tn(cot, activated)
        back = back + mm_nt(hidden, up_part)
    gsum_ref[...] = cot.astype(f32) + norm_back(back, unit2, spread2)


def forward(pieces, perm, bias, triple, project, up, down, lon_windows):
    count = perm.shape[1]
    windows = count // TOK
    out_shape = [
        shape((count, C), bf16),
        shape((count, C), bf16),
        shape((count, C), bf16),
        shape((windows * HEADS, TOK, TOK), bf16),
        shape((count, C), bf16),
        shape((count, C), bf16),
        shape((count, C), f32),
        shape((count, 1), f32),
        shape((count, C), f32),
        shape((C, FF), f32),
        shape((C, FF), f32),
    ]
    return pl.pallas_call(
        functools.partial(forward_kernel, windows, lon_windows),
        out_shape=out_shape,
        in_specs=vmem(10),
        out_specs=vmem(len(out_shape)),
        scratch_shapes=[pltpu.VMEM((count, C), f32), pltpu.VMEM((count, C), bf16), pltpu.VMEM((count, C), f32)],
        compiler_params=pltpu.CompilerParams(vmem_limit_bytes=28 * MIB),
        cost_estimate=cost(3 * 10**9, 16 * MIB),
        name="forward",
    )(*pieces, perm, bias, triple, project, up, down)


def windows_back_kernel(windows, q_ref, k_ref, v_ref, p_ref, gsum_ref, project_ref, gq_ref, gk_ref, gv_ref):
    masks = head_masks(TOK)
    masks_b = [mask.astype(bf16) for mask in masks]

    def window_step(w, carry):
        rows = pl.ds(pl.multiple_of(w * TOK, TOK), TOK)
        grad = gsum_ref[rows, :].astype(bf16)
        grad_mixed = mm_nt(grad, project_ref[...])
        grad_mixed_b = grad_mixed.astype(bf16)
        probs_b = p_ref[pl.ds(w * HEADS, HEADS)].reshape(HEADS * TOK, TOK)
        probs = probs_b.astype(f32)
        grad_probs = mm_nt(stacked(grad_mixed_b, masks_b), v_ref[rows, :])
        inner = jnp.sum(grad_probs * probs, -1, keepdims=True)
        scaled = (probs * (grad_probs - inner) * score_scale).astype(bf16)
        grad_q = head_sum(mm(scaled, k_ref[rows, :]), masks)
        grad_mixed_t = grad_mixed_b.astype(f32).T.astype(bf16)
        query_t = q_ref[rows, :].astype(f32).T.astype(bf16)
        grad_k, grad_v = [], []
        for h in range(HEADS):
            spot = slice(h * HEAD, (h + 1) * HEAD)
            span = slice(h * TOK, (h + 1) * TOK)
            grad_k.append(mm(query_t[spot], scaled[span]))
            grad_v.append(mm(grad_mixed_t[spot], probs_b[span]))
        gq_ref[rows, :] = grad_q.astype(bf16)
        gk_ref[rows, :] = jnp.concatenate(grad_k, axis=0).T.astype(bf16)
        gv_ref[rows, :] = jnp.concatenate(grad_v, axis=0).T.astype(bf16)
        return carry

    lax.fori_loop(0, windows, window_step, 0, unroll=True)


def windows_back(q, k, v, p, gsum, project):
    count = q.shape[0]
    return pl.pallas_call(
        functools.partial(windows_back_kernel, count // TOK),
        out_shape=[shape((count, C), bf16)] * 3,
        in_specs=vmem(6),
        out_specs=vmem(3),
        compiler_params=pltpu.CompilerParams(vmem_limit_bytes=28 * MIB),
        cost_estimate=cost(3 * 10**9, 16 * MIB),
        name="windows_back",
    )(q, k, v, p, gsum, project)


def halved(rows):
    return -(-rows // 16) * 8


def tokens_back_kernel(
    sizes, gq_ref, gk_ref, gv_ref, mixed_ref, normed_ref, unit_ref, spread_ref, gsum_ref, perm_ref, triple_ref,
    up_grad_ref, down_grad_ref, *rest,
):
    flag_refs, rest = rest[: len(sizes)], rest[len(sizes) :]
    outs, (land_ref, keep_ref, send_ref, total_ref) = rest[: len(sizes)], rest[len(sizes) :]
    normed = normed_ref[...]
    triple = triple_ref[...]
    grad_normed = jnp.zeros(unit_ref.shape, f32)
    parts = []
    for n, ref in enumerate((gq_ref, gk_ref, gv_ref)):
        grad = ref[...]
        grad_normed = grad_normed + mm_nt(grad, triple[:, n * C : (n + 1) * C])
        parts.append(mm_tn(normed, grad))
    parts.append(mm_tn(mixed_ref[...], gsum_ref[...].astype(bf16)))
    total_ref[...] = jnp.concatenate(parts, axis=1)
    grad_normed = grad_normed.astype(bf16).astype(f32)
    grad_tokens = gsum_ref[...] + norm_back(grad_normed, unit_ref[...], spread_ref[...])
    pieces = mm(one_hot(perm_ref), grad_tokens.astype(bf16))
    land = jnp.zeros((EXTRA, C), f32)
    start = 0
    for size, out, flag_ref in zip(sizes, outs, flag_refs):
        piece = pieces[start : start + size]
        flags = flag_ref[size - 8 : size + 8, :].astype(f32)[8:, :size]
        land = land + mm(flags.astype(bf16), piece.astype(bf16))
        half = halved(size)
        second = jnp.concatenate([piece[half:], jnp.zeros((2 * half - size, C), f32)], axis=0)
        out[...] = jnp.concatenate([piece[:half], second], axis=1).astype(bf16)
        start += size
    land_ref[...] = land[0:1]
    split_parts((up_grad_ref, down_grad_ref, total_ref), keep_ref, send_ref)


def tokens_back(grads, mixed, normed, unit, spread, gsum, perm, triple, up_grad, down_grad, pieces, sizes):
    out_shape = [shape((halved(size), 2 * C), bf16) for size in sizes] + [
        shape((1, C), f32),
        shape((QUADS * CHUNK, FF), f32),
        shape((QUADS * CHUNK, FF), bf16),
    ]
    return pl.pallas_call(
        functools.partial(tokens_back_kernel, sizes),
        out_shape=out_shape,
        in_specs=vmem(12 + len(pieces)),
        out_specs=vmem(len(out_shape)),
        scratch_shapes=[pltpu.VMEM((C, FF), f32)],
        compiler_params=pltpu.CompilerParams(vmem_limit_bytes=28 * MIB),
        cost_estimate=cost(2 * 10**9, 8 * MIB),
        name="tokens_back",
    )(*grads, mixed, normed, unit, spread, gsum, perm, triple, up_grad, down_grad, *pieces)


def home_kernel(sizes, own_ref, north_ref, side_ref, corner_ref, perm_ref, out_ref):
    pieces = []
    for size, ref in zip(sizes, (own_ref, north_ref, side_ref, corner_ref)):
        wide = ref[...].astype(f32)
        pieces += [wide[:, :C], wide[: size - wide.shape[0], C:]]
    pieces = jnp.concatenate(pieces, axis=0).astype(bf16)
    out_ref[...] = mm(one_hot(perm_ref), pieces).astype(bf16)


def to_home(pieces, sizes, rows, cols):
    count = Z * rows * cols
    perm = spots(np.argsort(np.concatenate(piece_rows(rows, cols))))
    return pl.pallas_call(
        functools.partial(home_kernel, sizes),
        out_shape=shape((count, C), bf16),
        in_specs=vmem(5),
        out_specs=vmem(1)[0],
        compiler_params=pltpu.CompilerParams(vmem_limit_bytes=32 * MIB),
        cost_estimate=cost(2 * count * count * C, 4 * MIB),
        name="to_home",
    )(*pieces, perm)


def core_add_kernel(keep_ref, got_ref, *refs):
    refs[-1][...] = (keep_ref[...] + got_ref[...].astype(f32)).astype(bf16)


def chip_add_kernel(got_ref, land_ref, own_ref, send_ref, total_ref):
    got = got_ref[...].astype(f32)
    total = got[:CHUNK]
    for g in range(1, QUADS):
        total = total + got[g * CHUNK : (g + 1) * CHUNK]
    land = jnp.concatenate([land_ref[...], jnp.zeros((1, FF - C), f32)], axis=1)
    land = jnp.concatenate([land, jnp.zeros((EXTRA - 1, FF), f32)], axis=0)
    total_ref[...] = jnp.concatenate([total, land], axis=0)
    deep = position()[2] & 1
    own_ref[...] = total_ref[pl.ds(pl.multiple_of(deep * HALF, 8), HALF), :]
    send_ref[...] = total_ref[pl.ds(pl.multiple_of((1 - deep) * HALF, 8), HALF), :].astype(bf16)


def add_kernel(one_ref, two_ref, out_ref):
    out_ref[...] = (one_ref[...].astype(f32) + two_ref[...].astype(f32)).astype(bf16)


def deep_join_kernel(own_ref, got_ref, out_ref):
    own, got = own_ref[...].astype(f32), got_ref[...].astype(f32)
    swap = position()[2] & 1 == 1
    both = [jnp.where(swap, got, own), jnp.where(swap, own, got)]
    out_ref[...] = jnp.concatenate(both, axis=0).astype(bf16)


def join_kernel(*refs):
    refs[-1][...] = jnp.concatenate([ref[...] for ref in refs[:-1]], axis=0)


def small_call(kernel, out_shape, args, name, after=(), scratch=()):
    return pl.pallas_call(
        kernel,
        out_shape=out_shape,
        in_specs=vmem(len(args)) + [pl.BlockSpec(memory_space=pl.ANY)] * len(after),
        out_specs=vmem(len(out_shape)),
        scratch_shapes=scratch,
        compiler_params=pltpu.CompilerParams(vmem_limit_bytes=16 * MIB),
        cost_estimate=cost(10**6, 2 * MIB),
        name=name,
    )(*args, *after)


def finish_kernel(far, chunks_ref, *refs):
    if far:
        before_ref, refs = refs[0], refs[5:]
    outs, land_ref, (up_ref, down_ref, triple_ref, project_ref, lands_ref, sems) = refs[:4], refs[4], refs[5:]
    core, chip, _ = position()
    side = 1 - core if far else core
    for g in range(QUADS):
        chunk = chunks_ref[g * FULL : (g + 1) * FULL, :].astype(f32)
        block = jnp.bitwise_xor(chip, g)
        rows = chunk_rows(block)
        up_ref[rows, :] = chunk[:PART]
        down_ref[rows, :] = chunk[PART : 2 * PART]
        triple_ref[rows, :] = chunk[2 * PART : CHUNK, : 3 * C]
        project_ref[rows, :] = chunk[2 * PART : CHUNK, 3 * C :]
        lands_ref[pl.ds(pl.multiple_of(block * EXTRA, EXTRA), EXTRA), :] = chunk[CHUNK:, :C]
    copies = []
    for n, (source, out) in enumerate(zip((triple_ref, project_ref, up_ref, down_ref), outs)):
        rows = pl.ds(pl.multiple_of(side * QUADS * PART, 8), QUADS * PART)
        copies.append(pltpu.make_async_copy(source, out.at[rows, :], sems.at[n]))
    for copy in copies:
        copy.start()
    land = jnp.sum(lands_ref[...], 0, keepdims=True)
    land_ref[...] = land + before_ref[...] if far else land
    for copy in copies:
        copy.wait()


def finish(chunks, before=()):
    rows = QUADS * PART
    widths = (3 * C, C, FF, FF)
    hbm = [pl.BlockSpec(memory_space=pltpu.HBM)] * 4
    land, weights = before[4:], before[:4]
    return pl.pallas_call(
        functools.partial(finish_kernel, bool(before)),
        out_shape=[shape((C, width), f32) for width in widths] + [shape((1, C), f32)],
        in_specs=vmem(1 + len(land)) + hbm[: len(weights)],
        out_specs=hbm + vmem(1),
        scratch_shapes=[
            pltpu.VMEM((rows, FF), f32),
            pltpu.VMEM((rows, FF), f32),
            pltpu.VMEM((rows, 3 * C), f32),
            pltpu.VMEM((rows, C), f32),
            pltpu.VMEM((QUADS * EXTRA, C), f32),
            pltpu.SemaphoreType.DMA((4,)),
        ],
        input_output_aliases={2 + n: n for n in range(len(weights))},
        compiler_params=pltpu.CompilerParams(vmem_limit_bytes=16 * MIB),
        cost_estimate=cost(10**6, 2 * MIB),
        name="finish_far" if before else "finish_own",
    )(chunks, *land, *weights)


def reduce_all(keep, sent, land, shift, lon_count, after):
    core_move = lambda lon, lat: (lon, lat ^ 1)
    chip_move = lambda e: lambda lon, lat: (lon ^ (e & 1), lat ^ (2 * (e >> 1)))
    deep_move = lambda lon, lat: (lon ^ 2, lat)

    def one(rows):
        return [shape((rows, FF), bf16)]

    got = shift(sent, move=core_move)
    (parts,) = small_call(core_add_kernel, one(QUADS * CHUNK), (keep, got), "core_add", after=after)
    got = lax.all_to_all(parts, ("y", "x"), 0, 0, tiled=True)
    scratch = [pltpu.VMEM((FULL, FF), f32)]
    halves = [shape((HALF, FF), f32)] + one(HALF)
    keep, sent = small_call(chip_add_kernel, halves, (got, land), "chip_add", scratch=scratch)
    got = shift(sent, move=deep_move)
    (total,) = small_call(add_kernel, one(HALF), (keep, got), "deep_add")
    reach = 4
    while reach < lon_count:
        got = shift(total, move=lambda lon, lat, reach=reach: (lon ^ reach, lat))
        reach *= 2
        (total,) = small_call(add_kernel, one(HALF), (total, got), "far_add")
    got = shift(total, move=deep_move)
    (total,) = small_call(deep_join_kernel, one(FULL), (total, got), "deep_join")
    near = [total] + [shift(total, move=chip_move(e)) for e in range(1, QUADS)]
    (total,) = small_call(join_kernel, one(QUADS * FULL), near, "join")
    got = shift(total, move=core_move)
    return finish(got, finish(total))


AXES = ("deep", "x", "y", "core")


def send(value, lon_count, lat_count, move):
    pairs = []
    for lon in range(lon_count):
        for lat in range(lat_count):
            to_lon, to_lat = move(lon, lat)
            pairs.append((lon * lat_count + lat, (to_lon % lon_count) * lat_count + to_lat % lat_count))
    return lax.ppermute(value, AXES, pairs)


def body(
    lon_count, lat_count,
    tokens, cotangent, land_sea, land_vector, triple_weight, project_weight, up_weight, down_weight, earth_bias,
):
    levels, rows, cols, features = tokens.shape
    shift = functools.partial(send, lon_count=lon_count, lat_count=lat_count)
    lon_windows = cols // WW

    own, north, side, corner = pack(tokens, cotangent, land_sea, land_vector, rows, cols)
    north = shift(north, move=lambda lon, lat: (lon, lat + 1))
    side = shift(side, move=lambda lon, lat: (lon + 1, lat))
    corner = shift(corner, move=lambda lon, lat: (lon + 1, lat + 1))
    bias = expand_bias(earth_bias)

    places = window_rows(rows, cols)
    sizes = [part.size for part in piece_rows(rows, cols)]
    pieces = (own, north, side, corner)
    q, k, v, p, mixed, normed, unit, spread, gsum, up, down = forward(
        pieces, spots(places), bias, triple_weight, project_weight, up_weight, down_weight.T, lon_windows
    )
    grads = windows_back(q, k, v, p, gsum, project_weight)
    own, north, side, corner, land, keep, sent = tokens_back(
        grads, mixed, normed, unit, spread, gsum, spots(np.argsort(places)), triple_weight, up, down, pieces, sizes
    )
    north = shift(north, move=lambda lon, lat: (lon, lat - 1))
    side = shift(side, move=lambda lon, lat: (lon - 1, lat))
    corner = shift(corner, move=lambda lon, lat: (lon - 1, lat - 1))
    after = (north, side, corner)
    triple, project, up, down, land = reduce_all(keep, sent, land, shift, lon_count, after)
    grad_tokens = to_home((own, north, side, corner), sizes, rows, cols)
    return grad_tokens.reshape(tokens.shape), triple, project, up, down.T, land.reshape(features)


def solution(mesh):
    lon_count, lat_count = mesh.shape["lon"], mesh.shape["lat"]
    fine = jax.sharding.Mesh(mesh.devices.reshape(lon_count // 2, 2, lat_count // 2, 2), AXES)
    lon, lat = AXES[:2], AXES[2:]
    return jax.shard_map(
        functools.partial(body, lon_count, lat_count),
        mesh=fine,
        in_specs=(
            P(None, lat, lon, None),
            P(None, lat, lon, None),
            P(lat, lon),
            P(),
            P(),
            P(),
            P(),
            P(),
            P(lat, None, None, None, None),
        ),
        out_specs=(P(None, lat, lon, None), P(), P(), P(), P(), P()),
        check_vma=False,
    )
```

```python
import functools
import math

import jax
import jax.numpy as jnp
import numpy as np
from jax import lax
from jax.experimental import pallas as pl
from jax.experimental.pallas import tpu as pltpu
from jax.sharding import PartitionSpec as P

Z = 4
WZ = 2
WH = 6
WW = 12
C = 192
HEADS = 6
HEAD = 32
FF = 768
HZ, HH, HW = WZ // 2, WH // 2, WW // 2
TOK = WZ * WH * WW
PLACES = WZ * WH
RELW = 2 * WW - 1
STRIP = -(-RELW * PLACES // 128) * 128

mask_fill = -10000.0
norm_eps = 1e-05
log2e = 1.4426950408889634
root_half = 0.7071067811865476
inv_root_tau = 0.3989422804014327
score_scale = HEAD**-0.5

f32 = jnp.float32
bf16 = jnp.bfloat16
MIB = 1 << 20

QUADS = 4
PART = C // (2 * QUADS)
EXTRA = 8
MLP_ROWS, ATTN_ROWS = 2 * PART, PART + EXTRA
CHUNK = 3 * PART
FULL = CHUNK + EXTRA


def mm(a, b):
    return lax.dot_general(a, b, (((1,), (0,)), ((), ())), preferred_element_type=f32)


def mm_nt(a, b):
    return lax.dot_general(a, b, (((1,), (1,)), ((), ())), preferred_element_type=f32)


def mm_tn(a, b):
    return lax.dot_general(a, b, (((0,), (0,)), ((), ())), preferred_element_type=f32)


def unit_norm(values):
    average = jnp.mean(values, -1, keepdims=True)
    centred = values - average
    variance = jnp.mean(centred * centred, -1, keepdims=True)
    spread = lax.rsqrt(variance + norm_eps)
    return centred * spread, spread


def norm_back(upstream, unit, spread):
    first = jnp.mean(upstream, -1, keepdims=True)
    second = jnp.mean(upstream * unit, -1, keepdims=True)
    return spread * (upstream - first - unit * second)


def piece_rows(rows, cols):
    home = np.arange(Z * rows * cols).reshape(Z, rows, cols)
    top, low = slice(0, rows - HH), slice(rows - HH, rows)
    west, east = slice(0, cols - HW), slice(cols - HW, cols)
    parts = [home[:, top, west], home[:, low, west], home[:, top, east], home[:, low, east]]
    return [part.reshape(-1) for part in parts]


def window_rows(rows, cols):
    sizes = [part.size for part in piece_rows(rows, cols)]
    starts = np.cumsum([0] + sizes)
    own, north, side, corner = [np.arange(starts[k], starts[k + 1]) for k in range(4)]
    frame = np.zeros((Z, rows, cols), np.int64)
    frame[:, HH:, HW:] = own.reshape(Z, rows - HH, cols - HW)
    frame[:, :HH, HW:] = north.reshape(Z, HH, cols - HW)
    frame[:, HH:, :HW] = side.reshape(Z, rows - HH, HW)
    frame[:, :HH, :HW] = corner.reshape(Z, HH, HW)
    frame = np.roll(frame, HZ, axis=0)
    frame = frame.reshape(Z // WZ, WZ, rows // WH, WH, cols // WW, WW)
    return frame.transpose(0, 2, 4, 5, 1, 3).reshape(-1)


def spots(places):
    return jnp.asarray(np.argsort(places).astype(np.int32)[None])


def one_hot(spot_ref):
    count = spot_ref.shape[1]
    rows = lax.broadcasted_iota(jnp.int32, (count, count), 0)
    return (rows == spot_ref[...]).astype(f32).astype(bf16)


def vmem(count):
    return [pl.BlockSpec(memory_space=pltpu.VMEM)] * count


def shape(dims, dtype):
    return jax.ShapeDtypeStruct(dims, dtype)


def cost(flops, moved):
    return pl.CostEstimate(flops=flops, bytes_accessed=moved, transcendentals=0)


def land_column(land_ref, rows, cols):
    eye = (
        lax.broadcasted_iota(jnp.int32, (cols, cols), 0)
        == lax.broadcasted_iota(jnp.int32, (cols, cols), 1)
    ).astype(f32)
    land = land_ref[...].astype(f32)
    parts = [jnp.sum(eye * land[i : i + 1, :], -1, keepdims=True) for i in range(rows)]
    return jnp.concatenate(parts, axis=0)


def pack_kernel(rows, cols, *refs):
    sources, outs, (tokens_ref, cot_ref, land_ref, vec_ref, perm_ref, sems) = refs[:5], refs[5:-6], refs[-6:]
    copies = [
        pltpu.make_async_copy(source, target, sems.at[n])
        for n, (source, target) in enumerate(zip(sources, (tokens_ref, cot_ref, land_ref, vec_ref, perm_ref)))
    ]
    for copy in copies:
        copy.start()
    for copy in copies:
        copy.wait()
    column = land_column(land_ref, rows, cols)
    added = column * vec_ref[...]
    added = jnp.concatenate([added] * Z, axis=0)
    embedded = (tokens_ref[...].astype(f32) + added).astype(bf16)
    perm = one_hot(perm_ref)
    left = mm(perm, embedded)
    right = mm(perm, cot_ref[...])
    packed = jnp.concatenate([left, right], axis=1)
    column = jnp.concatenate([column] * Z, axis=0)
    flags = mm(perm, jnp.broadcast_to(column, (column.shape[0], 128)).astype(bf16))
    start = 0
    for out in outs:
        count = out.shape[0] - EXTRA
        eye = lax.broadcasted_iota(jnp.int32, (count, count), 0) == lax.broadcasted_iota(jnp.int32, (count, count), 1)
        row = jnp.sum(jnp.where(eye, flags[start : start + count, 0:1], 0.0), 0, keepdims=True)
        row = jnp.concatenate([row, jnp.zeros((1, 2 * C - count), f32)], axis=1)
        row = jnp.broadcast_to(row, (EXTRA, 2 * C))
        out[...] = jnp.concatenate([packed[start : start + count], row], axis=0).astype(bf16)
        start += count


def pack(tokens, cotangent, land_sea, vector, rows, cols):
    parts = piece_rows(rows, cols)
    perm = spots(np.concatenate(parts))
    count = Z * rows * cols
    return pl.pallas_call(
        functools.partial(pack_kernel, rows, cols),
        out_shape=[shape((part.size + EXTRA, 2 * C), bf16) for part in parts],
        in_specs=[pl.BlockSpec(memory_space=pltpu.HBM)] * 5,
        out_specs=vmem(4),
        scratch_shapes=[
            pltpu.VMEM((count, C), bf16),
            pltpu.VMEM((count, C), bf16),
            pltpu.VMEM((rows, cols), jnp.int32),
            pltpu.VMEM((1, C), f32),
            pltpu.VMEM((1, count), jnp.int32),
            pltpu.SemaphoreType.DMA((5,)),
        ],
        cost_estimate=cost(4 * count * count * C, 4 * MIB),
        name="pack",
    )(tokens.reshape(count, C), cotangent.reshape(count, C), land_sea, vector.reshape(1, C), perm)


def floor_div(values, divisor):
    return (values * (65536 // divisor + 1)) >> 16


def bias_kernel(levels, table_ref, out_ref, *wide_refs):
    groups = levels * HEADS
    pairs = PLACES * PLACES
    row = lax.broadcasted_iota(jnp.int32, (HEADS * RELW, HEADS * STRIP), 0)
    lane = lax.broadcasted_iota(jnp.int32, (HEADS * RELW, HEADS * STRIP), 1)
    head = floor_div(row, RELW)
    ahead = lane - (head * STRIP + (RELW - 1 - (row - head * RELW)) * PLACES)
    onehot = ((ahead >= 0) & (ahead < PLACES)).astype(f32).astype(bf16)
    for level in range(levels):
        table = table_ref[:, level, :].T
        high = table.astype(bf16)
        rest = table - high.astype(f32)
        wide = mm(high, onehot) + mm(rest.astype(bf16), onehot)
        for head in range(HEADS):
            for n, wide_ref in enumerate(wide_refs):
                start = head * STRIP + n * 128
                wide_ref[(level * HEADS + head) * pairs : (level * HEADS + head + 1) * pairs, :] = wide[:, start : start + 128]
    strips = groups * PLACES
    parts = []
    for n, wide_ref in enumerate(wide_refs):
        place = lax.broadcasted_iota(jnp.int32, (strips, 128), 1) + n * 128
        place = place - floor_div(place, PLACES) * PLACES
        part = jnp.zeros((strips, 128), f32)
        for p in range(PLACES):
            part = jnp.where(place == p, wide_ref[pl.ds(p, strips, stride=PLACES), :], part)
        parts.append(part)
    strip = jnp.concatenate(parts, axis=1)
    row = lax.broadcasted_iota(jnp.int32, (strips, STRIP), 0)
    lane = lax.broadcasted_iota(jnp.int32, (strips, STRIP), 1)
    own, other = row - floor_div(row, PLACES) * PLACES, lane - floor_div(lane, PLACES) * PLACES
    low_own, low_other = (own < HZ * WH).astype(jnp.int32), (other < HZ * WH).astype(jnp.int32)
    first_level = (row < HEADS * PLACES).astype(jnp.int32)
    own_lat, other_lat = own + WH * low_own, other + WH * low_other
    north_own, north_other = (own_lat < WH + HH).astype(jnp.int32), (other_lat < WH + HH).astype(jnp.int32)
    pole = (lax.axis_index("y") + lax.axis_index("core") == 0).astype(jnp.int32)
    differs = first_level * (low_own ^ low_other) + pole * (north_own ^ north_other)
    strip = jnp.where(differs > 0, strip + mask_fill, strip) * log2e
    for w in range(WW):
        start = (WW - 1 - w) * PLACES
        part = strip[:, start : start + TOK]
        for g in range(groups):
            out_ref[g, w * PLACES : (w + 1) * PLACES, :] = part[g * PLACES : (g + 1) * PLACES, :]


def expand_bias(table):
    levels = table.shape[1]
    groups = levels * HEADS
    pairs = PLACES * PLACES
    flat = table[0].transpose(1, 3, 0, 2).reshape(HEADS * RELW, levels, pairs)
    return pl.pallas_call(
        functools.partial(bias_kernel, levels),
        out_shape=shape((groups, TOK, TOK), f32),
        in_specs=vmem(1),
        out_specs=vmem(1)[0],
        scratch_shapes=[pltpu.VMEM((groups * pairs, 128), f32)] * (STRIP // 128),
        compiler_params=pltpu.CompilerParams(vmem_limit_bytes=28 * MIB),
        cost_estimate=cost(10**9, 8 * MIB),
        name="bias",
    )(flat)


def head_masks(count):
    lane = lax.broadcasted_iota(jnp.int32, (count, C), 1)
    return [((lane >= h * HEAD) & (lane < (h + 1) * HEAD)).astype(f32) for h in range(HEADS)]


def stacked(values, masks):
    return jnp.concatenate([values * mask for mask in masks], axis=0)


def head_sum(values, masks):
    total = values[:TOK] * masks[0]
    for h in range(1, HEADS):
        total = total + values[h * TOK : (h + 1) * TOK] * masks[h]
    return total


def position():
    return lax.axis_index("core"), lax.axis_index("y") * 2 + lax.axis_index("x"), lax.axis_index("deep")


def chunk_rows(block):
    return pl.ds(pl.multiple_of(block * PART, PART), PART)


def split_parts(total_refs, keep_ref, send_ref):
    core, chip, _ = position()
    for out, side in ((keep_ref, core), (send_ref, 1 - core)):
        parts = []
        for g in range(QUADS):
            rows = chunk_rows(side * QUADS + jnp.bitwise_xor(chip, g))
            parts += [ref[rows, :] for ref in total_refs]
        out[...] = jnp.concatenate(parts, axis=0).astype(out.dtype)


def forward_kernel(
    windows, lon_windows,
    own_ref, north_ref, side_ref, corner_ref, perm_ref, bias_ref, triple_ref, project_ref, up_ref, down_ref,
    q_ref, k_ref, v_ref, p_ref, mixed_ref, normed_ref, unit_ref, spread_ref, gsum_ref, keep_ref, send_ref,
    branch_ref, cot_ref, emb_ref, up_grad_ref, down_grad_ref,
):
    pieces = [ref[...].astype(f32)[:-EXTRA] for ref in (own_ref, north_ref, side_ref, corner_ref)]
    pieces = jnp.concatenate(pieces, axis=0).astype(bf16)
    ordered = mm(one_hot(perm_ref), pieces)
    emb = ordered[:, :C]
    emb_ref[...] = emb
    cot_ref[...] = ordered[:, C:].astype(bf16)
    unit, spread = unit_norm(emb)
    unit_ref[...] = unit
    spread_ref[...] = spread
    normed = unit.astype(bf16)
    normed_ref[...] = normed
    packed = mm(normed, triple_ref[...])
    q_ref[...] = packed[:, :C].astype(bf16)
    k_ref[...] = packed[:, C : 2 * C].astype(bf16)
    v_ref[...] = packed[:, 2 * C :].astype(bf16)
    masks = head_masks(TOK)
    masks_b = [mask.astype(bf16) for mask in masks]

    def window_step(w, carry):
        rows = pl.ds(pl.multiple_of(w * TOK, TOK), TOK)
        level = w // lon_windows
        scores = mm_nt(stacked(q_ref[rows, :], masks_b), k_ref[rows, :])
        bias = bias_ref[pl.ds(level * HEADS, HEADS)].reshape(HEADS * TOK, TOK)
        raised = jnp.exp2(scores * (score_scale * log2e) + bias)
        probs = raised * (1.0 / jnp.sum(raised, -1, keepdims=True))
        probs_b = probs.astype(bf16)
        p_ref[pl.ds(w * HEADS, HEADS)] = probs_b.reshape(HEADS, TOK, TOK)
        mixed = head_sum(mm(probs_b, v_ref[rows, :]), masks).astype(bf16)
        mixed_ref[rows, :] = mixed
        branch_ref[rows, :] = mm(mixed, project_ref[...])
        return carry

    lax.fori_loop(0, windows, window_step, 0, unroll=True)

    attended = branch_ref[...].astype(bf16).astype(f32)
    unit2, spread2 = unit_norm(emb_ref[...] + attended)
    normed2 = unit2.astype(bf16)
    cot = cot_ref[...]
    back = jnp.zeros(unit2.shape, f32)
    block = 256
    for start in range(0, FF, block):
        cols = slice(start, start + block)
        up_part = up_ref[:, cols]
        pre = mm(normed2, up_part)
        upstream = mm(cot, down_ref[:, cols])
        phi = 0.5 * (1.0 + lax.erf(pre * root_half))
        activated = (pre * phi).astype(bf16)
        slope = phi + pre * inv_root_tau * jnp.exp2(pre * pre * (-0.5 * log2e))
        hidden = (upstream * slope).astype(bf16)
        up_grad_ref[:, cols] = mm_tn(normed2, hidden)
        down_grad_ref[:, cols] = mm_tn(cot, activated)
        back = back + mm_nt(hidden, up_part)
    gsum_ref[...] = cot.astype(f32) + norm_back(back, unit2, spread2)
    split_parts((up_grad_ref, down_grad_ref), keep_ref, send_ref)


def forward(pieces, perm, bias, triple, project, up, down, lon_windows):
    count = perm.shape[1]
    windows = count // TOK
    out_shape = [
        shape((count, C), bf16),
        shape((count, C), bf16),
        shape((count, C), bf16),
        shape((windows * HEADS, TOK, TOK), bf16),
        shape((count, C), bf16),
        shape((count, C), bf16),
        shape((count, C), f32),
        shape((count, 1), f32),
        shape((count, C), f32),
        shape((QUADS * 2 * PART, FF), f32),
        shape((QUADS * 2 * PART, FF), bf16),
    ]
    return pl.pallas_call(
        functools.partial(forward_kernel, windows, lon_windows),
        out_shape=out_shape,
        in_specs=vmem(10),
        out_specs=vmem(len(out_shape)),
        scratch_shapes=[pltpu.VMEM((count, C), f32), pltpu.VMEM((count, C), bf16), pltpu.VMEM((count, C), f32)]
        + [pltpu.VMEM((C, FF), f32)] * 2,
        compiler_params=pltpu.CompilerParams(vmem_limit_bytes=28 * MIB),
        cost_estimate=cost(3 * 10**9, 16 * MIB),
        name="forward",
    )(*pieces, perm, bias, triple, project, up, down)


def windows_back_kernel(windows, q_ref, k_ref, v_ref, p_ref, gsum_ref, project_ref, gq_ref, gk_ref, gv_ref):
    masks = head_masks(TOK)
    masks_b = [mask.astype(bf16) for mask in masks]

    def window_step(w, carry):
        rows = pl.ds(pl.multiple_of(w * TOK, TOK), TOK)
        grad = gsum_ref[rows, :].astype(bf16)
        grad_mixed = mm_nt(grad, project_ref[...])
        grad_mixed_b = grad_mixed.astype(bf16)
        probs_b = p_ref[pl.ds(w * HEADS, HEADS)].reshape(HEADS * TOK, TOK)
        probs = probs_b.astype(f32)
        grad_probs = mm_nt(stacked(grad_mixed_b, masks_b), v_ref[rows, :])
        inner = jnp.sum(grad_probs * probs, -1, keepdims=True)
        scaled = (probs * (grad_probs - inner) * score_scale).astype(bf16)
        grad_q = head_sum(mm(scaled, k_ref[rows, :]), masks)
        grad_mixed_t = grad_mixed_b.astype(f32).T.astype(bf16)
        query_t = q_ref[rows, :].astype(f32).T.astype(bf16)
        grad_k, grad_v = [], []
        for h in range(HEADS):
            spot = slice(h * HEAD, (h + 1) * HEAD)
            span = slice(h * TOK, (h + 1) * TOK)
            grad_k.append(mm(query_t[spot], scaled[span]))
            grad_v.append(mm(grad_mixed_t[spot], probs_b[span]))
        gq_ref[rows, :] = grad_q.astype(bf16)
        gk_ref[rows, :] = jnp.concatenate(grad_k, axis=0).T.astype(bf16)
        gv_ref[rows, :] = jnp.concatenate(grad_v, axis=0).T.astype(bf16)
        return carry

    lax.fori_loop(0, windows, window_step, 0, unroll=True)


def windows_back(q, k, v, p, gsum, project):
    count = q.shape[0]
    return pl.pallas_call(
        functools.partial(windows_back_kernel, count // TOK),
        out_shape=[shape((count, C), bf16)] * 3,
        in_specs=vmem(6),
        out_specs=vmem(3),
        compiler_params=pltpu.CompilerParams(vmem_limit_bytes=28 * MIB),
        cost_estimate=cost(3 * 10**9, 16 * MIB),
        name="windows_back",
    )(q, k, v, p, gsum, project)


def halved(rows):
    return -(-rows // 16) * 8


def tokens_back_kernel(
    sizes, after, gq_ref, gk_ref, gv_ref, mixed_ref, normed_ref, unit_ref, spread_ref, gsum_ref, perm_ref, triple_ref,
    *rest,
):
    flag_refs, rest = rest[: len(sizes)], rest[len(sizes) + after :]
    outs, (land_ref, total_ref) = rest[: len(sizes)], rest[len(sizes) :]
    normed = normed_ref[...]
    triple = triple_ref[...]
    grad_normed = jnp.zeros(unit_ref.shape, f32)
    parts = []
    for n, ref in enumerate((gq_ref, gk_ref, gv_ref)):
        grad = ref[...]
        grad_normed = grad_normed + mm_nt(grad, triple[:, n * C : (n + 1) * C])
        parts.append(mm_tn(normed, grad))
    parts.append(mm_tn(mixed_ref[...], gsum_ref[...].astype(bf16)))
    total_ref[...] = jnp.concatenate(parts, axis=1)
    grad_normed = grad_normed.astype(bf16).astype(f32)
    grad_tokens = gsum_ref[...] + norm_back(grad_normed, unit_ref[...], spread_ref[...])
    pieces = mm(one_hot(perm_ref), grad_tokens.astype(bf16))
    land = jnp.zeros((EXTRA, C), f32)
    start = 0
    for size, out, flag_ref in zip(sizes, outs, flag_refs):
        piece = pieces[start : start + size]
        flags = flag_ref[size - 8 : size + 8, :].astype(f32)[8:, :size]
        land = land + mm(flags.astype(bf16), piece.astype(bf16))
        half = halved(size)
        second = jnp.concatenate([piece[half:], jnp.zeros((2 * half - size, C), f32)], axis=0)
        out[...] = jnp.concatenate([piece[:half], second], axis=1).astype(bf16)
        start += size
    land_ref[...] = land[0:1]


def tokens_back(grads, mixed, normed, unit, spread, gsum, perm, triple, pieces, sizes, after):
    out_shape = [shape((halved(size), 2 * C), bf16) for size in sizes] + [
        shape((1, C), f32),
        shape((C, FF), f32),
    ]
    return pl.pallas_call(
        functools.partial(tokens_back_kernel, sizes, len(after)),
        out_shape=out_shape,
        in_specs=vmem(10 + len(pieces)) + [pl.BlockSpec(memory_space=pl.ANY)] * len(after),
        out_specs=vmem(len(out_shape)),
        compiler_params=pltpu.CompilerParams(vmem_limit_bytes=28 * MIB),
        cost_estimate=cost(2 * 10**9, 8 * MIB),
        name="tokens_back",
    )(*grads, mixed, normed, unit, spread, gsum, perm, triple, *pieces, *after)


def home_kernel(sizes, own_ref, north_ref, side_ref, corner_ref, perm_ref, out_ref):
    pieces = []
    for size, ref in zip(sizes, (own_ref, north_ref, side_ref, corner_ref)):
        wide = ref[...].astype(f32)
        pieces += [wide[:, :C], wide[: size - wide.shape[0], C:]]
    pieces = jnp.concatenate(pieces, axis=0).astype(bf16)
    out_ref[...] = mm(one_hot(perm_ref), pieces).astype(bf16)


def to_home(pieces, sizes, rows, cols):
    count = Z * rows * cols
    perm = spots(np.argsort(np.concatenate(piece_rows(rows, cols))))
    return pl.pallas_call(
        functools.partial(home_kernel, sizes),
        out_shape=shape((count, C), bf16),
        in_specs=vmem(5),
        out_specs=vmem(1)[0],
        compiler_params=pltpu.CompilerParams(vmem_limit_bytes=32 * MIB),
        cost_estimate=cost(2 * count * count * C, 4 * MIB),
        name="to_home",
    )(*pieces, perm)


def attn_split_kernel(total_ref, *refs):
    split_parts((total_ref,), *refs[-2:])


def core_add_kernel(keep_ref, got_ref, *refs):
    own_ref, outs = refs[-QUADS], refs[1 - QUADS :]
    rows = own_ref.shape[0]
    total = keep_ref[...] + got_ref[...].astype(f32)
    own_ref[...] = total[:rows]
    for e, out in enumerate(outs, 1):
        out[...] = total[e * rows : (e + 1) * rows].astype(bf16)


def chip_add_kernel(keep_ref, *refs):
    gots, (own_ref, send_ref, total_ref) = refs[:-3], refs[-3:]
    total = keep_ref[...]
    for ref in gots[: QUADS - 1]:
        total = total + ref[...].astype(f32)
    parts = [total]
    for ref in gots[QUADS - 1 :]:
        land = jnp.concatenate([ref[...], jnp.zeros((1, FF - C), f32)], axis=1)
        parts += [land, jnp.zeros((EXTRA - 1, FF), f32)]
    total_ref[...] = jnp.concatenate(parts, axis=0)
    deep = position()[2] & 1
    half = own_ref.shape[0]
    own_ref[...] = total_ref[pl.ds(pl.multiple_of(deep * half, 8), half), :]
    send_ref[...] = total_ref[pl.ds(pl.multiple_of((1 - deep) * half, 8), half), :].astype(bf16)


def add_kernel(one_ref, two_ref, out_ref):
    out_ref[...] = (one_ref[...].astype(f32) + two_ref[...].astype(f32)).astype(bf16)


def deep_join_kernel(*refs):
    swap = position()[2] & 1 == 1
    both = []
    for own_ref, got_ref in zip(refs[:-1:2], refs[1:-1:2]):
        own, got = own_ref[...].astype(f32), got_ref[...].astype(f32)
        both += [jnp.where(swap, got, own), jnp.where(swap, own, got)]
    refs[-1][...] = jnp.concatenate(both, axis=0).astype(bf16)


def join_kernel(*refs):
    refs[-1][...] = jnp.concatenate([ref[...] for ref in refs[:-1]], axis=0)


def small_call(kernel, out_shape, args, name, after=(), scratch=()):
    return pl.pallas_call(
        kernel,
        out_shape=out_shape,
        in_specs=vmem(len(args)) + [pl.BlockSpec(memory_space=pl.ANY)] * len(after),
        out_specs=vmem(len(out_shape)),
        scratch_shapes=scratch,
        compiler_params=pltpu.CompilerParams(vmem_limit_bytes=16 * MIB),
        cost_estimate=cost(10**6, 2 * MIB),
        name=name,
    )(*args, *after)


def finish_kernel(far, chunks_ref, *refs):
    if far:
        before_ref, refs = refs[0], refs[5:]
    outs, land_ref, (up_ref, down_ref, triple_ref, project_ref, lands_ref, sems) = refs[:4], refs[4], refs[5:]
    core, chip, _ = position()
    side = 1 - core if far else core
    for g in range(QUADS):
        chunk = chunks_ref[g * FULL : (g + 1) * FULL, :].astype(f32)
        block = jnp.bitwise_xor(chip, g)
        rows = chunk_rows(block)
        up_ref[rows, :] = chunk[:PART]
        down_ref[rows, :] = chunk[PART : 2 * PART]
        triple_ref[rows, :] = chunk[2 * PART : CHUNK, : 3 * C]
        project_ref[rows, :] = chunk[2 * PART : CHUNK, 3 * C :]
        lands_ref[pl.ds(pl.multiple_of(block * EXTRA, EXTRA), EXTRA), :] = chunk[CHUNK:, :C]
    copies = []
    for n, (source, out) in enumerate(zip((triple_ref, project_ref, up_ref, down_ref), outs)):
        rows = pl.ds(pl.multiple_of(side * QUADS * PART, 8), QUADS * PART)
        copies.append(pltpu.make_async_copy(source, out.at[rows, :], sems.at[n]))
    for copy in copies:
        copy.start()
    land = jnp.sum(lands_ref[...], 0, keepdims=True)
    land_ref[...] = land + before_ref[...] if far else land
    for copy in copies:
        copy.wait()


def finish(chunks, before=()):
    rows = QUADS * PART
    widths = (3 * C, C, FF, FF)
    hbm = [pl.BlockSpec(memory_space=pltpu.HBM)] * 4
    land, weights = before[4:], before[:4]
    return pl.pallas_call(
        functools.partial(finish_kernel, bool(before)),
        out_shape=[shape((C, width), f32) for width in widths] + [shape((1, C), f32)],
        in_specs=vmem(1 + len(land)) + hbm[: len(weights)],
        out_specs=hbm + vmem(1),
        scratch_shapes=[
            pltpu.VMEM((rows, FF), f32),
            pltpu.VMEM((rows, FF), f32),
            pltpu.VMEM((rows, 3 * C), f32),
            pltpu.VMEM((rows, C), f32),
            pltpu.VMEM((QUADS * EXTRA, C), f32),
            pltpu.SemaphoreType.DMA((4,)),
        ],
        input_output_aliases={2 + n: n for n in range(len(weights))},
        compiler_params=pltpu.CompilerParams(vmem_limit_bytes=16 * MIB),
        cost_estimate=cost(10**6, 2 * MIB),
        name="finish_far" if before else "finish_own",
    )(chunks, *land, *weights)


def core_move(lon, lat):
    return lon, lat ^ 1


def chip_move(distance):
    return lambda lon, lat: (lon ^ (distance & 1), lat ^ (2 * (distance >> 1)))


def deep_move(distance):
    return lambda lon, lat: (lon ^ (2 * distance), lat)


def one(rows):
    return [shape((rows, FF), bf16)]


def sum_near(keep, sent, shift, name, after=()):
    rows = keep.shape[0] // QUADS
    got = shift(sent, move=core_move)
    parts = [shape((rows, FF), f32)] + one(rows) * (QUADS - 1)
    own, *parts = small_call(core_add_kernel, parts, (keep, got), name + "_core_add", after=after)
    return own, [shift(value, move=chip_move(e)) for e, value in enumerate(parts, 1)]


def sum_far(own, gots, land, shift, lon_count, name):
    half = (own.shape[0] + EXTRA * len(land)) // 2
    halves = [shape((half, FF), f32)] + one(half)
    scratch = [pltpu.VMEM((2 * half, FF), f32)]
    keep, sent = small_call(chip_add_kernel, halves, (own, *gots, *land), name + "_chip_add", scratch=scratch)
    got = shift(sent, move=deep_move(1))
    (total,) = small_call(add_kernel, one(half), (keep, got), name + "_deep_add")
    reach = 2
    while reach < lon_count // 2:
        got = shift(total, move=deep_move(reach))
        reach *= 2
        (total,) = small_call(add_kernel, one(half), (total, got), name + "_far_add")
    return total, shift(total, move=deep_move(1))


def gather_up(halves, shift):
    (total,) = small_call(deep_join_kernel, one(FULL), halves, "deep_join")
    near = [total] + [shift(total, move=chip_move(e)) for e in range(1, QUADS)]
    (total,) = small_call(join_kernel, one(QUADS * FULL), near, "join")
    got = shift(total, move=core_move)
    return finish(got, finish(total))


AXES = ("deep", "x", "y", "core")


def send(value, lon_count, lat_count, move):
    pairs = []
    for lon in range(lon_count):
        for lat in range(lat_count):
            to_lon, to_lat = move(lon, lat)
            pairs.append((lon * lat_count + lat, (to_lon % lon_count) * lat_count + to_lat % lat_count))
    return lax.ppermute(value, AXES, pairs)


def body(
    lon_count, lat_count,
    tokens, cotangent, land_sea, land_vector, triple_weight, project_weight, up_weight, down_weight, earth_bias,
):
    levels, rows, cols, features = tokens.shape
    shift = functools.partial(send, lon_count=lon_count, lat_count=lat_count)
    lon_windows = cols // WW

    own, north, side, corner = pack(tokens, cotangent, land_sea, land_vector, rows, cols)
    north = shift(north, move=lambda lon, lat: (lon, lat + 1))
    side = shift(side, move=lambda lon, lat: (lon + 1, lat))
    corner = shift(corner, move=lambda lon, lat: (lon + 1, lat + 1))
    bias = expand_bias(earth_bias)

    places = window_rows(rows, cols)
    sizes = [part.size for part in piece_rows(rows, cols)]
    pieces = (own, north, side, corner)
    q, k, v, p, mixed, normed, unit, spread, gsum, keep, sent = forward(
        pieces, spots(places), bias, triple_weight, project_weight, up_weight, down_weight.T, lon_windows
    )
    mlp_own, mlp_gots = sum_near(keep, sent, shift, "mlp")
    grads = windows_back(q, k, v, p, gsum, project_weight)
    own, north, side, corner, land, total = tokens_back(
        grads, mixed, normed, unit, spread, gsum, spots(np.argsort(places)), triple_weight, pieces, sizes, (mlp_own,)
    )
    north = shift(north, move=lambda lon, lat: (lon, lat - 1))
    side = shift(side, move=lambda lon, lat: (lon - 1, lat))
    corner = shift(corner, move=lambda lon, lat: (lon - 1, lat - 1))
    mlp_halves = sum_far(mlp_own, mlp_gots, (), shift, lon_count, "mlp")
    after = (north, side, corner)
    outs = [shape((QUADS * PART, FF), dtype) for dtype in (f32, bf16)]
    keep, sent = small_call(attn_split_kernel, outs, (total,), "attn_split", after=mlp_gots[:2])
    attn_halves = sum_far(*sum_near(keep, sent, shift, "attn", after), (land,), shift, lon_count, "attn")
    triple, project, up, down, land = gather_up((*mlp_halves, *attn_halves), shift)
    grad_tokens = to_home((own, north, side, corner), sizes, rows, cols)
    return grad_tokens.reshape(tokens.shape), triple, project, up, down.T, land.reshape(features)


def solution(mesh):
    lon_count, lat_count = mesh.shape["lon"], mesh.shape["lat"]
    fine = jax.sharding.Mesh(mesh.devices.reshape(lon_count // 2, 2, lat_count // 2, 2), AXES)
    lon, lat = AXES[:2], AXES[2:]
    return jax.shard_map(
        functools.partial(body, lon_count, lat_count),
        mesh=fine,
        in_specs=(
            P(None, lat, lon, None),
            P(None, lat, lon, None),
            P(lat, lon),
            P(),
            P(),
            P(),
            P(),
            P(),
            P(lat, None, None, None, None),
        ),
        out_specs=(P(None, lat, lon, None), P(), P(), P(), P(), P()),
        check_vma=False,
    )
```

```python
import functools
import math

import jax
import jax.numpy as jnp
import numpy as np
from jax import lax
from jax.experimental import pallas as pl
from jax.experimental.pallas import tpu as pltpu
from jax.sharding import PartitionSpec as P

Z = 4
WZ = 2
WH = 6
WW = 12
C = 192
HEADS = 6
HEAD = 32
FF = 768
HZ, HH, HW = WZ // 2, WH // 2, WW // 2
TOK = WZ * WH * WW
PLACES = WZ * WH
RELW = 2 * WW - 1
STRIP = -(-RELW * PLACES // 128) * 128

mask_fill = -10000.0
norm_eps = 1e-05
log2e = 1.4426950408889634
root_half = 0.7071067811865476
inv_root_tau = 0.3989422804014327
score_scale = HEAD**-0.5

f32 = jnp.float32
bf16 = jnp.bfloat16
MIB = 1 << 20

QUADS = 4
PART = C // (2 * QUADS)
CHUNK = 3 * PART
EXTRA = 8
FULL = CHUNK + EXTRA
HALF, WIDE = FULL // 2, FF // 2


def mm(a, b):
    return lax.dot_general(a, b, (((1,), (0,)), ((), ())), preferred_element_type=f32)


def mm_nt(a, b):
    return lax.dot_general(a, b, (((1,), (1,)), ((), ())), preferred_element_type=f32)


def mm_tn(a, b):
    return lax.dot_general(a, b, (((0,), (0,)), ((), ())), preferred_element_type=f32)


def unit_norm(values):
    average = jnp.mean(values, -1, keepdims=True)
    centred = values - average
    variance = jnp.mean(centred * centred, -1, keepdims=True)
    spread = lax.rsqrt(variance + norm_eps)
    return centred * spread, spread


def norm_back(upstream, unit, spread):
    first = jnp.mean(upstream, -1, keepdims=True)
    second = jnp.mean(upstream * unit, -1, keepdims=True)
    return spread * (upstream - first - unit * second)


def piece_rows(rows, cols):
    home = np.arange(Z * rows * cols).reshape(Z, rows, cols)
    top, low = slice(0, rows - HH), slice(rows - HH, rows)
    west, east = slice(0, cols - HW), slice(cols - HW, cols)
    parts = [home[:, top, west], home[:, low, west], home[:, top, east], home[:, low, east]]
    return [part.reshape(-1) for part in parts]


def window_rows(rows, cols):
    sizes = [part.size for part in piece_rows(rows, cols)]
    starts = np.cumsum([0] + sizes)
    own, north, side, corner = [np.arange(starts[k], starts[k + 1]) for k in range(4)]
    frame = np.zeros((Z, rows, cols), np.int64)
    frame[:, HH:, HW:] = own.reshape(Z, rows - HH, cols - HW)
    frame[:, :HH, HW:] = north.reshape(Z, HH, cols - HW)
    frame[:, HH:, :HW] = side.reshape(Z, rows - HH, HW)
    frame[:, :HH, :HW] = corner.reshape(Z, HH, HW)
    frame = np.roll(frame, HZ, axis=0)
    frame = frame.reshape(Z // WZ, WZ, rows // WH, WH, cols // WW, WW)
    return frame.transpose(0, 2, 4, 5, 1, 3).reshape(-1)


def spots(places):
    return jnp.asarray(np.argsort(places).astype(np.int32)[None])


def one_hot(spot_ref):
    count = spot_ref.shape[1]
    rows = lax.broadcasted_iota(jnp.int32, (count, count), 0)
    return (rows == spot_ref[...]).astype(f32).astype(bf16)


def vmem(count):
    return [pl.BlockSpec(memory_space=pltpu.VMEM)] * count


def shape(dims, dtype):
    return jax.ShapeDtypeStruct(dims, dtype)


def cost(flops, moved):
    return pl.CostEstimate(flops=flops, bytes_accessed=moved, transcendentals=0)


def land_column(land_ref, rows, cols):
    eye = (
        lax.broadcasted_iota(jnp.int32, (cols, cols), 0)
        == lax.broadcasted_iota(jnp.int32, (cols, cols), 1)
    ).astype(f32)
    land = land_ref[...].astype(f32)
    parts = [jnp.sum(eye * land[i : i + 1, :], -1, keepdims=True) for i in range(rows)]
    return jnp.concatenate(parts, axis=0)


def pack_kernel(rows, cols, *refs):
    sources, outs, (tokens_ref, cot_ref, land_ref, vec_ref, perm_ref, sems) = refs[:5], refs[5:-6], refs[-6:]
    copies = [
        pltpu.make_async_copy(source, target, sems.at[n])
        for n, (source, target) in enumerate(zip(sources, (tokens_ref, cot_ref, land_ref, vec_ref, perm_ref)))
    ]
    for copy in copies:
        copy.start()
    for copy in copies:
        copy.wait()
    column = land_column(land_ref, rows, cols)
    added = column * vec_ref[...]
    added = jnp.concatenate([added] * Z, axis=0)
    embedded = (tokens_ref[...].astype(f32) + added).astype(bf16)
    perm = one_hot(perm_ref)
    left = mm(perm, embedded)
    right = mm(perm, cot_ref[...])
    packed = jnp.concatenate([left, right], axis=1)
    start = 0
    for out in outs:
        out[...] = packed[start : start + out.shape[0]].astype(bf16)
        start += out.shape[0]


def pack(tokens, cotangent, land_sea, vector, rows, cols):
    parts = piece_rows(rows, cols)
    perm = spots(np.concatenate(parts))
    count = Z * rows * cols
    return pl.pallas_call(
        functools.partial(pack_kernel, rows, cols),
        out_shape=[shape((part.size, 2 * C), bf16) for part in parts],
        in_specs=[pl.BlockSpec(memory_space=pltpu.HBM)] * 5,
        out_specs=vmem(4),
        scratch_shapes=[
            pltpu.VMEM((count, C), bf16),
            pltpu.VMEM((count, C), bf16),
            pltpu.VMEM((rows, cols), jnp.int32),
            pltpu.VMEM((1, C), f32),
            pltpu.VMEM((1, count), jnp.int32),
            pltpu.SemaphoreType.DMA((5,)),
        ],
        cost_estimate=cost(4 * count * count * C, 4 * MIB),
        name="pack",
    )(tokens.reshape(count, C), cotangent.reshape(count, C), land_sea, vector.reshape(1, C), perm)


def floor_div(values, divisor):
    return (values * (65536 // divisor + 1)) >> 16


def bias_kernel(levels, table_ref, out_ref, *wide_refs):
    groups = levels * HEADS
    pairs = PLACES * PLACES
    row = lax.broadcasted_iota(jnp.int32, (HEADS * RELW, HEADS * STRIP), 0)
    lane = lax.broadcasted_iota(jnp.int32, (HEADS * RELW, HEADS * STRIP), 1)
    head = floor_div(row, RELW)
    ahead = lane - (head * STRIP + (RELW - 1 - (row - head * RELW)) * PLACES)
    onehot = ((ahead >= 0) & (ahead < PLACES)).astype(f32).astype(bf16)
    for level in range(levels):
        table = table_ref[:, level, :].T
        high = table.astype(bf16)
        rest = table - high.astype(f32)
        wide = mm(high, onehot) + mm(rest.astype(bf16), onehot)
        for head in range(HEADS):
            for n, wide_ref in enumerate(wide_refs):
                start = head * STRIP + n * 128
                wide_ref[(level * HEADS + head) * pairs : (level * HEADS + head + 1) * pairs, :] = wide[:, start : start + 128]
    strips = groups * PLACES
    parts = []
    for n, wide_ref in enumerate(wide_refs):
        place = lax.broadcasted_iota(jnp.int32, (strips, 128), 1) + n * 128
        place = place - floor_div(place, PLACES) * PLACES
        part = jnp.zeros((strips, 128), f32)
        for p in range(PLACES):
            part = jnp.where(place == p, wide_ref[pl.ds(p, strips, stride=PLACES), :], part)
        parts.append(part)
    strip = jnp.concatenate(parts, axis=1)
    row = lax.broadcasted_iota(jnp.int32, (strips, STRIP), 0)
    lane = lax.broadcasted_iota(jnp.int32, (strips, STRIP), 1)
    own, other = row - floor_div(row, PLACES) * PLACES, lane - floor_div(lane, PLACES) * PLACES
    low_own, low_other = (own < HZ * WH).astype(jnp.int32), (other < HZ * WH).astype(jnp.int32)
    first_level = (row < HEADS * PLACES).astype(jnp.int32)
    own_lat, other_lat = own + WH * low_own, other + WH * low_other
    north_own, north_other = (own_lat < WH + HH).astype(jnp.int32), (other_lat < WH + HH).astype(jnp.int32)
    pole = (lax.axis_index("y") + lax.axis_index("core") == 0).astype(jnp.int32)
    differs = first_level * (low_own ^ low_other) + pole * (north_own ^ north_other)
    strip = jnp.where(differs > 0, strip + mask_fill, strip) * log2e
    for w in range(WW):
        start = (WW - 1 - w) * PLACES
        part = strip[:, start : start + TOK]
        for g in range(groups):
            out_ref[g, w * PLACES : (w + 1) * PLACES, :] = part[g * PLACES : (g + 1) * PLACES, :]


def expand_bias(table):
    levels = table.shape[1]
    groups = levels * HEADS
    pairs = PLACES * PLACES
    flat = table[0].transpose(1, 3, 0, 2).reshape(HEADS * RELW, levels, pairs)
    return pl.pallas_call(
        functools.partial(bias_kernel, levels),
        out_shape=shape((groups, TOK, TOK), f32),
        in_specs=vmem(1),
        out_specs=vmem(1)[0],
        scratch_shapes=[pltpu.VMEM((groups * pairs, 128), f32)] * (STRIP // 128),
        compiler_params=pltpu.CompilerParams(vmem_limit_bytes=28 * MIB),
        cost_estimate=cost(10**9, 8 * MIB),
        name="bias",
    )(flat)


def head_masks(count):
    lane = lax.broadcasted_iota(jnp.int32, (count, C), 1)
    return [((lane >= h * HEAD) & (lane < (h + 1) * HEAD)).astype(f32) for h in range(HEADS)]


def stacked(values, masks):
    return jnp.concatenate([values * mask for mask in masks], axis=0)


def head_sum(values, masks):
    total = values[:TOK] * masks[0]
    for h in range(1, HEADS):
        total = total + values[h * TOK : (h + 1) * TOK] * masks[h]
    return total


def position():
    return lax.axis_index("core"), lax.axis_index("y") * 2 + lax.axis_index("x"), lax.axis_index("deep")


def chunk_rows(block):
    return pl.ds(pl.multiple_of(block * PART, PART), PART)


def split_parts(total_refs, keep_ref, send_ref):
    core, chip, _ = position()
    for out, side in ((keep_ref, core), (send_ref, 1 - core)):
        parts = []
        for g in range(QUADS):
            rows = chunk_rows(side * QUADS + jnp.bitwise_xor(chip, g))
            parts += [ref[rows, :] for ref in total_refs]
        out[...] = jnp.concatenate(parts, axis=0).astype(out.dtype)


def forward_kernel(
    windows, lon_windows,
    own_ref, north_ref, side_ref, corner_ref, perm_ref, bias_ref, triple_ref, project_ref, up_ref, down_ref,
    q_ref, k_ref, v_ref, p_ref, mixed_ref, normed_ref, unit_ref, spread_ref, gsum_ref, up_grad_ref, down_grad_ref,
    branch_ref, cot_ref, emb_ref,
):
    pieces = [ref[...].astype(f32) for ref in (own_ref, north_ref, side_ref, corner_ref)]
    pieces = jnp.concatenate(pieces, axis=0).astype(bf16)
    ordered = mm(one_hot(perm_ref), pieces)
    emb = ordered[:, :C]
    emb_ref[...] = emb
    cot_ref[...] = ordered[:, C:].astype(bf16)
    unit, spread = unit_norm(emb)
    unit_ref[...] = unit
    spread_ref[...] = spread
    normed = unit.astype(bf16)
    normed_ref[...] = normed
    packed = mm(normed, triple_ref[...])
    q_ref[...] = packed[:, :C].astype(bf16)
    k_ref[...] = packed[:, C : 2 * C].astype(bf16)
    v_ref[...] = packed[:, 2 * C :].astype(bf16)
    masks = head_masks(TOK)
    masks_b = [mask.astype(bf16) for mask in masks]

    def window_step(w, carry):
        rows = pl.ds(pl.multiple_of(w * TOK, TOK), TOK)
        level = w // lon_windows
        scores = mm_nt(stacked(q_ref[rows, :], masks_b), k_ref[rows, :])
        bias = bias_ref[pl.ds(level * HEADS, HEADS)].reshape(HEADS * TOK, TOK)
        raised = jnp.exp2(scores * (score_scale * log2e) + bias)
        probs = raised * (1.0 / jnp.sum(raised, -1, keepdims=True))
        probs_b = probs.astype(bf16)
        p_ref[pl.ds(w * HEADS, HEADS)] = probs_b.reshape(HEADS, TOK, TOK)
        mixed = head_sum(mm(probs_b, v_ref[rows, :]), masks).astype(bf16)
        mixed_ref[rows, :] = mixed
        branch_ref[rows, :] = mm(mixed, project_ref[...])
        return carry

    lax.fori_loop(0, windows, window_step, 0, unroll=True)

    attended = branch_ref[...].astype(bf16).astype(f32)
    unit2, spread2 = unit_norm(emb_ref[...] + attended)
    normed2 = unit2.astype(bf16)
    cot = cot_ref[...]
    back = jnp.zeros(unit2.shape, f32)
    block = 256
    for start in range(0, FF, block):
        cols = slice(start, start + block)
        up_part = up_ref[:, cols]
        pre = mm(normed2, up_part)
        upstream = mm(cot, down_ref[:, cols])
        phi = 0.5 * (1.0 + lax.erf(pre * root_half))
        activated = (pre * phi).astype(bf16)
        slope = phi + pre * inv_root_tau * jnp.exp2(pre * pre * (-0.5 * log2e))
        hidden = (upstream * slope).astype(bf16)
        up_grad_ref[:, cols] = mm_tn(normed2, hidden)
        down_grad_ref[:, cols] = mm_tn(cot, activated)
        back = back + mm_nt(hidden, up_part)
    gsum_ref[...] = cot.astype(f32) + norm_back(back, unit2, spread2)


def forward(pieces, perm, bias, triple, project, up, down, lon_windows):
    count = perm.shape[1]
    windows = count // TOK
    out_shape = [
        shape((count, C), bf16),
        shape((count, C), bf16),
        shape((count, C), bf16),
        shape((windows * HEADS, TOK, TOK), bf16),
        shape((count, C), bf16),
        shape((count, C), bf16),
        shape((count, C), f32),
        shape((count, 1), f32),
        shape((count, C), f32),
        shape((C, FF), f32),
        shape((C, FF), f32),
    ]
    return pl.pallas_call(
        functools.partial(forward_kernel, windows, lon_windows),
        out_shape=out_shape,
        in_specs=vmem(10),
        out_specs=vmem(len(out_shape)),
        scratch_shapes=[pltpu.VMEM((count, C), f32), pltpu.VMEM((count, C), bf16), pltpu.VMEM((count, C), f32)],
        compiler_params=pltpu.CompilerParams(vmem_limit_bytes=28 * MIB),
        cost_estimate=cost(3 * 10**9, 16 * MIB),
        name="forward",
    )(*pieces, perm, bias, triple, project, up, down)


def windows_back_kernel(windows, q_ref, k_ref, v_ref, p_ref, gsum_ref, project_ref, gq_ref, gk_ref, gv_ref):
    masks = head_masks(TOK)
    masks_b = [mask.astype(bf16) for mask in masks]

    def window_step(w, carry):
        rows = pl.ds(pl.multiple_of(w * TOK, TOK), TOK)
        grad = gsum_ref[rows, :].astype(bf16)
        grad_mixed = mm_nt(grad, project_ref[...])
        grad_mixed_b = grad_mixed.astype(bf16)
        probs_b = p_ref[pl.ds(w * HEADS, HEADS)].reshape(HEADS * TOK, TOK)
        probs = probs_b.astype(f32)
        grad_probs = mm_nt(stacked(grad_mixed_b, masks_b), v_ref[rows, :])
        inner = jnp.sum(grad_probs * probs, -1, keepdims=True)
        scaled = (probs * (grad_probs - inner) * score_scale).astype(bf16)
        grad_q = head_sum(mm(scaled, k_ref[rows, :]), masks)
        grad_mixed_t = grad_mixed_b.astype(f32).T.astype(bf16)
        query_t = q_ref[rows, :].astype(f32).T.astype(bf16)
        grad_k, grad_v = [], []
        for h in range(HEADS):
            spot = slice(h * HEAD, (h + 1) * HEAD)
            span = slice(h * TOK, (h + 1) * TOK)
            grad_k.append(mm(query_t[spot], scaled[span]))
            grad_v.append(mm(grad_mixed_t[spot], probs_b[span]))
        gq_ref[rows, :] = grad_q.astype(bf16)
        gk_ref[rows, :] = jnp.concatenate(grad_k, axis=0).T.astype(bf16)
        gv_ref[rows, :] = jnp.concatenate(grad_v, axis=0).T.astype(bf16)
        return carry

    lax.fori_loop(0, windows, window_step, 0, unroll=True)


def windows_back(q, k, v, p, gsum, project):
    count = q.shape[0]
    return pl.pallas_call(
        functools.partial(windows_back_kernel, count // TOK),
        out_shape=[shape((count, C), bf16)] * 3,
        in_specs=vmem(6),
        out_specs=vmem(3),
        compiler_params=pltpu.CompilerParams(vmem_limit_bytes=28 * MIB),
        cost_estimate=cost(3 * 10**9, 16 * MIB),
        name="windows_back",
    )(q, k, v, p, gsum, project)


def halved(rows):
    return -(-rows // 16) * 8


def tokens_back_kernel(
    sizes, gq_ref, gk_ref, gv_ref, mixed_ref, normed_ref, unit_ref, spread_ref, gsum_ref, perm_ref, triple_ref,
    up_grad_ref, down_grad_ref, *rest,
):
    outs, (keep_ref, send_ref, total_ref) = rest[: len(sizes)], rest[len(sizes) :]
    normed = normed_ref[...]
    triple = triple_ref[...]
    grad_normed = jnp.zeros(unit_ref.shape, f32)
    parts = []
    for n, ref in enumerate((gq_ref, gk_ref, gv_ref)):
        grad = ref[...]
        grad_normed = grad_normed + mm_nt(grad, triple[:, n * C : (n + 1) * C])
        parts.append(mm_tn(normed, grad))
    parts.append(mm_tn(mixed_ref[...], gsum_ref[...].astype(bf16)))
    total_ref[...] = jnp.concatenate(parts, axis=1)
    grad_normed = grad_normed.astype(bf16).astype(f32)
    grad_tokens = gsum_ref[...] + norm_back(grad_normed, unit_ref[...], spread_ref[...])
    pieces = mm(one_hot(perm_ref), grad_tokens.astype(bf16))
    start = 0
    for size, out in zip(sizes, outs):
        piece = pieces[start : start + size]
        half = halved(size)
        second = jnp.concatenate([piece[half:], jnp.zeros((2 * half - size, C), f32)], axis=0)
        out[...] = jnp.concatenate([piece[:half], second], axis=1).astype(bf16)
        start += size
    split_parts((up_grad_ref, down_grad_ref, total_ref), keep_ref, send_ref)


def tokens_back(grads, mixed, normed, unit, spread, gsum, perm, triple, up_grad, down_grad, sizes):
    out_shape = [shape((halved(size), 2 * C), bf16) for size in sizes] + [
        shape((QUADS * CHUNK, FF), f32),
        shape((QUADS * CHUNK, FF), bf16),
    ]
    return pl.pallas_call(
        functools.partial(tokens_back_kernel, sizes),
        out_shape=out_shape,
        in_specs=vmem(12),
        out_specs=vmem(len(out_shape)),
        scratch_shapes=[pltpu.VMEM((C, FF), f32)],
        compiler_params=pltpu.CompilerParams(vmem_limit_bytes=28 * MIB),
        cost_estimate=cost(2 * 10**9, 8 * MIB),
        name="tokens_back",
    )(*grads, mixed, normed, unit, spread, gsum, perm, triple, up_grad, down_grad)


def home_kernel(sizes, rows, cols, own_ref, north_ref, side_ref, corner_ref, perm_ref, land_ref, out_ref, sum_ref):
    pieces = []
    for size, ref in zip(sizes, (own_ref, north_ref, side_ref, corner_ref)):
        wide = ref[...].astype(f32)
        pieces += [wide[:, :C], wide[: size - wide.shape[0], C:]]
    pieces = jnp.concatenate(pieces, axis=0).astype(bf16)
    grads = mm(one_hot(perm_ref), pieces)
    out_ref[...] = grads.astype(bf16)
    column = jnp.concatenate([land_column(land_ref, rows, cols)] * Z, axis=0)
    sum_ref[...] = jnp.sum(grads * column, 0, keepdims=True)


def to_home(pieces, land_sea, sizes, rows, cols):
    count = Z * rows * cols
    perm = spots(np.argsort(np.concatenate(piece_rows(rows, cols))))
    return pl.pallas_call(
        functools.partial(home_kernel, sizes, rows, cols),
        out_shape=[shape((count, C), bf16), shape((1, C), f32)],
        in_specs=vmem(6),
        out_specs=vmem(2),
        compiler_params=pltpu.CompilerParams(vmem_limit_bytes=32 * MIB),
        cost_estimate=cost(2 * count * count * C, 4 * MIB),
        name="to_home",
    )(*pieces, perm, land_sea)


def core_add_kernel(keep_ref, got_ref, *refs):
    own_ref, outs = refs[-QUADS], refs[1 - QUADS :]
    total = keep_ref[...] + got_ref[...].astype(f32)
    own_ref[...] = total[:CHUNK]
    for e, out in enumerate(outs, 1):
        out[...] = total[e * CHUNK : (e + 1) * CHUNK].astype(bf16)


def quarter(whole_ref, distance):
    who = jnp.bitwise_xor(position()[2] & (QUADS - 1), distance)
    return whole_ref.at[who & 1, pl.ds(pl.multiple_of((who >> 1) * HALF, 8), HALF), :]


def chip_add_kernel(keep_ref, *refs):
    gots, land_ref, outs, total_ref = refs[: QUADS - 1], refs[QUADS - 1], refs[QUADS:-1], refs[-1]
    total = keep_ref[...]
    for ref in gots:
        total = total + ref[...].astype(f32)
    land = jnp.concatenate([land_ref[...], jnp.zeros((1, FF - C), f32)], axis=1)
    total = jnp.concatenate([total, land, jnp.zeros((EXTRA - 1, FF), f32)], axis=0)
    for side in range(2):
        total_ref[side] = total[:, side * WIDE : (side + 1) * WIDE]
    for e, out in enumerate(outs):
        out[...] = quarter(total_ref, e)[...].astype(out.dtype)


def add_kernel(*refs):
    total = refs[0][...].astype(f32)
    for ref in refs[1:-1]:
        total = total + ref[...].astype(f32)
    refs[-1][...] = total.astype(bf16)


def deep_join_kernel(*refs):
    parts, (out_ref, total_ref) = refs[:-2], refs[-2:]
    for e, ref in enumerate(parts):
        quarter(total_ref, e)[...] = ref[...].astype(f32)
    out_ref[...] = jnp.concatenate([total_ref[0], total_ref[1]], axis=1).astype(bf16)


def join_kernel(*refs):
    refs[-1][...] = jnp.concatenate([ref[...] for ref in refs[:-1]], axis=0)


def small_call(kernel, out_shape, args, name, after=(), scratch=()):
    return pl.pallas_call(
        kernel,
        out_shape=out_shape,
        in_specs=vmem(len(args)) + [pl.BlockSpec(memory_space=pl.ANY)] * len(after),
        out_specs=vmem(len(out_shape)),
        scratch_shapes=scratch,
        compiler_params=pltpu.CompilerParams(vmem_limit_bytes=16 * MIB),
        cost_estimate=cost(10**6, 2 * MIB),
        name=name,
    )(*args, *after)


def finish_kernel(far, chunks_ref, *refs):
    if far:
        before_ref, refs = refs[0], refs[5:]
    outs, land_ref, (up_ref, down_ref, triple_ref, project_ref, lands_ref, sems) = refs[:4], refs[4], refs[5:]
    core, chip, _ = position()
    side = 1 - core if far else core
    for g in range(QUADS):
        chunk = chunks_ref[g * FULL : (g + 1) * FULL, :].astype(f32)
        block = jnp.bitwise_xor(chip, g)
        rows = chunk_rows(block)
        up_ref[rows, :] = chunk[:PART]
        down_ref[rows, :] = chunk[PART : 2 * PART]
        triple_ref[rows, :] = chunk[2 * PART : CHUNK, : 3 * C]
        project_ref[rows, :] = chunk[2 * PART : CHUNK, 3 * C :]
        lands_ref[pl.ds(pl.multiple_of(block * EXTRA, EXTRA), EXTRA), :] = chunk[CHUNK:, :C]
    copies = []
    for n, (source, out) in enumerate(zip((triple_ref, project_ref, up_ref, down_ref), outs)):
        rows = pl.ds(pl.multiple_of(side * QUADS * PART, 8), QUADS * PART)
        copies.append(pltpu.make_async_copy(source, out.at[rows, :], sems.at[n]))
    for copy in copies:
        copy.start()
    land = jnp.sum(lands_ref[...], 0, keepdims=True)
    land_ref[...] = land + before_ref[...] if far else land
    for copy in copies:
        copy.wait()


def finish(chunks, before=()):
    rows = QUADS * PART
    widths = (3 * C, C, FF, FF)
    hbm = [pl.BlockSpec(memory_space=pltpu.HBM)] * 4
    land, weights = before[4:], before[:4]
    return pl.pallas_call(
        functools.partial(finish_kernel, bool(before)),
        out_shape=[shape((C, width), f32) for width in widths] + [shape((1, C), f32)],
        in_specs=vmem(1 + len(land)) + hbm[: len(weights)],
        out_specs=hbm + vmem(1),
        scratch_shapes=[
            pltpu.VMEM((rows, FF), f32),
            pltpu.VMEM((rows, FF), f32),
            pltpu.VMEM((rows, 3 * C), f32),
            pltpu.VMEM((rows, C), f32),
            pltpu.VMEM((QUADS * EXTRA, C), f32),
            pltpu.SemaphoreType.DMA((4,)),
        ],
        input_output_aliases={2 + n: n for n in range(len(weights))},
        compiler_params=pltpu.CompilerParams(vmem_limit_bytes=16 * MIB),
        cost_estimate=cost(10**6, 2 * MIB),
        name="finish_far" if before else "finish_own",
    )(chunks, *land, *weights)


def reduce_all(keep, sent, land, shift, lon_count, after):
    core_move = lambda lon, lat: (lon, lat ^ 1)
    chip_move = lambda e: lambda lon, lat: (lon ^ (e & 1), lat ^ (2 * (e >> 1)))
    deep_move = lambda e: lambda lon, lat: (lon ^ (2 * e), lat)

    def one(rows):
        return [shape((rows, FF), bf16)]

    got = shift(sent, move=core_move)
    parts = [shape((CHUNK, FF), f32)] + one(CHUNK) * (QUADS - 1)
    own, *parts = small_call(core_add_kernel, parts, (keep, got), "core_add", after=after)
    gots = [shift(value, move=chip_move(e)) for e, value in enumerate(parts, 1)]
    scratch = [pltpu.VMEM((2, FULL, WIDE), f32)]
    small = [shape((HALF, WIDE), bf16)]
    quarters = [shape((HALF, WIDE), f32)] + small * (QUADS - 1)
    own, *parts = small_call(chip_add_kernel, quarters, (own, *gots, land), "chip_add", scratch=scratch)
    gots = [shift(value, move=deep_move(e)) for e, value in enumerate(parts, 1)]
    (total,) = small_call(add_kernel, small, (own, *gots), "deep_add")
    reach = QUADS
    while reach < lon_count // 2:
        got = shift(total, move=deep_move(reach))
        reach *= 2
        (total,) = small_call(add_kernel, small, (total, got), "far_add")
    parts = [total] + [shift(total, move=deep_move(e)) for e in range(1, QUADS)]
    (total,) = small_call(deep_join_kernel, one(FULL), parts, "deep_join", scratch=scratch)
    near = [total] + [shift(total, move=chip_move(e)) for e in range(1, QUADS)]
    (total,) = small_call(join_kernel, one(QUADS * FULL), near, "join")
    got = shift(total, move=core_move)
    return finish(got, finish(total))


AXES = ("deep", "x", "y", "core")


def send(value, lon_count, lat_count, move):
    pairs = []
    for lon in range(lon_count):
        for lat in range(lat_count):
            to_lon, to_lat = move(lon, lat)
            pairs.append((lon * lat_count + lat, (to_lon % lon_count) * lat_count + to_lat % lat_count))
    return lax.ppermute(value, AXES, pairs)


def body(
    lon_count, lat_count,
    tokens, cotangent, land_sea, land_vector, triple_weight, project_weight, up_weight, down_weight, earth_bias,
):
    levels, rows, cols, features = tokens.shape
    shift = functools.partial(send, lon_count=lon_count, lat_count=lat_count)
    lon_windows = cols // WW

    own, north, side, corner = pack(tokens, cotangent, land_sea, land_vector, rows, cols)
    north = shift(north, move=lambda lon, lat: (lon, lat + 1))
    side = shift(side, move=lambda lon, lat: (lon + 1, lat))
    corner = shift(corner, move=lambda lon, lat: (lon + 1, lat + 1))
    bias = expand_bias(earth_bias)

    places = window_rows(rows, cols)
    sizes = [part.size for part in piece_rows(rows, cols)]
    pieces = (own, north, side, corner)
    q, k, v, p, mixed, normed, unit, spread, gsum, up, down = forward(
        pieces, spots(places), bias, triple_weight, project_weight, up_weight, down_weight.T, lon_windows
    )
    grads = windows_back(q, k, v, p, gsum, project_weight)
    own, north, side, corner, keep, sent = tokens_back(
        grads, mixed, normed, unit, spread, gsum, spots(np.argsort(places)), triple_weight, up, down, sizes
    )
    north = shift(north, move=lambda lon, lat: (lon, lat - 1))
    side = shift(side, move=lambda lon, lat: (lon - 1, lat))
    corner = shift(corner, move=lambda lon, lat: (lon - 1, lat - 1))
    after = (north, side, corner)
    grad_tokens, land = to_home((own, north, side, corner), land_sea, sizes, rows, cols)
    triple, project, up, down, land = reduce_all(keep, sent, land, shift, lon_count, after)
    return grad_tokens.reshape(tokens.shape), triple, project, up, down.T, land.reshape(features)


def solution(mesh):
    lon_count, lat_count = mesh.shape["lon"], mesh.shape["lat"]
    fine = jax.sharding.Mesh(mesh.devices.reshape(lon_count // 2, 2, lat_count // 2, 2), AXES)
    lon, lat = AXES[:2], AXES[2:]
    return jax.shard_map(
        functools.partial(body, lon_count, lat_count),
        mesh=fine,
        in_specs=(
            P(None, lat, lon, None),
            P(None, lat, lon, None),
            P(lat, lon),
            P(),
            P(),
            P(),
            P(),
            P(),
            P(lat, None, None, None, None),
        ),
        out_specs=(P(None, lat, lon, None), P(), P(), P(), P(), P()),
        check_vma=False,
    )
```

```python
import functools
import math

import jax
import jax.numpy as jnp
import numpy as np
from jax import lax
from jax.experimental import pallas as pl
from jax.experimental.pallas import tpu as pltpu
from jax.sharding import PartitionSpec as P

Z = 4
WZ = 2
WH = 6
WW = 12
C = 192
HEADS = 6
HEAD = 32
FF = 768
HZ, HH, HW = WZ // 2, WH // 2, WW // 2
TOK = WZ * WH * WW
PLACES = WZ * WH
RELW = 2 * WW - 1
STRIP = -(-RELW * PLACES // 128) * 128

mask_fill = -10000.0
norm_eps = 1e-05
log2e = 1.4426950408889634
root_half = 0.7071067811865476
inv_root_tau = 0.3989422804014327
score_scale = HEAD**-0.5

f32 = jnp.float32
bf16 = jnp.bfloat16
MIB = 1 << 20

QUADS = 4
PART = C // (2 * QUADS)
CHUNK = 3 * PART
EXTRA = 8
FULL = CHUNK + EXTRA


def mm(a, b):
    return lax.dot_general(a, b, (((1,), (0,)), ((), ())), preferred_element_type=f32)


def mm_nt(a, b):
    return lax.dot_general(a, b, (((1,), (1,)), ((), ())), preferred_element_type=f32)


def mm_tn(a, b):
    return lax.dot_general(a, b, (((0,), (0,)), ((), ())), preferred_element_type=f32)


def unit_norm(values):
    average = jnp.mean(values, -1, keepdims=True)
    centred = values - average
    variance = jnp.mean(centred * centred, -1, keepdims=True)
    spread = lax.rsqrt(variance + norm_eps)
    return centred * spread, spread


def norm_back(upstream, unit, spread):
    first = jnp.mean(upstream, -1, keepdims=True)
    second = jnp.mean(upstream * unit, -1, keepdims=True)
    return spread * (upstream - first - unit * second)


def piece_rows(rows, cols):
    home = np.arange(Z * rows * cols).reshape(Z, rows, cols)
    top, low = slice(0, rows - HH), slice(rows - HH, rows)
    west, east = slice(0, cols - HW), slice(cols - HW, cols)
    parts = [home[:, top, west], home[:, low, west], home[:, top, east], home[:, low, east]]
    return [part.reshape(-1) for part in parts]


def window_rows(rows, cols):
    sizes = [part.size for part in piece_rows(rows, cols)]
    starts = np.cumsum([0] + sizes)
    own, north, side, corner = [np.arange(starts[k], starts[k + 1]) for k in range(4)]
    frame = np.zeros((Z, rows, cols), np.int64)
    frame[:, HH:, HW:] = own.reshape(Z, rows - HH, cols - HW)
    frame[:, :HH, HW:] = north.reshape(Z, HH, cols - HW)
    frame[:, HH:, :HW] = side.reshape(Z, rows - HH, HW)
    frame[:, :HH, :HW] = corner.reshape(Z, HH, HW)
    frame = np.roll(frame, HZ, axis=0)
    frame = frame.reshape(Z // WZ, WZ, rows // WH, WH, cols // WW, WW)
    return frame.transpose(0, 2, 4, 5, 1, 3).reshape(-1)


def spots(places):
    return jnp.asarray(np.argsort(places).astype(np.int32)[None])


def one_hot(spot_ref):
    count = spot_ref.shape[1]
    rows = lax.broadcasted_iota(jnp.int32, (count, count), 0)
    return (rows == spot_ref[...]).astype(f32).astype(bf16)


def vmem(count):
    return [pl.BlockSpec(memory_space=pltpu.VMEM)] * count


def shape(dims, dtype):
    return jax.ShapeDtypeStruct(dims, dtype)


def cost(flops, moved):
    return pl.CostEstimate(flops=flops, bytes_accessed=moved, transcendentals=0)


def land_column(land_ref, rows, cols):
    eye = (
        lax.broadcasted_iota(jnp.int32, (cols, cols), 0)
        == lax.broadcasted_iota(jnp.int32, (cols, cols), 1)
    ).astype(f32)
    land = land_ref[...].astype(f32)
    parts = [jnp.sum(eye * land[i : i + 1, :], -1, keepdims=True) for i in range(rows)]
    return jnp.concatenate(parts, axis=0)


def pack_kernel(rows, cols, *refs):
    sources, outs, (tokens_ref, cot_ref, land_ref, vec_ref, perm_ref, sems) = refs[:5], refs[5:-6], refs[-6:]
    copies = [
        pltpu.make_async_copy(source, target, sems.at[n])
        for n, (source, target) in enumerate(zip(sources, (tokens_ref, cot_ref, land_ref, vec_ref, perm_ref)))
    ]
    for copy in copies:
        copy.start()
    for copy in copies:
        copy.wait()
    column = land_column(land_ref, rows, cols)
    added = column * vec_ref[...]
    added = jnp.concatenate([added] * Z, axis=0)
    embedded = (tokens_ref[...].astype(f32) + added).astype(bf16)
    perm = one_hot(perm_ref)
    left = mm(perm, embedded)
    right = mm(perm, cot_ref[...])
    packed = jnp.concatenate([left, right], axis=1)
    start = 0
    for out in outs:
        out[...] = packed[start : start + out.shape[0]].astype(bf16)
        start += out.shape[0]


def pack(tokens, cotangent, land_sea, vector, rows, cols):
    parts = piece_rows(rows, cols)
    perm = spots(np.concatenate(parts))
    count = Z * rows * cols
    return pl.pallas_call(
        functools.partial(pack_kernel, rows, cols),
        out_shape=[shape((part.size, 2 * C), bf16) for part in parts],
        in_specs=[pl.BlockSpec(memory_space=pltpu.HBM)] * 5,
        out_specs=vmem(4),
        scratch_shapes=[
            pltpu.VMEM((count, C), bf16),
            pltpu.VMEM((count, C), bf16),
            pltpu.VMEM((rows, cols), jnp.int32),
            pltpu.VMEM((1, C), f32),
            pltpu.VMEM((1, count), jnp.int32),
            pltpu.SemaphoreType.DMA((5,)),
        ],
        cost_estimate=cost(4 * count * count * C, 4 * MIB),
        name="pack",
    )(tokens.reshape(count, C), cotangent.reshape(count, C), land_sea, vector.reshape(1, C), perm)


def floor_div(values, divisor):
    return (values * (65536 // divisor + 1)) >> 16


def bias_kernel(levels, table_ref, out_ref, *wide_refs):
    groups = levels * HEADS
    pairs = PLACES * PLACES
    row = lax.broadcasted_iota(jnp.int32, (HEADS * RELW, HEADS * STRIP), 0)
    lane = lax.broadcasted_iota(jnp.int32, (HEADS * RELW, HEADS * STRIP), 1)
    head = floor_div(row, RELW)
    ahead = lane - (head * STRIP + (RELW - 1 - (row - head * RELW)) * PLACES)
    onehot = ((ahead >= 0) & (ahead < PLACES)).astype(f32).astype(bf16)
    for level in range(levels):
        table = table_ref[:, level, :].T
        high = table.astype(bf16)
        rest = table - high.astype(f32)
        wide = mm(high, onehot) + mm(rest.astype(bf16), onehot)
        for head in range(HEADS):
            for n, wide_ref in enumerate(wide_refs):
                start = head * STRIP + n * 128
                wide_ref[(level * HEADS + head) * pairs : (level * HEADS + head + 1) * pairs, :] = wide[:, start : start + 128]
    strips = groups * PLACES
    parts = []
    for n, wide_ref in enumerate(wide_refs):
        place = lax.broadcasted_iota(jnp.int32, (strips, 128), 1) + n * 128
        place = place - floor_div(place, PLACES) * PLACES
        part = jnp.zeros((strips, 128), f32)
        for p in range(PLACES):
            part = jnp.where(place == p, wide_ref[pl.ds(p, strips, stride=PLACES), :], part)
        parts.append(part)
    strip = jnp.concatenate(parts, axis=1)
    row = lax.broadcasted_iota(jnp.int32, (strips, STRIP), 0)
    lane = lax.broadcasted_iota(jnp.int32, (strips, STRIP), 1)
    own, other = row - floor_div(row, PLACES) * PLACES, lane - floor_div(lane, PLACES) * PLACES
    low_own, low_other = (own < HZ * WH).astype(jnp.int32), (other < HZ * WH).astype(jnp.int32)
    first_level = (row < HEADS * PLACES).astype(jnp.int32)
    own_lat, other_lat = own + WH * low_own, other + WH * low_other
    north_own, north_other = (own_lat < WH + HH).astype(jnp.int32), (other_lat < WH + HH).astype(jnp.int32)
    pole = (lax.axis_index("y") + lax.axis_index("core") == 0).astype(jnp.int32)
    differs = first_level * (low_own ^ low_other) + pole * (north_own ^ north_other)
    strip = jnp.where(differs > 0, strip + mask_fill, strip) * log2e
    for w in range(WW):
        start = (WW - 1 - w) * PLACES
        part = strip[:, start : start + TOK]
        for g in range(groups):
            out_ref[g, w * PLACES : (w + 1) * PLACES, :] = part[g * PLACES : (g + 1) * PLACES, :]


def expand_bias(table):
    levels = table.shape[1]
    groups = levels * HEADS
    pairs = PLACES * PLACES
    flat = table[0].transpose(1, 3, 0, 2).reshape(HEADS * RELW, levels, pairs)
    return pl.pallas_call(
        functools.partial(bias_kernel, levels),
        out_shape=shape((groups, TOK, TOK), f32),
        in_specs=vmem(1),
        out_specs=vmem(1)[0],
        scratch_shapes=[pltpu.VMEM((groups * pairs, 128), f32)] * (STRIP // 128),
        compiler_params=pltpu.CompilerParams(vmem_limit_bytes=28 * MIB),
        cost_estimate=cost(10**9, 8 * MIB),
        name="bias",
    )(flat)


def head_masks(count):
    lane = lax.broadcasted_iota(jnp.int32, (count, C), 1)
    return [((lane >= h * HEAD) & (lane < (h + 1) * HEAD)).astype(f32) for h in range(HEADS)]


def stacked(values, masks):
    return jnp.concatenate([values * mask for mask in masks], axis=0)


def head_sum(values, masks):
    total = values[:TOK] * masks[0]
    for h in range(1, HEADS):
        total = total + values[h * TOK : (h + 1) * TOK] * masks[h]
    return total


def position():
    return lax.axis_index("core"), lax.axis_index("y") * 2 + lax.axis_index("x"), lax.axis_index("deep")


def chunk_rows(block):
    return pl.ds(pl.multiple_of(block * PART, PART), PART)


def split_parts(total_refs, keep_ref, send_ref):
    core, chip, _ = position()
    for out, side in ((keep_ref, core), (send_ref, 1 - core)):
        parts = []
        for g in range(QUADS):
            rows = chunk_rows(side * QUADS + jnp.bitwise_xor(chip, g))
            parts += [ref[rows, :] for ref in total_refs]
        out[...] = jnp.concatenate(parts, axis=0).astype(out.dtype)


def normal_cdf(x):
    bell = jnp.exp2(x * x * (-0.5 * log2e))
    base = 1.0 + (0.3275911 * root_half) * jnp.abs(x)
    t = 1.0 / base
    poly = -0.5 * 1.453152027 + t * (0.5 * 1.061405429)
    poly = 0.5 * 1.421413741 + t * poly
    poly = -0.5 * 0.284496736 + t * poly
    poly = 0.5 * 0.254829592 + t * poly
    tail = poly * t * bell
    return jnp.where(x < 0.0, tail, 1.0 - tail), bell


def forward_kernel(
    windows, lon_windows,
    own_ref, north_ref, side_ref, corner_ref, perm_ref, bias_ref, triple_ref, project_ref, up_ref, down_ref,
    q_ref, k_ref, v_ref, p_ref, mixed_ref, normed_ref, unit_ref, spread_ref, gsum_ref, up_grad_ref, down_grad_ref,
    branch_ref, cot_ref, emb_ref,
):
    pieces = [ref[...].astype(f32) for ref in (own_ref, north_ref, side_ref, corner_ref)]
    pieces = jnp.concatenate(pieces, axis=0).astype(bf16)
    ordered = mm(one_hot(perm_ref), pieces)
    emb = ordered[:, :C]
    emb_ref[...] = emb
    cot_ref[...] = ordered[:, C:].astype(bf16)
    unit, spread = unit_norm(emb)
    unit_ref[...] = unit
    spread_ref[...] = spread
    normed = unit.astype(bf16)
    normed_ref[...] = normed
    packed = mm(normed, triple_ref[...])
    q_ref[...] = packed[:, :C].astype(bf16)
    k_ref[...] = packed[:, C : 2 * C].astype(bf16)
    v_ref[...] = packed[:, 2 * C :].astype(bf16)
    masks = head_masks(TOK)
    masks_b = [mask.astype(bf16) for mask in masks]

    def window_step(w, carry):
        rows = pl.ds(pl.multiple_of(w * TOK, TOK), TOK)
        level = w // lon_windows
        scores = mm_nt(stacked(q_ref[rows, :], masks_b), k_ref[rows, :])
        bias = bias_ref[pl.ds(level * HEADS, HEADS)].reshape(HEADS * TOK, TOK)
        raised = jnp.exp2(scores * (score_scale * log2e) + bias)
        probs = raised * (1.0 / jnp.sum(raised, -1, keepdims=True))
        probs_b = probs.astype(bf16)
        p_ref[pl.ds(w * HEADS, HEADS)] = probs_b.reshape(HEADS, TOK, TOK)
        mixed = head_sum(mm(probs_b, v_ref[rows, :]), masks).astype(bf16)
        mixed_ref[rows, :] = mixed
        branch_ref[rows, :] = mm(mixed, project_ref[...])
        return carry

    lax.fori_loop(0, windows, window_step, 0, unroll=True)

    attended = branch_ref[...].astype(bf16).astype(f32)
    unit2, spread2 = unit_norm(emb_ref[...] + attended)
    normed2 = unit2.astype(bf16)
    cot = cot_ref[...]
    back = jnp.zeros(unit2.shape, f32)
    block = 256
    for start in range(0, FF, block):
        cols = slice(start, start + block)
        up_part = up_ref[:, cols]
        pre = mm(normed2, up_part)
        upstream = mm(cot, down_ref[:, cols])
        phi, bell = normal_cdf(pre)
        activated = (pre * phi).astype(bf16)
        slope = phi + pre * inv_root_tau * bell
        hidden = (upstream * slope).astype(bf16)
        up_grad_ref[:, cols] = mm_tn(normed2, hidden)
        down_grad_ref[:, cols] = mm_tn(cot, activated)
        back = back + mm_nt(hidden, up_part)
    gsum_ref[...] = cot.astype(f32) + norm_back(back, unit2, spread2)


def forward(pieces, perm, bias, triple, project, up, down, lon_windows):
    count = perm.shape[1]
    windows = count // TOK
    out_shape = [
        shape((count, C), bf16),
        shape((count, C), bf16),
        shape((count, C), bf16),
        shape((windows * HEADS, TOK, TOK), bf16),
        shape((count, C), bf16),
        shape((count, C), bf16),
        shape((count, C), f32),
        shape((count, 1), f32),
        shape((count, C), f32),
        shape((C, FF), f32),
        shape((C, FF), f32),
    ]
    return pl.pallas_call(
        functools.partial(forward_kernel, windows, lon_windows),
        out_shape=out_shape,
        in_specs=vmem(10),
        out_specs=vmem(len(out_shape)),
        scratch_shapes=[pltpu.VMEM((count, C), f32), pltpu.VMEM((count, C), bf16), pltpu.VMEM((count, C), f32)],
        compiler_params=pltpu.CompilerParams(vmem_limit_bytes=28 * MIB),
        cost_estimate=cost(3 * 10**9, 16 * MIB),
        name="forward",
    )(*pieces, perm, bias, triple, project, up, down)


def windows_back_kernel(windows, q_ref, k_ref, v_ref, p_ref, gsum_ref, project_ref, gq_ref, gk_ref, gv_ref):
    masks = head_masks(TOK)
    masks_b = [mask.astype(bf16) for mask in masks]

    def window_step(w, carry):
        rows = pl.ds(pl.multiple_of(w * TOK, TOK), TOK)
        grad = gsum_ref[rows, :].astype(bf16)
        grad_mixed = mm_nt(grad, project_ref[...])
        grad_mixed_b = grad_mixed.astype(bf16)
        probs_b = p_ref[pl.ds(w * HEADS, HEADS)].reshape(HEADS * TOK, TOK)
        probs = probs_b.astype(f32)
        grad_mixed_h = stacked(grad_mixed_b, masks_b)
        grad_probs = mm_nt(grad_mixed_h, v_ref[rows, :])
        inner = jnp.sum(grad_probs * probs, -1, keepdims=True)
        scaled = (probs * (grad_probs - inner) * score_scale).astype(bf16)
        grad_q = head_sum(mm(scaled, k_ref[rows, :]), masks)
        gq_ref[rows, :] = grad_q.astype(bf16)
        gk_ref[rows, :] = mm_tn(scaled, stacked(q_ref[rows, :], masks_b)).astype(bf16)
        gv_ref[rows, :] = mm_tn(probs_b, grad_mixed_h).astype(bf16)
        return carry

    lax.fori_loop(0, windows, window_step, 0, unroll=True)


def windows_back(q, k, v, p, gsum, project):
    count = q.shape[0]
    return pl.pallas_call(
        functools.partial(windows_back_kernel, count // TOK),
        out_shape=[shape((count, C), bf16)] * 3,
        in_specs=vmem(6),
        out_specs=vmem(3),
        compiler_params=pltpu.CompilerParams(vmem_limit_bytes=28 * MIB),
        cost_estimate=cost(3 * 10**9, 16 * MIB),
        name="windows_back",
    )(q, k, v, p, gsum, project)


def halved(rows):
    return -(-rows // 16) * 8


def tokens_back_kernel(
    sizes, gq_ref, gk_ref, gv_ref, mixed_ref, normed_ref, unit_ref, spread_ref, gsum_ref, perm_ref, triple_ref,
    up_grad_ref, down_grad_ref, *rest,
):
    outs, (keep_ref, send_ref, total_ref) = rest[: len(sizes)], rest[len(sizes) :]
    normed = normed_ref[...]
    triple = triple_ref[...]
    grad_normed = jnp.zeros(unit_ref.shape, f32)
    parts = []
    for n, ref in enumerate((gq_ref, gk_ref, gv_ref)):
        grad = ref[...]
        grad_normed = grad_normed + mm_nt(grad, triple[:, n * C : (n + 1) * C])
        parts.append(mm_tn(normed, grad))
    parts.append(mm_tn(mixed_ref[...], gsum_ref[...].astype(bf16)))
    total_ref[...] = jnp.concatenate(parts, axis=1)
    grad_normed = grad_normed.astype(bf16).astype(f32)
    grad_tokens = gsum_ref[...] + norm_back(grad_normed, unit_ref[...], spread_ref[...])
    pieces = mm(one_hot(perm_ref), grad_tokens.astype(bf16))
    start = 0
    for size, out in zip(sizes, outs):
        piece = pieces[start : start + size]
        half = halved(size)
        second = jnp.concatenate([piece[half:], jnp.zeros((2 * half - size, C), f32)], axis=0)
        out[...] = jnp.concatenate([piece[:half], second], axis=1).astype(bf16)
        start += size
    split_parts((up_grad_ref, down_grad_ref, total_ref), keep_ref, send_ref)


def tokens_back(grads, mixed, normed, unit, spread, gsum, perm, triple, up_grad, down_grad, sizes):
    out_shape = [shape((halved(size), 2 * C), bf16) for size in sizes] + [
        shape((QUADS * CHUNK, FF), f32),
        shape((QUADS * CHUNK, FF), bf16),
    ]
    return pl.pallas_call(
        functools.partial(tokens_back_kernel, sizes),
        out_shape=out_shape,
        in_specs=vmem(12),
        out_specs=vmem(len(out_shape)),
        scratch_shapes=[pltpu.VMEM((C, FF), f32)],
        compiler_params=pltpu.CompilerParams(vmem_limit_bytes=28 * MIB),
        cost_estimate=cost(2 * 10**9, 8 * MIB),
        name="tokens_back",
    )(*grads, mixed, normed, unit, spread, gsum, perm, triple, up_grad, down_grad)


def home_kernel(sizes, rows, cols, own_ref, north_ref, side_ref, corner_ref, perm_ref, land_ref, out_ref, sum_ref):
    pieces = []
    for size, ref in zip(sizes, (own_ref, north_ref, side_ref, corner_ref)):
        wide = ref[...].astype(f32)
        pieces += [wide[:, :C], wide[: size - wide.shape[0], C:]]
    pieces = jnp.concatenate(pieces, axis=0).astype(bf16)
    grads = mm(one_hot(perm_ref), pieces)
    out_ref[...] = grads.astype(bf16)
    column = jnp.concatenate([land_column(land_ref, rows, cols)] * Z, axis=0)
    sum_ref[...] = jnp.sum(grads * column, 0, keepdims=True)


def to_home(pieces, land_sea, sizes, rows, cols):
    count = Z * rows * cols
    perm = spots(np.argsort(np.concatenate(piece_rows(rows, cols))))
    return pl.pallas_call(
        functools.partial(home_kernel, sizes, rows, cols),
        out_shape=[shape((count, C), bf16), shape((1, C), f32)],
        in_specs=vmem(6),
        out_specs=vmem(2),
        compiler_params=pltpu.CompilerParams(vmem_limit_bytes=32 * MIB),
        cost_estimate=cost(2 * count * count * C, 4 * MIB),
        name="to_home",
    )(*pieces, perm, land_sea)


def core_add_kernel(keep_ref, got_ref, *refs):
    own_ref, outs = refs[-QUADS], refs[1 - QUADS :]
    total = keep_ref[...] + got_ref[...].astype(f32)
    own_ref[...] = total[:CHUNK]
    for e, out in enumerate(outs, 1):
        out[...] = total[e * CHUNK : (e + 1) * CHUNK].astype(bf16)


def chip_add_kernel(keep_ref, *refs):
    gots, (land_ref, out_ref) = refs[:-2], refs[-2:]
    total = keep_ref[...]
    for ref in gots:
        total = total + ref[...].astype(f32)
    land = jnp.concatenate([land_ref[...], jnp.zeros((1, FF - C), f32)], axis=1)
    out_ref[...] = jnp.concatenate([total, land, jnp.zeros((EXTRA - 1, FF), f32)], axis=0).astype(bf16)


def add_kernel(one_ref, two_ref, out_ref):
    out_ref[...] = (one_ref[...].astype(f32) + two_ref[...].astype(f32)).astype(bf16)


def join_kernel(*refs):
    refs[-1][...] = jnp.concatenate([ref[...] for ref in refs[:-1]], axis=0)


def small_call(kernel, out_shape, args, name, after=(), scratch=()):
    return pl.pallas_call(
        kernel,
        out_shape=out_shape,
        in_specs=vmem(len(args)) + [pl.BlockSpec(memory_space=pl.ANY)] * len(after),
        out_specs=vmem(len(out_shape)),
        scratch_shapes=scratch,
        compiler_params=pltpu.CompilerParams(vmem_limit_bytes=16 * MIB),
        cost_estimate=cost(10**6, 2 * MIB),
        name=name,
    )(*args, *after)


def finish_kernel(far, chunks_ref, *refs):
    if far:
        before_ref, refs = refs[0], refs[5:]
    outs, land_ref, (up_ref, down_ref, triple_ref, project_ref, lands_ref, sems) = refs[:4], refs[4], refs[5:]
    core, chip, _ = position()
    side = 1 - core if far else core
    for g in range(QUADS):
        chunk = chunks_ref[g * FULL : (g + 1) * FULL, :].astype(f32)
        block = jnp.bitwise_xor(chip, g)
        rows = chunk_rows(block)
        up_ref[rows, :] = chunk[:PART]
        down_ref[rows, :] = chunk[PART : 2 * PART]
        triple_ref[rows, :] = chunk[2 * PART : CHUNK, : 3 * C]
        project_ref[rows, :] = chunk[2 * PART : CHUNK, 3 * C :]
        lands_ref[pl.ds(pl.multiple_of(block * EXTRA, EXTRA), EXTRA), :] = chunk[CHUNK:, :C]
    copies = []
    for n, (source, out) in enumerate(zip((triple_ref, project_ref, up_ref, down_ref), outs)):
        rows = pl.ds(pl.multiple_of(side * QUADS * PART, 8), QUADS * PART)
        copies.append(pltpu.make_async_copy(source, out.at[rows, :], sems.at[n]))
    for copy in copies:
        copy.start()
    land = jnp.sum(lands_ref[...], 0, keepdims=True)
    land_ref[...] = land + before_ref[...] if far else land
    for copy in copies:
        copy.wait()


def finish(chunks, before=()):
    rows = QUADS * PART
    widths = (3 * C, C, FF, FF)
    hbm = [pl.BlockSpec(memory_space=pltpu.HBM)] * 4
    land, weights = before[4:], before[:4]
    return pl.pallas_call(
        functools.partial(finish_kernel, bool(before)),
        out_shape=[shape((C, width), f32) for width in widths] + [shape((1, C), f32)],
        in_specs=vmem(1 + len(land)) + hbm[: len(weights)],
        out_specs=hbm + vmem(1),
        scratch_shapes=[
            pltpu.VMEM((rows, FF), f32),
            pltpu.VMEM((rows, FF), f32),
            pltpu.VMEM((rows, 3 * C), f32),
            pltpu.VMEM((rows, C), f32),
            pltpu.VMEM((QUADS * EXTRA, C), f32),
            pltpu.SemaphoreType.DMA((4,)),
        ],
        input_output_aliases={2 + n: n for n in range(len(weights))},
        compiler_params=pltpu.CompilerParams(vmem_limit_bytes=16 * MIB),
        cost_estimate=cost(10**6, 2 * MIB),
        name="finish_far" if before else "finish_own",
    )(chunks, *land, *weights)


def reduce_all(keep, sent, land, shift, lon_count, after):
    core_move = lambda lon, lat: (lon, lat ^ 1)
    chip_move = lambda e: lambda lon, lat: (lon ^ (e & 1), lat ^ (2 * (e >> 1)))
    deep_move = lambda e: lambda lon, lat: (lon ^ (2 * e), lat)

    def one(rows):
        return [shape((rows, FF), bf16)]

    got = shift(sent, move=core_move)
    parts = [shape((CHUNK, FF), f32)] + one(CHUNK) * (QUADS - 1)
    own, *parts = small_call(core_add_kernel, parts, (keep, got), "core_add", after=after)
    gots = [shift(value, move=chip_move(e)) for e, value in enumerate(parts, 1)]
    (total,) = small_call(chip_add_kernel, one(FULL), (own, *gots, land), "chip_add")
    reach = 1
    while reach < lon_count // 2:
        got = shift(total, move=deep_move(reach))
        reach *= 2
        (total,) = small_call(add_kernel, one(FULL), (total, got), "deep_add")
    near = [total] + [shift(total, move=chip_move(e)) for e in range(1, QUADS)]
    (total,) = small_call(join_kernel, one(QUADS * FULL), near, "join")
    got = shift(total, move=core_move)
    return finish(got, finish(total))


AXES = ("deep", "x", "y", "core")


def send(value, lon_count, lat_count, move):
    pairs = []
    for lon in range(lon_count):
        for lat in range(lat_count):
            to_lon, to_lat = move(lon, lat)
            pairs.append((lon * lat_count + lat, (to_lon % lon_count) * lat_count + to_lat % lat_count))
    return lax.ppermute(value, AXES, pairs)


def body(
    lon_count, lat_count,
    tokens, cotangent, land_sea, land_vector, triple_weight, project_weight, up_weight, down_weight, earth_bias,
):
    levels, rows, cols, features = tokens.shape
    shift = functools.partial(send, lon_count=lon_count, lat_count=lat_count)
    lon_windows = cols // WW

    own, north, side, corner = pack(tokens, cotangent, land_sea, land_vector, rows, cols)
    north = shift(north, move=lambda lon, lat: (lon, lat + 1))
    side = shift(side, move=lambda lon, lat: (lon + 1, lat))
    corner = shift(corner, move=lambda lon, lat: (lon + 1, lat + 1))
    bias = expand_bias(earth_bias)

    places = window_rows(rows, cols)
    sizes = [part.size for part in piece_rows(rows, cols)]
    pieces = (own, north, side, corner)
    q, k, v, p, mixed, normed, unit, spread, gsum, up, down = forward(
        pieces, spots(places), bias, triple_weight, project_weight, up_weight, down_weight.T, lon_windows
    )
    grads = windows_back(q, k, v, p, gsum, project_weight)
    own, north, side, corner, keep, sent = tokens_back(
        grads, mixed, normed, unit, spread, gsum, spots(np.argsort(places)), triple_weight, up, down, sizes
    )
    north = shift(north, move=lambda lon, lat: (lon, lat - 1))
    side = shift(side, move=lambda lon, lat: (lon - 1, lat))
    corner = shift(corner, move=lambda lon, lat: (lon - 1, lat - 1))
    after = (north, side, corner)
    grad_tokens, land = to_home((own, north, side, corner), land_sea, sizes, rows, cols)
    triple, project, up, down, land = reduce_all(keep, sent, land, shift, lon_count, after)
    return grad_tokens.reshape(tokens.shape), triple, project, up, down.T, land.reshape(features)


def solution(mesh):
    lon_count, lat_count = mesh.shape["lon"], mesh.shape["lat"]
    fine = jax.sharding.Mesh(mesh.devices.reshape(lon_count // 2, 2, lat_count // 2, 2), AXES)
    lon, lat = AXES[:2], AXES[2:]
    return jax.shard_map(
        functools.partial(body, lon_count, lat_count),
        mesh=fine,
        in_specs=(
            P(None, lat, lon, None),
            P(None, lat, lon, None),
            P(lat, lon),
            P(),
            P(),
            P(),
            P(),
            P(),
            P(lat, None, None, None, None),
        ),
        out_specs=(P(None, lat, lon, None), P(), P(), P(), P(), P()),
        check_vma=False,
    )
```

```python
import functools
import math

import jax
import jax.numpy as jnp
import numpy as np
from jax import lax
from jax.experimental import pallas as pl
from jax.experimental.pallas import tpu as pltpu
from jax.sharding import PartitionSpec as P

Z = 4
WZ = 2
WH = 6
WW = 12
C = 192
HEADS = 6
HEAD = 32
FF = 768
HZ, HH, HW = WZ // 2, WH // 2, WW // 2
TOK = WZ * WH * WW
PLACES = WZ * WH
RELW = 2 * WW - 1
STRIP = -(-RELW * PLACES // 128) * 128

mask_fill = -10000.0
norm_eps = 1e-05
log2e = 1.4426950408889634
root_half = 0.7071067811865476
inv_root_tau = 0.3989422804014327
score_scale = HEAD**-0.5

f32 = jnp.float32
bf16 = jnp.bfloat16
MIB = 1 << 20

QUADS = 4
PART = C // (2 * QUADS)
CHUNK = 3 * PART
EXTRA = 8
FULL = CHUNK + EXTRA


def mm(a, b):
    return lax.dot_general(a, b, (((1,), (0,)), ((), ())), preferred_element_type=f32)


def mm_nt(a, b):
    return lax.dot_general(a, b, (((1,), (1,)), ((), ())), preferred_element_type=f32)


def mm_tn(a, b):
    return lax.dot_general(a, b, (((0,), (0,)), ((), ())), preferred_element_type=f32)


def unit_norm(values):
    average = jnp.mean(values, -1, keepdims=True)
    centred = values - average
    variance = jnp.mean(centred * centred, -1, keepdims=True)
    spread = lax.rsqrt(variance + norm_eps)
    return centred * spread, spread


def norm_back(upstream, unit, spread):
    first = jnp.mean(upstream, -1, keepdims=True)
    second = jnp.mean(upstream * unit, -1, keepdims=True)
    return spread * (upstream - first - unit * second)


def piece_rows(rows, cols):
    home = np.arange(Z * rows * cols).reshape(Z, rows, cols)
    top, low = slice(0, rows - HH), slice(rows - HH, rows)
    west, east = slice(0, cols - HW), slice(cols - HW, cols)
    parts = [home[:, top, west], home[:, low, west], home[:, top, east], home[:, low, east]]
    return [part.reshape(-1) for part in parts]


def window_rows(rows, cols):
    sizes = [part.size for part in piece_rows(rows, cols)]
    starts = np.cumsum([0] + sizes)
    own, north, side, corner = [np.arange(starts[k], starts[k + 1]) for k in range(4)]
    frame = np.zeros((Z, rows, cols), np.int64)
    frame[:, HH:, HW:] = own.reshape(Z, rows - HH, cols - HW)
    frame[:, :HH, HW:] = north.reshape(Z, HH, cols - HW)
    frame[:, HH:, :HW] = side.reshape(Z, rows - HH, HW)
    frame[:, :HH, :HW] = corner.reshape(Z, HH, HW)
    frame = np.roll(frame, HZ, axis=0)
    frame = frame.reshape(Z // WZ, WZ, rows // WH, WH, cols // WW, WW)
    return frame.transpose(0, 2, 4, 5, 1, 3).reshape(-1)


def spots(places):
    return jnp.asarray(np.argsort(places).astype(np.int32)[None])


def one_hot(spot_ref):
    count = spot_ref.shape[1]
    rows = lax.broadcasted_iota(jnp.int32, (count, count), 0)
    return (rows == spot_ref[...]).astype(f32).astype(bf16)


def vmem(count):
    return [pl.BlockSpec(memory_space=pltpu.VMEM)] * count


def shape(dims, dtype):
    return jax.ShapeDtypeStruct(dims, dtype)


def cost(flops, moved):
    return pl.CostEstimate(flops=flops, bytes_accessed=moved, transcendentals=0)


def land_column(land_ref, rows, cols):
    eye = (
        lax.broadcasted_iota(jnp.int32, (cols, cols), 0)
        == lax.broadcasted_iota(jnp.int32, (cols, cols), 1)
    ).astype(f32)
    land = land_ref[...].astype(f32)
    parts = [jnp.sum(eye * land[i : i + 1, :], -1, keepdims=True) for i in range(rows)]
    return jnp.concatenate(parts, axis=0)


def pack_kernel(rows, cols, *refs):
    sources, outs, (tokens_ref, cot_ref, land_ref, vec_ref, perm_ref, sems) = refs[:5], refs[5:-6], refs[-6:]
    copies = [
        pltpu.make_async_copy(source, target, sems.at[n])
        for n, (source, target) in enumerate(zip(sources, (tokens_ref, cot_ref, land_ref, vec_ref, perm_ref)))
    ]
    for copy in copies:
        copy.start()
    for copy in copies:
        copy.wait()
    column = land_column(land_ref, rows, cols)
    added = column * vec_ref[...]
    added = jnp.concatenate([added] * Z, axis=0)
    embedded = (tokens_ref[...].astype(f32) + added).astype(bf16)
    perm = one_hot(perm_ref)
    left = mm(perm, embedded)
    right = mm(perm, cot_ref[...])
    packed = jnp.concatenate([left, right], axis=1)
    start = 0
    for out in outs:
        out[...] = packed[start : start + out.shape[0]].astype(bf16)
        start += out.shape[0]


def pack(tokens, cotangent, land_sea, vector, rows, cols):
    parts = piece_rows(rows, cols)
    perm = spots(np.concatenate(parts))
    count = Z * rows * cols
    return pl.pallas_call(
        functools.partial(pack_kernel, rows, cols),
        out_shape=[shape((part.size, 2 * C), bf16) for part in parts],
        in_specs=[pl.BlockSpec(memory_space=pltpu.HBM)] * 5,
        out_specs=vmem(4),
        scratch_shapes=[
            pltpu.VMEM((count, C), bf16),
            pltpu.VMEM((count, C), bf16),
            pltpu.VMEM((rows, cols), jnp.int32),
            pltpu.VMEM((1, C), f32),
            pltpu.VMEM((1, count), jnp.int32),
            pltpu.SemaphoreType.DMA((5,)),
        ],
        cost_estimate=cost(4 * count * count * C, 4 * MIB),
        name="pack",
    )(tokens.reshape(count, C), cotangent.reshape(count, C), land_sea, vector.reshape(1, C), perm)


def floor_div(values, divisor):
    return (values * (65536 // divisor + 1)) >> 16


def bias_kernel(levels, table_ref, out_ref, *wide_refs):
    groups = levels * HEADS
    pairs = PLACES * PLACES
    row = lax.broadcasted_iota(jnp.int32, (HEADS * RELW, HEADS * STRIP), 0)
    lane = lax.broadcasted_iota(jnp.int32, (HEADS * RELW, HEADS * STRIP), 1)
    head = floor_div(row, RELW)
    ahead = lane - (head * STRIP + (RELW - 1 - (row - head * RELW)) * PLACES)
    onehot = ((ahead >= 0) & (ahead < PLACES)).astype(f32).astype(bf16)
    for level in range(levels):
        table = table_ref[:, level, :].T
        high = table.astype(bf16)
        rest = table - high.astype(f32)
        wide = mm(high, onehot) + mm(rest.astype(bf16), onehot)
        for head in range(HEADS):
            for n, wide_ref in enumerate(wide_refs):
                start = head * STRIP + n * 128
                wide_ref[(level * HEADS + head) * pairs : (level * HEADS + head + 1) * pairs, :] = wide[:, start : start + 128]
    strips = groups * PLACES
    parts = []
    for n, wide_ref in enumerate(wide_refs):
        place = lax.broadcasted_iota(jnp.int32, (strips, 128), 1) + n * 128
        place = place - floor_div(place, PLACES) * PLACES
        part = jnp.zeros((strips, 128), f32)
        for p in range(PLACES):
            part = jnp.where(place == p, wide_ref[pl.ds(p, strips, stride=PLACES), :], part)
        parts.append(part)
    strip = jnp.concatenate(parts, axis=1)
    row = lax.broadcasted_iota(jnp.int32, (strips, STRIP), 0)
    lane = lax.broadcasted_iota(jnp.int32, (strips, STRIP), 1)
    own, other = row - floor_div(row, PLACES) * PLACES, lane - floor_div(lane, PLACES) * PLACES
    low_own, low_other = (own < HZ * WH).astype(jnp.int32), (other < HZ * WH).astype(jnp.int32)
    first_level = (row < HEADS * PLACES).astype(jnp.int32)
    own_lat, other_lat = own + WH * low_own, other + WH * low_other
    north_own, north_other = (own_lat < WH + HH).astype(jnp.int32), (other_lat < WH + HH).astype(jnp.int32)
    pole = (lax.axis_index("y") + lax.axis_index("core") == 0).astype(jnp.int32)
    differs = first_level * (low_own ^ low_other) + pole * (north_own ^ north_other)
    strip = jnp.where(differs > 0, strip + mask_fill, strip) * log2e
    for w in range(WW):
        start = (WW - 1 - w) * PLACES
        part = strip[:, start : start + TOK]
        for g in range(groups):
            out_ref[g, w * PLACES : (w + 1) * PLACES, :] = part[g * PLACES : (g + 1) * PLACES, :]


def expand_bias(table):
    levels = table.shape[1]
    groups = levels * HEADS
    pairs = PLACES * PLACES
    flat = table[0].transpose(1, 3, 0, 2).reshape(HEADS * RELW, levels, pairs)
    return pl.pallas_call(
        functools.partial(bias_kernel, levels),
        out_shape=shape((groups, TOK, TOK), f32),
        in_specs=vmem(1),
        out_specs=vmem(1)[0],
        scratch_shapes=[pltpu.VMEM((groups * pairs, 128), f32)] * (STRIP // 128),
        compiler_params=pltpu.CompilerParams(vmem_limit_bytes=28 * MIB),
        cost_estimate=cost(10**9, 8 * MIB),
        name="bias",
    )(flat)


def head_masks(count):
    lane = lax.broadcasted_iota(jnp.int32, (count, C), 1)
    return [((lane >= h * HEAD) & (lane < (h + 1) * HEAD)).astype(f32) for h in range(HEADS)]


def stacked(values, masks):
    return jnp.concatenate([values * mask for mask in masks], axis=0)


def head_sum(values, masks):
    total = values[:TOK] * masks[0]
    for h in range(1, HEADS):
        total = total + values[h * TOK : (h + 1) * TOK] * masks[h]
    return total


def position():
    return lax.axis_index("core"), lax.axis_index("y") * 2 + lax.axis_index("x"), lax.axis_index("deep")


def chunk_rows(block):
    return pl.ds(pl.multiple_of(block * PART, PART), PART)


def split_parts(total_refs, keep_ref, send_ref):
    core, chip, _ = position()
    for out, side in ((keep_ref, core), (send_ref, 1 - core)):
        parts = []
        for g in range(QUADS):
            rows = chunk_rows(side * QUADS + jnp.bitwise_xor(chip, g))
            parts += [ref[rows, :] for ref in total_refs]
        out[...] = jnp.concatenate(parts, axis=0).astype(out.dtype)


def forward_kernel(
    windows, lon_windows,
    own_ref, north_ref, side_ref, corner_ref, perm_ref, bias_ref, triple_ref, project_ref, up_ref, down_ref,
    q_ref, k_ref, v_ref, p_ref, mixed_ref, normed_ref, unit_ref, spread_ref, gsum_ref, up_grad_ref, down_grad_ref,
    branch_ref, cot_ref, emb_ref,
):
    pieces = [ref[...].astype(f32) for ref in (own_ref, north_ref, side_ref, corner_ref)]
    pieces = jnp.concatenate(pieces, axis=0).astype(bf16)
    ordered = mm(one_hot(perm_ref), pieces)
    emb = ordered[:, :C]
    emb_ref[...] = emb
    cot_ref[...] = ordered[:, C:].astype(bf16)
    unit, spread = unit_norm(emb)
    unit_ref[...] = unit
    spread_ref[...] = spread
    normed = unit.astype(bf16)
    normed_ref[...] = normed
    packed = mm(normed, triple_ref[...])
    q_ref[...] = packed[:, :C].astype(bf16)
    k_ref[...] = packed[:, C : 2 * C].astype(bf16)
    v_ref[...] = packed[:, 2 * C :].astype(bf16)
    masks = head_masks(TOK)
    masks_b = [mask.astype(bf16) for mask in masks]

    def window_step(w, carry):
        rows = pl.ds(pl.multiple_of(w * TOK, TOK), TOK)
        level = w // lon_windows
        scores = mm_nt(stacked(q_ref[rows, :], masks_b), k_ref[rows, :])
        bias = bias_ref[pl.ds(level * HEADS, HEADS)].reshape(HEADS * TOK, TOK)
        raised = jnp.exp2(scores * (score_scale * log2e) + bias)
        probs = raised * (1.0 / jnp.sum(raised, -1, keepdims=True))
        probs_b = probs.astype(bf16)
        p_ref[pl.ds(w * HEADS, HEADS)] = probs_b.reshape(HEADS, TOK, TOK)
        mixed = head_sum(mm(probs_b, v_ref[rows, :]), masks).astype(bf16)
        mixed_ref[rows, :] = mixed
        branch_ref[rows, :] = mm(mixed, project_ref[...])
        return carry

    lax.fori_loop(0, windows, window_step, 0, unroll=True)

    attended = branch_ref[...].astype(bf16).astype(f32)
    unit2, spread2 = unit_norm(emb_ref[...] + attended)
    normed2 = unit2.astype(bf16)
    cot = cot_ref[...]
    back = jnp.zeros(unit2.shape, f32)
    block = 256
    for start in range(0, FF, block):
        cols = slice(start, start + block)
        up_part = up_ref[:, cols]
        pre = mm(normed2, up_part)
        upstream = mm(cot, down_ref[:, cols])
        phi = 0.5 * (1.0 + lax.erf(pre * root_half))
        activated = (pre * phi).astype(bf16)
        slope = phi + pre * inv_root_tau * jnp.exp2(pre * pre * (-0.5 * log2e))
        hidden = (upstream * slope).astype(bf16)
        up_grad_ref[:, cols] = mm_tn(normed2, hidden)
        down_grad_ref[:, cols] = mm_tn(cot, activated)
        back = back + mm_nt(hidden, up_part)
    gsum_ref[...] = cot.astype(f32) + norm_back(back, unit2, spread2)


def windows_back_kernel(windows, q_ref, k_ref, v_ref, p_ref, gsum_ref, project_ref, gq_ref, gk_ref, gv_ref):
    masks = head_masks(TOK)
    masks_b = [mask.astype(bf16) for mask in masks]

    def window_step(w, carry):
        rows = pl.ds(pl.multiple_of(w * TOK, TOK), TOK)
        grad = gsum_ref[rows, :].astype(bf16)
        grad_mixed = mm_nt(grad, project_ref[...])
        grad_mixed_b = grad_mixed.astype(bf16)
        probs_b = p_ref[pl.ds(w * HEADS, HEADS)].reshape(HEADS * TOK, TOK)
        probs = probs_b.astype(f32)
        grad_probs = mm_nt(stacked(grad_mixed_b, masks_b), v_ref[rows, :])
        inner = jnp.sum(grad_probs * probs, -1, keepdims=True)
        scaled = (probs * (grad_probs - inner) * score_scale).astype(bf16)
        grad_q = head_sum(mm(scaled, k_ref[rows, :]), masks)
        grad_mixed_t = grad_mixed_b.astype(f32).T.astype(bf16)
        query_t = q_ref[rows, :].astype(f32).T.astype(bf16)
        grad_k, grad_v = [], []
        for h in range(HEADS):
            spot = slice(h * HEAD, (h + 1) * HEAD)
            span = slice(h * TOK, (h + 1) * TOK)
            grad_k.append(mm(query_t[spot], scaled[span]))
            grad_v.append(mm(grad_mixed_t[spot], probs_b[span]))
        gq_ref[rows, :] = grad_q.astype(bf16)
        gk_ref[rows, :] = jnp.concatenate(grad_k, axis=0).T.astype(bf16)
        gv_ref[rows, :] = jnp.concatenate(grad_v, axis=0).T.astype(bf16)
        return carry

    lax.fori_loop(0, windows, window_step, 0, unroll=True)


def halved(rows):
    return -(-rows // 16) * 8


def tokens_back_kernel(
    sizes, gq_ref, gk_ref, gv_ref, mixed_ref, normed_ref, unit_ref, spread_ref, gsum_ref, perm_ref, triple_ref,
    up_grad_ref, down_grad_ref, *rest,
):
    outs, (keep_ref, send_ref, total_ref) = rest[: len(sizes)], rest[len(sizes) :]
    normed = normed_ref[...]
    triple = triple_ref[...]
    grad_normed = jnp.zeros(unit_ref.shape, f32)
    parts = []
    for n, ref in enumerate((gq_ref, gk_ref, gv_ref)):
        grad = ref[...]
        grad_normed = grad_normed + mm_nt(grad, triple[:, n * C : (n + 1) * C])
        parts.append(mm_tn(normed, grad))
    parts.append(mm_tn(mixed_ref[...], gsum_ref[...].astype(bf16)))
    total_ref[...] = jnp.concatenate(parts, axis=1)
    grad_normed = grad_normed.astype(bf16).astype(f32)
    grad_tokens = gsum_ref[...] + norm_back(grad_normed, unit_ref[...], spread_ref[...])
    pieces = mm(one_hot(perm_ref), grad_tokens.astype(bf16))
    start = 0
    for size, out in zip(sizes, outs):
        piece = pieces[start : start + size]
        half = halved(size)
        second = jnp.concatenate([piece[half:], jnp.zeros((2 * half - size, C), f32)], axis=0)
        out[...] = jnp.concatenate([piece[:half], second], axis=1).astype(bf16)
        start += size
    split_parts((up_grad_ref, down_grad_ref, total_ref), keep_ref, send_ref)


def block_kernel(windows, lon_windows, sizes, *refs):
    ins, refs = refs[:11], refs[11:]
    pieces, (perm_ref, back_perm_ref, bias_ref, triple_ref, project_ref, up_ref, down_ref) = ins[:4], ins[4:]
    outs, refs = refs[: len(sizes) + 2], refs[len(sizes) + 2 :]
    q, k, v, p, mixed, normed, unit, spread, gsum, up_grad, down_grad, branch, cot, emb, gq, gk, gv, total = refs
    forward_kernel(
        windows, lon_windows, *pieces, perm_ref, bias_ref, triple_ref, project_ref, up_ref, down_ref,
        q, k, v, p, mixed, normed, unit, spread, gsum, up_grad, down_grad, branch, cot, emb,
    )
    windows_back_kernel(windows, q, k, v, p, gsum, project_ref, gq, gk, gv)
    tokens_back_kernel(
        sizes, gq, gk, gv, mixed, normed, unit, spread, gsum, back_perm_ref, triple_ref, up_grad, down_grad, *outs, total
    )


def block(pieces, perm, back_perm, bias, triple, project, up, down, lon_windows, sizes):
    count = perm.shape[1]
    windows = count // TOK
    out_shape = [shape((halved(size), 2 * C), bf16) for size in sizes] + [
        shape((QUADS * CHUNK, FF), f32),
        shape((QUADS * CHUNK, FF), bf16),
    ]
    rows = [pltpu.VMEM((count, C), dtype) for dtype in (bf16, f32)]
    return pl.pallas_call(
        functools.partial(block_kernel, windows, lon_windows, sizes),
        out_shape=out_shape,
        in_specs=vmem(11),
        out_specs=vmem(len(out_shape)),
        scratch_shapes=rows[:1] * 3
        + [pltpu.VMEM((windows * HEADS, TOK, TOK), bf16)]
        + rows[:1] * 2
        + [rows[1], pltpu.VMEM((count, 1), f32), rows[1]]
        + [pltpu.VMEM((C, FF), f32)] * 2
        + [rows[1], rows[0], rows[1]]
        + rows[:1] * 3
        + [pltpu.VMEM((C, FF), f32)],
        compiler_params=pltpu.CompilerParams(vmem_limit_bytes=32 * MIB),
        cost_estimate=cost(8 * 10**9, 16 * MIB),
        name="block",
    )(*pieces, perm, back_perm, bias, triple, project, up, down)


def home_kernel(sizes, rows, cols, own_ref, north_ref, side_ref, corner_ref, perm_ref, land_ref, out_ref, sum_ref):
    pieces = []
    for size, ref in zip(sizes, (own_ref, north_ref, side_ref, corner_ref)):
        wide = ref[...].astype(f32)
        pieces += [wide[:, :C], wide[: size - wide.shape[0], C:]]
    pieces = jnp.concatenate(pieces, axis=0).astype(bf16)
    grads = mm(one_hot(perm_ref), pieces)
    out_ref[...] = grads.astype(bf16)
    column = jnp.concatenate([land_column(land_ref, rows, cols)] * Z, axis=0)
    sum_ref[...] = jnp.sum(grads * column, 0, keepdims=True)


def to_home(pieces, land_sea, sizes, rows, cols):
    count = Z * rows * cols
    perm = spots(np.argsort(np.concatenate(piece_rows(rows, cols))))
    return pl.pallas_call(
        functools.partial(home_kernel, sizes, rows, cols),
        out_shape=[shape((count, C), bf16), shape((1, C), f32)],
        in_specs=vmem(6),
        out_specs=vmem(2),
        compiler_params=pltpu.CompilerParams(vmem_limit_bytes=32 * MIB),
        cost_estimate=cost(2 * count * count * C, 4 * MIB),
        name="to_home",
    )(*pieces, perm, land_sea)


def core_add_kernel(keep_ref, got_ref, *refs):
    own_ref, outs = refs[-QUADS], refs[1 - QUADS :]
    total = keep_ref[...] + got_ref[...].astype(f32)
    own_ref[...] = total[:CHUNK]
    for e, out in enumerate(outs, 1):
        out[...] = total[e * CHUNK : (e + 1) * CHUNK].astype(bf16)


def chip_add_kernel(keep_ref, *refs):
    gots, (land_ref, out_ref) = refs[:-2], refs[-2:]
    total = keep_ref[...]
    for ref in gots:
        total = total + ref[...].astype(f32)
    land = jnp.concatenate([land_ref[...], jnp.zeros((1, FF - C), f32)], axis=1)
    out_ref[...] = jnp.concatenate([total, land, jnp.zeros((EXTRA - 1, FF), f32)], axis=0).astype(bf16)


def add_kernel(one_ref, two_ref, out_ref):
    out_ref[...] = (one_ref[...].astype(f32) + two_ref[...].astype(f32)).astype(bf16)


def join_kernel(*refs):
    refs[-1][...] = jnp.concatenate([ref[...] for ref in refs[:-1]], axis=0)


def small_call(kernel, out_shape, args, name, after=(), scratch=()):
    return pl.pallas_call(
        kernel,
        out_shape=out_shape,
        in_specs=vmem(len(args)) + [pl.BlockSpec(memory_space=pl.ANY)] * len(after),
        out_specs=vmem(len(out_shape)),
        scratch_shapes=scratch,
        compiler_params=pltpu.CompilerParams(vmem_limit_bytes=16 * MIB),
        cost_estimate=cost(10**6, 2 * MIB),
        name=name,
    )(*args, *after)


def finish_kernel(far, chunks_ref, *refs):
    if far:
        before_ref, refs = refs[0], refs[5:]
    outs, land_ref, (up_ref, down_ref, triple_ref, project_ref, lands_ref, sum_ref, sems) = refs[:4], refs[4], refs[5:]
    core, chip, _ = position()
    side = 1 - core if far else core
    for g in range(QUADS):
        chunk = chunks_ref[g * FULL : (g + 1) * FULL, :].astype(f32)
        block = jnp.bitwise_xor(chip, g)
        rows = chunk_rows(block)
        up_ref[rows, :] = chunk[:PART]
        down_ref[rows, :] = chunk[PART : 2 * PART]
        triple_ref[rows, :] = chunk[2 * PART : CHUNK, : 3 * C]
        project_ref[rows, :] = chunk[2 * PART : CHUNK, 3 * C :]
        lands_ref[pl.ds(pl.multiple_of(block * EXTRA, EXTRA), EXTRA), :] = chunk[CHUNK:, :C]
    copies = []
    for n, (source, out) in enumerate(zip((triple_ref, project_ref, up_ref, down_ref), outs)):
        rows = pl.ds(pl.multiple_of(side * QUADS * PART, 8), QUADS * PART)
        copies.append(pltpu.make_async_copy(source, out.at[rows, :], sems.at[n]))
    for copy in copies:
        copy.start()
    land = jnp.sum(lands_ref[...], 0, keepdims=True)
    if far:
        sum_ref[...] = land + before_ref[...]
        copies.append(pltpu.make_async_copy(sum_ref, land_ref, sems.at[4]))
        copies[-1].start()
    else:
        land_ref[...] = land
    for copy in copies:
        copy.wait()


def finish(chunks, before=()):
    rows = QUADS * PART
    widths = (3 * C, C, FF, FF)
    hbm = [pl.BlockSpec(memory_space=pltpu.HBM)] * 4
    land, weights = before[4:], before[:4]
    return pl.pallas_call(
        functools.partial(finish_kernel, bool(before)),
        out_shape=[shape((C, width), f32) for width in widths] + [shape((1, C), f32)],
        in_specs=vmem(1 + len(land)) + hbm[: len(weights)],
        out_specs=hbm + (hbm[:1] if before else vmem(1)),
        scratch_shapes=[
            pltpu.VMEM((rows, FF), f32),
            pltpu.VMEM((rows, FF), f32),
            pltpu.VMEM((rows, 3 * C), f32),
            pltpu.VMEM((rows, C), f32),
            pltpu.VMEM((QUADS * EXTRA, C), f32),
            pltpu.VMEM((1, C), f32),
            pltpu.SemaphoreType.DMA((5,)),
        ],
        input_output_aliases={2 + n: n for n in range(len(weights))},
        compiler_params=pltpu.CompilerParams(vmem_limit_bytes=16 * MIB),
        cost_estimate=cost(10**6, 2 * MIB),
        name="finish_far" if before else "finish_own",
    )(chunks, *land, *weights)


def reduce_all(keep, sent, land, shift, lon_count, after):
    core_move = lambda lon, lat: (lon, lat ^ 1)
    chip_move = lambda e: lambda lon, lat: (lon ^ (e & 1), lat ^ (2 * (e >> 1)))
    deep_move = lambda e: lambda lon, lat: (lon ^ (2 * e), lat)

    def one(rows):
        return [shape((rows, FF), bf16)]

    got = shift(sent, move=core_move)
    parts = [shape((CHUNK, FF), f32)] + one(CHUNK) * (QUADS - 1)
    own, *parts = small_call(core_add_kernel, parts, (keep, got), "core_add", after=after)
    gots = [shift(value, move=chip_move(e)) for e, value in enumerate(parts, 1)]
    (total,) = small_call(chip_add_kernel, one(FULL), (own, *gots, land), "chip_add")
    reach = 1
    while reach < lon_count // 2:
        got = shift(total, move=deep_move(reach))
        reach *= 2
        (total,) = small_call(add_kernel, one(FULL), (total, got), "deep_add")
    near = [total] + [shift(total, move=chip_move(e)) for e in range(1, QUADS)]
    (total,) = small_call(join_kernel, one(QUADS * FULL), near, "join")
    got = shift(total, move=core_move)
    return finish(got, finish(total))


AXES = ("deep", "x", "y", "core")


def send(value, lon_count, lat_count, move):
    pairs = []
    for lon in range(lon_count):
        for lat in range(lat_count):
            to_lon, to_lat = move(lon, lat)
            pairs.append((lon * lat_count + lat, (to_lon % lon_count) * lat_count + to_lat % lat_count))
    return lax.ppermute(value, AXES, pairs)


def body(
    lon_count, lat_count,
    tokens, cotangent, land_sea, land_vector, triple_weight, project_weight, up_weight, down_weight, earth_bias,
):
    levels, rows, cols, features = tokens.shape
    shift = functools.partial(send, lon_count=lon_count, lat_count=lat_count)
    lon_windows = cols // WW

    own, north, side, corner = pack(tokens, cotangent, land_sea, land_vector, rows, cols)
    north = shift(north, move=lambda lon, lat: (lon, lat + 1))
    side = shift(side, move=lambda lon, lat: (lon + 1, lat))
    corner = shift(corner, move=lambda lon, lat: (lon + 1, lat + 1))
    bias = expand_bias(earth_bias)

    places = window_rows(rows, cols)
    sizes = [part.size for part in piece_rows(rows, cols)]
    pieces = (own, north, side, corner)
    own, north, side, corner, keep, sent = block(
        pieces, spots(places), spots(np.argsort(places)), bias,
        triple_weight, project_weight, up_weight, down_weight.T, lon_windows, sizes,
    )
    north = shift(north, move=lambda lon, lat: (lon, lat - 1))
    side = shift(side, move=lambda lon, lat: (lon - 1, lat))
    corner = shift(corner, move=lambda lon, lat: (lon - 1, lat - 1))
    after = (north, side, corner)
    grad_tokens, land = to_home((own, north, side, corner), land_sea, sizes, rows, cols)
    triple, project, up, down, land = reduce_all(keep, sent, land, shift, lon_count, after)
    return grad_tokens.reshape(tokens.shape), triple, project, up, down.T, land.reshape(features)


def solution(mesh):
    lon_count, lat_count = mesh.shape["lon"], mesh.shape["lat"]
    fine = jax.sharding.Mesh(mesh.devices.reshape(lon_count // 2, 2, lat_count // 2, 2), AXES)
    lon, lat = AXES[:2], AXES[2:]
    return jax.shard_map(
        functools.partial(body, lon_count, lat_count),
        mesh=fine,
        in_specs=(
            P(None, lat, lon, None),
            P(None, lat, lon, None),
            P(lat, lon),
            P(),
            P(),
            P(),
            P(),
            P(),
            P(lat, None, None, None, None),
        ),
        out_specs=(P(None, lat, lon, None), P(), P(), P(), P(), P()),
        check_vma=False,
    )
```

```python
import functools
import math

import jax
import jax.numpy as jnp
import numpy as np
from jax import lax
from jax.experimental import pallas as pl
from jax.experimental.pallas import tpu as pltpu
from jax.sharding import PartitionSpec as P

Z = 4
WZ = 2
WH = 6
WW = 12
C = 192
HEADS = 6
HEAD = 32
FF = 768
HZ, HH, HW = WZ // 2, WH // 2, WW // 2
TOK = WZ * WH * WW
PLACES = WZ * WH
RELW = 2 * WW - 1
STRIP = -(-RELW * PLACES // 128) * 128

mask_fill = -10000.0
norm_eps = 1e-05
log2e = 1.4426950408889634
root_half = 0.7071067811865476
inv_root_tau = 0.3989422804014327
score_scale = HEAD**-0.5

f32 = jnp.float32
bf16 = jnp.bfloat16
MIB = 1 << 20

QUADS = 4
PART = C // (2 * QUADS)
CHUNK = 3 * PART
EXTRA = 8
FULL = CHUNK + EXTRA


def mm(a, b):
    return lax.dot_general(a, b, (((1,), (0,)), ((), ())), preferred_element_type=f32)


def mm_nt(a, b):
    return lax.dot_general(a, b, (((1,), (1,)), ((), ())), preferred_element_type=f32)


def mm_tn(a, b):
    return lax.dot_general(a, b, (((0,), (0,)), ((), ())), preferred_element_type=f32)


def unit_norm(values):
    average = jnp.mean(values, -1, keepdims=True)
    centred = values - average
    variance = jnp.mean(centred * centred, -1, keepdims=True)
    spread = lax.rsqrt(variance + norm_eps)
    return centred * spread, spread


def norm_back(upstream, unit, spread):
    first = jnp.mean(upstream, -1, keepdims=True)
    second = jnp.mean(upstream * unit, -1, keepdims=True)
    return spread * (upstream - first - unit * second)


def piece_rows(rows, cols):
    home = np.arange(Z * rows * cols).reshape(Z, rows, cols)
    top, low = slice(0, rows - HH), slice(rows - HH, rows)
    west, east = slice(0, cols - HW), slice(cols - HW, cols)
    parts = [home[:, top, west], home[:, low, west], home[:, top, east], home[:, low, east]]
    return [part.reshape(-1) for part in parts]


def window_rows(rows, cols):
    sizes = [part.size for part in piece_rows(rows, cols)]
    starts = np.cumsum([0] + sizes)
    own, north, side, corner = [np.arange(starts[k], starts[k + 1]) for k in range(4)]
    frame = np.zeros((Z, rows, cols), np.int64)
    frame[:, HH:, HW:] = own.reshape(Z, rows - HH, cols - HW)
    frame[:, :HH, HW:] = north.reshape(Z, HH, cols - HW)
    frame[:, HH:, :HW] = side.reshape(Z, rows - HH, HW)
    frame[:, :HH, :HW] = corner.reshape(Z, HH, HW)
    frame = np.roll(frame, HZ, axis=0)
    frame = frame.reshape(Z // WZ, WZ, rows // WH, WH, cols // WW, WW)
    return frame.transpose(0, 2, 4, 5, 1, 3).reshape(-1)


def spots(places):
    return jnp.asarray(np.argsort(places).astype(np.int32)[None])


def one_hot(spot_ref):
    count = spot_ref.shape[1]
    rows = lax.broadcasted_iota(jnp.int32, (count, count), 0)
    return (rows == spot_ref[...]).astype(f32).astype(bf16)


def vmem(count):
    return [pl.BlockSpec(memory_space=pltpu.VMEM)] * count


def shape(dims, dtype):
    return jax.ShapeDtypeStruct(dims, dtype)


def cost(flops, moved):
    return pl.CostEstimate(flops=flops, bytes_accessed=moved, transcendentals=0)


def land_column(land_ref, rows, cols):
    eye = (
        lax.broadcasted_iota(jnp.int32, (cols, cols), 0)
        == lax.broadcasted_iota(jnp.int32, (cols, cols), 1)
    ).astype(f32)
    land = land_ref[...].astype(f32)
    parts = [jnp.sum(eye * land[i : i + 1, :], -1, keepdims=True) for i in range(rows)]
    return jnp.concatenate(parts, axis=0)


def pack_kernel(rows, cols, *refs):
    sources, outs, (tokens_ref, cot_ref, land_ref, vec_ref, perm_ref, sems) = refs[:5], refs[5:-6], refs[-6:]
    copies = [
        pltpu.make_async_copy(source, target, sems.at[n])
        for n, (source, target) in enumerate(zip(sources, (tokens_ref, cot_ref, land_ref, vec_ref, perm_ref)))
    ]
    for copy in copies:
        copy.start()
    for copy in copies:
        copy.wait()
    column = land_column(land_ref, rows, cols)
    added = column * vec_ref[...]
    added = jnp.concatenate([added] * Z, axis=0)
    embedded = (tokens_ref[...].astype(f32) + added).astype(bf16)
    perm = one_hot(perm_ref)
    left = mm(perm, embedded)
    right = mm(perm, cot_ref[...])
    packed = jnp.concatenate([left, right], axis=1)
    column = jnp.concatenate([column] * Z, axis=0)
    flags = mm(perm, jnp.broadcast_to(column, (column.shape[0], 128)).astype(bf16))
    start = 0
    for out in outs:
        count = out.shape[0] - EXTRA
        eye = lax.broadcasted_iota(jnp.int32, (count, count), 0) == lax.broadcasted_iota(jnp.int32, (count, count), 1)
        row = jnp.sum(jnp.where(eye, flags[start : start + count, 0:1], 0.0), 0, keepdims=True)
        row = jnp.concatenate([row, jnp.zeros((1, 2 * C - count), f32)], axis=1)
        row = jnp.broadcast_to(row, (EXTRA, 2 * C))
        out[...] = jnp.concatenate([packed[start : start + count], row], axis=0).astype(bf16)
        start += count


def pack(tokens, cotangent, land_sea, vector, rows, cols):
    parts = piece_rows(rows, cols)
    perm = spots(np.concatenate(parts))
    count = Z * rows * cols
    return pl.pallas_call(
        functools.partial(pack_kernel, rows, cols),
        out_shape=[shape((part.size + EXTRA, 2 * C), bf16) for part in parts],
        in_specs=[pl.BlockSpec(memory_space=pltpu.HBM)] * 5,
        out_specs=vmem(4),
        scratch_shapes=[
            pltpu.VMEM((count, C), bf16),
            pltpu.VMEM((count, C), bf16),
            pltpu.VMEM((rows, cols), jnp.int32),
            pltpu.VMEM((1, C), f32),
            pltpu.VMEM((1, count), jnp.int32),
            pltpu.SemaphoreType.DMA((5,)),
        ],
        cost_estimate=cost(4 * count * count * C, 4 * MIB),
        name="pack",
    )(tokens.reshape(count, C), cotangent.reshape(count, C), land_sea, vector.reshape(1, C), perm)


def floor_div(values, divisor):
    return (values * (65536 // divisor + 1)) >> 16


def bias_kernel(levels, table_ref, out_ref, *wide_refs):
    groups = levels * HEADS
    pairs = PLACES * PLACES
    row = lax.broadcasted_iota(jnp.int32, (HEADS * RELW, HEADS * STRIP), 0)
    lane = lax.broadcasted_iota(jnp.int32, (HEADS * RELW, HEADS * STRIP), 1)
    head = floor_div(row, RELW)
    ahead = lane - (head * STRIP + (RELW - 1 - (row - head * RELW)) * PLACES)
    onehot = ((ahead >= 0) & (ahead < PLACES)).astype(f32).astype(bf16)
    for level in range(levels):
        table = table_ref[:, level, :].T
        high = table.astype(bf16)
        rest = table - high.astype(f32)
        wide = mm(high, onehot) + mm(rest.astype(bf16), onehot)
        for head in range(HEADS):
            for n, wide_ref in enumerate(wide_refs):
                start = head * STRIP + n * 128
                wide_ref[(level * HEADS + head) * pairs : (level * HEADS + head + 1) * pairs, :] = wide[:, start : start + 128]
    strips = groups * PLACES
    parts = []
    for n, wide_ref in enumerate(wide_refs):
        place = lax.broadcasted_iota(jnp.int32, (strips, 128), 1) + n * 128
        place = place - floor_div(place, PLACES) * PLACES
        part = jnp.zeros((strips, 128), f32)
        for p in range(PLACES):
            part = jnp.where(place == p, wide_ref[pl.ds(p, strips, stride=PLACES), :], part)
        parts.append(part)
    strip = jnp.concatenate(parts, axis=1)
    row = lax.broadcasted_iota(jnp.int32, (strips, STRIP), 0)
    lane = lax.broadcasted_iota(jnp.int32, (strips, STRIP), 1)
    own, other = row - floor_div(row, PLACES) * PLACES, lane - floor_div(lane, PLACES) * PLACES
    low_own, low_other = (own < HZ * WH).astype(jnp.int32), (other < HZ * WH).astype(jnp.int32)
    first_level = (row < HEADS * PLACES).astype(jnp.int32)
    own_lat, other_lat = own + WH * low_own, other + WH * low_other
    north_own, north_other = (own_lat < WH + HH).astype(jnp.int32), (other_lat < WH + HH).astype(jnp.int32)
    pole = (lax.axis_index("y") + lax.axis_index("core") == 0).astype(jnp.int32)
    differs = first_level * (low_own ^ low_other) + pole * (north_own ^ north_other)
    strip = jnp.where(differs > 0, strip + mask_fill, strip) * log2e
    for w in range(WW):
        start = (WW - 1 - w) * PLACES
        part = strip[:, start : start + TOK]
        for g in range(groups):
            out_ref[g, w * PLACES : (w + 1) * PLACES, :] = part[g * PLACES : (g + 1) * PLACES, :]


def expand_bias(table):
    levels = table.shape[1]
    groups = levels * HEADS
    pairs = PLACES * PLACES
    flat = table[0].transpose(1, 3, 0, 2).reshape(HEADS * RELW, levels, pairs)
    return pl.pallas_call(
        functools.partial(bias_kernel, levels),
        out_shape=shape((groups, TOK, TOK), f32),
        in_specs=vmem(1),
        out_specs=vmem(1)[0],
        scratch_shapes=[pltpu.VMEM((groups * pairs, 128), f32)] * (STRIP // 128),
        compiler_params=pltpu.CompilerParams(vmem_limit_bytes=28 * MIB),
        cost_estimate=cost(10**9, 8 * MIB),
        name="bias",
    )(flat)


def head_masks(count):
    lane = lax.broadcasted_iota(jnp.int32, (count, C), 1)
    return [((lane >= h * HEAD) & (lane < (h + 1) * HEAD)).astype(f32) for h in range(HEADS)]


def stacked(values, masks):
    return jnp.concatenate([values * mask for mask in masks], axis=0)


def head_sum(values, masks):
    total = values[:TOK] * masks[0]
    for h in range(1, HEADS):
        total = total + values[h * TOK : (h + 1) * TOK] * masks[h]
    return total


def position():
    return lax.axis_index("core"), lax.axis_index("y") * 2 + lax.axis_index("x"), lax.axis_index("deep")


def chunk_rows(block):
    return pl.ds(pl.multiple_of(block * PART, PART), PART)


def split_parts(total_refs, keep_ref, send_ref):
    core, chip, _ = position()
    for out, side in ((keep_ref, core), (send_ref, 1 - core)):
        parts = []
        for g in range(QUADS):
            rows = chunk_rows(side * QUADS + jnp.bitwise_xor(chip, g))
            parts += [ref[rows, :] for ref in total_refs]
        out[...] = jnp.concatenate(parts, axis=0).astype(out.dtype)


def forward_kernel(
    windows, lon_windows,
    own_ref, north_ref, side_ref, corner_ref, perm_ref, bias_ref, triple_ref, project_ref, up_ref, down_ref,
    q_ref, k_ref, v_ref, p_ref, mixed_ref, normed_ref, unit_ref, spread_ref, gsum_ref, up_grad_ref, down_grad_ref,
    branch_ref, cot_ref, emb_ref,
):
    pieces = [ref[...].astype(f32)[:-EXTRA] for ref in (own_ref, north_ref, side_ref, corner_ref)]
    pieces = jnp.concatenate(pieces, axis=0).astype(bf16)
    ordered = mm(one_hot(perm_ref), pieces)
    emb = ordered[:, :C]
    emb_ref[...] = emb
    cot_ref[...] = ordered[:, C:].astype(bf16)
    unit, spread = unit_norm(emb)
    unit_ref[...] = unit
    spread_ref[...] = spread
    normed = unit.astype(bf16)
    normed_ref[...] = normed
    packed = mm(normed, triple_ref[...])
    q_ref[...] = packed[:, :C].astype(bf16)
    k_ref[...] = packed[:, C : 2 * C].astype(bf16)
    v_ref[...] = packed[:, 2 * C :].astype(bf16)
    masks = head_masks(TOK)
    masks_b = [mask.astype(bf16) for mask in masks]

    def window_step(w, carry):
        rows = pl.ds(pl.multiple_of(w * TOK, TOK), TOK)
        level = w // lon_windows
        scores = mm_nt(stacked(q_ref[rows, :], masks_b), k_ref[rows, :])
        bias = bias_ref[pl.ds(level * HEADS, HEADS)].reshape(HEADS * TOK, TOK)
        raised = jnp.exp2(scores * (score_scale * log2e) + bias)
        probs = raised * (1.0 / jnp.sum(raised, -1, keepdims=True))
        probs_b = probs.astype(bf16)
        p_ref[pl.ds(w * HEADS, HEADS)] = probs_b.reshape(HEADS, TOK, TOK)
        mixed = head_sum(mm(probs_b, v_ref[rows, :]), masks).astype(bf16)
        mixed_ref[rows, :] = mixed
        branch_ref[rows, :] = mm(mixed, project_ref[...])
        return carry

    lax.fori_loop(0, windows, window_step, 0, unroll=True)

    attended = branch_ref[...].astype(bf16).astype(f32)
    unit2, spread2 = unit_norm(emb_ref[...] + attended)
    normed2 = unit2.astype(bf16)
    cot = cot_ref[...]
    back = jnp.zeros(unit2.shape, f32)
    block = 256
    for start in range(0, FF, block):
        cols = slice(start, start + block)
        up_part = up_ref[:, cols]
        pre = mm(normed2, up_part)
        upstream = mm(cot, down_ref[:, cols])
        phi = 0.5 * (1.0 + lax.erf(pre * root_half))
        activated = (pre * phi).astype(bf16)
        slope = phi + pre * inv_root_tau * jnp.exp2(pre * pre * (-0.5 * log2e))
        hidden = (upstream * slope).astype(bf16)
        up_grad_ref[:, cols] = mm_tn(normed2, hidden)
        down_grad_ref[:, cols] = mm_tn(cot, activated)
        back = back + mm_nt(hidden, up_part)
    gsum_ref[...] = cot.astype(f32) + norm_back(back, unit2, spread2)


def windows_back_kernel(windows, q_ref, k_ref, v_ref, p_ref, gsum_ref, project_ref, gq_ref, gk_ref, gv_ref):
    masks = head_masks(TOK)
    masks_b = [mask.astype(bf16) for mask in masks]

    def window_step(w, carry):
        rows = pl.ds(pl.multiple_of(w * TOK, TOK), TOK)
        grad = gsum_ref[rows, :].astype(bf16)
        grad_mixed = mm_nt(grad, project_ref[...])
        grad_mixed_b = grad_mixed.astype(bf16)
        probs_b = p_ref[pl.ds(w * HEADS, HEADS)].reshape(HEADS * TOK, TOK)
        probs = probs_b.astype(f32)
        grad_probs = mm_nt(stacked(grad_mixed_b, masks_b), v_ref[rows, :])
        inner = jnp.sum(grad_probs * probs, -1, keepdims=True)
        scaled = (probs * (grad_probs - inner) * score_scale).astype(bf16)
        grad_q = head_sum(mm(scaled, k_ref[rows, :]), masks)
        grad_mixed_t = grad_mixed_b.astype(f32).T.astype(bf16)
        query_t = q_ref[rows, :].astype(f32).T.astype(bf16)
        grad_k, grad_v = [], []
        for h in range(HEADS):
            spot = slice(h * HEAD, (h + 1) * HEAD)
            span = slice(h * TOK, (h + 1) * TOK)
            grad_k.append(mm(query_t[spot], scaled[span]))
            grad_v.append(mm(grad_mixed_t[spot], probs_b[span]))
        gq_ref[rows, :] = grad_q.astype(bf16)
        gk_ref[rows, :] = jnp.concatenate(grad_k, axis=0).T.astype(bf16)
        gv_ref[rows, :] = jnp.concatenate(grad_v, axis=0).T.astype(bf16)
        return carry

    lax.fori_loop(0, windows, window_step, 0, unroll=True)


def halved(rows):
    return -(-rows // 16) * 8


def tokens_back_kernel(
    sizes, gq_ref, gk_ref, gv_ref, mixed_ref, normed_ref, unit_ref, spread_ref, gsum_ref, perm_ref, triple_ref,
    up_grad_ref, down_grad_ref, *rest,
):
    flag_refs, rest = rest[: len(sizes)], rest[len(sizes) :]
    outs, (land_ref, keep_ref, send_ref, total_ref) = rest[: len(sizes) - 1], rest[len(sizes) - 1 :]
    normed = normed_ref[...]
    triple = triple_ref[...]
    grad_normed = jnp.zeros(unit_ref.shape, f32)
    parts = []
    for n, ref in enumerate((gq_ref, gk_ref, gv_ref)):
        grad = ref[...]
        grad_normed = grad_normed + mm_nt(grad, triple[:, n * C : (n + 1) * C])
        parts.append(mm_tn(normed, grad))
    parts.append(mm_tn(mixed_ref[...], gsum_ref[...].astype(bf16)))
    total_ref[...] = jnp.concatenate(parts, axis=1)
    grad_normed = grad_normed.astype(bf16).astype(f32)
    grad_tokens = gsum_ref[...] + norm_back(grad_normed, unit_ref[...], spread_ref[...])
    pieces = mm(one_hot(perm_ref), grad_tokens.astype(bf16))
    land = jnp.zeros((EXTRA, C), f32)
    start = 0
    wide = []
    for size, flag_ref in zip(sizes, flag_refs):
        piece = pieces[start : start + size]
        flags = flag_ref[size - 8 : size + 8, :].astype(f32)[8:, :size]
        land = land + mm(flags.astype(bf16), piece.astype(bf16))
        half = halved(size)
        second = jnp.concatenate([piece[half:], jnp.zeros((2 * half - size, C), f32)], axis=0)
        wide.append(jnp.concatenate([piece[:half], second], axis=1))
        start += size
    land_ref[...] = land[0:1]
    own, north, side, corner = wide
    for out, value in zip(outs, (own, jnp.concatenate([north, corner], axis=0), side)):
        out[...] = value.astype(bf16)
    split_parts((up_grad_ref, down_grad_ref, total_ref), keep_ref, send_ref)


def block_kernel(windows, lon_windows, sizes, *refs):
    ins, refs = refs[:11], refs[11:]
    pieces, (perm_ref, back_perm_ref, bias_ref, triple_ref, project_ref, up_ref, down_ref) = ins[:4], ins[4:]
    outs, refs = refs[: len(sizes) + 2], refs[len(sizes) + 2 :]
    q, k, v, p, mixed, normed, unit, spread, gsum, up_grad, down_grad, branch, cot, emb, gq, gk, gv, total = refs
    forward_kernel(
        windows, lon_windows, *pieces, perm_ref, bias_ref, triple_ref, project_ref, up_ref, down_ref,
        q, k, v, p, mixed, normed, unit, spread, gsum, up_grad, down_grad, branch, cot, emb,
    )
    windows_back_kernel(windows, q, k, v, p, gsum, project_ref, gq, gk, gv)
    tokens_back_kernel(
        sizes, gq, gk, gv, mixed, normed, unit, spread, gsum, back_perm_ref, triple_ref, up_grad, down_grad,
        *pieces, *outs, total,
    )


def block(pieces, perm, back_perm, bias, triple, project, up, down, lon_windows, sizes):
    count = perm.shape[1]
    windows = count // TOK
    own, north, side, corner = [halved(size) for size in sizes]
    out_shape = [shape((size, 2 * C), bf16) for size in (own, north + corner, side)] + [
        shape((1, C), f32),
        shape((QUADS * CHUNK, FF), f32),
        shape((QUADS * CHUNK, FF), bf16),
    ]
    rows = [pltpu.VMEM((count, C), dtype) for dtype in (bf16, f32)]
    return pl.pallas_call(
        functools.partial(block_kernel, windows, lon_windows, sizes),
        out_shape=out_shape,
        in_specs=vmem(11),
        out_specs=vmem(len(out_shape)),
        scratch_shapes=rows[:1] * 3
        + [pltpu.VMEM((windows * HEADS, TOK, TOK), bf16)]
        + rows[:1] * 2
        + [rows[1], pltpu.VMEM((count, 1), f32), rows[1]]
        + [pltpu.VMEM((C, FF), f32)] * 2
        + [rows[1], rows[0], rows[1]]
        + rows[:1] * 3
        + [pltpu.VMEM((C, FF), f32)],
        compiler_params=pltpu.CompilerParams(vmem_limit_bytes=32 * MIB),
        cost_estimate=cost(8 * 10**9, 16 * MIB),
        name="block",
    )(*pieces, perm, back_perm, bias, triple, project, up, down)


def side_kernel(side_ref, north_ref, *refs):
    corner = north_ref[...].astype(f32)[-side_ref.shape[0] :]
    refs[-1][...] = jnp.concatenate([side_ref[...].astype(f32), corner], axis=0).astype(bf16)


def home_kernel(sizes, own_ref, north_ref, side_ref, perm_ref, out_ref):
    wide = [ref[...].astype(f32) for ref in (own_ref, north_ref, side_ref)]
    half = wide[2].shape[0] // 2
    wide = [wide[0], wide[1][:-half], wide[2][:half], wide[2][half:]]
    pieces = []
    for size, value in zip(sizes, wide):
        pieces += [value[:, :C], value[: size - value.shape[0], C:]]
    pieces = jnp.concatenate(pieces, axis=0).astype(bf16)
    out_ref[...] = mm(one_hot(perm_ref), pieces).astype(bf16)


def to_home(own, north, side, sizes, rows, cols):
    count = Z * rows * cols
    perm = spots(np.argsort(np.concatenate(piece_rows(rows, cols))))
    return pl.pallas_call(
        functools.partial(home_kernel, sizes),
        out_shape=shape((count, C), bf16),
        in_specs=vmem(4),
        out_specs=vmem(1)[0],
        compiler_params=pltpu.CompilerParams(vmem_limit_bytes=32 * MIB),
        cost_estimate=cost(2 * count * count * C, 4 * MIB),
        name="to_home",
    )(own, north, side, perm)


def core_add_kernel(keep_ref, got_ref, *refs):
    own_ref, outs = refs[-QUADS], refs[1 - QUADS :]
    total = keep_ref[...] + got_ref[...].astype(f32)
    own_ref[...] = total[:CHUNK]
    for e, out in enumerate(outs, 1):
        out[...] = total[e * CHUNK : (e + 1) * CHUNK].astype(bf16)


def chip_add_kernel(keep_ref, *refs):
    gots, (land_ref, out_ref) = refs[:-2], refs[-2:]
    total = keep_ref[...]
    for ref in gots:
        total = total + ref[...].astype(f32)
    land = jnp.concatenate([land_ref[...], jnp.zeros((1, FF - C), f32)], axis=1)
    out_ref[...] = jnp.concatenate([total, land, jnp.zeros((EXTRA - 1, FF), f32)], axis=0).astype(bf16)


def add_kernel(one_ref, two_ref, *refs):
    refs[-1][...] = (one_ref[...].astype(f32) + two_ref[...].astype(f32)).astype(bf16)


def join_kernel(*refs):
    refs[-1][...] = jnp.concatenate([ref[...] for ref in refs[:-1]], axis=0)


def small_call(kernel, out_shape, args, name, after=(), scratch=()):
    return pl.pallas_call(
        kernel,
        out_shape=out_shape,
        in_specs=vmem(len(args)) + [pl.BlockSpec(memory_space=pl.ANY)] * len(after),
        out_specs=vmem(len(out_shape)),
        scratch_shapes=scratch,
        compiler_params=pltpu.CompilerParams(vmem_limit_bytes=16 * MIB),
        cost_estimate=cost(10**6, 2 * MIB),
        name=name,
    )(*args, *after)


def finish_kernel(far, chunks_ref, *refs):
    if far:
        before_ref, refs = refs[0], refs[5:]
    outs, land_ref, (up_ref, down_ref, triple_ref, project_ref, lands_ref, sum_ref, sems) = refs[:4], refs[4], refs[5:]
    core, chip, _ = position()
    side = 1 - core if far else core
    for g in range(QUADS):
        chunk = chunks_ref[g * FULL : (g + 1) * FULL, :].astype(f32)
        block = jnp.bitwise_xor(chip, g)
        rows = chunk_rows(block)
        up_ref[rows, :] = chunk[:PART]
        down_ref[rows, :] = chunk[PART : 2 * PART]
        triple_ref[rows, :] = chunk[2 * PART : CHUNK, : 3 * C]
        project_ref[rows, :] = chunk[2 * PART : CHUNK, 3 * C :]
        lands_ref[pl.ds(pl.multiple_of(block * EXTRA, EXTRA), EXTRA), :] = chunk[CHUNK:, :C]
    copies = []
    for n, (source, out) in enumerate(zip((triple_ref, project_ref, up_ref, down_ref), outs)):
        rows = pl.ds(pl.multiple_of(side * QUADS * PART, 8), QUADS * PART)
        copies.append(pltpu.make_async_copy(source, out.at[rows, :], sems.at[n]))
    for copy in copies:
        copy.start()
    land = jnp.sum(lands_ref[...], 0, keepdims=True)
    if far:
        sum_ref[...] = land + before_ref[...]
        copies.append(pltpu.make_async_copy(sum_ref, land_ref, sems.at[4]))
        copies[-1].start()
    else:
        land_ref[...] = land
    for copy in copies:
        copy.wait()


def finish(chunks, before=()):
    rows = QUADS * PART
    widths = (3 * C, C, FF, FF)
    hbm = [pl.BlockSpec(memory_space=pltpu.HBM)] * 4
    land, weights = before[4:], before[:4]
    return pl.pallas_call(
        functools.partial(finish_kernel, bool(before)),
        out_shape=[shape((C, width), f32) for width in widths] + [shape((1, C), f32)],
        in_specs=vmem(1 + len(land)) + hbm[: len(weights)],
        out_specs=hbm + (hbm[:1] if before else vmem(1)),
        scratch_shapes=[
            pltpu.VMEM((rows, FF), f32),
            pltpu.VMEM((rows, FF), f32),
            pltpu.VMEM((rows, 3 * C), f32),
            pltpu.VMEM((rows, C), f32),
            pltpu.VMEM((QUADS * EXTRA, C), f32),
            pltpu.VMEM((1, C), f32),
            pltpu.SemaphoreType.DMA((5,)),
        ],
        input_output_aliases={2 + n: n for n in range(len(weights))},
        compiler_params=pltpu.CompilerParams(vmem_limit_bytes=16 * MIB),
        cost_estimate=cost(10**6, 2 * MIB),
        name="finish_far" if before else "finish_own",
    )(chunks, *land, *weights)


def reduce_all(keep, sent, land, side, north, shift, lon_count):
    core_move = lambda lon, lat: (lon, lat ^ 1)
    chip_move = lambda e: lambda lon, lat: (lon ^ (e & 1), lat ^ (2 * (e >> 1)))
    deep_move = lambda e: lambda lon, lat: (lon ^ (2 * e), lat)

    def one(rows):
        return [shape((rows, FF), bf16)]

    got = shift(sent, move=core_move)
    parts = [shape((CHUNK, FF), f32)] + one(CHUNK) * (QUADS - 1)
    own, *parts = small_call(core_add_kernel, parts, (keep, got), "core_add", after=(north,))
    gots = [shift(value, move=chip_move(e)) for e, value in enumerate(parts, 1)]
    (total,) = small_call(chip_add_kernel, one(FULL), (own, *gots, land), "chip_add")
    (side,) = small_call(side_kernel, [shape((2 * side.shape[0], 2 * C), bf16)], (side, north), "side", after=(total,))
    side = shift(side, move=lambda lon, lat: (lon - 1, lat))
    reach = 1
    while reach < lon_count // 2:
        got = shift(total, move=deep_move(reach))
        reach *= 2
        waits = () if reach < lon_count // 2 else (side,)
        (total,) = small_call(add_kernel, one(FULL), (total, got), "deep_add", after=waits)
    near = [total] + [shift(total, move=chip_move(e)) for e in range(1, QUADS)]
    (total,) = small_call(join_kernel, one(QUADS * FULL), near, "join")
    got = shift(total, move=core_move)
    return finish(got, finish(total)), side


AXES = ("deep", "x", "y", "core")


def send(value, lon_count, lat_count, move):
    pairs = []
    for lon in range(lon_count):
        for lat in range(lat_count):
            to_lon, to_lat = move(lon, lat)
            pairs.append((lon * lat_count + lat, (to_lon % lon_count) * lat_count + to_lat % lat_count))
    return lax.ppermute(value, AXES, pairs)


def body(
    lon_count, lat_count,
    tokens, cotangent, land_sea, land_vector, triple_weight, project_weight, up_weight, down_weight, earth_bias,
):
    levels, rows, cols, features = tokens.shape
    shift = functools.partial(send, lon_count=lon_count, lat_count=lat_count)
    lon_windows = cols // WW

    own, north, side, corner = pack(tokens, cotangent, land_sea, land_vector, rows, cols)
    north = shift(north, move=lambda lon, lat: (lon, lat + 1))
    side = shift(side, move=lambda lon, lat: (lon + 1, lat))
    corner = shift(corner, move=lambda lon, lat: (lon + 1, lat + 1))
    bias = expand_bias(earth_bias)

    places = window_rows(rows, cols)
    sizes = [part.size for part in piece_rows(rows, cols)]
    pieces = (own, north, side, corner)
    own, north, side, land, keep, sent = block(
        pieces, spots(places), spots(np.argsort(places)), bias,
        triple_weight, project_weight, up_weight, down_weight.T, lon_windows, sizes,
    )
    north = shift(north, move=lambda lon, lat: (lon, lat - 1))
    (triple, project, up, down, land), side = reduce_all(keep, sent, land, side, north, shift, lon_count)
    grad_tokens = to_home(own, north, side, sizes, rows, cols)
    return grad_tokens.reshape(tokens.shape), triple, project, up, down.T, land.reshape(features)


def solution(mesh):
    lon_count, lat_count = mesh.shape["lon"], mesh.shape["lat"]
    fine = jax.sharding.Mesh(mesh.devices.reshape(lon_count // 2, 2, lat_count // 2, 2), AXES)
    lon, lat = AXES[:2], AXES[2:]
    return jax.shard_map(
        functools.partial(body, lon_count, lat_count),
        mesh=fine,
        in_specs=(
            P(None, lat, lon, None),
            P(None, lat, lon, None),
            P(lat, lon),
            P(),
            P(),
            P(),
            P(),
            P(),
            P(lat, None, None, None, None),
        ),
        out_specs=(P(None, lat, lon, None), P(), P(), P(), P(), P()),
        check_vma=False,
    )
```

```python
import functools
import math

import jax
import jax.numpy as jnp
import numpy as np
from jax import lax
from jax.experimental import pallas as pl
from jax.experimental.pallas import tpu as pltpu
from jax.sharding import PartitionSpec as P

Z = 4
WZ = 2
WH = 6
WW = 12
C = 192
HEADS = 6
HEAD = 32
FF = 768
HZ, HH, HW = WZ // 2, WH // 2, WW // 2
TOK = WZ * WH * WW
PLACES = WZ * WH
RELW = 2 * WW - 1
SPOTS = PLACES // 2
STRIP = -(-RELW * SPOTS // 128) * 128
RUN, SHORT = WW * SPOTS, (WW - HW) * SPOTS

mask_fill = -10000.0
norm_eps = 1e-05
log2e = 1.4426950408889634
root_half = 0.7071067811865476
inv_root_tau = 0.3989422804014327
score_scale = HEAD**-0.5

f32 = jnp.float32
bf16 = jnp.bfloat16
MIB = 1 << 20

QUADS = 4
PART = C // (2 * QUADS)
CHUNK = 3 * PART
EXTRA = 8
FULL = CHUNK + EXTRA


def mm(a, b):
    return lax.dot_general(a, b, (((1,), (0,)), ((), ())), preferred_element_type=f32)


def mm_nt(a, b):
    return lax.dot_general(a, b, (((1,), (1,)), ((), ())), preferred_element_type=f32)


def mm_tn(a, b):
    return lax.dot_general(a, b, (((0,), (0,)), ((), ())), preferred_element_type=f32)


def unit_norm(values):
    average = jnp.mean(values, -1, keepdims=True)
    centred = values - average
    variance = jnp.mean(centred * centred, -1, keepdims=True)
    spread = lax.rsqrt(variance + norm_eps)
    return centred * spread, spread


def norm_back(upstream, unit, spread):
    first = jnp.mean(upstream, -1, keepdims=True)
    second = jnp.mean(upstream * unit, -1, keepdims=True)
    return spread * (upstream - first - unit * second)


def piece_rows(rows, cols):
    home = np.arange(Z * rows * cols).reshape(Z, rows, cols)

    def run(level, row, col, width):
        levels = [(level * WZ + z - HZ) % Z for z in range(WZ)]
        return home[levels, row : row + HH, col : col + width].transpose(2, 0, 1).reshape(-1)

    levels = range(Z // WZ)
    parts = []
    for row in (0, rows - HH):
        whole = [run(a, row, w * WW - HW, WW) for w in range(1, cols // WW) for a in levels]
        parts.append(np.concatenate(whole + [run(a, row, 0, WW - HW) for a in levels]))
    for row in (0, rows - HH):
        parts.append(np.concatenate([run(a, row, cols - HW, HW) for a in levels]))
    return parts


def window_runs(lon_windows):
    levels = Z // WZ
    whole = (lon_windows - 1) * levels
    runs = [[(1, n * RUN, RUN), (0, n * RUN, RUN)] for n in range(whole)]
    for a in range(levels):
        inner = whole * RUN + a * SHORT
        west = (a * (RUN - SHORT), RUN - SHORT)
        runs.append([(3, *west), (1, inner, SHORT), (2, *west), (0, inner, SHORT)])
    return runs


def spots(places):
    return jnp.asarray(np.argsort(places).astype(np.int32)[None])


def one_hot(spot_ref):
    count = spot_ref.shape[1]
    rows = lax.broadcasted_iota(jnp.int32, (count, count), 0)
    return (rows == spot_ref[...]).astype(f32).astype(bf16)


def vmem(count):
    return [pl.BlockSpec(memory_space=pltpu.VMEM)] * count


def shape(dims, dtype):
    return jax.ShapeDtypeStruct(dims, dtype)


def cost(flops, moved):
    return pl.CostEstimate(flops=flops, bytes_accessed=moved, transcendentals=0)


def land_column(land_ref, rows, cols):
    eye = (
        lax.broadcasted_iota(jnp.int32, (cols, cols), 0)
        == lax.broadcasted_iota(jnp.int32, (cols, cols), 1)
    ).astype(f32)
    land = land_ref[...].astype(f32)
    parts = [jnp.sum(eye * land[i : i + 1, :], -1, keepdims=True) for i in range(rows)]
    return jnp.concatenate(parts, axis=0)


def pack_kernel(rows, cols, *refs):
    sources, outs, (tokens_ref, cot_ref, land_ref, vec_ref, perm_ref, sems) = refs[:5], refs[5:-6], refs[-6:]
    copies = [
        pltpu.make_async_copy(source, target, sems.at[n])
        for n, (source, target) in enumerate(zip(sources, (tokens_ref, cot_ref, land_ref, vec_ref, perm_ref)))
    ]
    for copy in copies:
        copy.start()
    for copy in copies:
        copy.wait()
    column = land_column(land_ref, rows, cols)
    added = column * vec_ref[...]
    added = jnp.concatenate([added] * Z, axis=0)
    embedded = (tokens_ref[...].astype(f32) + added).astype(bf16)
    perm = one_hot(perm_ref)
    left = mm(perm, embedded)
    right = mm(perm, cot_ref[...])
    packed = jnp.concatenate([left, right], axis=1)
    start = 0
    for out in outs:
        out[...] = packed[start : start + out.shape[0]].astype(bf16)
        start += out.shape[0]


def pack(tokens, cotangent, land_sea, vector, rows, cols):
    parts = piece_rows(rows, cols)
    perm = spots(np.concatenate(parts))
    count = Z * rows * cols
    return pl.pallas_call(
        functools.partial(pack_kernel, rows, cols),
        out_shape=[shape((part.size, 2 * C), bf16) for part in parts],
        in_specs=[pl.BlockSpec(memory_space=pltpu.HBM)] * 5,
        out_specs=vmem(4),
        scratch_shapes=[
            pltpu.VMEM((count, C), bf16),
            pltpu.VMEM((count, C), bf16),
            pltpu.VMEM((rows, cols), jnp.int32),
            pltpu.VMEM((1, C), f32),
            pltpu.VMEM((1, count), jnp.int32),
            pltpu.SemaphoreType.DMA((5,)),
        ],
        cost_estimate=cost(4 * count * count * C, 4 * MIB),
        name="pack",
    )(tokens.reshape(count, C), cotangent.reshape(count, C), land_sea, vector.reshape(1, C), perm)


def floor_div(values, divisor):
    return (values * (65536 // divisor + 1)) >> 16


def remainder(values, divisor):
    return values - floor_div(values, divisor) * divisor


def place_order(order):
    half = floor_div(order, SPOTS)
    spot = order - half * SPOTS
    level = floor_div(spot, HH)
    return level * WH + half * HH + (spot - level * HH)


def bias_kernel(levels, table_ref, out_ref, *wide_refs):
    groups = levels * HEADS
    pairs = PLACES * PLACES
    row = lax.broadcasted_iota(jnp.int32, (HEADS * RELW, HEADS * STRIP), 0)
    lane = lax.broadcasted_iota(jnp.int32, (HEADS * RELW, HEADS * STRIP), 1)
    head = floor_div(row, RELW)
    ahead = lane - (head * STRIP + (RELW - 1 - (row - head * RELW)) * SPOTS)
    onehot = ((ahead >= 0) & (ahead < SPOTS)).astype(f32).astype(bf16)
    row = lax.broadcasted_iota(jnp.int32, (pairs, pairs), 0)
    source = place_order(floor_div(row, PLACES)) * PLACES + remainder(row, PLACES)
    reorder = (lax.broadcasted_iota(jnp.int32, (pairs, pairs), 1) == source).astype(f32).astype(bf16)
    for level in range(levels):
        table = table_ref[:, level, :].T
        high = table.astype(bf16)
        rest = (table - high.astype(f32)).astype(bf16)
        wide = mm(mm(reorder, high).astype(bf16), onehot) + mm(mm(reorder, rest).astype(bf16), onehot)
        for head in range(HEADS):
            for n, wide_ref in enumerate(wide_refs):
                start = head * STRIP + n * 128
                wide_ref[(level * HEADS + head) * pairs : (level * HEADS + head + 1) * pairs, :] = wide[:, start : start + 128]
    strips = groups * PLACES
    row = lax.broadcasted_iota(jnp.int32, (strips, STRIP), 0)
    spot = remainder(lax.broadcasted_iota(jnp.int32, (strips, STRIP), 1), SPOTS)
    own = remainder(row, PLACES)
    first_level = (row < HEADS * PLACES).astype(jnp.int32)
    own_north = (own < SPOTS).astype(jnp.int32)
    own_low = (own - SPOTS * (1 - own_north) < HZ * HH).astype(jnp.int32)
    low = (spot < HZ * HH).astype(jnp.int32)
    pole = (lax.axis_index("y") + lax.axis_index("core") == 0).astype(jnp.int32)
    halves = []
    for half in range(2):
        parts = []
        for n, wide_ref in enumerate(wide_refs):
            here = spot[:, n * 128 : (n + 1) * 128]
            part = jnp.zeros((strips, 128), f32)
            for p in range(SPOTS):
                place = p // HH * WH + half * HH + p % HH
                part = jnp.where(here == p, wide_ref[pl.ds(place, strips, stride=PLACES), :], part)
            parts.append(part)
        strip = jnp.concatenate(parts, axis=1)
        differs = first_level * (own_low ^ low) + pole * (own_north ^ (1 - half))
        halves.append(jnp.where(differs > 0, strip + mask_fill, strip) * log2e)
    for w in range(WW):
        start = (WW - 1 - w) * SPOTS
        part = jnp.concatenate([strip[:, start : start + RUN] for strip in halves], axis=1)
        for g in range(groups):
            for half in range(2):
                rows = part[g * PLACES + half * SPOTS : g * PLACES + (half + 1) * SPOTS, :]
                out_ref[g, half * RUN + w * SPOTS : half * RUN + (w + 1) * SPOTS, :] = rows


def expand_bias(table):
    levels = table.shape[1]
    groups = levels * HEADS
    pairs = PLACES * PLACES
    flat = table[0].transpose(1, 3, 0, 2).reshape(HEADS * RELW, levels, pairs)
    return pl.pallas_call(
        functools.partial(bias_kernel, levels),
        out_shape=shape((groups, TOK, TOK), f32),
        in_specs=vmem(1),
        out_specs=vmem(1)[0],
        scratch_shapes=[pltpu.VMEM((groups * pairs, 128), f32)] * (STRIP // 128),
        compiler_params=pltpu.CompilerParams(vmem_limit_bytes=28 * MIB),
        cost_estimate=cost(10**9, 8 * MIB),
        name="bias",
    )(flat)


def head_masks(count):
    lane = lax.broadcasted_iota(jnp.int32, (count, C), 1)
    return [((lane >= h * HEAD) & (lane < (h + 1) * HEAD)).astype(f32) for h in range(HEADS)]


def stacked(values, masks):
    return jnp.concatenate([values * mask for mask in masks], axis=0)


def head_sum(values, masks):
    total = values[:TOK] * masks[0]
    for h in range(1, HEADS):
        total = total + values[h * TOK : (h + 1) * TOK] * masks[h]
    return total


def position():
    return lax.axis_index("core"), lax.axis_index("y") * 2 + lax.axis_index("x"), lax.axis_index("deep")


def chunk_rows(block):
    return pl.ds(pl.multiple_of(block * PART, PART), PART)


def split_parts(total_refs, keep_ref, send_ref):
    core, chip, _ = position()
    for out, side in ((keep_ref, core), (send_ref, 1 - core)):
        parts = []
        for g in range(QUADS):
            rows = chunk_rows(side * QUADS + jnp.bitwise_xor(chip, g))
            parts += [ref[rows, :] for ref in total_refs]
        out[...] = jnp.concatenate(parts, axis=0).astype(out.dtype)


def forward_kernel(
    windows, lon_windows,
    own_ref, north_ref, side_ref, corner_ref, bias_ref, triple_ref, project_ref, up_ref, down_ref,
    q_ref, k_ref, v_ref, p_ref, mixed_ref, normed_ref, unit_ref, spread_ref, gsum_ref, up_grad_ref, down_grad_ref,
    branch_ref, cot_ref, emb_ref,
):
    pieces = [ref[...].astype(f32) for ref in (own_ref, north_ref, side_ref, corner_ref)]
    runs = [run for window in window_runs(lon_windows) for run in window]
    ordered = jnp.concatenate([pieces[n][start : start + count] for n, start, count in runs], axis=0)
    emb = ordered[:, :C]
    emb_ref[...] = emb
    cot_ref[...] = ordered[:, C:].astype(bf16)
    unit, spread = unit_norm(emb)
    unit_ref[...] = unit
    spread_ref[...] = spread
    normed = unit.astype(bf16)
    normed_ref[...] = normed
    packed = mm(normed, triple_ref[...])
    q_ref[...] = packed[:, :C].astype(bf16)
    k_ref[...] = packed[:, C : 2 * C].astype(bf16)
    v_ref[...] = packed[:, 2 * C :].astype(bf16)
    masks = head_masks(TOK)
    masks_b = [mask.astype(bf16) for mask in masks]

    def window_step(w, carry):
        rows = pl.ds(pl.multiple_of(w * TOK, TOK), TOK)
        level = w % (Z // WZ)
        scores = mm_nt(stacked(q_ref[rows, :], masks_b), k_ref[rows, :])
        bias = bias_ref[pl.ds(level * HEADS, HEADS)].reshape(HEADS * TOK, TOK)
        raised = jnp.exp2(scores * (score_scale * log2e) + bias)
        probs = raised * (1.0 / jnp.sum(raised, -1, keepdims=True))
        probs_b = probs.astype(bf16)
        p_ref[pl.ds(w * HEADS, HEADS)] = probs_b.reshape(HEADS, TOK, TOK)
        mixed = head_sum(mm(probs_b, v_ref[rows, :]), masks).astype(bf16)
        mixed_ref[rows, :] = mixed
        branch_ref[rows, :] = mm(mixed, project_ref[...])
        return carry

    lax.fori_loop(0, windows, window_step, 0, unroll=True)

    attended = branch_ref[...].astype(bf16).astype(f32)
    unit2, spread2 = unit_norm(emb_ref[...] + attended)
    normed2 = unit2.astype(bf16)
    cot = cot_ref[...]
    back = jnp.zeros(unit2.shape, f32)
    block = 256
    for start in range(0, FF, block):
        cols = slice(start, start + block)
        up_part = up_ref[:, cols]
        pre = mm(normed2, up_part)
        upstream = mm(cot, down_ref[:, cols])
        phi = 0.5 * (1.0 + lax.erf(pre * root_half))
        activated = (pre * phi).astype(bf16)
        slope = phi + pre * inv_root_tau * jnp.exp2(pre * pre * (-0.5 * log2e))
        hidden = (upstream * slope).astype(bf16)
        up_grad_ref[:, cols] = mm_tn(normed2, hidden)
        down_grad_ref[:, cols] = mm_tn(cot, activated)
        back = back + mm_nt(hidden, up_part)
    gsum_ref[...] = cot.astype(f32) + norm_back(back, unit2, spread2)


def windows_back_kernel(windows, q_ref, k_ref, v_ref, p_ref, gsum_ref, project_ref, gq_ref, gk_ref, gv_ref):
    masks = head_masks(TOK)
    masks_b = [mask.astype(bf16) for mask in masks]

    def window_step(w, carry):
        rows = pl.ds(pl.multiple_of(w * TOK, TOK), TOK)
        grad = gsum_ref[rows, :].astype(bf16)
        grad_mixed = mm_nt(grad, project_ref[...])
        grad_mixed_b = grad_mixed.astype(bf16)
        probs_b = p_ref[pl.ds(w * HEADS, HEADS)].reshape(HEADS * TOK, TOK)
        probs = probs_b.astype(f32)
        grad_probs = mm_nt(stacked(grad_mixed_b, masks_b), v_ref[rows, :])
        inner = jnp.sum(grad_probs * probs, -1, keepdims=True)
        scaled = (probs * (grad_probs - inner) * score_scale).astype(bf16)
        grad_q = head_sum(mm(scaled, k_ref[rows, :]), masks)
        grad_mixed_t = grad_mixed_b.astype(f32).T.astype(bf16)
        query_t = q_ref[rows, :].astype(f32).T.astype(bf16)
        grad_k, grad_v = [], []
        for h in range(HEADS):
            spot = slice(h * HEAD, (h + 1) * HEAD)
            span = slice(h * TOK, (h + 1) * TOK)
            grad_k.append(mm(query_t[spot], scaled[span]))
            grad_v.append(mm(grad_mixed_t[spot], probs_b[span]))
        gq_ref[rows, :] = grad_q.astype(bf16)
        gk_ref[rows, :] = jnp.concatenate(grad_k, axis=0).T.astype(bf16)
        gv_ref[rows, :] = jnp.concatenate(grad_v, axis=0).T.astype(bf16)
        return carry

    lax.fori_loop(0, windows, window_step, 0, unroll=True)


def halved(rows):
    return -(-rows // 16) * 8


def tokens_back_kernel(
    lon_windows, sizes, gq_ref, gk_ref, gv_ref, mixed_ref, normed_ref, unit_ref, spread_ref, gsum_ref, triple_ref,
    up_grad_ref, down_grad_ref, *rest,
):
    outs, (keep_ref, send_ref, total_ref) = rest[: len(sizes)], rest[len(sizes) :]
    normed = normed_ref[...]
    triple = triple_ref[...]
    grad_normed = jnp.zeros(unit_ref.shape, f32)
    parts = []
    for n, ref in enumerate((gq_ref, gk_ref, gv_ref)):
        grad = ref[...]
        grad_normed = grad_normed + mm_nt(grad, triple[:, n * C : (n + 1) * C])
        parts.append(mm_tn(normed, grad))
    parts.append(mm_tn(mixed_ref[...], gsum_ref[...].astype(bf16)))
    total_ref[...] = jnp.concatenate(parts, axis=1)
    grad_normed = grad_normed.astype(bf16).astype(f32)
    grad_tokens = gsum_ref[...] + norm_back(grad_normed, unit_ref[...], spread_ref[...])
    parts, at = [[] for _ in sizes], 0
    for n, start, count in [run for window in window_runs(lon_windows) for run in window]:
        parts[n].append((start, grad_tokens[at : at + count]))
        at += count
    for size, out, part in zip(sizes, outs, parts):
        piece = jnp.concatenate([value for _, value in sorted(part, key=lambda item: item[0])], axis=0)
        half = halved(size)
        second = jnp.concatenate([piece[half:], jnp.zeros((2 * half - size, C), f32)], axis=0)
        out[...] = jnp.concatenate([piece[:half], second], axis=1).astype(bf16)
    split_parts((up_grad_ref, down_grad_ref, total_ref), keep_ref, send_ref)


def block_kernel(windows, lon_windows, sizes, *refs):
    ins, refs = refs[:9], refs[9:]
    pieces, (bias_ref, triple_ref, project_ref, up_ref, down_ref) = ins[:4], ins[4:]
    outs, refs = refs[: len(sizes) + 2], refs[len(sizes) + 2 :]
    q, k, v, p, mixed, normed, unit, spread, gsum, up_grad, down_grad, branch, cot, emb, gq, gk, gv, total = refs
    forward_kernel(
        windows, lon_windows, *pieces, bias_ref, triple_ref, project_ref, up_ref, down_ref,
        q, k, v, p, mixed, normed, unit, spread, gsum, up_grad, down_grad, branch, cot, emb,
    )
    windows_back_kernel(windows, q, k, v, p, gsum, project_ref, gq, gk, gv)
    tokens_back_kernel(
        lon_windows, sizes, gq, gk, gv, mixed, normed, unit, spread, gsum, triple_ref, up_grad, down_grad, *outs, total
    )


def block(pieces, bias, triple, project, up, down, lon_windows, sizes):
    count = sum(sizes)
    windows = count // TOK
    out_shape = [shape((halved(size), 2 * C), bf16) for size in sizes] + [
        shape((QUADS * CHUNK, FF), f32),
        shape((QUADS * CHUNK, FF), bf16),
    ]
    rows = [pltpu.VMEM((count, C), dtype) for dtype in (bf16, f32)]
    return pl.pallas_call(
        functools.partial(block_kernel, windows, lon_windows, sizes),
        out_shape=out_shape,
        in_specs=vmem(9),
        out_specs=vmem(len(out_shape)),
        scratch_shapes=rows[:1] * 3
        + [pltpu.VMEM((windows * HEADS, TOK, TOK), bf16)]
        + rows[:1] * 2
        + [rows[1], pltpu.VMEM((count, 1), f32), rows[1]]
        + [pltpu.VMEM((C, FF), f32)] * 2
        + [rows[1], rows[0], rows[1]]
        + rows[:1] * 3
        + [pltpu.VMEM((C, FF), f32)],
        compiler_params=pltpu.CompilerParams(vmem_limit_bytes=32 * MIB),
        cost_estimate=cost(8 * 10**9, 16 * MIB),
        name="block",
    )(*pieces, bias, triple, project, up, down)


def home_kernel(sizes, rows, cols, own_ref, north_ref, side_ref, corner_ref, perm_ref, land_ref, out_ref, sum_ref):
    pieces = []
    for size, ref in zip(sizes, (own_ref, north_ref, side_ref, corner_ref)):
        wide = ref[...].astype(f32)
        pieces += [wide[:, :C], wide[: size - wide.shape[0], C:]]
    pieces = jnp.concatenate(pieces, axis=0).astype(bf16)
    grads = mm(one_hot(perm_ref), pieces)
    out_ref[...] = grads.astype(bf16)
    column = jnp.concatenate([land_column(land_ref, rows, cols)] * Z, axis=0)
    sum_ref[...] = jnp.sum(grads * column, 0, keepdims=True)


def to_home(pieces, land_sea, sizes, rows, cols):
    count = Z * rows * cols
    perm = spots(np.argsort(np.concatenate(piece_rows(rows, cols))))
    return pl.pallas_call(
        functools.partial(home_kernel, sizes, rows, cols),
        out_shape=[shape((count, C), bf16), shape((1, C), f32)],
        in_specs=vmem(6),
        out_specs=vmem(2),
        compiler_params=pltpu.CompilerParams(vmem_limit_bytes=32 * MIB),
        cost_estimate=cost(2 * count * count * C, 4 * MIB),
        name="to_home",
    )(*pieces, perm, land_sea)


def core_add_kernel(keep_ref, got_ref, *refs):
    own_ref, outs = refs[-QUADS], refs[1 - QUADS :]
    total = keep_ref[...] + got_ref[...].astype(f32)
    own_ref[...] = total[:CHUNK]
    for e, out in enumerate(outs, 1):
        out[...] = total[e * CHUNK : (e + 1) * CHUNK].astype(bf16)


def chip_add_kernel(keep_ref, *refs):
    gots, (land_ref, out_ref) = refs[:-2], refs[-2:]
    total = keep_ref[...]
    for ref in gots:
        total = total + ref[...].astype(f32)
    land = jnp.concatenate([land_ref[...], jnp.zeros((1, FF - C), f32)], axis=1)
    out_ref[...] = jnp.concatenate([total, land, jnp.zeros((EXTRA - 1, FF), f32)], axis=0).astype(bf16)


def add_kernel(one_ref, two_ref, out_ref):
    out_ref[...] = (one_ref[...].astype(f32) + two_ref[...].astype(f32)).astype(bf16)


def join_kernel(*refs):
    refs[-1][...] = jnp.concatenate([ref[...] for ref in refs[:-1]], axis=0)


def small_call(kernel, out_shape, args, name, after=(), scratch=()):
    return pl.pallas_call(
        kernel,
        out_shape=out_shape,
        in_specs=vmem(len(args)) + [pl.BlockSpec(memory_space=pl.ANY)] * len(after),
        out_specs=vmem(len(out_shape)),
        scratch_shapes=scratch,
        compiler_params=pltpu.CompilerParams(vmem_limit_bytes=16 * MIB),
        cost_estimate=cost(10**6, 2 * MIB),
        name=name,
    )(*args, *after)


def finish_kernel(far, chunks_ref, *refs):
    if far:
        before_ref, refs = refs[0], refs[5:]
    outs, land_ref, (up_ref, down_ref, triple_ref, project_ref, lands_ref, sum_ref, sems) = refs[:4], refs[4], refs[5:]
    core, chip, _ = position()
    side = 1 - core if far else core
    for g in range(QUADS):
        chunk = chunks_ref[g * FULL : (g + 1) * FULL, :].astype(f32)
        block = jnp.bitwise_xor(chip, g)
        rows = chunk_rows(block)
        up_ref[rows, :] = chunk[:PART]
        down_ref[rows, :] = chunk[PART : 2 * PART]
        triple_ref[rows, :] = chunk[2 * PART : CHUNK, : 3 * C]
        project_ref[rows, :] = chunk[2 * PART : CHUNK, 3 * C :]
        lands_ref[pl.ds(pl.multiple_of(block * EXTRA, EXTRA), EXTRA), :] = chunk[CHUNK:, :C]
    copies = []
    for n, (source, out) in enumerate(zip((triple_ref, project_ref, up_ref, down_ref), outs)):
        rows = pl.ds(pl.multiple_of(side * QUADS * PART, 8), QUADS * PART)
        copies.append(pltpu.make_async_copy(source, out.at[rows, :], sems.at[n]))
    for copy in copies:
        copy.start()
    land = jnp.sum(lands_ref[...], 0, keepdims=True)
    if far:
        sum_ref[...] = land + before_ref[...]
        copies.append(pltpu.make_async_copy(sum_ref, land_ref, sems.at[4]))
        copies[-1].start()
    else:
        land_ref[...] = land
    for copy in copies:
        copy.wait()


def finish(chunks, before=()):
    rows = QUADS * PART
    widths = (3 * C, C, FF, FF)
    hbm = [pl.BlockSpec(memory_space=pltpu.HBM)] * 4
    land, weights = before[4:], before[:4]
    return pl.pallas_call(
        functools.partial(finish_kernel, bool(before)),
        out_shape=[shape((C, width), f32) for width in widths] + [shape((1, C), f32)],
        in_specs=vmem(1 + len(land)) + hbm[: len(weights)],
        out_specs=hbm + (hbm[:1] if before else vmem(1)),
        scratch_shapes=[
            pltpu.VMEM((rows, FF), f32),
            pltpu.VMEM((rows, FF), f32),
            pltpu.VMEM((rows, 3 * C), f32),
            pltpu.VMEM((rows, C), f32),
            pltpu.VMEM((QUADS * EXTRA, C), f32),
            pltpu.VMEM((1, C), f32),
            pltpu.SemaphoreType.DMA((5,)),
        ],
        input_output_aliases={2 + n: n for n in range(len(weights))},
        compiler_params=pltpu.CompilerParams(vmem_limit_bytes=16 * MIB),
        cost_estimate=cost(10**6, 2 * MIB),
        name="finish_far" if before else "finish_own",
    )(chunks, *land, *weights)


def reduce_all(keep, sent, land, shift, lon_count, after):
    core_move = lambda lon, lat: (lon, lat ^ 1)
    chip_move = lambda e: lambda lon, lat: (lon ^ (e & 1), lat ^ (2 * (e >> 1)))
    deep_move = lambda e: lambda lon, lat: (lon ^ (2 * e), lat)

    def one(rows):
        return [shape((rows, FF), bf16)]

    got = shift(sent, move=core_move)
    parts = [shape((CHUNK, FF), f32)] + one(CHUNK) * (QUADS - 1)
    own, *parts = small_call(core_add_kernel, parts, (keep, got), "core_add", after=after)
    gots = [shift(value, move=chip_move(e)) for e, value in enumerate(parts, 1)]
    (total,) = small_call(chip_add_kernel, one(FULL), (own, *gots, land), "chip_add")
    reach = 1
    while reach < lon_count // 2:
        got = shift(total, move=deep_move(reach))
        reach *= 2
        (total,) = small_call(add_kernel, one(FULL), (total, got), "deep_add")
    near = [total] + [shift(total, move=chip_move(e)) for e in range(1, QUADS)]
    (total,) = small_call(join_kernel, one(QUADS * FULL), near, "join")
    got = shift(total, move=core_move)
    return finish(got, finish(total))


AXES = ("deep", "x", "y", "core")


def send(value, lon_count, lat_count, move):
    pairs = []
    for lon in range(lon_count):
        for lat in range(lat_count):
            to_lon, to_lat = move(lon, lat)
            pairs.append((lon * lat_count + lat, (to_lon % lon_count) * lat_count + to_lat % lat_count))
    return lax.ppermute(value, AXES, pairs)


def body(
    lon_count, lat_count,
    tokens, cotangent, land_sea, land_vector, triple_weight, project_weight, up_weight, down_weight, earth_bias,
):
    levels, rows, cols, features = tokens.shape
    shift = functools.partial(send, lon_count=lon_count, lat_count=lat_count)
    lon_windows = cols // WW

    own, north, side, corner = pack(tokens, cotangent, land_sea, land_vector, rows, cols)
    north = shift(north, move=lambda lon, lat: (lon, lat + 1))
    side = shift(side, move=lambda lon, lat: (lon + 1, lat))
    corner = shift(corner, move=lambda lon, lat: (lon + 1, lat + 1))
    bias = expand_bias(earth_bias)

    sizes = [part.size for part in piece_rows(rows, cols)]
    pieces = (own, north, side, corner)
    own, north, side, corner, keep, sent = block(
        pieces, bias, triple_weight, project_weight, up_weight, down_weight.T, lon_windows, sizes
    )
    north = shift(north, move=lambda lon, lat: (lon, lat - 1))
    side = shift(side, move=lambda lon, lat: (lon - 1, lat))
    corner = shift(corner, move=lambda lon, lat: (lon - 1, lat - 1))
    after = (north, side, corner)
    grad_tokens, land = to_home((own, north, side, corner), land_sea, sizes, rows, cols)
    triple, project, up, down, land = reduce_all(keep, sent, land, shift, lon_count, after)
    return grad_tokens.reshape(tokens.shape), triple, project, up, down.T, land.reshape(features)


def solution(mesh):
    lon_count, lat_count = mesh.shape["lon"], mesh.shape["lat"]
    fine = jax.sharding.Mesh(mesh.devices.reshape(lon_count // 2, 2, lat_count // 2, 2), AXES)
    lon, lat = AXES[:2], AXES[2:]
    return jax.shard_map(
        functools.partial(body, lon_count, lat_count),
        mesh=fine,
        in_specs=(
            P(None, lat, lon, None),
            P(None, lat, lon, None),
            P(lat, lon),
            P(),
            P(),
            P(),
            P(),
            P(),
            P(lat, None, None, None, None),
        ),
        out_specs=(P(None, lat, lon, None), P(), P(), P(), P(), P()),
        check_vma=False,
    )
```

```python
import functools
import math

import jax
import jax.numpy as jnp
import numpy as np
from jax import lax
from jax.experimental import pallas as pl
from jax.experimental.pallas import tpu as pltpu
from jax.sharding import PartitionSpec as P

Z = 4
WZ = 2
WH = 6
WW = 12
C = 192
HEADS = 6
HEAD = 32
FF = 768
HZ, HH, HW = WZ // 2, WH // 2, WW // 2
TOK = WZ * WH * WW
PLACES = WZ * WH
RELW = 2 * WW - 1
SPOTS = PLACES // 2
STRIP = -(-RELW * SPOTS // 128) * 128
RUN, SHORT = WW * SPOTS, (WW - HW) * SPOTS

mask_fill = -10000.0
norm_eps = 1e-05
log2e = 1.4426950408889634
root_half = 0.7071067811865476
inv_root_tau = 0.3989422804014327
score_scale = HEAD**-0.5

f32 = jnp.float32
bf16 = jnp.bfloat16
MIB = 1 << 20

QUADS = 4
PART = C // (2 * QUADS)
CHUNK = 3 * PART
BLOCKS = FF // 128
EXTRA = 8
FULL = BLOCKS * CHUNK + EXTRA
FIRST = FULL // 16 * 8


def mm(a, b):
    return lax.dot_general(a, b, (((1,), (0,)), ((), ())), preferred_element_type=f32)


def mm_nt(a, b):
    return lax.dot_general(a, b, (((1,), (1,)), ((), ())), preferred_element_type=f32)


def mm_tn(a, b):
    return lax.dot_general(a, b, (((0,), (0,)), ((), ())), preferred_element_type=f32)


def unit_norm(values):
    average = jnp.mean(values, -1, keepdims=True)
    centred = values - average
    variance = jnp.mean(centred * centred, -1, keepdims=True)
    spread = lax.rsqrt(variance + norm_eps)
    return centred * spread, spread


def norm_back(upstream, unit, spread):
    first = jnp.mean(upstream, -1, keepdims=True)
    second = jnp.mean(upstream * unit, -1, keepdims=True)
    return spread * (upstream - first - unit * second)


def piece_rows(rows, cols):
    home = np.arange(Z * rows * cols).reshape(Z, rows, cols)

    def run(level, row, col, width):
        levels = [(level * WZ + z - HZ) % Z for z in range(WZ)]
        return home[levels, row : row + HH, col : col + width].transpose(2, 0, 1).reshape(-1)

    levels = range(Z // WZ)
    parts = []
    for row in (0, rows - HH):
        whole = [run(a, row, w * WW - HW, WW) for w in range(1, cols // WW) for a in levels]
        parts.append(np.concatenate(whole + [run(a, row, 0, WW - HW) for a in levels]))
    for row in (0, rows - HH):
        parts.append(np.concatenate([run(a, row, cols - HW, HW) for a in levels]))
    return parts


def window_runs(lon_windows):
    levels = Z // WZ
    whole = (lon_windows - 1) * levels
    runs = [[(1, n * RUN, RUN), (0, n * RUN, RUN)] for n in range(whole)]
    for a in range(levels):
        inner = whole * RUN + a * SHORT
        west = (a * (RUN - SHORT), RUN - SHORT)
        runs.append([(3, *west), (1, inner, SHORT), (2, *west), (0, inner, SHORT)])
    return runs


def spots(places):
    return jnp.asarray(np.argsort(places).astype(np.int32)[None])


def one_hot(spot_ref):
    count = spot_ref.shape[1]
    rows = lax.broadcasted_iota(jnp.int32, (count, count), 0)
    return (rows == spot_ref[...]).astype(f32).astype(bf16)


def vmem(count):
    return [pl.BlockSpec(memory_space=pltpu.VMEM)] * count


def shape(dims, dtype):
    return jax.ShapeDtypeStruct(dims, dtype)


def cost(flops, moved):
    return pl.CostEstimate(flops=flops, bytes_accessed=moved, transcendentals=0)


def land_column(land_ref, rows, cols):
    eye = (
        lax.broadcasted_iota(jnp.int32, (cols, cols), 0)
        == lax.broadcasted_iota(jnp.int32, (cols, cols), 1)
    ).astype(f32)
    land = land_ref[...].astype(f32)
    parts = [jnp.sum(eye * land[i : i + 1, :], -1, keepdims=True) for i in range(rows)]
    return jnp.concatenate(parts, axis=0)


def pack_kernel(rows, cols, *refs):
    sources, outs, (tokens_ref, cot_ref, land_ref, vec_ref, perm_ref, sems) = refs[:5], refs[5:-6], refs[-6:]
    copies = [
        pltpu.make_async_copy(source, target, sems.at[n])
        for n, (source, target) in enumerate(zip(sources, (tokens_ref, cot_ref, land_ref, vec_ref, perm_ref)))
    ]
    for copy in copies:
        copy.start()
    for copy in copies:
        copy.wait()
    column = land_column(land_ref, rows, cols)
    added = column * vec_ref[...]
    added = jnp.concatenate([added] * Z, axis=0)
    embedded = (tokens_ref[...].astype(f32) + added).astype(bf16)
    perm = one_hot(perm_ref)
    left = mm(perm, embedded)
    right = mm(perm, cot_ref[...])
    packed = jnp.concatenate([left, right], axis=1)
    start = 0
    for out in outs:
        out[...] = packed[start : start + out.shape[0]].astype(bf16)
        start += out.shape[0]


def pack(tokens, cotangent, land_sea, vector, rows, cols):
    parts = piece_rows(rows, cols)
    perm = spots(np.concatenate(parts))
    count = Z * rows * cols
    return pl.pallas_call(
        functools.partial(pack_kernel, rows, cols),
        out_shape=[shape((part.size, 2 * C), bf16) for part in parts],
        in_specs=[pl.BlockSpec(memory_space=pltpu.HBM)] * 5,
        out_specs=vmem(4),
        scratch_shapes=[
            pltpu.VMEM((count, C), bf16),
            pltpu.VMEM((count, C), bf16),
            pltpu.VMEM((rows, cols), jnp.int32),
            pltpu.VMEM((1, C), f32),
            pltpu.VMEM((1, count), jnp.int32),
            pltpu.SemaphoreType.DMA((5,)),
        ],
        cost_estimate=cost(4 * count * count * C, 4 * MIB),
        name="pack",
    )(tokens.reshape(count, C), cotangent.reshape(count, C), land_sea, vector.reshape(1, C), perm)


def floor_div(values, divisor):
    return (values * (65536 // divisor + 1)) >> 16


def remainder(values, divisor):
    return values - floor_div(values, divisor) * divisor


def place_order(order):
    half = floor_div(order, SPOTS)
    spot = order - half * SPOTS
    level = floor_div(spot, HH)
    return level * WH + half * HH + (spot - level * HH)


def bias_kernel(levels, table_ref, out_ref, *wide_refs):
    groups = levels * HEADS
    pairs = PLACES * PLACES
    row = lax.broadcasted_iota(jnp.int32, (HEADS * RELW, HEADS * STRIP), 0)
    lane = lax.broadcasted_iota(jnp.int32, (HEADS * RELW, HEADS * STRIP), 1)
    head = floor_div(row, RELW)
    ahead = lane - (head * STRIP + (RELW - 1 - (row - head * RELW)) * SPOTS)
    onehot = ((ahead >= 0) & (ahead < SPOTS)).astype(f32).astype(bf16)
    row = lax.broadcasted_iota(jnp.int32, (pairs, pairs), 0)
    source = place_order(floor_div(row, PLACES)) * PLACES + remainder(row, PLACES)
    reorder = (lax.broadcasted_iota(jnp.int32, (pairs, pairs), 1) == source).astype(f32).astype(bf16)
    for level in range(levels):
        table = table_ref[:, level, :].T
        high = table.astype(bf16)
        rest = (table - high.astype(f32)).astype(bf16)
        wide = mm(mm(reorder, high).astype(bf16), onehot) + mm(mm(reorder, rest).astype(bf16), onehot)
        for head in range(HEADS):
            for n, wide_ref in enumerate(wide_refs):
                start = head * STRIP + n * 128
                wide_ref[(level * HEADS + head) * pairs : (level * HEADS + head + 1) * pairs, :] = wide[:, start : start + 128]
    strips = groups * PLACES
    row = lax.broadcasted_iota(jnp.int32, (strips, STRIP), 0)
    spot = remainder(lax.broadcasted_iota(jnp.int32, (strips, STRIP), 1), SPOTS)
    own = remainder(row, PLACES)
    first_level = (row < HEADS * PLACES).astype(jnp.int32)
    own_north = (own < SPOTS).astype(jnp.int32)
    own_low = (own - SPOTS * (1 - own_north) < HZ * HH).astype(jnp.int32)
    low = (spot < HZ * HH).astype(jnp.int32)
    pole = (lax.axis_index("y") + lax.axis_index("core") == 0).astype(jnp.int32)
    halves = []
    for half in range(2):
        parts = []
        for n, wide_ref in enumerate(wide_refs):
            here = spot[:, n * 128 : (n + 1) * 128]
            part = jnp.zeros((strips, 128), f32)
            for p in range(SPOTS):
                place = p // HH * WH + half * HH + p % HH
                part = jnp.where(here == p, wide_ref[pl.ds(place, strips, stride=PLACES), :], part)
            parts.append(part)
        strip = jnp.concatenate(parts, axis=1)
        differs = first_level * (own_low ^ low) + pole * (own_north ^ (1 - half))
        halves.append(jnp.where(differs > 0, strip + mask_fill, strip) * log2e)
    for w in range(WW):
        start = (WW - 1 - w) * SPOTS
        part = jnp.concatenate([strip[:, start : start + RUN] for strip in halves], axis=1)
        for g in range(groups):
            for half in range(2):
                rows = part[g * PLACES + half * SPOTS : g * PLACES + (half + 1) * SPOTS, :]
                out_ref[g, half * RUN + w * SPOTS : half * RUN + (w + 1) * SPOTS, :] = rows


def expand_bias(table):
    levels = table.shape[1]
    groups = levels * HEADS
    pairs = PLACES * PLACES
    flat = table[0].transpose(1, 3, 0, 2).reshape(HEADS * RELW, levels, pairs)
    return pl.pallas_call(
        functools.partial(bias_kernel, levels),
        out_shape=shape((groups, TOK, TOK), f32),
        in_specs=vmem(1),
        out_specs=vmem(1)[0],
        scratch_shapes=[pltpu.VMEM((groups * pairs, 128), f32)] * (STRIP // 128),
        compiler_params=pltpu.CompilerParams(vmem_limit_bytes=28 * MIB),
        cost_estimate=cost(10**9, 8 * MIB),
        name="bias",
    )(flat)


def head_masks(count):
    lane = lax.broadcasted_iota(jnp.int32, (count, C), 1)
    return [((lane >= h * HEAD) & (lane < (h + 1) * HEAD)).astype(f32) for h in range(HEADS)]


def stacked(values, masks):
    return jnp.concatenate([values * mask for mask in masks], axis=0)


def head_sum(values, masks):
    total = values[:TOK] * masks[0]
    for h in range(1, HEADS):
        total = total + values[h * TOK : (h + 1) * TOK] * masks[h]
    return total


def position():
    return lax.axis_index("core"), lax.axis_index("y") * 2 + lax.axis_index("x"), lax.axis_index("deep")


def chunk_rows(block):
    return pl.ds(pl.multiple_of(block * PART, PART), PART)


def split_parts(total_refs, keep_ref, send_ref):
    core, chip, _ = position()
    for out, side in ((keep_ref, core), (send_ref, 1 - core)):
        parts = []
        for g in range(QUADS):
            rows = chunk_rows(side * QUADS + jnp.bitwise_xor(chip, g))
            parts += [ref[rows, :] for ref in total_refs]
        out[...] = jnp.concatenate(parts, axis=0).astype(out.dtype)


def forward_kernel(
    windows, lon_windows,
    own_ref, north_ref, side_ref, corner_ref, bias_ref, triple_ref, project_ref, up_ref, down_ref,
    q_ref, k_ref, v_ref, p_ref, mixed_ref, normed_ref, unit_ref, spread_ref, gsum_ref, up_grad_ref, down_grad_ref,
    branch_ref, cot_ref, emb_ref,
):
    pieces = [ref[...].astype(f32) for ref in (own_ref, north_ref, side_ref, corner_ref)]
    runs = [run for window in window_runs(lon_windows) for run in window]
    ordered = jnp.concatenate([pieces[n][start : start + count] for n, start, count in runs], axis=0)
    emb = ordered[:, :C]
    emb_ref[...] = emb
    cot_ref[...] = ordered[:, C:].astype(bf16)
    unit, spread = unit_norm(emb)
    unit_ref[...] = unit
    spread_ref[...] = spread
    normed = unit.astype(bf16)
    normed_ref[...] = normed
    packed = mm(normed, triple_ref[...])
    q_ref[...] = packed[:, :C].astype(bf16)
    k_ref[...] = packed[:, C : 2 * C].astype(bf16)
    v_ref[...] = packed[:, 2 * C :].astype(bf16)
    masks = head_masks(TOK)
    masks_b = [mask.astype(bf16) for mask in masks]

    def window_step(w, carry):
        rows = pl.ds(pl.multiple_of(w * TOK, TOK), TOK)
        level = w % (Z // WZ)
        scores = mm_nt(stacked(q_ref[rows, :], masks_b), k_ref[rows, :])
        bias = bias_ref[pl.ds(level * HEADS, HEADS)].reshape(HEADS * TOK, TOK)
        raised = jnp.exp2(scores * (score_scale * log2e) + bias)
        probs = raised * (1.0 / jnp.sum(raised, -1, keepdims=True))
        probs_b = probs.astype(bf16)
        p_ref[pl.ds(w * HEADS, HEADS)] = probs_b.reshape(HEADS, TOK, TOK)
        mixed = head_sum(mm(probs_b, v_ref[rows, :]), masks).astype(bf16)
        mixed_ref[rows, :] = mixed
        branch_ref[rows, :] = mm(mixed, project_ref[...])
        return carry

    lax.fori_loop(0, windows, window_step, 0, unroll=True)

    attended = branch_ref[...].astype(bf16).astype(f32)
    unit2, spread2 = unit_norm(emb_ref[...] + attended)
    normed2 = unit2.astype(bf16)
    cot = cot_ref[...]
    back = jnp.zeros(unit2.shape, f32)
    block = 256
    for start in range(0, FF, block):
        cols = slice(start, start + block)
        up_part = up_ref[:, cols]
        pre = mm(normed2, up_part)
        upstream = mm(cot, down_ref[:, cols])
        phi = 0.5 * (1.0 + lax.erf(pre * root_half))
        activated = (pre * phi).astype(bf16)
        slope = phi + pre * inv_root_tau * jnp.exp2(pre * pre * (-0.5 * log2e))
        hidden = (upstream * slope).astype(bf16)
        up_grad_ref[:, cols] = mm_tn(normed2, hidden)
        down_grad_ref[:, cols] = mm_tn(cot, activated)
        back = back + mm_nt(hidden, up_part)
    gsum_ref[...] = cot.astype(f32) + norm_back(back, unit2, spread2)


def windows_back_kernel(windows, q_ref, k_ref, v_ref, p_ref, gsum_ref, project_ref, gq_ref, gk_ref, gv_ref):
    masks = head_masks(TOK)
    masks_b = [mask.astype(bf16) for mask in masks]

    def window_step(w, carry):
        rows = pl.ds(pl.multiple_of(w * TOK, TOK), TOK)
        grad = gsum_ref[rows, :].astype(bf16)
        grad_mixed = mm_nt(grad, project_ref[...])
        grad_mixed_b = grad_mixed.astype(bf16)
        probs_b = p_ref[pl.ds(w * HEADS, HEADS)].reshape(HEADS * TOK, TOK)
        probs = probs_b.astype(f32)
        grad_probs = mm_nt(stacked(grad_mixed_b, masks_b), v_ref[rows, :])
        inner = jnp.sum(grad_probs * probs, -1, keepdims=True)
        scaled = (probs * (grad_probs - inner) * score_scale).astype(bf16)
        grad_q = head_sum(mm(scaled, k_ref[rows, :]), masks)
        grad_mixed_t = grad_mixed_b.astype(f32).T.astype(bf16)
        query_t = q_ref[rows, :].astype(f32).T.astype(bf16)
        grad_k, grad_v = [], []
        for h in range(HEADS):
            spot = slice(h * HEAD, (h + 1) * HEAD)
            span = slice(h * TOK, (h + 1) * TOK)
            grad_k.append(mm(query_t[spot], scaled[span]))
            grad_v.append(mm(grad_mixed_t[spot], probs_b[span]))
        gq_ref[rows, :] = grad_q.astype(bf16)
        gk_ref[rows, :] = jnp.concatenate(grad_k, axis=0).T.astype(bf16)
        gv_ref[rows, :] = jnp.concatenate(grad_v, axis=0).T.astype(bf16)
        return carry

    lax.fori_loop(0, windows, window_step, 0, unroll=True)


def halved(rows):
    return -(-rows // 16) * 8


def tokens_back_kernel(
    lon_windows, sizes, gq_ref, gk_ref, gv_ref, mixed_ref, normed_ref, unit_ref, spread_ref, gsum_ref, triple_ref,
    up_grad_ref, down_grad_ref, *rest,
):
    outs, (keep_ref, send_ref, total_ref) = rest[: len(sizes)], rest[len(sizes) :]
    normed = normed_ref[...]
    triple = triple_ref[...]
    grad_normed = jnp.zeros(unit_ref.shape, f32)
    parts = []
    for n, ref in enumerate((gq_ref, gk_ref, gv_ref)):
        grad = ref[...]
        grad_normed = grad_normed + mm_nt(grad, triple[:, n * C : (n + 1) * C])
        parts.append(mm_tn(normed, grad))
    parts.append(mm_tn(mixed_ref[...], gsum_ref[...].astype(bf16)))
    total_ref[...] = jnp.concatenate(parts, axis=1)
    grad_normed = grad_normed.astype(bf16).astype(f32)
    grad_tokens = gsum_ref[...] + norm_back(grad_normed, unit_ref[...], spread_ref[...])
    parts, at = [[] for _ in sizes], 0
    for n, start, count in [run for window in window_runs(lon_windows) for run in window]:
        parts[n].append((start, grad_tokens[at : at + count]))
        at += count
    for size, out, part in zip(sizes, outs, parts):
        piece = jnp.concatenate([value for _, value in sorted(part, key=lambda item: item[0])], axis=0)
        half = halved(size)
        second = jnp.concatenate([piece[half:], jnp.zeros((2 * half - size, C), f32)], axis=0)
        out[...] = jnp.concatenate([piece[:half], second], axis=1).astype(bf16)
    split_parts((up_grad_ref, down_grad_ref, total_ref), keep_ref, send_ref)


def block_kernel(windows, lon_windows, sizes, *refs):
    ins, refs = refs[:9], refs[9:]
    pieces, (bias_ref, triple_ref, project_ref, up_ref, down_ref) = ins[:4], ins[4:]
    outs, refs = refs[: len(sizes) + 2], refs[len(sizes) + 2 :]
    q, k, v, p, mixed, normed, unit, spread, gsum, up_grad, down_grad, branch, cot, emb, gq, gk, gv, total = refs
    forward_kernel(
        windows, lon_windows, *pieces, bias_ref, triple_ref, project_ref, up_ref, down_ref,
        q, k, v, p, mixed, normed, unit, spread, gsum, up_grad, down_grad, branch, cot, emb,
    )
    windows_back_kernel(windows, q, k, v, p, gsum, project_ref, gq, gk, gv)
    tokens_back_kernel(
        lon_windows, sizes, gq, gk, gv, mixed, normed, unit, spread, gsum, triple_ref, up_grad, down_grad, *outs, total
    )


def block(pieces, bias, triple, project, up, down, lon_windows, sizes):
    count = sum(sizes)
    windows = count // TOK
    out_shape = [shape((halved(size), 2 * C), bf16) for size in sizes] + [
        shape((QUADS * CHUNK, FF), f32),
        shape((QUADS * CHUNK, FF), bf16),
    ]
    rows = [pltpu.VMEM((count, C), dtype) for dtype in (bf16, f32)]
    return pl.pallas_call(
        functools.partial(block_kernel, windows, lon_windows, sizes),
        out_shape=out_shape,
        in_specs=vmem(9),
        out_specs=vmem(len(out_shape)),
        scratch_shapes=rows[:1] * 3
        + [pltpu.VMEM((windows * HEADS, TOK, TOK), bf16)]
        + rows[:1] * 2
        + [rows[1], pltpu.VMEM((count, 1), f32), rows[1]]
        + [pltpu.VMEM((C, FF), f32)] * 2
        + [rows[1], rows[0], rows[1]]
        + rows[:1] * 3
        + [pltpu.VMEM((C, FF), f32)],
        compiler_params=pltpu.CompilerParams(vmem_limit_bytes=32 * MIB),
        cost_estimate=cost(8 * 10**9, 16 * MIB),
        name="block",
    )(*pieces, bias, triple, project, up, down)


def home_kernel(sizes, rows, cols, own_ref, north_ref, side_ref, corner_ref, perm_ref, land_ref, out_ref, sum_ref):
    pieces = []
    for size, ref in zip(sizes, (own_ref, north_ref, side_ref, corner_ref)):
        wide = ref[...].astype(f32)
        pieces += [wide[:, :C], wide[: size - wide.shape[0], C:]]
    pieces = jnp.concatenate(pieces, axis=0).astype(bf16)
    grads = mm(one_hot(perm_ref), pieces)
    out_ref[...] = grads.astype(bf16)
    column = jnp.concatenate([land_column(land_ref, rows, cols)] * Z, axis=0)
    sum_ref[...] = jnp.sum(grads * column, 0, keepdims=True)


def to_home(pieces, land_sea, sizes, rows, cols):
    count = Z * rows * cols
    perm = spots(np.argsort(np.concatenate(piece_rows(rows, cols))))
    return pl.pallas_call(
        functools.partial(home_kernel, sizes, rows, cols),
        out_shape=[shape((count, C), bf16), shape((1, C), f32)],
        in_specs=vmem(6),
        out_specs=vmem(2),
        compiler_params=pltpu.CompilerParams(vmem_limit_bytes=32 * MIB),
        cost_estimate=cost(2 * count * count * C, 4 * MIB),
        name="to_home",
    )(*pieces, perm, land_sea)


def core_add_kernel(keep_ref, got_ref, *refs):
    own_ref, outs = refs[-QUADS], refs[1 - QUADS :]
    total = keep_ref[...] + got_ref[...].astype(f32)
    own_ref[...] = total[:CHUNK]
    for e, out in enumerate(outs, 1):
        out[...] = total[e * CHUNK : (e + 1) * CHUNK].astype(bf16)


def chip_add_kernel(keep_ref, *refs):
    gots, (land_ref, first_ref, second_ref) = refs[:-3], refs[-3:]
    total = keep_ref[...]
    for ref in gots:
        total = total + ref[...].astype(f32)
    land = land_ref[...]
    rest = jnp.concatenate([land[:, 128:], jnp.zeros((1, 2 * 128 - C), f32)], axis=1)
    parts = [total[:, n * 128 : (n + 1) * 128] for n in range(BLOCKS)]
    total = jnp.concatenate(parts + [land[:, :128], rest, jnp.zeros((EXTRA - 2, 128), f32)], axis=0)
    first_ref[...] = total[:FIRST].astype(bf16)
    second_ref[...] = total[FIRST:].astype(bf16)


def add_kernel(one_ref, two_ref, out_ref):
    out_ref[...] = (one_ref[...].astype(f32) + two_ref[...].astype(f32)).astype(bf16)


def join_kernel(*refs):
    refs[-1][...] = jnp.concatenate([ref[...] for ref in refs[:-1]], axis=0)


def small_call(kernel, out_shape, args, name, after=(), scratch=()):
    return pl.pallas_call(
        kernel,
        out_shape=out_shape,
        in_specs=vmem(len(args)) + [pl.BlockSpec(memory_space=pl.ANY)] * len(after),
        out_specs=vmem(len(out_shape)),
        scratch_shapes=scratch,
        compiler_params=pltpu.CompilerParams(vmem_limit_bytes=16 * MIB),
        cost_estimate=cost(10**6, 2 * MIB),
        name=name,
    )(*args, *after)


def finish_kernel(far, chunks_ref, *refs):
    if far:
        before_ref, refs = refs[0], refs[5:]
    outs, land_ref, (up_ref, down_ref, triple_ref, project_ref, lands_ref, sum_ref, sems) = refs[:4], refs[4], refs[5:]
    core, chip, _ = position()
    side = 1 - core if far else core
    for g in range(QUADS):
        tiles = chunks_ref[g * FULL : (g + 1) * FULL, :].astype(f32)
        chunk = jnp.concatenate([tiles[n * CHUNK : (n + 1) * CHUNK] for n in range(BLOCKS)], axis=1)
        block = jnp.bitwise_xor(chip, g)
        rows = chunk_rows(block)
        up_ref[rows, :] = chunk[:PART]
        down_ref[rows, :] = chunk[PART : 2 * PART]
        triple_ref[rows, :] = chunk[2 * PART : CHUNK, : 3 * C]
        project_ref[rows, :] = chunk[2 * PART : CHUNK, 3 * C :]
        lands_ref[pl.ds(pl.multiple_of(block * EXTRA, EXTRA), EXTRA), :] = tiles[BLOCKS * CHUNK :]
    copies = []
    for n, (source, out) in enumerate(zip((triple_ref, project_ref, up_ref, down_ref), outs)):
        rows = pl.ds(pl.multiple_of(side * QUADS * PART, 8), QUADS * PART)
        copies.append(pltpu.make_async_copy(source, out.at[rows, :], sems.at[n]))
    for copy in copies:
        copy.start()
    lands = lands_ref[...]
    lands = [sum(lands[g * EXTRA + n : g * EXTRA + n + 1] for g in range(QUADS)) for n in range(2)]
    land = jnp.concatenate([lands[0], lands[1][:, : C - 128]], axis=1)
    if far:
        sum_ref[...] = land + before_ref[...]
        copies.append(pltpu.make_async_copy(sum_ref, land_ref, sems.at[4]))
        copies[-1].start()
    else:
        land_ref[...] = land
    for copy in copies:
        copy.wait()


def finish(chunks, before=()):
    rows = QUADS * PART
    widths = (3 * C, C, FF, FF)
    hbm = [pl.BlockSpec(memory_space=pltpu.HBM)] * 4
    land, weights = before[4:], before[:4]
    return pl.pallas_call(
        functools.partial(finish_kernel, bool(before)),
        out_shape=[shape((C, width), f32) for width in widths] + [shape((1, C), f32)],
        in_specs=vmem(1 + len(land)) + hbm[: len(weights)],
        out_specs=hbm + (hbm[:1] if before else vmem(1)),
        scratch_shapes=[
            pltpu.VMEM((rows, FF), f32),
            pltpu.VMEM((rows, FF), f32),
            pltpu.VMEM((rows, 3 * C), f32),
            pltpu.VMEM((rows, C), f32),
            pltpu.VMEM((QUADS * EXTRA, 128), f32),
            pltpu.VMEM((1, C), f32),
            pltpu.SemaphoreType.DMA((5,)),
        ],
        input_output_aliases={2 + n: n for n in range(len(weights))},
        compiler_params=pltpu.CompilerParams(vmem_limit_bytes=16 * MIB),
        cost_estimate=cost(10**6, 2 * MIB),
        name="finish_far" if before else "finish_own",
    )(chunks, *land, *weights)


def reduce_all(keep, sent, land, shift, lon_count, after):
    core_move = lambda lon, lat: (lon, lat ^ 1)
    chip_move = lambda e: lambda lon, lat: (lon ^ (e & 1), lat ^ (2 * (e >> 1)))
    deep_move = lambda e: lambda lon, lat: (lon ^ (2 * e), lat)

    def one(rows):
        return [shape((rows, FF), bf16)]

    got = shift(sent, move=core_move)
    parts = [shape((CHUNK, FF), f32)] + one(CHUNK) * (QUADS - 1)
    own, *parts = small_call(core_add_kernel, parts, (keep, got), "core_add", after=after)
    gots = [shift(value, move=chip_move(e)) for e, value in enumerate(parts, 1)]
    sides = [shape((rows, 128), bf16) for rows in (FIRST, FULL - FIRST)]
    totals = small_call(chip_add_kernel, sides, (own, *gots, land), "chip_add")
    steps = [(1, 3), (2, 1)]
    while 2 ** len(steps) < lon_count // 2:
        steps.append((2 ** len(steps),) * 2)
    for step in steps:
        gots = [shift(total, move=deep_move(e)) for total, e in zip(totals, step)]
        totals = [
            small_call(add_kernel, [side], pair, "deep_add")[0] for side, pair in zip(sides, zip(totals, gots))
        ]
    (total,) = small_call(join_kernel, [shape((FULL, 128), bf16)], totals, "deep_join")
    near = [total] + [shift(total, move=chip_move(e)) for e in range(1, QUADS)]
    (total,) = small_call(join_kernel, [shape((QUADS * FULL, 128), bf16)], near, "join")
    got = shift(total, move=core_move)
    return finish(got, finish(total))


AXES = ("deep", "x", "y", "core")


def send(value, lon_count, lat_count, move):
    pairs = []
    for lon in range(lon_count):
        for lat in range(lat_count):
            to_lon, to_lat = move(lon, lat)
            pairs.append((lon * lat_count + lat, (to_lon % lon_count) * lat_count + to_lat % lat_count))
    return lax.ppermute(value, AXES, pairs)


def body(
    lon_count, lat_count,
    tokens, cotangent, land_sea, land_vector, triple_weight, project_weight, up_weight, down_weight, earth_bias,
):
    levels, rows, cols, features = tokens.shape
    shift = functools.partial(send, lon_count=lon_count, lat_count=lat_count)
    lon_windows = cols // WW

    own, north, side, corner = pack(tokens, cotangent, land_sea, land_vector, rows, cols)
    north = shift(north, move=lambda lon, lat: (lon, lat + 1))
    side = shift(side, move=lambda lon, lat: (lon + 1, lat))
    corner = shift(corner, move=lambda lon, lat: (lon + 1, lat + 1))
    bias = expand_bias(earth_bias)

    sizes = [part.size for part in piece_rows(rows, cols)]
    pieces = (own, north, side, corner)
    own, north, side, corner, keep, sent = block(
        pieces, bias, triple_weight, project_weight, up_weight, down_weight.T, lon_windows, sizes
    )
    north = shift(north, move=lambda lon, lat: (lon, lat - 1))
    side = shift(side, move=lambda lon, lat: (lon - 1, lat))
    corner = shift(corner, move=lambda lon, lat: (lon - 1, lat - 1))
    after = (north, side, corner)
    grad_tokens, land = to_home((own, north, side, corner), land_sea, sizes, rows, cols)
    triple, project, up, down, land = reduce_all(keep, sent, land, shift, lon_count, after)
    return grad_tokens.reshape(tokens.shape), triple, project, up, down.T, land.reshape(features)


def solution(mesh):
    lon_count, lat_count = mesh.shape["lon"], mesh.shape["lat"]
    fine = jax.sharding.Mesh(mesh.devices.reshape(lon_count // 2, 2, lat_count // 2, 2), AXES)
    lon, lat = AXES[:2], AXES[2:]
    return jax.shard_map(
        functools.partial(body, lon_count, lat_count),
        mesh=fine,
        in_specs=(
            P(None, lat, lon, None),
            P(None, lat, lon, None),
            P(lat, lon),
            P(),
            P(),
            P(),
            P(),
            P(),
            P(lat, None, None, None, None),
        ),
        out_specs=(P(None, lat, lon, None), P(), P(), P(), P(), P()),
        check_vma=False,
    )
```

```python
import functools
import math

import jax
import jax.numpy as jnp
import numpy as np
from jax import lax
from jax.experimental import pallas as pl
from jax.experimental.pallas import tpu as pltpu
from jax.sharding import PartitionSpec as P

Z = 4
WZ = 2
WH = 6
WW = 12
C = 192
HEADS = 6
HEAD = 32
FF = 768
HZ, HH, HW = WZ // 2, WH // 2, WW // 2
TOK = WZ * WH * WW
PLACES = WZ * WH
RELW = 2 * WW - 1
SPOTS = PLACES // 2
STRIP = -(-RELW * SPOTS // 128) * 128
RUN, SHORT = WW * SPOTS, (WW - HW) * SPOTS

mask_fill = -10000.0
norm_eps = 1e-05
log2e = 1.4426950408889634
root_half = 0.7071067811865476
inv_root_tau = 0.3989422804014327
score_scale = HEAD**-0.5

f32 = jnp.float32
bf16 = jnp.bfloat16
MIB = 1 << 20

QUADS = 4
PART = C // (2 * QUADS)
CHUNK = 3 * PART
BLOCKS = FF // 128
EXTRA = 8
FULL = BLOCKS * CHUNK + EXTRA


def mm(a, b):
    return lax.dot_general(a, b, (((1,), (0,)), ((), ())), preferred_element_type=f32)


def mm_nt(a, b):
    return lax.dot_general(a, b, (((1,), (1,)), ((), ())), preferred_element_type=f32)


def mm_tn(a, b):
    return lax.dot_general(a, b, (((0,), (0,)), ((), ())), preferred_element_type=f32)


def unit_norm(values):
    average = jnp.mean(values, -1, keepdims=True)
    centred = values - average
    variance = jnp.mean(centred * centred, -1, keepdims=True)
    spread = lax.rsqrt(variance + norm_eps)
    return centred * spread, spread


def norm_back(upstream, unit, spread):
    first = jnp.mean(upstream, -1, keepdims=True)
    second = jnp.mean(upstream * unit, -1, keepdims=True)
    return spread * (upstream - first - unit * second)


def piece_rows(rows, cols):
    home = np.arange(Z * rows * cols).reshape(Z, rows, cols)

    def run(level, row, col, width):
        levels = [(level * WZ + z - HZ) % Z for z in range(WZ)]
        return home[levels, row : row + HH, col : col + width].transpose(2, 0, 1).reshape(-1)

    levels = range(Z // WZ)
    parts = []
    for row in (0, rows - HH):
        whole = [run(a, row, w * WW - HW, WW) for w in range(1, cols // WW) for a in levels]
        parts.append(np.concatenate(whole + [run(a, row, 0, WW - HW) for a in levels]))
    for row in (0, rows - HH):
        parts.append(np.concatenate([run(a, row, cols - HW, HW) for a in levels]))
    return parts


def window_runs(lon_windows):
    levels = Z // WZ
    whole = (lon_windows - 1) * levels
    runs = [[(1, n * RUN, RUN), (0, n * RUN, RUN)] for n in range(whole)]
    for a in range(levels):
        inner = whole * RUN + a * SHORT
        west = (a * (RUN - SHORT), RUN - SHORT)
        runs.append([(3, *west), (1, inner, SHORT), (2, *west), (0, inner, SHORT)])
    return runs


def spots(places):
    return jnp.asarray(np.argsort(places).astype(np.int32)[None])


def one_hot(spot_ref):
    count = spot_ref.shape[1]
    rows = lax.broadcasted_iota(jnp.int32, (count, count), 0)
    return (rows == spot_ref[...]).astype(f32).astype(bf16)


def vmem(count):
    return [pl.BlockSpec(memory_space=pltpu.VMEM)] * count


def shape(dims, dtype):
    return jax.ShapeDtypeStruct(dims, dtype)


def cost(flops, moved):
    return pl.CostEstimate(flops=flops, bytes_accessed=moved, transcendentals=0)


def land_column(land_ref, rows, cols):
    eye = (
        lax.broadcasted_iota(jnp.int32, (cols, cols), 0)
        == lax.broadcasted_iota(jnp.int32, (cols, cols), 1)
    ).astype(f32)
    land = land_ref[...].astype(f32)
    parts = [jnp.sum(eye * land[i : i + 1, :], -1, keepdims=True) for i in range(rows)]
    return jnp.concatenate(parts, axis=0)


def pack_kernel(rows, cols, *refs):
    sources, outs, (tokens_ref, cot_ref, land_ref, vec_ref, perm_ref, sems) = refs[:5], refs[5:-6], refs[-6:]
    copies = [
        pltpu.make_async_copy(source, target, sems.at[n])
        for n, (source, target) in enumerate(zip(sources, (tokens_ref, cot_ref, land_ref, vec_ref, perm_ref)))
    ]
    for copy in copies:
        copy.start()
    for copy in copies:
        copy.wait()
    column = land_column(land_ref, rows, cols)
    added = column * vec_ref[...]
    added = jnp.concatenate([added] * Z, axis=0)
    embedded = (tokens_ref[...].astype(f32) + added).astype(bf16)
    perm = one_hot(perm_ref)
    left = mm(perm, embedded)
    right = mm(perm, cot_ref[...])
    packed = jnp.concatenate([left, right], axis=1)
    start = 0
    for out in outs:
        out[...] = packed[start : start + out.shape[0]].astype(bf16)
        start += out.shape[0]


def pack(tokens, cotangent, land_sea, vector, rows, cols):
    parts = piece_rows(rows, cols)
    perm = spots(np.concatenate(parts))
    count = Z * rows * cols
    return pl.pallas_call(
        functools.partial(pack_kernel, rows, cols),
        out_shape=[shape((part.size, 2 * C), bf16) for part in parts],
        in_specs=[pl.BlockSpec(memory_space=pltpu.HBM)] * 5,
        out_specs=vmem(4),
        scratch_shapes=[
            pltpu.VMEM((count, C), bf16),
            pltpu.VMEM((count, C), bf16),
            pltpu.VMEM((rows, cols), jnp.int32),
            pltpu.VMEM((1, C), f32),
            pltpu.VMEM((1, count), jnp.int32),
            pltpu.SemaphoreType.DMA((5,)),
        ],
        cost_estimate=cost(4 * count * count * C, 4 * MIB),
        name="pack",
    )(tokens.reshape(count, C), cotangent.reshape(count, C), land_sea, vector.reshape(1, C), perm)


def floor_div(values, divisor):
    return (values * (65536 // divisor + 1)) >> 16


def remainder(values, divisor):
    return values - floor_div(values, divisor) * divisor


def place_order(order):
    half = floor_div(order, SPOTS)
    spot = order - half * SPOTS
    level = floor_div(spot, HH)
    return level * WH + half * HH + (spot - level * HH)


def bias_kernel(levels, table_ref, out_ref, *wide_refs):
    groups = levels * HEADS
    pairs = PLACES * PLACES
    row = lax.broadcasted_iota(jnp.int32, (HEADS * RELW, HEADS * STRIP), 0)
    lane = lax.broadcasted_iota(jnp.int32, (HEADS * RELW, HEADS * STRIP), 1)
    head = floor_div(row, RELW)
    ahead = lane - (head * STRIP + (RELW - 1 - (row - head * RELW)) * SPOTS)
    onehot = ((ahead >= 0) & (ahead < SPOTS)).astype(f32).astype(bf16)
    row = lax.broadcasted_iota(jnp.int32, (pairs, pairs), 0)
    source = place_order(floor_div(row, PLACES)) * PLACES + remainder(row, PLACES)
    reorder = (lax.broadcasted_iota(jnp.int32, (pairs, pairs), 1) == source).astype(f32).astype(bf16)
    for level in range(levels):
        table = table_ref[:, level, :].T
        high = table.astype(bf16)
        rest = (table - high.astype(f32)).astype(bf16)
        wide = mm(mm(reorder, high).astype(bf16), onehot) + mm(mm(reorder, rest).astype(bf16), onehot)
        for head in range(HEADS):
            for n, wide_ref in enumerate(wide_refs):
                start = head * STRIP + n * 128
                wide_ref[(level * HEADS + head) * pairs : (level * HEADS + head + 1) * pairs, :] = wide[:, start : start + 128]
    strips = groups * PLACES
    row = lax.broadcasted_iota(jnp.int32, (strips, STRIP), 0)
    spot = remainder(lax.broadcasted_iota(jnp.int32, (strips, STRIP), 1), SPOTS)
    own = remainder(row, PLACES)
    first_level = (row < HEADS * PLACES).astype(jnp.int32)
    own_north = (own < SPOTS).astype(jnp.int32)
    own_low = (own - SPOTS * (1 - own_north) < HZ * HH).astype(jnp.int32)
    low = (spot < HZ * HH).astype(jnp.int32)
    pole = (lax.axis_index("y") + lax.axis_index("core") == 0).astype(jnp.int32)
    halves = []
    for half in range(2):
        parts = []
        for n, wide_ref in enumerate(wide_refs):
            here = spot[:, n * 128 : (n + 1) * 128]
            part = jnp.zeros((strips, 128), f32)
            for p in range(SPOTS):
                place = p // HH * WH + half * HH + p % HH
                part = jnp.where(here == p, wide_ref[pl.ds(place, strips, stride=PLACES), :], part)
            parts.append(part)
        strip = jnp.concatenate(parts, axis=1)
        differs = first_level * (own_low ^ low) + pole * (own_north ^ (1 - half))
        halves.append(jnp.where(differs > 0, strip + mask_fill, strip) * log2e)
    for w in range(WW):
        start = (WW - 1 - w) * SPOTS
        part = jnp.concatenate([strip[:, start : start + RUN] for strip in halves], axis=1)
        for g in range(groups):
            for half in range(2):
                rows = part[g * PLACES + half * SPOTS : g * PLACES + (half + 1) * SPOTS, :]
                out_ref[g, half * RUN + w * SPOTS : half * RUN + (w + 1) * SPOTS, :] = rows


def expand_bias(table):
    levels = table.shape[1]
    groups = levels * HEADS
    pairs = PLACES * PLACES
    flat = table[0].transpose(1, 3, 0, 2).reshape(HEADS * RELW, levels, pairs)
    return pl.pallas_call(
        functools.partial(bias_kernel, levels),
        out_shape=shape((groups, TOK, TOK), f32),
        in_specs=vmem(1),
        out_specs=vmem(1)[0],
        scratch_shapes=[pltpu.VMEM((groups * pairs, 128), f32)] * (STRIP // 128),
        compiler_params=pltpu.CompilerParams(vmem_limit_bytes=28 * MIB),
        cost_estimate=cost(10**9, 8 * MIB),
        name="bias",
    )(flat)


def head_masks(count):
    lane = lax.broadcasted_iota(jnp.int32, (count, C), 1)
    return [((lane >= h * HEAD) & (lane < (h + 1) * HEAD)).astype(f32) for h in range(HEADS)]


def stacked(values, masks):
    return jnp.concatenate([values * mask for mask in masks], axis=0)


def head_sum(values, masks):
    total = values[:TOK] * masks[0]
    for h in range(1, HEADS):
        total = total + values[h * TOK : (h + 1) * TOK] * masks[h]
    return total


def position():
    return lax.axis_index("core"), lax.axis_index("y") * 2 + lax.axis_index("x"), lax.axis_index("deep")


def chunk_rows(block):
    return pl.ds(pl.multiple_of(block * PART, PART), PART)


def split_parts(total_refs, keep_ref, send_ref):
    core, chip, _ = position()
    for out, side in ((keep_ref, core), (send_ref, 1 - core)):
        parts = []
        for g in range(QUADS):
            rows = chunk_rows(side * QUADS + jnp.bitwise_xor(chip, g))
            parts += [ref[rows, :] for ref in total_refs]
        out[...] = jnp.concatenate(parts, axis=0).astype(out.dtype)


def attend(first, runs, pieces, bias_ref, triple_ref, project_ref, *refs):
    q_ref, k_ref, v_ref, p_ref, mixed_ref, normed_ref, unit_ref, spread_ref, summed_ref, cot_ref = refs
    pieces = [piece.astype(f32) for piece in pieces]
    ordered = jnp.concatenate([pieces[n][start : start + count] for n, start, count in runs], axis=0)
    emb = ordered[:, :C]
    cot_ref[...] = ordered[:, C:].astype(bf16)
    unit, spread = unit_norm(emb)
    unit_ref[...] = unit
    spread_ref[...] = spread
    normed = unit.astype(bf16)
    normed_ref[...] = normed
    packed = mm(normed, triple_ref[...])
    q_ref[...] = packed[:, :C].astype(bf16)
    k_ref[...] = packed[:, C : 2 * C].astype(bf16)
    v_ref[...] = packed[:, 2 * C :].astype(bf16)
    masks = head_masks(TOK)
    masks_b = [mask.astype(bf16) for mask in masks]
    for w in range(emb.shape[0] // TOK):
        rows = slice(w * TOK, (w + 1) * TOK)
        heads = slice(w * HEADS, (w + 1) * HEADS)
        level = (first + w) % (Z // WZ)
        scores = mm_nt(stacked(q_ref[rows, :], masks_b), k_ref[rows, :])
        bias = bias_ref[level * HEADS : (level + 1) * HEADS].reshape(HEADS * TOK, TOK)
        raised = jnp.exp2(scores * (score_scale * log2e) + bias)
        probs = raised * (1.0 / jnp.sum(raised, -1, keepdims=True))
        probs_b = probs.astype(bf16)
        p_ref[heads] = probs_b.reshape(HEADS, TOK, TOK)
        mixed = head_sum(mm(probs_b, v_ref[rows, :]), masks).astype(bf16)
        mixed_ref[rows, :] = mixed
        summed_ref[rows, :] = emb[rows] + mm(mixed, project_ref[...]).astype(bf16).astype(f32)


def feed_back(summed, cot, up_ref, down_ref, gsum_ref, up_grad_ref, down_grad_ref):
    unit2, spread2 = unit_norm(summed)
    normed2 = unit2.astype(bf16)
    back = jnp.zeros(unit2.shape, f32)
    block = 256
    for start in range(0, FF, block):
        cols = slice(start, start + block)
        up_part = up_ref[:, cols]
        pre = mm(normed2, up_part)
        upstream = mm(cot, down_ref[:, cols])
        phi = 0.5 * (1.0 + lax.erf(pre * root_half))
        activated = (pre * phi).astype(bf16)
        slope = phi + pre * inv_root_tau * jnp.exp2(pre * pre * (-0.5 * log2e))
        hidden = (upstream * slope).astype(bf16)
        up_grad_ref[:, cols] = mm_tn(normed2, hidden)
        down_grad_ref[:, cols] = mm_tn(cot, activated)
        back = back + mm_nt(hidden, up_part)
    gsum_ref[...] = cot.astype(f32) + norm_back(back, unit2, spread2)


def attend_back(at, q_ref, k_ref, v_ref, p_ref, gsum_ref, project_ref, gq_ref, gk_ref, gv_ref):
    masks = head_masks(TOK)
    masks_b = [mask.astype(bf16) for mask in masks]
    for w in range(q_ref.shape[0] // TOK):
        rows = slice(w * TOK, (w + 1) * TOK)
        full_rows = slice(at + w * TOK, at + (w + 1) * TOK)
        grad = gsum_ref[full_rows, :].astype(bf16)
        grad_mixed_b = mm_nt(grad, project_ref[...]).astype(bf16)
        probs_b = p_ref[w * HEADS : (w + 1) * HEADS].reshape(HEADS * TOK, TOK)
        probs = probs_b.astype(f32)
        grad_probs = mm_nt(stacked(grad_mixed_b, masks_b), v_ref[rows, :])
        inner = jnp.sum(grad_probs * probs, -1, keepdims=True)
        scaled = (probs * (grad_probs - inner) * score_scale).astype(bf16)
        grad_q = head_sum(mm(scaled, k_ref[rows, :]), masks)
        grad_mixed_t = grad_mixed_b.astype(f32).T.astype(bf16)
        query_t = q_ref[rows, :].astype(f32).T.astype(bf16)
        grad_k, grad_v = [], []
        for h in range(HEADS):
            spot = slice(h * HEAD, (h + 1) * HEAD)
            span = slice(h * TOK, (h + 1) * TOK)
            grad_k.append(mm(query_t[spot], scaled[span]))
            grad_v.append(mm(grad_mixed_t[spot], probs_b[span]))
        gq_ref[full_rows, :] = grad_q.astype(bf16)
        gk_ref[full_rows, :] = jnp.concatenate(grad_k, axis=0).T.astype(bf16)
        gv_ref[full_rows, :] = jnp.concatenate(grad_v, axis=0).T.astype(bf16)


def halved(rows):
    return -(-rows // 16) * 8


def tokens_back(
    lon_windows, sizes, gq_ref, gk_ref, gv_ref, mixed, normed, unit, spread, gsum_ref, triple_ref, up_grad_ref, down_grad_ref,
    *rest,
):
    outs, (keep_ref, send_ref, total_ref) = rest[: len(sizes)], rest[len(sizes) :]
    triple = triple_ref[...]
    grad_normed = jnp.zeros(unit.shape, f32)
    parts = []
    for n, ref in enumerate((gq_ref, gk_ref, gv_ref)):
        grad = ref[...]
        grad_normed = grad_normed + mm_nt(grad, triple[:, n * C : (n + 1) * C])
        parts.append(mm_tn(normed, grad))
    parts.append(mm_tn(mixed, gsum_ref[...].astype(bf16)))
    total_ref[...] = jnp.concatenate(parts, axis=1)
    grad_normed = grad_normed.astype(bf16).astype(f32)
    grad_tokens = gsum_ref[...] + norm_back(grad_normed, unit, spread)
    parts, at = [[] for _ in sizes], 0
    for n, start, count in [run for window in window_runs(lon_windows) for run in window]:
        parts[n].append((start, grad_tokens[at : at + count]))
        at += count
    for size, out, part in zip(sizes, outs, parts):
        piece = jnp.concatenate([value for _, value in sorted(part, key=lambda item: item[0])], axis=0)
        half = halved(size)
        second = jnp.concatenate([piece[half:], jnp.zeros((2 * half - size, C), f32)], axis=0)
        out[...] = jnp.concatenate([piece[:half], second], axis=1).astype(bf16)
    split_parts((up_grad_ref, down_grad_ref, total_ref), keep_ref, send_ref)


def saved_shapes(count):
    dims = [((count, C), bf16)] * 3 + [((count // TOK * HEADS, TOK, TOK), bf16)] + [((count, C), bf16)] * 2
    return dims + [((count, C), f32), ((count, 1), f32), ((count, C), f32), ((count, C), bf16)]


SAVED = len(saved_shapes(TOK))


def split_runs(lon_windows):
    windows = window_runs(lon_windows)
    whole = (lon_windows - 1) * (Z // WZ)
    return whole, *[[run for window in part for run in window] for part in (windows[:whole], windows[whole:])]


def near_kernel(lon_windows, own_ref, north_ref, *refs):
    runs = split_runs(lon_windows)[1]
    attend(0, runs, (own_ref[...], north_ref[...]), *refs)


def near_block(own, north, bias, triple, project, lon_windows):
    count = split_runs(lon_windows)[0] * TOK
    return pl.pallas_call(
        functools.partial(near_kernel, lon_windows),
        out_shape=[shape(*dims) for dims in saved_shapes(count)],
        in_specs=vmem(5),
        out_specs=vmem(SAVED),
        compiler_params=pltpu.CompilerParams(vmem_limit_bytes=24 * MIB),
        cost_estimate=cost(3 * 10**9, 8 * MIB),
        name="near_block",
    )(own, north, bias, triple, project)


def block_kernel(lon_windows, sizes, *refs):
    whole, _, runs = split_runs(lon_windows)
    pieces, refs = refs[:4], refs[4:]
    (bias_ref, triple_ref, project_ref, up_ref, down_ref), refs = refs[:5], refs[5:]
    near, refs = refs[:SAVED], refs[SAVED:]
    outs, refs = refs[: len(sizes) + 2], refs[len(sizes) + 2 :]
    far, (gsum, up_grad, down_grad, gq, gk, gv, total) = refs[:SAVED], refs[SAVED:]
    attend(whole, runs, [ref[...] for ref in pieces], bias_ref, triple_ref, project_ref, *far)
    mixed, normed, unit, spread, summed, cot = [
        jnp.concatenate([one[...], other[...]], axis=0) for one, other in zip(near[4:], far[4:])
    ]
    feed_back(summed, cot, up_ref, down_ref, gsum, up_grad, down_grad)
    attend_back(0, *near[:4], gsum, project_ref, gq, gk, gv)
    attend_back(whole * TOK, *far[:4], gsum, project_ref, gq, gk, gv)
    tokens_back(lon_windows, sizes, gq, gk, gv, mixed, normed, unit, spread, gsum, triple_ref, up_grad, down_grad, *outs, total)


def block(pieces, bias, triple, project, up, down, near, lon_windows, sizes):
    count = sum(sizes)
    out_shape = [shape((halved(size), 2 * C), bf16) for size in sizes] + [
        shape((QUADS * CHUNK, FF), f32),
        shape((QUADS * CHUNK, FF), bf16),
    ]
    return pl.pallas_call(
        functools.partial(block_kernel, lon_windows, sizes),
        out_shape=out_shape,
        in_specs=vmem(9 + SAVED),
        out_specs=vmem(len(out_shape)),
        scratch_shapes=[pltpu.VMEM(*dims) for dims in saved_shapes(count - near[0].shape[0])]
        + [pltpu.VMEM((count, C), f32)]
        + [pltpu.VMEM((C, FF), f32)] * 2
        + [pltpu.VMEM((count, C), bf16)] * 3
        + [pltpu.VMEM((C, FF), f32)],
        compiler_params=pltpu.CompilerParams(vmem_limit_bytes=28 * MIB),
        cost_estimate=cost(8 * 10**9, 16 * MIB),
        name="block",
    )(*pieces, bias, triple, project, up, down, *near)


def home_kernel(sizes, rows, cols, own_ref, north_ref, side_ref, corner_ref, perm_ref, land_ref, out_ref, sum_ref):
    pieces = []
    for size, ref in zip(sizes, (own_ref, north_ref, side_ref, corner_ref)):
        wide = ref[...].astype(f32)
        pieces += [wide[:, :C], wide[: size - wide.shape[0], C:]]
    pieces = jnp.concatenate(pieces, axis=0).astype(bf16)
    grads = mm(one_hot(perm_ref), pieces)
    out_ref[...] = grads.astype(bf16)
    column = jnp.concatenate([land_column(land_ref, rows, cols)] * Z, axis=0)
    sum_ref[...] = jnp.sum(grads * column, 0, keepdims=True)


def to_home(pieces, land_sea, sizes, rows, cols):
    count = Z * rows * cols
    perm = spots(np.argsort(np.concatenate(piece_rows(rows, cols))))
    return pl.pallas_call(
        functools.partial(home_kernel, sizes, rows, cols),
        out_shape=[shape((count, C), bf16), shape((1, C), f32)],
        in_specs=vmem(6),
        out_specs=vmem(2),
        compiler_params=pltpu.CompilerParams(vmem_limit_bytes=32 * MIB),
        cost_estimate=cost(2 * count * count * C, 4 * MIB),
        name="to_home",
    )(*pieces, perm, land_sea)


def core_add_kernel(keep_ref, got_ref, *refs):
    own_ref, outs = refs[-QUADS], refs[1 - QUADS :]
    total = keep_ref[...] + got_ref[...].astype(f32)
    own_ref[...] = total[:CHUNK]
    for e, out in enumerate(outs, 1):
        out[...] = total[e * CHUNK : (e + 1) * CHUNK].astype(bf16)


def chip_add_kernel(keep_ref, *refs):
    gots, (land_ref, out_ref) = refs[:-2], refs[-2:]
    total = keep_ref[...]
    for ref in gots:
        total = total + ref[...].astype(f32)
    land = land_ref[...]
    rest = jnp.concatenate([land[:, 128:], jnp.zeros((1, 2 * 128 - C), f32)], axis=1)
    parts = [total[:, n * 128 : (n + 1) * 128] for n in range(BLOCKS)]
    total = jnp.concatenate(parts + [land[:, :128], rest, jnp.zeros((EXTRA - 2, 128), f32)], axis=0)
    out_ref[...] = total.astype(bf16)


def add_kernel(one_ref, two_ref, out_ref):
    out_ref[...] = (one_ref[...].astype(f32) + two_ref[...].astype(f32)).astype(bf16)


def join_kernel(*refs):
    refs[-1][...] = jnp.concatenate([ref[...] for ref in refs[:-1]], axis=0)


def small_call(kernel, out_shape, args, name, after=(), scratch=()):
    return pl.pallas_call(
        kernel,
        out_shape=out_shape,
        in_specs=vmem(len(args)) + [pl.BlockSpec(memory_space=pl.ANY)] * len(after),
        out_specs=vmem(len(out_shape)),
        scratch_shapes=scratch,
        compiler_params=pltpu.CompilerParams(vmem_limit_bytes=16 * MIB),
        cost_estimate=cost(10**6, 2 * MIB),
        name=name,
    )(*args, *after)


def finish_kernel(far, chunks_ref, *refs):
    if far:
        before_ref, refs = refs[0], refs[5:]
    outs, land_ref, (up_ref, down_ref, triple_ref, project_ref, lands_ref, sum_ref, sems) = refs[:4], refs[4], refs[5:]
    core, chip, _ = position()
    side = 1 - core if far else core
    for g in range(QUADS):
        tiles = chunks_ref[g * FULL : (g + 1) * FULL, :].astype(f32)
        chunk = jnp.concatenate([tiles[n * CHUNK : (n + 1) * CHUNK] for n in range(BLOCKS)], axis=1)
        block = jnp.bitwise_xor(chip, g)
        rows = chunk_rows(block)
        up_ref[rows, :] = chunk[:PART]
        down_ref[rows, :] = chunk[PART : 2 * PART]
        triple_ref[rows, :] = chunk[2 * PART : CHUNK, : 3 * C]
        project_ref[rows, :] = chunk[2 * PART : CHUNK, 3 * C :]
        lands_ref[pl.ds(pl.multiple_of(block * EXTRA, EXTRA), EXTRA), :] = tiles[BLOCKS * CHUNK :]
    copies = []
    for n, (source, out) in enumerate(zip((triple_ref, project_ref, up_ref, down_ref), outs)):
        rows = pl.ds(pl.multiple_of(side * QUADS * PART, 8), QUADS * PART)
        copies.append(pltpu.make_async_copy(source, out.at[rows, :], sems.at[n]))
    for copy in copies:
        copy.start()
    lands = lands_ref[...]
    lands = [sum(lands[g * EXTRA + n : g * EXTRA + n + 1] for g in range(QUADS)) for n in range(2)]
    land = jnp.concatenate([lands[0], lands[1][:, : C - 128]], axis=1)
    if far:
        sum_ref[...] = land + before_ref[...]
        copies.append(pltpu.make_async_copy(sum_ref, land_ref, sems.at[4]))
        copies[-1].start()
    else:
        land_ref[...] = land
    for copy in copies:
        copy.wait()


def finish(chunks, before=()):
    rows = QUADS * PART
    widths = (3 * C, C, FF, FF)
    hbm = [pl.BlockSpec(memory_space=pltpu.HBM)] * 4
    land, weights = before[4:], before[:4]
    return pl.pallas_call(
        functools.partial(finish_kernel, bool(before)),
        out_shape=[shape((C, width), f32) for width in widths] + [shape((1, C), f32)],
        in_specs=vmem(1 + len(land)) + hbm[: len(weights)],
        out_specs=hbm + (hbm[:1] if before else vmem(1)),
        scratch_shapes=[
            pltpu.VMEM((rows, FF), f32),
            pltpu.VMEM((rows, FF), f32),
            pltpu.VMEM((rows, 3 * C), f32),
            pltpu.VMEM((rows, C), f32),
            pltpu.VMEM((QUADS * EXTRA, 128), f32),
            pltpu.VMEM((1, C), f32),
            pltpu.SemaphoreType.DMA((5,)),
        ],
        input_output_aliases={2 + n: n for n in range(len(weights))},
        compiler_params=pltpu.CompilerParams(vmem_limit_bytes=16 * MIB),
        cost_estimate=cost(10**6, 2 * MIB),
        name="finish_far" if before else "finish_own",
    )(chunks, *land, *weights)


def reduce_all(keep, sent, land, shift, lon_count, after):
    core_move = lambda lon, lat: (lon, lat ^ 1)
    chip_move = lambda e: lambda lon, lat: (lon ^ (e & 1), lat ^ (2 * (e >> 1)))
    deep_move = lambda e: lambda lon, lat: (lon ^ (2 * e), lat)

    def one(rows):
        return [shape((rows, FF), bf16)]

    got = shift(sent, move=core_move)
    parts = [shape((CHUNK, FF), f32)] + one(CHUNK) * (QUADS - 1)
    own, *parts = small_call(core_add_kernel, parts, (keep, got), "core_add", after=after)
    gots = [shift(value, move=chip_move(e)) for e, value in enumerate(parts, 1)]
    full = [shape((FULL, 128), bf16)]
    (total,) = small_call(chip_add_kernel, full, (own, *gots, land), "chip_add")
    reach = 1
    while reach < lon_count // 2:
        got = shift(total, move=deep_move(reach))
        reach *= 2
        (total,) = small_call(add_kernel, full, (total, got), "deep_add")
    near = [total] + [shift(total, move=chip_move(e)) for e in range(1, QUADS)]
    (total,) = small_call(join_kernel, [shape((QUADS * FULL, 128), bf16)], near, "join")
    got = shift(total, move=core_move)
    return finish(got, finish(total))


AXES = ("deep", "x", "y", "core")


def send(value, lon_count, lat_count, move):
    pairs = []
    for lon in range(lon_count):
        for lat in range(lat_count):
            to_lon, to_lat = move(lon, lat)
            pairs.append((lon * lat_count + lat, (to_lon % lon_count) * lat_count + to_lat % lat_count))
    return lax.ppermute(value, AXES, pairs)


def body(
    lon_count, lat_count,
    tokens, cotangent, land_sea, land_vector, triple_weight, project_weight, up_weight, down_weight, earth_bias,
):
    levels, rows, cols, features = tokens.shape
    shift = functools.partial(send, lon_count=lon_count, lat_count=lat_count)
    lon_windows = cols // WW

    own, north, side, corner = pack(tokens, cotangent, land_sea, land_vector, rows, cols)
    north = shift(north, move=lambda lon, lat: (lon, lat + 1))
    side = shift(side, move=lambda lon, lat: (lon + 1, lat))
    corner = shift(corner, move=lambda lon, lat: (lon + 1, lat + 1))
    bias = expand_bias(earth_bias)

    sizes = [part.size for part in piece_rows(rows, cols)]
    pieces = (own, north, side, corner)
    near = near_block(own, north, bias, triple_weight, project_weight, lon_windows)
    own, north, side, corner, keep, sent = block(
        pieces, bias, triple_weight, project_weight, up_weight, down_weight.T, near, lon_windows, sizes
    )
    north = shift(north, move=lambda lon, lat: (lon, lat - 1))
    side = shift(side, move=lambda lon, lat: (lon - 1, lat))
    corner = shift(corner, move=lambda lon, lat: (lon - 1, lat - 1))
    after = (north, side, corner)
    grad_tokens, land = to_home((own, north, side, corner), land_sea, sizes, rows, cols)
    triple, project, up, down, land = reduce_all(keep, sent, land, shift, lon_count, after)
    return grad_tokens.reshape(tokens.shape), triple, project, up, down.T, land.reshape(features)


def solution(mesh):
    lon_count, lat_count = mesh.shape["lon"], mesh.shape["lat"]
    fine = jax.sharding.Mesh(mesh.devices.reshape(lon_count // 2, 2, lat_count // 2, 2), AXES)
    lon, lat = AXES[:2], AXES[2:]
    return jax.shard_map(
        functools.partial(body, lon_count, lat_count),
        mesh=fine,
        in_specs=(
            P(None, lat, lon, None),
            P(None, lat, lon, None),
            P(lat, lon),
            P(),
            P(),
            P(),
            P(),
            P(),
            P(lat, None, None, None, None),
        ),
        out_specs=(P(None, lat, lon, None), P(), P(), P(), P(), P()),
        check_vma=False,
    )
```

```python
import functools
import math

import jax
import jax.numpy as jnp
import numpy as np
from jax import lax
from jax.experimental import pallas as pl
from jax.experimental.pallas import tpu as pltpu
from jax.sharding import PartitionSpec as P

Z = 4
WZ = 2
WH = 6
WW = 12
C = 192
HEADS = 6
HEAD = 32
FF = 768
HZ, HH, HW = WZ // 2, WH // 2, WW // 2
TOK = WZ * WH * WW
PLACES = WZ * WH
RELW = 2 * WW - 1
SPOTS = PLACES // 2
STRIP = -(-RELW * SPOTS // 128) * 128
RUN, SHORT = WW * SPOTS, (WW - HW) * SPOTS

mask_fill = -10000.0
norm_eps = 1e-05
log2e = 1.4426950408889634
root_half = 0.7071067811865476
inv_root_tau = 0.3989422804014327
score_scale = HEAD**-0.5

f32 = jnp.float32
bf16 = jnp.bfloat16
MIB = 1 << 20

QUADS = 4
PART = C // (2 * QUADS)
CHUNK = 3 * PART
BLOCKS = FF // 128
EXTRA = 8
FULL = BLOCKS * CHUNK + EXTRA


def mm(a, b):
    return lax.dot_general(a, b, (((1,), (0,)), ((), ())), preferred_element_type=f32)


def mm_nt(a, b):
    return lax.dot_general(a, b, (((1,), (1,)), ((), ())), preferred_element_type=f32)


def mm_tn(a, b):
    return lax.dot_general(a, b, (((0,), (0,)), ((), ())), preferred_element_type=f32)


def unit_norm(values):
    average = jnp.mean(values, -1, keepdims=True)
    centred = values - average
    variance = jnp.mean(centred * centred, -1, keepdims=True)
    spread = lax.rsqrt(variance + norm_eps)
    return centred * spread, spread


def norm_back(upstream, unit, spread):
    first = jnp.mean(upstream, -1, keepdims=True)
    second = jnp.mean(upstream * unit, -1, keepdims=True)
    return spread * (upstream - first - unit * second)


def piece_rows(rows, cols):
    home = np.arange(Z * rows * cols).reshape(Z, rows, cols)

    def run(level, row, col, width):
        levels = [(level * WZ + z - HZ) % Z for z in range(WZ)]
        return home[levels, row : row + HH, col : col + width].transpose(2, 0, 1).reshape(-1)

    levels = range(Z // WZ)
    parts = []
    for row in (0, rows - HH):
        whole = [run(a, row, w * WW - HW, WW) for w in range(1, cols // WW) for a in levels]
        parts.append(np.concatenate(whole + [run(a, row, 0, WW - HW) for a in levels]))
    for row in (0, rows - HH):
        parts.append(np.concatenate([run(a, row, cols - HW, HW) for a in levels]))
    return parts


def window_runs(lon_windows):
    levels = Z // WZ
    whole = (lon_windows - 1) * levels
    runs = [[(1, n * RUN, RUN), (0, n * RUN, RUN)] for n in range(whole)]
    for a in range(levels):
        inner = whole * RUN + a * SHORT
        west = (a * (RUN - SHORT), RUN - SHORT)
        runs.append([(3, *west), (1, inner, SHORT), (2, *west), (0, inner, SHORT)])
    return runs


def spots(places):
    return jnp.asarray(np.argsort(places).astype(np.int32)[None])


def one_hot(spot_ref):
    count = spot_ref.shape[1]
    rows = lax.broadcasted_iota(jnp.int32, (count, count), 0)
    return (rows == spot_ref[...]).astype(f32).astype(bf16)


def vmem(count):
    return [pl.BlockSpec(memory_space=pltpu.VMEM)] * count


def shape(dims, dtype):
    return jax.ShapeDtypeStruct(dims, dtype)


def cost(flops, moved):
    return pl.CostEstimate(flops=flops, bytes_accessed=moved, transcendentals=0)


def land_column(land_ref, rows, cols):
    eye = (
        lax.broadcasted_iota(jnp.int32, (cols, cols), 0)
        == lax.broadcasted_iota(jnp.int32, (cols, cols), 1)
    ).astype(f32)
    land = land_ref[...].astype(f32)
    parts = [jnp.sum(eye * land[i : i + 1, :], -1, keepdims=True) for i in range(rows)]
    return jnp.concatenate(parts, axis=0)


def pack_kernel(rows, cols, *refs):
    sources, outs, (tokens_ref, cot_ref, land_ref, vec_ref, perm_ref, sems) = refs[:5], refs[5:-6], refs[-6:]
    copies = [
        pltpu.make_async_copy(source, target, sems.at[n])
        for n, (source, target) in enumerate(zip(sources, (tokens_ref, cot_ref, land_ref, vec_ref, perm_ref)))
    ]
    for copy in copies:
        copy.start()
    for copy in copies:
        copy.wait()
    column = land_column(land_ref, rows, cols)
    added = column * vec_ref[...]
    added = jnp.concatenate([added] * Z, axis=0)
    embedded = (tokens_ref[...].astype(f32) + added).astype(bf16)
    perm = one_hot(perm_ref)
    left = mm(perm, embedded)
    right = mm(perm, cot_ref[...])
    packed = jnp.concatenate([left, right], axis=1)
    column = jnp.concatenate([column] * Z, axis=0)
    flags = mm(perm, jnp.broadcast_to(column, (column.shape[0], 128)).astype(bf16))
    start = 0
    for out in outs:
        count = out.shape[0] - EXTRA
        eye = lax.broadcasted_iota(jnp.int32, (count, count), 0) == lax.broadcasted_iota(jnp.int32, (count, count), 1)
        row = jnp.sum(jnp.where(eye, flags[start : start + count, 0:1], 0.0), 0, keepdims=True)
        row = jnp.concatenate([row, jnp.zeros((1, 2 * C - count), f32)], axis=1)
        row = jnp.broadcast_to(row, (EXTRA, 2 * C))
        out[...] = jnp.concatenate([packed[start : start + count], row], axis=0).astype(bf16)
        start += count


def pack(tokens, cotangent, land_sea, vector, rows, cols):
    parts = piece_rows(rows, cols)
    perm = spots(np.concatenate(parts))
    count = Z * rows * cols
    return pl.pallas_call(
        functools.partial(pack_kernel, rows, cols),
        out_shape=[shape((part.size + EXTRA, 2 * C), bf16) for part in parts],
        in_specs=[pl.BlockSpec(memory_space=pltpu.HBM)] * 5,
        out_specs=vmem(4),
        scratch_shapes=[
            pltpu.VMEM((count, C), bf16),
            pltpu.VMEM((count, C), bf16),
            pltpu.VMEM((rows, cols), jnp.int32),
            pltpu.VMEM((1, C), f32),
            pltpu.VMEM((1, count), jnp.int32),
            pltpu.SemaphoreType.DMA((5,)),
        ],
        cost_estimate=cost(4 * count * count * C, 4 * MIB),
        name="pack",
    )(tokens.reshape(count, C), cotangent.reshape(count, C), land_sea, vector.reshape(1, C), perm)


def floor_div(values, divisor):
    return (values * (65536 // divisor + 1)) >> 16


def remainder(values, divisor):
    return values - floor_div(values, divisor) * divisor


def place_order(order):
    half = floor_div(order, SPOTS)
    spot = order - half * SPOTS
    level = floor_div(spot, HH)
    return level * WH + half * HH + (spot - level * HH)


def bias_kernel(levels, table_ref, out_ref, *wide_refs):
    groups = levels * HEADS
    pairs = PLACES * PLACES
    row = lax.broadcasted_iota(jnp.int32, (HEADS * RELW, HEADS * STRIP), 0)
    lane = lax.broadcasted_iota(jnp.int32, (HEADS * RELW, HEADS * STRIP), 1)
    head = floor_div(row, RELW)
    ahead = lane - (head * STRIP + (RELW - 1 - (row - head * RELW)) * SPOTS)
    onehot = ((ahead >= 0) & (ahead < SPOTS)).astype(f32).astype(bf16)
    row = lax.broadcasted_iota(jnp.int32, (pairs, pairs), 0)
    source = place_order(floor_div(row, PLACES)) * PLACES + remainder(row, PLACES)
    reorder = (lax.broadcasted_iota(jnp.int32, (pairs, pairs), 1) == source).astype(f32).astype(bf16)
    for level in range(levels):
        table = table_ref[:, level, :].T
        high = table.astype(bf16)
        rest = (table - high.astype(f32)).astype(bf16)
        wide = mm(mm(reorder, high).astype(bf16), onehot) + mm(mm(reorder, rest).astype(bf16), onehot)
        for head in range(HEADS):
            for n, wide_ref in enumerate(wide_refs):
                start = head * STRIP + n * 128
                wide_ref[(level * HEADS + head) * pairs : (level * HEADS + head + 1) * pairs, :] = wide[:, start : start + 128]
    strips = groups * PLACES
    row = lax.broadcasted_iota(jnp.int32, (strips, STRIP), 0)
    spot = remainder(lax.broadcasted_iota(jnp.int32, (strips, STRIP), 1), SPOTS)
    own = remainder(row, PLACES)
    first_level = (row < HEADS * PLACES).astype(jnp.int32)
    own_north = (own < SPOTS).astype(jnp.int32)
    own_low = (own - SPOTS * (1 - own_north) < HZ * HH).astype(jnp.int32)
    low = (spot < HZ * HH).astype(jnp.int32)
    pole = (lax.axis_index("y") + lax.axis_index("core") == 0).astype(jnp.int32)
    halves = []
    for half in range(2):
        parts = []
        for n, wide_ref in enumerate(wide_refs):
            here = spot[:, n * 128 : (n + 1) * 128]
            part = jnp.zeros((strips, 128), f32)
            for p in range(SPOTS):
                place = p // HH * WH + half * HH + p % HH
                part = jnp.where(here == p, wide_ref[pl.ds(place, strips, stride=PLACES), :], part)
            parts.append(part)
        strip = jnp.concatenate(parts, axis=1)
        differs = first_level * (own_low ^ low) + pole * (own_north ^ (1 - half))
        halves.append(jnp.where(differs > 0, strip + mask_fill, strip) * log2e)
    for w in range(WW):
        start = (WW - 1 - w) * SPOTS
        part = jnp.concatenate([strip[:, start : start + RUN] for strip in halves], axis=1)
        for g in range(groups):
            for half in range(2):
                rows = part[g * PLACES + half * SPOTS : g * PLACES + (half + 1) * SPOTS, :]
                out_ref[g, half * RUN + w * SPOTS : half * RUN + (w + 1) * SPOTS, :] = rows


def expand_bias(table):
    levels = table.shape[1]
    groups = levels * HEADS
    pairs = PLACES * PLACES
    flat = table[0].transpose(1, 3, 0, 2).reshape(HEADS * RELW, levels, pairs)
    return pl.pallas_call(
        functools.partial(bias_kernel, levels),
        out_shape=shape((groups, TOK, TOK), f32),
        in_specs=vmem(1),
        out_specs=vmem(1)[0],
        scratch_shapes=[pltpu.VMEM((groups * pairs, 128), f32)] * (STRIP // 128),
        compiler_params=pltpu.CompilerParams(vmem_limit_bytes=28 * MIB),
        cost_estimate=cost(10**9, 8 * MIB),
        name="bias",
    )(flat)


def head_masks(count):
    lane = lax.broadcasted_iota(jnp.int32, (count, C), 1)
    return [((lane >= h * HEAD) & (lane < (h + 1) * HEAD)).astype(f32) for h in range(HEADS)]


def stacked(values, masks):
    return jnp.concatenate([values * mask for mask in masks], axis=0)


def head_sum(values, masks):
    total = values[:TOK] * masks[0]
    for h in range(1, HEADS):
        total = total + values[h * TOK : (h + 1) * TOK] * masks[h]
    return total


def position():
    return lax.axis_index("core"), lax.axis_index("y") * 2 + lax.axis_index("x"), lax.axis_index("deep")


def chunk_rows(block):
    return pl.ds(pl.multiple_of(block * PART, PART), PART)


def split_parts(total_refs, keep_ref, send_ref):
    core, chip, _ = position()
    for out, side in ((keep_ref, core), (send_ref, 1 - core)):
        parts = []
        for g in range(QUADS):
            rows = chunk_rows(side * QUADS + jnp.bitwise_xor(chip, g))
            parts += [ref[rows, :] for ref in total_refs]
        out[...] = jnp.concatenate(parts, axis=0).astype(out.dtype)


def attend(first, runs, pieces, bias_ref, triple_ref, project_ref, *refs):
    q_ref, k_ref, v_ref, p_ref, mixed_ref, normed_ref, unit_ref, spread_ref, summed_ref, cot_ref = refs
    pieces = [piece.astype(f32) for piece in pieces]
    ordered = jnp.concatenate([pieces[n][start : start + count] for n, start, count in runs], axis=0)
    emb = ordered[:, :C]
    cot_ref[...] = ordered[:, C:].astype(bf16)
    unit, spread = unit_norm(emb)
    unit_ref[...] = unit
    spread_ref[...] = spread
    normed = unit.astype(bf16)
    normed_ref[...] = normed
    packed = mm(normed, triple_ref[...])
    q_ref[...] = packed[:, :C].astype(bf16)
    k_ref[...] = packed[:, C : 2 * C].astype(bf16)
    v_ref[...] = packed[:, 2 * C :].astype(bf16)
    masks = head_masks(TOK)
    masks_b = [mask.astype(bf16) for mask in masks]
    for w in range(emb.shape[0] // TOK):
        rows = slice(w * TOK, (w + 1) * TOK)
        heads = slice(w * HEADS, (w + 1) * HEADS)
        level = (first + w) % (Z // WZ)
        scores = mm_nt(stacked(q_ref[rows, :], masks_b), k_ref[rows, :])
        bias = bias_ref[level * HEADS : (level + 1) * HEADS].reshape(HEADS * TOK, TOK)
        raised = jnp.exp2(scores * (score_scale * log2e) + bias)
        probs = raised * (1.0 / jnp.sum(raised, -1, keepdims=True))
        probs_b = probs.astype(bf16)
        p_ref[heads] = probs_b.reshape(HEADS, TOK, TOK)
        mixed = head_sum(mm(probs_b, v_ref[rows, :]), masks).astype(bf16)
        mixed_ref[rows, :] = mixed
        summed_ref[rows, :] = emb[rows] + mm(mixed, project_ref[...]).astype(bf16).astype(f32)


def feed_back(summed, cot, up_ref, down_ref, gsum_ref, up_grad_ref, down_grad_ref):
    unit2, spread2 = unit_norm(summed)
    normed2 = unit2.astype(bf16)
    back = jnp.zeros(unit2.shape, f32)
    block = 256
    for start in range(0, FF, block):
        cols = slice(start, start + block)
        up_part = up_ref[:, cols]
        pre = mm(normed2, up_part)
        upstream = mm(cot, down_ref[:, cols])
        phi = 0.5 * (1.0 + lax.erf(pre * root_half))
        activated = (pre * phi).astype(bf16)
        slope = phi + pre * inv_root_tau * jnp.exp2(pre * pre * (-0.5 * log2e))
        hidden = (upstream * slope).astype(bf16)
        up_grad_ref[:, cols] = mm_tn(normed2, hidden)
        down_grad_ref[:, cols] = mm_tn(cot, activated)
        back = back + mm_nt(hidden, up_part)
    gsum_ref[...] = cot.astype(f32) + norm_back(back, unit2, spread2)


def attend_back(at, q_ref, k_ref, v_ref, p_ref, gsum_ref, project_ref, gq_ref, gk_ref, gv_ref):
    masks = head_masks(TOK)
    masks_b = [mask.astype(bf16) for mask in masks]
    for w in range(q_ref.shape[0] // TOK):
        rows = slice(w * TOK, (w + 1) * TOK)
        full_rows = slice(at + w * TOK, at + (w + 1) * TOK)
        grad = gsum_ref[full_rows, :].astype(bf16)
        grad_mixed_b = mm_nt(grad, project_ref[...]).astype(bf16)
        probs_b = p_ref[w * HEADS : (w + 1) * HEADS].reshape(HEADS * TOK, TOK)
        probs = probs_b.astype(f32)
        grad_probs = mm_nt(stacked(grad_mixed_b, masks_b), v_ref[rows, :])
        inner = jnp.sum(grad_probs * probs, -1, keepdims=True)
        scaled = (probs * (grad_probs - inner) * score_scale).astype(bf16)
        grad_q = head_sum(mm(scaled, k_ref[rows, :]), masks)
        grad_mixed_t = grad_mixed_b.astype(f32).T.astype(bf16)
        query_t = q_ref[rows, :].astype(f32).T.astype(bf16)
        grad_k, grad_v = [], []
        for h in range(HEADS):
            spot = slice(h * HEAD, (h + 1) * HEAD)
            span = slice(h * TOK, (h + 1) * TOK)
            grad_k.append(mm(query_t[spot], scaled[span]))
            grad_v.append(mm(grad_mixed_t[spot], probs_b[span]))
        gq_ref[full_rows, :] = grad_q.astype(bf16)
        gk_ref[full_rows, :] = jnp.concatenate(grad_k, axis=0).T.astype(bf16)
        gv_ref[full_rows, :] = jnp.concatenate(grad_v, axis=0).T.astype(bf16)


def halved(rows):
    return -(-rows // 16) * 8


def tokens_back(
    lon_windows, sizes, gq_ref, gk_ref, gv_ref, mixed, normed, unit, spread, gsum_ref, triple_ref, up_grad_ref, down_grad_ref,
    *rest,
):
    flag_refs, rest = rest[: len(sizes)], rest[len(sizes) :]
    outs, (land_ref, keep_ref, send_ref, total_ref) = rest[: len(sizes) - 1], rest[len(sizes) - 1 :]
    triple = triple_ref[...]
    grad_normed = jnp.zeros(unit.shape, f32)
    parts = []
    for n, ref in enumerate((gq_ref, gk_ref, gv_ref)):
        grad = ref[...]
        grad_normed = grad_normed + mm_nt(grad, triple[:, n * C : (n + 1) * C])
        parts.append(mm_tn(normed, grad))
    parts.append(mm_tn(mixed, gsum_ref[...].astype(bf16)))
    total_ref[...] = jnp.concatenate(parts, axis=1)
    grad_normed = grad_normed.astype(bf16).astype(f32)
    grad_tokens = gsum_ref[...] + norm_back(grad_normed, unit, spread)
    parts, at = [[] for _ in sizes], 0
    for n, start, count in [run for window in window_runs(lon_windows) for run in window]:
        parts[n].append((start, grad_tokens[at : at + count]))
        at += count
    land = jnp.zeros((EXTRA, C), f32)
    wide = []
    for size, flag_ref, part in zip(sizes, flag_refs, parts):
        piece = jnp.concatenate([value for _, value in sorted(part, key=lambda item: item[0])], axis=0)
        flags = flag_ref[size - 8 : size + 8, :].astype(f32)[8:, :size]
        land = land + mm(flags.astype(bf16), piece.astype(bf16))
        half = halved(size)
        second = jnp.concatenate([piece[half:], jnp.zeros((2 * half - size, C), f32)], axis=0)
        wide.append(jnp.concatenate([piece[:half], second], axis=1))
    land_ref[...] = land[0:1]
    own, north, side, corner = wide
    for out, value in zip(outs, (own, jnp.concatenate([north, corner], axis=0), side)):
        out[...] = value.astype(bf16)
    split_parts((up_grad_ref, down_grad_ref, total_ref), keep_ref, send_ref)


def saved_shapes(count):
    dims = [((count, C), bf16)] * 3 + [((count // TOK * HEADS, TOK, TOK), bf16)] + [((count, C), bf16)] * 2
    return dims + [((count, C), f32), ((count, 1), f32), ((count, C), f32), ((count, C), bf16)]


SAVED = len(saved_shapes(TOK))


def split_runs(lon_windows):
    windows = window_runs(lon_windows)
    whole = (lon_windows - 1) * (Z // WZ)
    return whole, *[[run for window in part for run in window] for part in (windows[:whole], windows[whole:])]


def near_kernel(lon_windows, own_ref, north_ref, *refs):
    runs = split_runs(lon_windows)[1]
    attend(0, runs, (own_ref[...], north_ref[...]), *refs)


def near_block(own, north, bias, triple, project, lon_windows):
    count = split_runs(lon_windows)[0] * TOK
    return pl.pallas_call(
        functools.partial(near_kernel, lon_windows),
        out_shape=[shape(*dims) for dims in saved_shapes(count)],
        in_specs=vmem(5),
        out_specs=vmem(SAVED),
        compiler_params=pltpu.CompilerParams(vmem_limit_bytes=24 * MIB),
        cost_estimate=cost(3 * 10**9, 8 * MIB),
        name="near_block",
    )(own, north, bias, triple, project)


def block_kernel(lon_windows, sizes, *refs):
    whole, _, runs = split_runs(lon_windows)
    pieces, refs = refs[:4], refs[4:]
    (bias_ref, triple_ref, project_ref, up_ref, down_ref), refs = refs[:5], refs[5:]
    near, refs = refs[:SAVED], refs[SAVED:]
    outs, refs = refs[: len(sizes) + 2], refs[len(sizes) + 2 :]
    far, (gsum, up_grad, down_grad, gq, gk, gv, total) = refs[:SAVED], refs[SAVED:]
    attend(whole, runs, [ref[...] for ref in pieces], bias_ref, triple_ref, project_ref, *far)
    mixed, normed, unit, spread, summed, cot = [
        jnp.concatenate([one[...], other[...]], axis=0) for one, other in zip(near[4:], far[4:])
    ]
    feed_back(summed, cot, up_ref, down_ref, gsum, up_grad, down_grad)
    attend_back(0, *near[:4], gsum, project_ref, gq, gk, gv)
    attend_back(whole * TOK, *far[:4], gsum, project_ref, gq, gk, gv)
    tokens_back(
        lon_windows, sizes, gq, gk, gv, mixed, normed, unit, spread, gsum, triple_ref, up_grad, down_grad,
        *pieces, *outs, total,
    )


def block(pieces, bias, triple, project, up, down, near, lon_windows, sizes):
    count = sum(sizes)
    own, north, side, corner = [halved(size) for size in sizes]
    out_shape = [shape((size, 2 * C), bf16) for size in (own, north + corner, side)] + [
        shape((1, C), f32),
        shape((QUADS * CHUNK, FF), f32),
        shape((QUADS * CHUNK, FF), bf16),
    ]
    return pl.pallas_call(
        functools.partial(block_kernel, lon_windows, sizes),
        out_shape=out_shape,
        in_specs=vmem(9 + SAVED),
        out_specs=vmem(len(out_shape)),
        scratch_shapes=[pltpu.VMEM(*dims) for dims in saved_shapes(count - near[0].shape[0])]
        + [pltpu.VMEM((count, C), f32)]
        + [pltpu.VMEM((C, FF), f32)] * 2
        + [pltpu.VMEM((count, C), bf16)] * 3
        + [pltpu.VMEM((C, FF), f32)],
        compiler_params=pltpu.CompilerParams(vmem_limit_bytes=28 * MIB),
        cost_estimate=cost(8 * 10**9, 16 * MIB),
        name="block",
    )(*pieces, bias, triple, project, up, down, *near)


def side_kernel(side_ref, north_ref, *refs):
    corner = north_ref[...].astype(f32)[-side_ref.shape[0] :]
    refs[-1][...] = jnp.concatenate([side_ref[...].astype(f32), corner], axis=0).astype(bf16)


def home_kernel(sizes, own_ref, north_ref, side_ref, perm_ref, out_ref):
    wide = [ref[...].astype(f32) for ref in (own_ref, north_ref, side_ref)]
    half = wide[2].shape[0] // 2
    wide = [wide[0], wide[1][:-half], wide[2][:half], wide[2][half:]]
    pieces = []
    for size, value in zip(sizes, wide):
        pieces += [value[:, :C], value[: size - value.shape[0], C:]]
    pieces = jnp.concatenate(pieces, axis=0).astype(bf16)
    out_ref[...] = mm(one_hot(perm_ref), pieces).astype(bf16)


def to_home(own, north, side, sizes, rows, cols):
    count = Z * rows * cols
    perm = spots(np.argsort(np.concatenate(piece_rows(rows, cols))))
    return pl.pallas_call(
        functools.partial(home_kernel, sizes),
        out_shape=shape((count, C), bf16),
        in_specs=vmem(4),
        out_specs=vmem(1)[0],
        compiler_params=pltpu.CompilerParams(vmem_limit_bytes=32 * MIB),
        cost_estimate=cost(2 * count * count * C, 4 * MIB),
        name="to_home",
    )(own, north, side, perm)


def core_add_kernel(keep_ref, got_ref, *refs):
    own_ref, outs = refs[-QUADS], refs[1 - QUADS :]
    total = keep_ref[...] + got_ref[...].astype(f32)
    own_ref[...] = total[:CHUNK]
    for e, out in enumerate(outs, 1):
        out[...] = total[e * CHUNK : (e + 1) * CHUNK].astype(bf16)


def chip_add_kernel(keep_ref, *refs):
    gots, (land_ref, out_ref) = refs[:-2], refs[-2:]
    total = keep_ref[...]
    for ref in gots:
        total = total + ref[...].astype(f32)
    land = land_ref[...]
    rest = jnp.concatenate([land[:, 128:], jnp.zeros((1, 2 * 128 - C), f32)], axis=1)
    parts = [total[:, n * 128 : (n + 1) * 128] for n in range(BLOCKS)]
    total = jnp.concatenate(parts + [land[:, :128], rest, jnp.zeros((EXTRA - 2, 128), f32)], axis=0)
    out_ref[...] = total.astype(bf16)


def add_kernel(one_ref, two_ref, *refs):
    refs[-1][...] = (one_ref[...].astype(f32) + two_ref[...].astype(f32)).astype(bf16)


def join_kernel(*refs):
    refs[-1][...] = jnp.concatenate([ref[...] for ref in refs[:-1]], axis=0)


def small_call(kernel, out_shape, args, name, after=(), scratch=()):
    return pl.pallas_call(
        kernel,
        out_shape=out_shape,
        in_specs=vmem(len(args)) + [pl.BlockSpec(memory_space=pl.ANY)] * len(after),
        out_specs=vmem(len(out_shape)),
        scratch_shapes=scratch,
        compiler_params=pltpu.CompilerParams(vmem_limit_bytes=16 * MIB),
        cost_estimate=cost(10**6, 2 * MIB),
        name=name,
    )(*args, *after)


def finish_kernel(far, chunks_ref, *refs):
    if far:
        before_ref, refs = refs[0], refs[5:]
    outs, land_ref, (up_ref, down_ref, triple_ref, project_ref, lands_ref, sum_ref, sems) = refs[:4], refs[4], refs[5:]
    core, chip, _ = position()
    side = 1 - core if far else core
    for g in range(QUADS):
        tiles = chunks_ref[g * FULL : (g + 1) * FULL, :].astype(f32)
        chunk = jnp.concatenate([tiles[n * CHUNK : (n + 1) * CHUNK] for n in range(BLOCKS)], axis=1)
        block = jnp.bitwise_xor(chip, g)
        rows = chunk_rows(block)
        up_ref[rows, :] = chunk[:PART]
        down_ref[rows, :] = chunk[PART : 2 * PART]
        triple_ref[rows, :] = chunk[2 * PART : CHUNK, : 3 * C]
        project_ref[rows, :] = chunk[2 * PART : CHUNK, 3 * C :]
        lands_ref[pl.ds(pl.multiple_of(block * EXTRA, EXTRA), EXTRA), :] = tiles[BLOCKS * CHUNK :]
    copies = []
    for n, (source, out) in enumerate(zip((triple_ref, project_ref, up_ref, down_ref), outs)):
        rows = pl.ds(pl.multiple_of(side * QUADS * PART, 8), QUADS * PART)
        copies.append(pltpu.make_async_copy(source, out.at[rows, :], sems.at[n]))
    for copy in copies:
        copy.start()
    lands = lands_ref[...]
    lands = [sum(lands[g * EXTRA + n : g * EXTRA + n + 1] for g in range(QUADS)) for n in range(2)]
    land = jnp.concatenate([lands[0], lands[1][:, : C - 128]], axis=1)
    if far:
        sum_ref[...] = land + before_ref[...]
        copies.append(pltpu.make_async_copy(sum_ref, land_ref, sems.at[4]))
        copies[-1].start()
    else:
        land_ref[...] = land
    for copy in copies:
        copy.wait()


def finish(chunks, before=()):
    rows = QUADS * PART
    widths = (3 * C, C, FF, FF)
    hbm = [pl.BlockSpec(memory_space=pltpu.HBM)] * 4
    land, weights = before[4:], before[:4]
    return pl.pallas_call(
        functools.partial(finish_kernel, bool(before)),
        out_shape=[shape((C, width), f32) for width in widths] + [shape((1, C), f32)],
        in_specs=vmem(1 + len(land)) + hbm[: len(weights)],
        out_specs=hbm + (hbm[:1] if before else vmem(1)),
        scratch_shapes=[
            pltpu.VMEM((rows, FF), f32),
            pltpu.VMEM((rows, FF), f32),
            pltpu.VMEM((rows, 3 * C), f32),
            pltpu.VMEM((rows, C), f32),
            pltpu.VMEM((QUADS * EXTRA, 128), f32),
            pltpu.VMEM((1, C), f32),
            pltpu.SemaphoreType.DMA((5,)),
        ],
        input_output_aliases={2 + n: n for n in range(len(weights))},
        compiler_params=pltpu.CompilerParams(vmem_limit_bytes=16 * MIB),
        cost_estimate=cost(10**6, 2 * MIB),
        name="finish_far" if before else "finish_own",
    )(chunks, *land, *weights)


def reduce_all(keep, sent, land, side, north, shift, lon_count):
    core_move = lambda lon, lat: (lon, lat ^ 1)
    chip_move = lambda e: lambda lon, lat: (lon ^ (e & 1), lat ^ (2 * (e >> 1)))
    deep_move = lambda e: lambda lon, lat: (lon ^ (2 * e), lat)

    def one(rows):
        return [shape((rows, FF), bf16)]

    got = shift(sent, move=core_move)
    parts = [shape((CHUNK, FF), f32)] + one(CHUNK) * (QUADS - 1)
    own, *parts = small_call(core_add_kernel, parts, (keep, got), "core_add", after=(north,))
    gots = [shift(value, move=chip_move(e)) for e, value in enumerate(parts, 1)]
    full = [shape((FULL, 128), bf16)]
    (total,) = small_call(chip_add_kernel, full, (own, *gots, land), "chip_add")
    (side,) = small_call(side_kernel, [shape((2 * side.shape[0], 2 * C), bf16)], (side, north), "side", after=(total,))
    side = shift(side, move=lambda lon, lat: (lon - 1, lat))
    reach, waits = 1, (side,)
    while reach < lon_count // 2:
        got = shift(total, move=deep_move(reach))
        reach *= 2
        (total,) = small_call(add_kernel, full, (total, got), "deep_add", after=waits)
        waits = ()
    near = [total] + [shift(total, move=chip_move(e)) for e in range(1, QUADS)]
    (total,) = small_call(join_kernel, [shape((QUADS * FULL, 128), bf16)], near, "join")
    got = shift(total, move=core_move)
    return finish(got, finish(total)), side


AXES = ("deep", "x", "y", "core")


def send(value, lon_count, lat_count, move):
    pairs = []
    for lon in range(lon_count):
        for lat in range(lat_count):
            to_lon, to_lat = move(lon, lat)
            pairs.append((lon * lat_count + lat, (to_lon % lon_count) * lat_count + to_lat % lat_count))
    return lax.ppermute(value, AXES, pairs)


def body(
    lon_count, lat_count,
    tokens, cotangent, land_sea, land_vector, triple_weight, project_weight, up_weight, down_weight, earth_bias,
):
    levels, rows, cols, features = tokens.shape
    shift = functools.partial(send, lon_count=lon_count, lat_count=lat_count)
    lon_windows = cols // WW

    own, north, side, corner = pack(tokens, cotangent, land_sea, land_vector, rows, cols)
    north = shift(north, move=lambda lon, lat: (lon, lat + 1))
    side = shift(side, move=lambda lon, lat: (lon + 1, lat))
    corner = shift(corner, move=lambda lon, lat: (lon + 1, lat + 1))
    bias = expand_bias(earth_bias)

    sizes = [part.size for part in piece_rows(rows, cols)]
    pieces = (own, north, side, corner)
    near = near_block(own, north, bias, triple_weight, project_weight, lon_windows)
    own, north, side, land, keep, sent = block(
        pieces, bias, triple_weight, project_weight, up_weight, down_weight.T, near, lon_windows, sizes
    )
    north = shift(north, move=lambda lon, lat: (lon, lat - 1))
    (triple, project, up, down, land), side = reduce_all(keep, sent, land, side, north, shift, lon_count)
    grad_tokens = to_home(own, north, side, sizes, rows, cols)
    return grad_tokens.reshape(tokens.shape), triple, project, up, down.T, land.reshape(features)


def solution(mesh):
    lon_count, lat_count = mesh.shape["lon"], mesh.shape["lat"]
    fine = jax.sharding.Mesh(mesh.devices.reshape(lon_count // 2, 2, lat_count // 2, 2), AXES)
    lon, lat = AXES[:2], AXES[2:]
    return jax.shard_map(
        functools.partial(body, lon_count, lat_count),
        mesh=fine,
        in_specs=(
            P(None, lat, lon, None),
            P(None, lat, lon, None),
            P(lat, lon),
            P(),
            P(),
            P(),
            P(),
            P(),
            P(lat, None, None, None, None),
        ),
        out_specs=(P(None, lat, lon, None), P(), P(), P(), P(), P()),
        check_vma=False,
    )
```

```python
import functools
import math

import jax
import jax.numpy as jnp
import numpy as np
from jax import lax
from jax.experimental import pallas as pl
from jax.experimental.pallas import tpu as pltpu
from jax.sharding import PartitionSpec as P

Z = 4
WZ = 2
WH = 6
WW = 12
C = 192
HEADS = 6
HEAD = 32
FF = 768
HZ, HH, HW = WZ // 2, WH // 2, WW // 2
TOK = WZ * WH * WW
PLACES = WZ * WH
RELW = 2 * WW - 1
SPOTS = PLACES // 2
STRIP = -(-RELW * SPOTS // 128) * 128
RUN, SHORT = WW * SPOTS, (WW - HW) * SPOTS

mask_fill = -10000.0
norm_eps = 1e-05
log2e = 1.4426950408889634
root_half = 0.7071067811865476
inv_root_tau = 0.3989422804014327
score_scale = HEAD**-0.5

f32 = jnp.float32
bf16 = jnp.bfloat16
MIB = 1 << 20

QUADS = 4
PART = C // (2 * QUADS)
CHUNK = 3 * PART
BLOCKS = FF // 128
EXTRA = 8
FULL = BLOCKS * CHUNK + EXTRA


def mm(a, b):
    return lax.dot_general(a, b, (((1,), (0,)), ((), ())), preferred_element_type=f32)


def mm_nt(a, b):
    return lax.dot_general(a, b, (((1,), (1,)), ((), ())), preferred_element_type=f32)


def mm_tn(a, b):
    return lax.dot_general(a, b, (((0,), (0,)), ((), ())), preferred_element_type=f32)


def unit_norm(values):
    average = jnp.mean(values, -1, keepdims=True)
    centred = values - average
    variance = jnp.mean(centred * centred, -1, keepdims=True)
    spread = lax.rsqrt(variance + norm_eps)
    return centred * spread, spread


def norm_back(upstream, unit, spread):
    first = jnp.mean(upstream, -1, keepdims=True)
    second = jnp.mean(upstream * unit, -1, keepdims=True)
    return spread * (upstream - first - unit * second)


def piece_rows(rows, cols):
    home = np.arange(Z * rows * cols).reshape(Z, rows, cols)

    def run(level, row, col, width):
        levels = [(level * WZ + z - HZ) % Z for z in range(WZ)]
        return home[levels, row : row + HH, col : col + width].transpose(2, 0, 1).reshape(-1)

    levels = range(Z // WZ)
    parts = []
    for row in (0, rows - HH):
        whole = [run(a, row, w * WW - HW, WW) for w in range(1, cols // WW) for a in levels]
        parts.append(np.concatenate(whole + [run(a, row, 0, WW - HW) for a in levels]))
    for row in (0, rows - HH):
        parts.append(np.concatenate([run(a, row, cols - HW, HW) for a in levels]))
    return parts


def window_runs(lon_windows):
    levels = Z // WZ
    whole = (lon_windows - 1) * levels
    runs = [[(1, n * RUN, RUN), (0, n * RUN, RUN)] for n in range(whole)]
    for a in range(levels):
        inner = whole * RUN + a * SHORT
        west = (a * (RUN - SHORT), RUN - SHORT)
        runs.append([(3, *west), (1, inner, SHORT), (2, *west), (0, inner, SHORT)])
    return runs


def spots(places):
    return jnp.asarray(np.argsort(places).astype(np.int32)[None])


def one_hot(spot_ref):
    count = spot_ref.shape[1]
    rows = lax.broadcasted_iota(jnp.int32, (count, count), 0)
    return (rows == spot_ref[...]).astype(f32).astype(bf16)


def vmem(count):
    return [pl.BlockSpec(memory_space=pltpu.VMEM)] * count


def shape(dims, dtype):
    return jax.ShapeDtypeStruct(dims, dtype)


def cost(flops, moved):
    return pl.CostEstimate(flops=flops, bytes_accessed=moved, transcendentals=0)


def land_column(land_ref, rows, cols):
    eye = (
        lax.broadcasted_iota(jnp.int32, (cols, cols), 0)
        == lax.broadcasted_iota(jnp.int32, (cols, cols), 1)
    ).astype(f32)
    land = land_ref[...].astype(f32)
    parts = [jnp.sum(eye * land[i : i + 1, :], -1, keepdims=True) for i in range(rows)]
    return jnp.concatenate(parts, axis=0)


def pack_kernel(rows, cols, *refs):
    sources, outs, (tokens_ref, cot_ref, land_ref, vec_ref, perm_ref, sems) = refs[:5], refs[5:-6], refs[-6:]
    copies = [
        pltpu.make_async_copy(source, target, sems.at[n])
        for n, (source, target) in enumerate(zip(sources, (tokens_ref, cot_ref, land_ref, vec_ref, perm_ref)))
    ]
    for copy in reversed(copies):
        copy.start()
    copies[4].wait()
    perm = one_hot(perm_ref)
    copies[2].wait()
    column = land_column(land_ref, rows, cols)
    copies[3].wait()
    added = column * vec_ref[...]
    added = jnp.concatenate([added] * Z, axis=0)
    copies[0].wait()
    embedded = (tokens_ref[...].astype(f32) + added).astype(bf16)
    left = mm(perm, embedded)
    copies[1].wait()
    right = mm(perm, cot_ref[...])
    packed = jnp.concatenate([left, right], axis=1)
    start = 0
    for out in outs:
        out[...] = packed[start : start + out.shape[0]].astype(bf16)
        start += out.shape[0]


def pack(tokens, cotangent, land_sea, vector, rows, cols):
    parts = piece_rows(rows, cols)
    perm = spots(np.concatenate(parts))
    count = Z * rows * cols
    return pl.pallas_call(
        functools.partial(pack_kernel, rows, cols),
        out_shape=[shape((part.size, 2 * C), bf16) for part in parts],
        in_specs=[pl.BlockSpec(memory_space=pltpu.HBM)] * 5,
        out_specs=vmem(4),
        scratch_shapes=[
            pltpu.VMEM((count, C), bf16),
            pltpu.VMEM((count, C), bf16),
            pltpu.VMEM((rows, cols), jnp.int32),
            pltpu.VMEM((1, C), f32),
            pltpu.VMEM((1, count), jnp.int32),
            pltpu.SemaphoreType.DMA((5,)),
        ],
        cost_estimate=cost(4 * count * count * C, 4 * MIB),
        name="pack",
    )(tokens.reshape(count, C), cotangent.reshape(count, C), land_sea, vector.reshape(1, C), perm)


def floor_div(values, divisor):
    return (values * (65536 // divisor + 1)) >> 16


def remainder(values, divisor):
    return values - floor_div(values, divisor) * divisor


def place_order(order):
    half = floor_div(order, SPOTS)
    spot = order - half * SPOTS
    level = floor_div(spot, HH)
    return level * WH + half * HH + (spot - level * HH)


def bias_kernel(levels, table_ref, out_ref, *wide_refs):
    groups = levels * HEADS
    pairs = PLACES * PLACES
    row = lax.broadcasted_iota(jnp.int32, (HEADS * RELW, 1), 0)
    head = floor_div(row, RELW)
    start = head * STRIP + (RELW - 1 - (row - head * RELW)) * SPOTS
    ahead = lax.broadcasted_iota(jnp.int32, (HEADS * RELW, HEADS * STRIP), 1) - start
    onehot = ((ahead >= 0) & (ahead < SPOTS)).astype(f32).astype(bf16)
    row = lax.broadcasted_iota(jnp.int32, (pairs, 1), 0)
    source = place_order(floor_div(row, PLACES)) * PLACES + remainder(row, PLACES)
    reorder = (lax.broadcasted_iota(jnp.int32, (pairs, pairs), 1) == source).astype(f32).astype(bf16)
    tables = [table_ref[:, level, :].T for level in range(levels)]
    wide = jnp.zeros((levels * pairs, HEADS * STRIP), f32)
    for _ in range(2):
        terms = [table.astype(bf16) for table in tables]
        tables = [table - term.astype(f32) for table, term in zip(tables, terms)]
        ordered = jnp.concatenate([mm(reorder, term) for term in terms], axis=0)
        wide = wide + mm(ordered.astype(bf16), onehot)
    for level in range(levels):
        for head in range(HEADS):
            for n, wide_ref in enumerate(wide_refs):
                start = head * STRIP + n * 128
                rows = slice((level * HEADS + head) * pairs, (level * HEADS + head + 1) * pairs)
                wide_ref[rows, :] = wide[level * pairs : (level + 1) * pairs, start : start + 128]
    strips = groups * PLACES
    row = lax.broadcasted_iota(jnp.int32, (strips, 1), 0)
    spot = remainder(lax.broadcasted_iota(jnp.int32, (1, STRIP), 1), SPOTS)
    own = remainder(row, PLACES)
    first_level = (row < HEADS * PLACES).astype(jnp.int32)
    own_north = (own < SPOTS).astype(jnp.int32)
    own_low = (own - SPOTS * (1 - own_north) < HZ * HH).astype(jnp.int32)
    low = (spot < HZ * HH).astype(jnp.int32)
    pole = (lax.axis_index("y") + lax.axis_index("core") == 0).astype(jnp.int32)
    halves = []
    for half in range(2):
        parts = []
        for n, wide_ref in enumerate(wide_refs):
            here = spot[:, n * 128 : (n + 1) * 128]
            part = jnp.zeros((strips, 128), f32)
            for p in range(SPOTS):
                place = p // HH * WH + half * HH + p % HH
                part = jnp.where(here == p, wide_ref[pl.ds(place, strips, stride=PLACES), :], part)
            parts.append(part)
        strip = jnp.concatenate(parts, axis=1)
        differs = first_level * (own_low ^ low) + pole * (own_north ^ (1 - half))
        halves.append(jnp.where(differs > 0, strip + mask_fill, strip) * log2e)
    for w in range(WW):
        start = (WW - 1 - w) * SPOTS
        part = jnp.concatenate([strip[:, start : start + RUN] for strip in halves], axis=1)
        for g in range(groups):
            for half in range(2):
                rows = part[g * PLACES + half * SPOTS : g * PLACES + (half + 1) * SPOTS, :]
                out_ref[g, half * RUN + w * SPOTS : half * RUN + (w + 1) * SPOTS, :] = rows


def expand_bias(table):
    levels = table.shape[1]
    groups = levels * HEADS
    pairs = PLACES * PLACES
    flat = table[0].transpose(1, 3, 0, 2).reshape(HEADS * RELW, levels, pairs)
    return pl.pallas_call(
        functools.partial(bias_kernel, levels),
        out_shape=shape((groups, TOK, TOK), f32),
        in_specs=vmem(1),
        out_specs=vmem(1)[0],
        scratch_shapes=[pltpu.VMEM((groups * pairs, 128), f32)] * (STRIP // 128),
        compiler_params=pltpu.CompilerParams(vmem_limit_bytes=28 * MIB),
        cost_estimate=cost(10**9, 8 * MIB),
        name="bias",
    )(flat)


def head_masks(count):
    lane = lax.broadcasted_iota(jnp.int32, (count, C), 1)
    return [((lane >= h * HEAD) & (lane < (h + 1) * HEAD)).astype(f32) for h in range(HEADS)]


def stacked(values, masks):
    return jnp.concatenate([values * mask for mask in masks], axis=0)


def head_sum(values, masks):
    total = values[:TOK] * masks[0]
    for h in range(1, HEADS):
        total = total + values[h * TOK : (h + 1) * TOK] * masks[h]
    return total


def position():
    return lax.axis_index("core"), lax.axis_index("y") * 2 + lax.axis_index("x"), lax.axis_index("deep")


def chunk_rows(block):
    return pl.ds(pl.multiple_of(block * PART, PART), PART)


def split_parts(total_refs, keep_ref, send_ref):
    core, chip, _ = position()
    for out, side in ((keep_ref, core), (send_ref, 1 - core)):
        parts = []
        for g in range(QUADS):
            rows = chunk_rows(side * QUADS + jnp.bitwise_xor(chip, g))
            parts += [ref[rows, :] for ref in total_refs]
        out[...] = jnp.concatenate(parts, axis=0).astype(out.dtype)


def attend(first, runs, pieces, bias_ref, triple_ref, project_ref, *refs):
    q_ref, k_ref, v_ref, p_ref, mixed_ref, normed_ref, unit_ref, spread_ref, summed_ref, cot_ref = refs
    pieces = [piece.astype(f32) for piece in pieces]
    ordered = jnp.concatenate([pieces[n][start : start + count] for n, start, count in runs], axis=0)
    emb = ordered[:, :C]
    cot_ref[...] = ordered[:, C:].astype(bf16)
    unit, spread = unit_norm(emb)
    unit_ref[...] = unit
    spread_ref[...] = spread
    normed = unit.astype(bf16)
    normed_ref[...] = normed
    packed = mm(normed, triple_ref[...])
    q_ref[...] = packed[:, :C].astype(bf16)
    k_ref[...] = packed[:, C : 2 * C].astype(bf16)
    v_ref[...] = packed[:, 2 * C :].astype(bf16)
    masks = head_masks(TOK)
    masks_b = [mask.astype(bf16) for mask in masks]
    for w in range(emb.shape[0] // TOK):
        rows = slice(w * TOK, (w + 1) * TOK)
        heads = slice(w * HEADS, (w + 1) * HEADS)
        level = (first + w) % (Z // WZ)
        scores = mm_nt(stacked(q_ref[rows, :], masks_b), k_ref[rows, :])
        bias = bias_ref[level * HEADS : (level + 1) * HEADS].reshape(HEADS * TOK, TOK)
        raised = jnp.exp2(scores * (score_scale * log2e) + bias)
        probs = raised * (1.0 / jnp.sum(raised, -1, keepdims=True))
        probs_b = probs.astype(bf16)
        p_ref[heads] = probs_b.reshape(HEADS, TOK, TOK)
        mixed = head_sum(mm(probs_b, v_ref[rows, :]), masks).astype(bf16)
        mixed_ref[rows, :] = mixed
        summed_ref[rows, :] = emb[rows] + mm(mixed, project_ref[...]).astype(bf16).astype(f32)


def feed_back(summed, cot, up_ref, down_ref, gsum_ref, up_grad_ref, down_grad_ref):
    unit2, spread2 = unit_norm(summed)
    normed2 = unit2.astype(bf16)
    back = jnp.zeros(unit2.shape, f32)
    block = 256
    for start in range(0, FF, block):
        cols = slice(start, start + block)
        up_part = up_ref[:, cols]
        pre = mm(normed2, up_part)
        upstream = mm(cot, down_ref[:, cols])
        phi = 0.5 * (1.0 + lax.erf(pre * root_half))
        activated = (pre * phi).astype(bf16)
        slope = phi + pre * inv_root_tau * jnp.exp2(pre * pre * (-0.5 * log2e))
        hidden = (upstream * slope).astype(bf16)
        up_grad_ref[:, cols] = mm_tn(normed2, hidden)
        down_grad_ref[:, cols] = mm_tn(cot, activated)
        back = back + mm_nt(hidden, up_part)
    gsum_ref[...] = cot.astype(f32) + norm_back(back, unit2, spread2)


def attend_back(at, q_ref, k_ref, v_ref, p_ref, gsum_ref, project_ref, gq_ref, gk_ref, gv_ref):
    masks = head_masks(TOK)
    masks_b = [mask.astype(bf16) for mask in masks]
    for w in range(q_ref.shape[0] // TOK):
        rows = slice(w * TOK, (w + 1) * TOK)
        full_rows = slice(at + w * TOK, at + (w + 1) * TOK)
        grad = gsum_ref[full_rows, :].astype(bf16)
        grad_mixed_b = mm_nt(grad, project_ref[...]).astype(bf16)
        probs_b = p_ref[w * HEADS : (w + 1) * HEADS].reshape(HEADS * TOK, TOK)
        probs = probs_b.astype(f32)
        grad_probs = mm_nt(stacked(grad_mixed_b, masks_b), v_ref[rows, :])
        inner = jnp.sum(grad_probs * probs, -1, keepdims=True)
        scaled = (probs * (grad_probs - inner) * score_scale).astype(bf16)
        grad_q = head_sum(mm(scaled, k_ref[rows, :]), masks)
        grad_mixed_t = grad_mixed_b.astype(f32).T.astype(bf16)
        query_t = q_ref[rows, :].astype(f32).T.astype(bf16)
        grad_k, grad_v = [], []
        for h in range(HEADS):
            spot = slice(h * HEAD, (h + 1) * HEAD)
            span = slice(h * TOK, (h + 1) * TOK)
            grad_k.append(mm(query_t[spot], scaled[span]))
            grad_v.append(mm(grad_mixed_t[spot], probs_b[span]))
        gq_ref[full_rows, :] = grad_q.astype(bf16)
        gk_ref[full_rows, :] = jnp.concatenate(grad_k, axis=0).T.astype(bf16)
        gv_ref[full_rows, :] = jnp.concatenate(grad_v, axis=0).T.astype(bf16)


def halved(rows):
    return -(-rows // 16) * 8


def tokens_back(
    lon_windows, sizes, gq_ref, gk_ref, gv_ref, mixed, normed, unit, spread, gsum_ref, triple_ref, up_grad_ref, down_grad_ref,
    *rest,
):
    outs, (keep_ref, send_ref, total_ref) = rest[: len(sizes)], rest[len(sizes) :]
    triple = triple_ref[...]
    grad_normed = jnp.zeros(unit.shape, f32)
    parts = []
    for n, ref in enumerate((gq_ref, gk_ref, gv_ref)):
        grad = ref[...]
        grad_normed = grad_normed + mm_nt(grad, triple[:, n * C : (n + 1) * C])
        parts.append(mm_tn(normed, grad))
    parts.append(mm_tn(mixed, gsum_ref[...].astype(bf16)))
    total_ref[...] = jnp.concatenate(parts, axis=1)
    grad_normed = grad_normed.astype(bf16).astype(f32)
    grad_tokens = gsum_ref[...] + norm_back(grad_normed, unit, spread)
    parts, at = [[] for _ in sizes], 0
    for n, start, count in [run for window in window_runs(lon_windows) for run in window]:
        parts[n].append((start, grad_tokens[at : at + count]))
        at += count
    for size, out, part in zip(sizes, outs, parts):
        piece = jnp.concatenate([value for _, value in sorted(part, key=lambda item: item[0])], axis=0)
        half = halved(size)
        second = jnp.concatenate([piece[half:], jnp.zeros((2 * half - size, C), f32)], axis=0)
        out[...] = jnp.concatenate([piece[:half], second], axis=1).astype(bf16)
    split_parts((up_grad_ref, down_grad_ref, total_ref), keep_ref, send_ref)


def saved_shapes(count):
    dims = [((count, C), bf16)] * 3 + [((count // TOK * HEADS, TOK, TOK), bf16)] + [((count, C), bf16)] * 2
    return dims + [((count, C), f32), ((count, 1), f32), ((count, C), f32), ((count, C), bf16)]


SAVED = len(saved_shapes(TOK))


def split_runs(lon_windows):
    windows = window_runs(lon_windows)
    whole = (lon_windows - 1) * (Z // WZ)
    return whole, *[[run for window in part for run in window] for part in (windows[:whole], windows[whole:])]


def near_kernel(lon_windows, own_ref, north_ref, *refs):
    runs = split_runs(lon_windows)[1]
    attend(0, runs, (own_ref[...], north_ref[...]), *refs)


def near_block(own, north, bias, triple, project, lon_windows):
    count = split_runs(lon_windows)[0] * TOK
    return pl.pallas_call(
        functools.partial(near_kernel, lon_windows),
        out_shape=[shape(*dims) for dims in saved_shapes(count)],
        in_specs=vmem(5),
        out_specs=vmem(SAVED),
        compiler_params=pltpu.CompilerParams(vmem_limit_bytes=24 * MIB),
        cost_estimate=cost(3 * 10**9, 8 * MIB),
        name="near_block",
    )(own, north, bias, triple, project)


def block_kernel(lon_windows, sizes, *refs):
    whole, _, runs = split_runs(lon_windows)
    pieces, refs = refs[:4], refs[4:]
    (bias_ref, triple_ref, project_ref, up_ref, down_ref), refs = refs[:5], refs[5:]
    near, refs = refs[:SAVED], refs[SAVED:]
    outs, refs = refs[: len(sizes) + 2], refs[len(sizes) + 2 :]
    far, (gsum, up_grad, down_grad, gq, gk, gv, total) = refs[:SAVED], refs[SAVED:]
    attend(whole, runs, [ref[...] for ref in pieces], bias_ref, triple_ref, project_ref, *far)
    mixed, normed, unit, spread, summed, cot = [
        jnp.concatenate([one[...], other[...]], axis=0) for one, other in zip(near[4:], far[4:])
    ]
    feed_back(summed, cot, up_ref, down_ref, gsum, up_grad, down_grad)
    attend_back(0, *near[:4], gsum, project_ref, gq, gk, gv)
    attend_back(whole * TOK, *far[:4], gsum, project_ref, gq, gk, gv)
    tokens_back(lon_windows, sizes, gq, gk, gv, mixed, normed, unit, spread, gsum, triple_ref, up_grad, down_grad, *outs, total)


def block(pieces, bias, triple, project, up, down, near, lon_windows, sizes):
    count = sum(sizes)
    out_shape = [shape((halved(size), 2 * C), bf16) for size in sizes] + [
        shape((QUADS * CHUNK, FF), f32),
        shape((QUADS * CHUNK, FF), bf16),
    ]
    return pl.pallas_call(
        functools.partial(block_kernel, lon_windows, sizes),
        out_shape=out_shape,
        in_specs=vmem(9 + SAVED),
        out_specs=vmem(len(out_shape)),
        scratch_shapes=[pltpu.VMEM(*dims) for dims in saved_shapes(count - near[0].shape[0])]
        + [pltpu.VMEM((count, C), f32)]
        + [pltpu.VMEM((C, FF), f32)] * 2
        + [pltpu.VMEM((count, C), bf16)] * 3
        + [pltpu.VMEM((C, FF), f32)],
        compiler_params=pltpu.CompilerParams(vmem_limit_bytes=28 * MIB),
        cost_estimate=cost(8 * 10**9, 16 * MIB),
        name="block",
    )(*pieces, bias, triple, project, up, down, *near)


def home_kernel(sizes, rows, cols, own_ref, north_ref, side_ref, corner_ref, perm_ref, land_ref, out_ref, sum_ref):
    pieces = []
    for size, ref in zip(sizes, (own_ref, north_ref, side_ref, corner_ref)):
        wide = ref[...].astype(f32)
        pieces += [wide[:, :C], wide[: size - wide.shape[0], C:]]
    pieces = jnp.concatenate(pieces, axis=0).astype(bf16)
    grads = mm(one_hot(perm_ref), pieces)
    out_ref[...] = grads.astype(bf16)
    column = jnp.concatenate([land_column(land_ref, rows, cols)] * Z, axis=0)
    sum_ref[...] = jnp.sum(grads * column, 0, keepdims=True)


def to_home(pieces, land_sea, sizes, rows, cols):
    count = Z * rows * cols
    perm = spots(np.argsort(np.concatenate(piece_rows(rows, cols))))
    return pl.pallas_call(
        functools.partial(home_kernel, sizes, rows, cols),
        out_shape=[shape((count, C), bf16), shape((1, C), f32)],
        in_specs=vmem(6),
        out_specs=vmem(2),
        compiler_params=pltpu.CompilerParams(vmem_limit_bytes=32 * MIB),
        cost_estimate=cost(2 * count * count * C, 4 * MIB),
        name="to_home",
    )(*pieces, perm, land_sea)


def core_add_kernel(keep_ref, got_ref, *refs):
    own_ref, outs = refs[-QUADS], refs[1 - QUADS :]
    total = keep_ref[...] + got_ref[...].astype(f32)
    own_ref[...] = total[:CHUNK]
    for e, out in enumerate(outs, 1):
        out[...] = total[e * CHUNK : (e + 1) * CHUNK].astype(bf16)


def chip_add_kernel(keep_ref, *refs):
    gots, (land_ref, out_ref) = refs[:-2], refs[-2:]
    total = keep_ref[...]
    for ref in gots:
        total = total + ref[...].astype(f32)
    land = land_ref[...]
    rest = jnp.concatenate([land[:, 128:], jnp.zeros((1, 2 * 128 - C), f32)], axis=1)
    parts = [total[:, n * 128 : (n + 1) * 128] for n in range(BLOCKS)]
    total = jnp.concatenate(parts + [land[:, :128], rest, jnp.zeros((EXTRA - 2, 128), f32)], axis=0)
    out_ref[...] = total.astype(bf16)


def add_kernel(one_ref, two_ref, out_ref):
    out_ref[...] = (one_ref[...].astype(f32) + two_ref[...].astype(f32)).astype(bf16)


def join_kernel(*refs):
    refs[-1][...] = jnp.concatenate([ref[...] for ref in refs[:-1]], axis=0)


def small_call(kernel, out_shape, args, name, after=(), scratch=()):
    return pl.pallas_call(
        kernel,
        out_shape=out_shape,
        in_specs=vmem(len(args)) + [pl.BlockSpec(memory_space=pl.ANY)] * len(after),
        out_specs=vmem(len(out_shape)),
        scratch_shapes=scratch,
        compiler_params=pltpu.CompilerParams(vmem_limit_bytes=16 * MIB),
        cost_estimate=cost(10**6, 2 * MIB),
        name=name,
    )(*args, *after)


def finish_kernel(far, chunks_ref, *refs):
    if far:
        before_ref, refs = refs[0], refs[5:]
    outs, land_ref, (up_ref, down_ref, triple_ref, project_ref, lands_ref, sum_ref, sems) = refs[:4], refs[4], refs[5:]
    core, chip, _ = position()
    side = 1 - core if far else core
    for g in range(QUADS):
        tiles = chunks_ref[g * FULL : (g + 1) * FULL, :].astype(f32)
        chunk = jnp.concatenate([tiles[n * CHUNK : (n + 1) * CHUNK] for n in range(BLOCKS)], axis=1)
        block = jnp.bitwise_xor(chip, g)
        rows = chunk_rows(block)
        up_ref[rows, :] = chunk[:PART]
        down_ref[rows, :] = chunk[PART : 2 * PART]
        triple_ref[rows, :] = chunk[2 * PART : CHUNK, : 3 * C]
        project_ref[rows, :] = chunk[2 * PART : CHUNK, 3 * C :]
        lands_ref[pl.ds(pl.multiple_of(block * EXTRA, EXTRA), EXTRA), :] = tiles[BLOCKS * CHUNK :]
    copies = []
    for n, (source, out) in enumerate(zip((triple_ref, project_ref, up_ref, down_ref), outs)):
        rows = pl.ds(pl.multiple_of(side * QUADS * PART, 8), QUADS * PART)
        copies.append(pltpu.make_async_copy(source, out.at[rows, :], sems.at[n]))
    for copy in copies:
        copy.start()
    lands = lands_ref[...]
    lands = [sum(lands[g * EXTRA + n : g * EXTRA + n + 1] for g in range(QUADS)) for n in range(2)]
    land = jnp.concatenate([lands[0], lands[1][:, : C - 128]], axis=1)
    if far:
        sum_ref[...] = land + before_ref[...]
        copies.append(pltpu.make_async_copy(sum_ref, land_ref, sems.at[4]))
        copies[-1].start()
    else:
        land_ref[...] = land
    for copy in copies:
        copy.wait()


def finish(chunks, before=()):
    rows = QUADS * PART
    widths = (3 * C, C, FF, FF)
    hbm = [pl.BlockSpec(memory_space=pltpu.HBM)] * 4
    land, weights = before[4:], before[:4]
    return pl.pallas_call(
        functools.partial(finish_kernel, bool(before)),
        out_shape=[shape((C, width), f32) for width in widths] + [shape((1, C), f32)],
        in_specs=vmem(1 + len(land)) + hbm[: len(weights)],
        out_specs=hbm + (hbm[:1] if before else vmem(1)),
        scratch_shapes=[
            pltpu.VMEM((rows, FF), f32),
            pltpu.VMEM((rows, FF), f32),
            pltpu.VMEM((rows, 3 * C), f32),
            pltpu.VMEM((rows, C), f32),
            pltpu.VMEM((QUADS * EXTRA, 128), f32),
            pltpu.VMEM((1, C), f32),
            pltpu.SemaphoreType.DMA((5,)),
        ],
        input_output_aliases={2 + n: n for n in range(len(weights))},
        compiler_params=pltpu.CompilerParams(vmem_limit_bytes=16 * MIB),
        cost_estimate=cost(10**6, 2 * MIB),
        name="finish_far" if before else "finish_own",
    )(chunks, *land, *weights)


def reduce_all(keep, sent, land, shift, lon_count, after):
    core_move = lambda lon, lat: (lon, lat ^ 1)
    chip_move = lambda e: lambda lon, lat: (lon ^ (e & 1), lat ^ (2 * (e >> 1)))
    deep_move = lambda e: lambda lon, lat: (lon ^ (2 * e), lat)

    def one(rows):
        return [shape((rows, FF), bf16)]

    got = shift(sent, move=core_move)
    parts = [shape((CHUNK, FF), f32)] + one(CHUNK) * (QUADS - 1)
    own, *parts = small_call(core_add_kernel, parts, (keep, got), "core_add", after=after)
    gots = [shift(value, move=chip_move(e)) for e, value in enumerate(parts, 1)]
    full = [shape((FULL, 128), bf16)]
    (total,) = small_call(chip_add_kernel, full, (own, *gots, land), "chip_add")
    reach = 1
    while reach < lon_count // 2:
        got = shift(total, move=deep_move(reach))
        reach *= 2
        (total,) = small_call(add_kernel, full, (total, got), "deep_add")
    near = [total] + [shift(total, move=chip_move(e)) for e in range(1, QUADS)]
    (total,) = small_call(join_kernel, [shape((QUADS * FULL, 128), bf16)], near, "join")
    got = shift(total, move=core_move)
    return finish(got, finish(total))


AXES = ("deep", "x", "y", "core")


def send(value, lon_count, lat_count, move):
    pairs = []
    for lon in range(lon_count):
        for lat in range(lat_count):
            to_lon, to_lat = move(lon, lat)
            pairs.append((lon * lat_count + lat, (to_lon % lon_count) * lat_count + to_lat % lat_count))
    return lax.ppermute(value, AXES, pairs)


def body(
    lon_count, lat_count,
    tokens, cotangent, land_sea, land_vector, triple_weight, project_weight, up_weight, down_weight, earth_bias,
):
    levels, rows, cols, features = tokens.shape
    shift = functools.partial(send, lon_count=lon_count, lat_count=lat_count)
    lon_windows = cols // WW

    own, north, side, corner = pack(tokens, cotangent, land_sea, land_vector, rows, cols)
    north = shift(north, move=lambda lon, lat: (lon, lat + 1))
    side = shift(side, move=lambda lon, lat: (lon + 1, lat))
    corner = shift(corner, move=lambda lon, lat: (lon + 1, lat + 1))
    bias = expand_bias(earth_bias)

    sizes = [part.size for part in piece_rows(rows, cols)]
    pieces = (own, north, side, corner)
    near = near_block(own, north, bias, triple_weight, project_weight, lon_windows)
    own, north, side, corner, keep, sent = block(
        pieces, bias, triple_weight, project_weight, up_weight, down_weight.T, near, lon_windows, sizes
    )
    north = shift(north, move=lambda lon, lat: (lon, lat - 1))
    side = shift(side, move=lambda lon, lat: (lon - 1, lat))
    corner = shift(corner, move=lambda lon, lat: (lon - 1, lat - 1))
    after = (north, side, corner)
    grad_tokens, land = to_home((own, north, side, corner), land_sea, sizes, rows, cols)
    triple, project, up, down, land = reduce_all(keep, sent, land, shift, lon_count, after)
    return grad_tokens.reshape(tokens.shape), triple, project, up, down.T, land.reshape(features)


def solution(mesh):
    lon_count, lat_count = mesh.shape["lon"], mesh.shape["lat"]
    fine = jax.sharding.Mesh(mesh.devices.reshape(lon_count // 2, 2, lat_count // 2, 2), AXES)
    lon, lat = AXES[:2], AXES[2:]
    return jax.shard_map(
        functools.partial(body, lon_count, lat_count),
        mesh=fine,
        in_specs=(
            P(None, lat, lon, None),
            P(None, lat, lon, None),
            P(lat, lon),
            P(),
            P(),
            P(),
            P(),
            P(),
            P(lat, None, None, None, None),
        ),
        out_specs=(P(None, lat, lon, None), P(), P(), P(), P(), P()),
        check_vma=False,
    )
```

```python
import functools
import math

import jax
import jax.numpy as jnp
import numpy as np
from jax import lax
from jax.experimental import pallas as pl
from jax.experimental.pallas import tpu as pltpu
from jax.sharding import PartitionSpec as P

Z = 4
WZ = 2
WH = 6
WW = 12
C = 192
HEADS = 6
HEAD = 32
FF = 768
HZ, HH, HW = WZ // 2, WH // 2, WW // 2
TOK = WZ * WH * WW
PLACES = WZ * WH
RELW = 2 * WW - 1
SPOTS = PLACES // 2
STRIP = -(-RELW * SPOTS // 128) * 128
RUN, SHORT = WW * SPOTS, (WW - HW) * SPOTS

mask_fill = -10000.0
norm_eps = 1e-05
log2e = 1.4426950408889634
root_half = 0.7071067811865476
inv_root_tau = 0.3989422804014327
score_scale = HEAD**-0.5

f32 = jnp.float32
bf16 = jnp.bfloat16
MIB = 1 << 20

QUADS = 4
FAR_FIRST = range(QUADS - 1, 0, -1)
PART = C // (2 * QUADS)
CHUNK = 3 * PART
BLOCKS = FF // 128
EXTRA = 8
FULL = BLOCKS * CHUNK + EXTRA


def mm(a, b):
    return lax.dot_general(a, b, (((1,), (0,)), ((), ())), preferred_element_type=f32)


def mm_nt(a, b):
    return lax.dot_general(a, b, (((1,), (1,)), ((), ())), preferred_element_type=f32)


def mm_tn(a, b):
    return lax.dot_general(a, b, (((0,), (0,)), ((), ())), preferred_element_type=f32)


def unit_norm(values):
    average = jnp.mean(values, -1, keepdims=True)
    centred = values - average
    variance = jnp.mean(centred * centred, -1, keepdims=True)
    spread = lax.rsqrt(variance + norm_eps)
    return centred * spread, spread


def norm_back(upstream, unit, spread):
    first = jnp.mean(upstream, -1, keepdims=True)
    second = jnp.mean(upstream * unit, -1, keepdims=True)
    return spread * (upstream - first - unit * second)


def piece_rows(rows, cols):
    home = np.arange(Z * rows * cols).reshape(Z, rows, cols)

    def run(level, row, col, width):
        levels = [(level * WZ + z - HZ) % Z for z in range(WZ)]
        return home[levels, row : row + HH, col : col + width].transpose(2, 0, 1).reshape(-1)

    levels = range(Z // WZ)
    parts = []
    for row in (0, rows - HH):
        whole = [run(a, row, w * WW - HW, WW) for w in range(1, cols // WW) for a in levels]
        parts.append(np.concatenate(whole + [run(a, row, 0, WW - HW) for a in levels]))
    for row in (0, rows - HH):
        parts.append(np.concatenate([run(a, row, cols - HW, HW) for a in levels]))
    return parts


def window_runs(lon_windows):
    levels = Z // WZ
    whole = (lon_windows - 1) * levels
    runs = [[(1, n * RUN, RUN), (0, n * RUN, RUN)] for n in range(whole)]
    for a in range(levels):
        inner = whole * RUN + a * SHORT
        west = (a * (RUN - SHORT), RUN - SHORT)
        runs.append([(3, *west), (1, inner, SHORT), (2, *west), (0, inner, SHORT)])
    return runs


def spots(places):
    return jnp.asarray(np.argsort(places).astype(np.int32)[None])


def one_hot(spot_ref):
    count = spot_ref.shape[1]
    rows = lax.broadcasted_iota(jnp.int32, (count, count), 0)
    return (rows == spot_ref[...]).astype(f32).astype(bf16)


def vmem(count):
    return [pl.BlockSpec(memory_space=pltpu.VMEM)] * count


def shape(dims, dtype):
    return jax.ShapeDtypeStruct(dims, dtype)


def cost(flops, moved):
    return pl.CostEstimate(flops=flops, bytes_accessed=moved, transcendentals=0)


def land_column(land_ref, rows, cols):
    eye = (
        lax.broadcasted_iota(jnp.int32, (cols, cols), 0)
        == lax.broadcasted_iota(jnp.int32, (cols, cols), 1)
    ).astype(f32)
    land = land_ref[...].astype(f32)
    parts = [jnp.sum(eye * land[i : i + 1, :], -1, keepdims=True) for i in range(rows)]
    return jnp.concatenate(parts, axis=0)


def pack_kernel(rows, cols, *refs):
    sources, outs, (tokens_ref, cot_ref, land_ref, vec_ref, perm_ref, sems) = refs[:5], refs[5:-6], refs[-6:]
    copies = [
        pltpu.make_async_copy(source, target, sems.at[n])
        for n, (source, target) in enumerate(zip(sources, (tokens_ref, cot_ref, land_ref, vec_ref, perm_ref)))
    ]
    for copy in copies:
        copy.start()
    for copy in copies:
        copy.wait()
    column = land_column(land_ref, rows, cols)
    added = column * vec_ref[...]
    added = jnp.concatenate([added] * Z, axis=0)
    embedded = (tokens_ref[...].astype(f32) + added).astype(bf16)
    perm = one_hot(perm_ref)
    left = mm(perm, embedded)
    right = mm(perm, cot_ref[...])
    packed = jnp.concatenate([left, right], axis=1)
    own_ref, north_ref, corner_ref, side_ref = outs
    start = 0
    for out in (own_ref, north_ref, side_ref, corner_ref):
        out[...] = packed[start : start + out.shape[0]].astype(bf16)
        start += out.shape[0]


def pack(tokens, cotangent, land_sea, vector, rows, cols):
    parts = piece_rows(rows, cols)
    perm = spots(np.concatenate(parts))
    count = Z * rows * cols
    return pl.pallas_call(
        functools.partial(pack_kernel, rows, cols),
        out_shape=[shape((parts[n].size, 2 * C), bf16) for n in (0, 1, 3, 2)],
        in_specs=[pl.BlockSpec(memory_space=pltpu.HBM)] * 5,
        out_specs=vmem(4),
        scratch_shapes=[
            pltpu.VMEM((count, C), bf16),
            pltpu.VMEM((count, C), bf16),
            pltpu.VMEM((rows, cols), jnp.int32),
            pltpu.VMEM((1, C), f32),
            pltpu.VMEM((1, count), jnp.int32),
            pltpu.SemaphoreType.DMA((5,)),
        ],
        cost_estimate=cost(4 * count * count * C, 4 * MIB),
        name="pack",
    )(tokens.reshape(count, C), cotangent.reshape(count, C), land_sea, vector.reshape(1, C), perm)


def floor_div(values, divisor):
    return (values * (65536 // divisor + 1)) >> 16


def remainder(values, divisor):
    return values - floor_div(values, divisor) * divisor


def place_order(order):
    half = floor_div(order, SPOTS)
    spot = order - half * SPOTS
    level = floor_div(spot, HH)
    return level * WH + half * HH + (spot - level * HH)


def bias_kernel(levels, table_ref, out_ref, *wide_refs):
    groups = levels * HEADS
    pairs = PLACES * PLACES
    row = lax.broadcasted_iota(jnp.int32, (HEADS * RELW, 1), 0)
    head = floor_div(row, RELW)
    start = head * STRIP + (RELW - 1 - (row - head * RELW)) * SPOTS
    ahead = lax.broadcasted_iota(jnp.int32, (HEADS * RELW, HEADS * STRIP), 1) - start
    onehot = ((ahead >= 0) & (ahead < SPOTS)).astype(f32).astype(bf16)
    row = lax.broadcasted_iota(jnp.int32, (pairs, 1), 0)
    source = place_order(floor_div(row, PLACES)) * PLACES + remainder(row, PLACES)
    reorder = (lax.broadcasted_iota(jnp.int32, (pairs, pairs), 1) == source).astype(f32).astype(bf16)
    tables = [table_ref[:, level, :].T for level in range(levels)]
    wide = jnp.zeros((levels * pairs, HEADS * STRIP), f32)
    for _ in range(2):
        terms = [table.astype(bf16) for table in tables]
        tables = [table - term.astype(f32) for table, term in zip(tables, terms)]
        ordered = jnp.concatenate([mm(reorder, term) for term in terms], axis=0)
        wide = wide + mm(ordered.astype(bf16), onehot)
    for level in range(levels):
        for head in range(HEADS):
            for n, wide_ref in enumerate(wide_refs):
                start = head * STRIP + n * 128
                rows = slice((level * HEADS + head) * pairs, (level * HEADS + head + 1) * pairs)
                wide_ref[rows, :] = wide[level * pairs : (level + 1) * pairs, start : start + 128]
    strips = groups * PLACES
    row = lax.broadcasted_iota(jnp.int32, (strips, 1), 0)
    spot = remainder(lax.broadcasted_iota(jnp.int32, (1, STRIP), 1), SPOTS)
    own = remainder(row, PLACES)
    first_level = (row < HEADS * PLACES).astype(jnp.int32)
    own_north = (own < SPOTS).astype(jnp.int32)
    own_low = (own - SPOTS * (1 - own_north) < HZ * HH).astype(jnp.int32)
    low = (spot < HZ * HH).astype(jnp.int32)
    pole = (lax.axis_index("y") + lax.axis_index("core") == 0).astype(jnp.int32)
    halves = []
    for half in range(2):
        parts = []
        for n, wide_ref in enumerate(wide_refs):
            here = spot[:, n * 128 : (n + 1) * 128]
            part = jnp.zeros((strips, 128), f32)
            for p in range(SPOTS):
                place = p // HH * WH + half * HH + p % HH
                part = jnp.where(here == p, wide_ref[pl.ds(place, strips, stride=PLACES), :], part)
            parts.append(part)
        strip = jnp.concatenate(parts, axis=1)
        differs = first_level * (own_low ^ low) + pole * (own_north ^ (1 - half))
        halves.append(jnp.where(differs > 0, strip + mask_fill, strip) * log2e)
    for w in range(WW):
        start = (WW - 1 - w) * SPOTS
        part = jnp.concatenate([strip[:, start : start + RUN] for strip in halves], axis=1)
        for g in range(groups):
            for half in range(2):
                rows = part[g * PLACES + half * SPOTS : g * PLACES + (half + 1) * SPOTS, :]
                out_ref[g, half * RUN + w * SPOTS : half * RUN + (w + 1) * SPOTS, :] = rows


def expand_bias(table):
    levels = table.shape[1]
    groups = levels * HEADS
    pairs = PLACES * PLACES
    flat = table[0].transpose(1, 3, 0, 2).reshape(HEADS * RELW, levels, pairs)
    return pl.pallas_call(
        functools.partial(bias_kernel, levels),
        out_shape=shape((groups, TOK, TOK), f32),
        in_specs=vmem(1),
        out_specs=vmem(1)[0],
        scratch_shapes=[pltpu.VMEM((groups * pairs, 128), f32)] * (STRIP // 128),
        compiler_params=pltpu.CompilerParams(vmem_limit_bytes=28 * MIB),
        cost_estimate=cost(10**9, 8 * MIB),
        name="bias",
    )(flat)


def head_masks(count):
    lane = lax.broadcasted_iota(jnp.int32, (count, C), 1)
    return [((lane >= h * HEAD) & (lane < (h + 1) * HEAD)).astype(f32) for h in range(HEADS)]


def stacked(values, masks):
    return jnp.concatenate([values * mask for mask in masks], axis=0)


def head_sum(values, masks):
    total = values[:TOK] * masks[0]
    for h in range(1, HEADS):
        total = total + values[h * TOK : (h + 1) * TOK] * masks[h]
    return total


def position():
    return lax.axis_index("core"), lax.axis_index("y") * 2 + lax.axis_index("x"), lax.axis_index("deep")


def chunk_rows(block):
    return pl.ds(pl.multiple_of(block * PART, PART), PART)


def split_parts(total_refs, keep_ref, send_ref):
    core, chip, _ = position()
    for out, side in ((keep_ref, core), (send_ref, 1 - core)):
        parts = []
        for g in range(QUADS):
            rows = chunk_rows(side * QUADS + jnp.bitwise_xor(chip, g))
            parts += [ref[rows, :] for ref in total_refs]
        out[...] = jnp.concatenate(parts, axis=0).astype(out.dtype)


def attend(first, runs, pieces, bias_ref, triple_ref, project_ref, *refs):
    q_ref, k_ref, v_ref, p_ref, mixed_ref, normed_ref, unit_ref, spread_ref, summed_ref, cot_ref = refs
    pieces = [piece.astype(f32) for piece in pieces]
    ordered = jnp.concatenate([pieces[n][start : start + count] for n, start, count in runs], axis=0)
    emb = ordered[:, :C]
    cot_ref[...] = ordered[:, C:].astype(bf16)
    unit, spread = unit_norm(emb)
    unit_ref[...] = unit
    spread_ref[...] = spread
    normed = unit.astype(bf16)
    normed_ref[...] = normed
    packed = mm(normed, triple_ref[...])
    q_ref[...] = packed[:, :C].astype(bf16)
    k_ref[...] = packed[:, C : 2 * C].astype(bf16)
    v_ref[...] = packed[:, 2 * C :].astype(bf16)
    masks = head_masks(TOK)
    masks_b = [mask.astype(bf16) for mask in masks]
    for w in range(emb.shape[0] // TOK):
        rows = slice(w * TOK, (w + 1) * TOK)
        heads = slice(w * HEADS, (w + 1) * HEADS)
        level = (first + w) % (Z // WZ)
        scores = mm_nt(stacked(q_ref[rows, :], masks_b), k_ref[rows, :])
        bias = bias_ref[level * HEADS : (level + 1) * HEADS].reshape(HEADS * TOK, TOK)
        raised = jnp.exp2(scores * (score_scale * log2e) + bias)
        probs = raised * (1.0 / jnp.sum(raised, -1, keepdims=True))
        probs_b = probs.astype(bf16)
        p_ref[heads] = probs_b.reshape(HEADS, TOK, TOK)
        mixed = head_sum(mm(probs_b, v_ref[rows, :]), masks).astype(bf16)
        mixed_ref[rows, :] = mixed
        summed_ref[rows, :] = emb[rows] + mm(mixed, project_ref[...]).astype(bf16).astype(f32)


def feed_back(summed, cot, up_ref, down_ref, gsum_ref, up_grad_ref, down_grad_ref):
    unit2, spread2 = unit_norm(summed)
    normed2 = unit2.astype(bf16)
    back = jnp.zeros(unit2.shape, f32)
    block = 256
    for start in range(0, FF, block):
        cols = slice(start, start + block)
        up_part = up_ref[:, cols]
        pre = mm(normed2, up_part)
        upstream = mm(cot, down_ref[:, cols])
        phi = 0.5 * (1.0 + lax.erf(pre * root_half))
        activated = (pre * phi).astype(bf16)
        slope = phi + pre * inv_root_tau * jnp.exp2(pre * pre * (-0.5 * log2e))
        hidden = (upstream * slope).astype(bf16)
        up_grad_ref[:, cols] = mm_tn(normed2, hidden)
        down_grad_ref[:, cols] = mm_tn(cot, activated)
        back = back + mm_nt(hidden, up_part)
    gsum_ref[...] = cot.astype(f32) + norm_back(back, unit2, spread2)


def attend_back(at, q_ref, k_ref, v_ref, p_ref, gsum_ref, project_ref, gq_ref, gk_ref, gv_ref):
    masks = head_masks(TOK)
    masks_b = [mask.astype(bf16) for mask in masks]
    for w in range(q_ref.shape[0] // TOK):
        rows = slice(w * TOK, (w + 1) * TOK)
        full_rows = slice(at + w * TOK, at + (w + 1) * TOK)
        grad = gsum_ref[full_rows, :].astype(bf16)
        grad_mixed_b = mm_nt(grad, project_ref[...]).astype(bf16)
        probs_b = p_ref[w * HEADS : (w + 1) * HEADS].reshape(HEADS * TOK, TOK)
        probs = probs_b.astype(f32)
        grad_probs = mm_nt(stacked(grad_mixed_b, masks_b), v_ref[rows, :])
        inner = jnp.sum(grad_probs * probs, -1, keepdims=True)
        scaled = (probs * (grad_probs - inner) * score_scale).astype(bf16)
        grad_q = head_sum(mm(scaled, k_ref[rows, :]), masks)
        grad_mixed_t = grad_mixed_b.astype(f32).T.astype(bf16)
        query_t = q_ref[rows, :].astype(f32).T.astype(bf16)
        grad_k, grad_v = [], []
        for h in range(HEADS):
            spot = slice(h * HEAD, (h + 1) * HEAD)
            span = slice(h * TOK, (h + 1) * TOK)
            grad_k.append(mm(query_t[spot], scaled[span]))
            grad_v.append(mm(grad_mixed_t[spot], probs_b[span]))
        gq_ref[full_rows, :] = grad_q.astype(bf16)
        gk_ref[full_rows, :] = jnp.concatenate(grad_k, axis=0).T.astype(bf16)
        gv_ref[full_rows, :] = jnp.concatenate(grad_v, axis=0).T.astype(bf16)


def halved(rows):
    return -(-rows // 16) * 8


def tokens_back(
    lon_windows, sizes, gq_ref, gk_ref, gv_ref, mixed, normed, unit, spread, gsum_ref, triple_ref, up_grad_ref, down_grad_ref,
    *rest,
):
    outs, (keep_ref, send_ref, total_ref) = rest[: len(sizes)], rest[len(sizes) :]
    triple = triple_ref[...]
    grad_normed = jnp.zeros(unit.shape, f32)
    parts = []
    for n, ref in enumerate((gq_ref, gk_ref, gv_ref)):
        grad = ref[...]
        grad_normed = grad_normed + mm_nt(grad, triple[:, n * C : (n + 1) * C])
        parts.append(mm_tn(normed, grad))
    parts.append(mm_tn(mixed, gsum_ref[...].astype(bf16)))
    total_ref[...] = jnp.concatenate(parts, axis=1)
    grad_normed = grad_normed.astype(bf16).astype(f32)
    grad_tokens = gsum_ref[...] + norm_back(grad_normed, unit, spread)
    parts, at = [[] for _ in sizes], 0
    for n, start, count in [run for window in window_runs(lon_windows) for run in window]:
        parts[n].append((start, grad_tokens[at : at + count]))
        at += count
    for size, out, part in zip(sizes, outs, parts):
        piece = jnp.concatenate([value for _, value in sorted(part, key=lambda item: item[0])], axis=0)
        half = halved(size)
        second = jnp.concatenate([piece[half:], jnp.zeros((2 * half - size, C), f32)], axis=0)
        out[...] = jnp.concatenate([piece[:half], second], axis=1).astype(bf16)
    split_parts((up_grad_ref, down_grad_ref, total_ref), keep_ref, send_ref)


def saved_shapes(count):
    dims = [((count, C), bf16)] * 3 + [((count // TOK * HEADS, TOK, TOK), bf16)] + [((count, C), bf16)] * 2
    return dims + [((count, C), f32), ((count, 1), f32), ((count, C), f32), ((count, C), bf16)]


SAVED = len(saved_shapes(TOK))


def split_runs(lon_windows):
    windows = window_runs(lon_windows)
    whole = (lon_windows - 1) * (Z // WZ)
    return whole, *[[run for window in part for run in window] for part in (windows[:whole], windows[whole:])]


def near_kernel(lon_windows, own_ref, north_ref, *refs):
    runs = split_runs(lon_windows)[1]
    attend(0, runs, (own_ref[...], north_ref[...]), *refs)


def near_block(own, north, bias, triple, project, lon_windows):
    count = split_runs(lon_windows)[0] * TOK
    return pl.pallas_call(
        functools.partial(near_kernel, lon_windows),
        out_shape=[shape(*dims) for dims in saved_shapes(count)],
        in_specs=vmem(5),
        out_specs=vmem(SAVED),
        compiler_params=pltpu.CompilerParams(vmem_limit_bytes=24 * MIB),
        cost_estimate=cost(3 * 10**9, 8 * MIB),
        name="near_block",
    )(own, north, bias, triple, project)


def block_kernel(lon_windows, sizes, *refs):
    whole, _, runs = split_runs(lon_windows)
    (own_ref, north_ref, corner_ref, side_ref), refs = refs[:4], refs[4:]
    pieces = (own_ref, north_ref, side_ref, corner_ref)
    (bias_ref, triple_ref, project_ref, up_ref, down_ref), refs = refs[:5], refs[5:]
    near, refs = refs[:SAVED], refs[SAVED:]
    outs, refs = refs[: len(sizes) + 2], refs[len(sizes) + 2 :]
    far, (gsum, up_grad, down_grad, gq, gk, gv, total) = refs[:SAVED], refs[SAVED:]
    attend(whole, runs, [ref[...] for ref in pieces], bias_ref, triple_ref, project_ref, *far)
    mixed, normed, unit, spread, summed, cot = [
        jnp.concatenate([one[...], other[...]], axis=0) for one, other in zip(near[4:], far[4:])
    ]
    feed_back(summed, cot, up_ref, down_ref, gsum, up_grad, down_grad)
    attend_back(0, *near[:4], gsum, project_ref, gq, gk, gv)
    attend_back(whole * TOK, *far[:4], gsum, project_ref, gq, gk, gv)
    tokens_back(lon_windows, sizes, gq, gk, gv, mixed, normed, unit, spread, gsum, triple_ref, up_grad, down_grad, *outs, total)


def block(pieces, bias, triple, project, up, down, near, lon_windows, sizes):
    count = sum(sizes)
    out_shape = [shape((halved(size), 2 * C), bf16) for size in sizes] + [
        shape((QUADS * CHUNK, FF), f32),
        shape((QUADS * CHUNK, FF), bf16),
    ]
    return pl.pallas_call(
        functools.partial(block_kernel, lon_windows, sizes),
        out_shape=out_shape,
        in_specs=vmem(9 + SAVED),
        out_specs=vmem(len(out_shape)),
        scratch_shapes=[pltpu.VMEM(*dims) for dims in saved_shapes(count - near[0].shape[0])]
        + [pltpu.VMEM((count, C), f32)]
        + [pltpu.VMEM((C, FF), f32)] * 2
        + [pltpu.VMEM((count, C), bf16)] * 3
        + [pltpu.VMEM((C, FF), f32)],
        compiler_params=pltpu.CompilerParams(vmem_limit_bytes=28 * MIB),
        cost_estimate=cost(8 * 10**9, 16 * MIB),
        name="block",
    )(*pieces, bias, triple, project, up, down, *near)


def home_kernel(sizes, rows, cols, own_ref, north_ref, side_ref, corner_ref, perm_ref, land_ref, out_ref, sum_ref):
    pieces = []
    for size, ref in zip(sizes, (own_ref, north_ref, side_ref, corner_ref)):
        wide = ref[...].astype(f32)
        pieces += [wide[:, :C], wide[: size - wide.shape[0], C:]]
    pieces = jnp.concatenate(pieces, axis=0).astype(bf16)
    grads = mm(one_hot(perm_ref), pieces)
    out_ref[...] = grads.astype(bf16)
    column = jnp.concatenate([land_column(land_ref, rows, cols)] * Z, axis=0)
    sum_ref[...] = jnp.sum(grads * column, 0, keepdims=True)


def to_home(pieces, land_sea, sizes, rows, cols):
    count = Z * rows * cols
    perm = spots(np.argsort(np.concatenate(piece_rows(rows, cols))))
    return pl.pallas_call(
        functools.partial(home_kernel, sizes, rows, cols),
        out_shape=[shape((count, C), bf16), shape((1, C), f32)],
        in_specs=vmem(6),
        out_specs=vmem(2),
        compiler_params=pltpu.CompilerParams(vmem_limit_bytes=32 * MIB),
        cost_estimate=cost(2 * count * count * C, 4 * MIB),
        name="to_home",
    )(*pieces, perm, land_sea)


def core_add_kernel(keep_ref, got_ref, *refs):
    own_ref, outs = refs[-QUADS], refs[1 - QUADS :]
    total = keep_ref[...] + got_ref[...].astype(f32)
    own_ref[...] = total[:CHUNK]
    for e, out in zip(FAR_FIRST, outs):
        out[...] = total[e * CHUNK : (e + 1) * CHUNK].astype(bf16)


def chip_add_kernel(keep_ref, *refs):
    gots, (land_ref, out_ref) = refs[:-2], refs[-2:]
    total = keep_ref[...]
    for ref in gots:
        total = total + ref[...].astype(f32)
    land = land_ref[...]
    rest = jnp.concatenate([land[:, 128:], jnp.zeros((1, 2 * 128 - C), f32)], axis=1)
    parts = [total[:, n * 128 : (n + 1) * 128] for n in range(BLOCKS)]
    total = jnp.concatenate(parts + [land[:, :128], rest, jnp.zeros((EXTRA - 2, 128), f32)], axis=0)
    out_ref[...] = total.astype(bf16)


def add_kernel(one_ref, two_ref, out_ref):
    out_ref[...] = (one_ref[...].astype(f32) + two_ref[...].astype(f32)).astype(bf16)


def join_kernel(*refs):
    refs[-1][...] = jnp.concatenate([ref[...] for ref in refs[:-1]], axis=0)


def small_call(kernel, out_shape, args, name, after=(), scratch=()):
    return pl.pallas_call(
        kernel,
        out_shape=out_shape,
        in_specs=vmem(len(args)) + [pl.BlockSpec(memory_space=pl.ANY)] * len(after),
        out_specs=vmem(len(out_shape)),
        scratch_shapes=scratch,
        compiler_params=pltpu.CompilerParams(vmem_limit_bytes=16 * MIB),
        cost_estimate=cost(10**6, 2 * MIB),
        name=name,
    )(*args, *after)


def finish_kernel(far, chunks_ref, *refs):
    if far:
        before_ref, refs = refs[0], refs[5:]
    outs, land_ref, (up_ref, down_ref, triple_ref, project_ref, lands_ref, sum_ref, sems) = refs[:4], refs[4], refs[5:]
    core, chip, _ = position()
    side = 1 - core if far else core
    for g in range(QUADS):
        tiles = chunks_ref[g * FULL : (g + 1) * FULL, :].astype(f32)
        chunk = jnp.concatenate([tiles[n * CHUNK : (n + 1) * CHUNK] for n in range(BLOCKS)], axis=1)
        block = jnp.bitwise_xor(chip, g)
        rows = chunk_rows(block)
        up_ref[rows, :] = chunk[:PART]
        down_ref[rows, :] = chunk[PART : 2 * PART]
        triple_ref[rows, :] = chunk[2 * PART : CHUNK, : 3 * C]
        project_ref[rows, :] = chunk[2 * PART : CHUNK, 3 * C :]
        lands_ref[pl.ds(pl.multiple_of(block * EXTRA, EXTRA), EXTRA), :] = tiles[BLOCKS * CHUNK :]
    copies = []
    for n, (source, out) in enumerate(zip((triple_ref, project_ref, up_ref, down_ref), outs)):
        rows = pl.ds(pl.multiple_of(side * QUADS * PART, 8), QUADS * PART)
        copies.append(pltpu.make_async_copy(source, out.at[rows, :], sems.at[n]))
    for copy in copies:
        copy.start()
    lands = lands_ref[...]
    lands = [sum(lands[g * EXTRA + n : g * EXTRA + n + 1] for g in range(QUADS)) for n in range(2)]
    land = jnp.concatenate([lands[0], lands[1][:, : C - 128]], axis=1)
    if far:
        sum_ref[...] = land + before_ref[...]
        copies.append(pltpu.make_async_copy(sum_ref, land_ref, sems.at[4]))
        copies[-1].start()
    else:
        land_ref[...] = land
    for copy in copies:
        copy.wait()


def finish(chunks, before=()):
    rows = QUADS * PART
    widths = (3 * C, C, FF, FF)
    hbm = [pl.BlockSpec(memory_space=pltpu.HBM)] * 4
    land, weights = before[4:], before[:4]
    return pl.pallas_call(
        functools.partial(finish_kernel, bool(before)),
        out_shape=[shape((C, width), f32) for width in widths] + [shape((1, C), f32)],
        in_specs=vmem(1 + len(land)) + hbm[: len(weights)],
        out_specs=hbm + (hbm[:1] if before else vmem(1)),
        scratch_shapes=[
            pltpu.VMEM((rows, FF), f32),
            pltpu.VMEM((rows, FF), f32),
            pltpu.VMEM((rows, 3 * C), f32),
            pltpu.VMEM((rows, C), f32),
            pltpu.VMEM((QUADS * EXTRA, 128), f32),
            pltpu.VMEM((1, C), f32),
            pltpu.SemaphoreType.DMA((5,)),
        ],
        input_output_aliases={2 + n: n for n in range(len(weights))},
        compiler_params=pltpu.CompilerParams(vmem_limit_bytes=16 * MIB),
        cost_estimate=cost(10**6, 2 * MIB),
        name="finish_far" if before else "finish_own",
    )(chunks, *land, *weights)


def reduce_all(keep, sent, land, shift, lon_count, after):
    core_move = lambda lon, lat: (lon, lat ^ 1)
    chip_move = lambda e: lambda lon, lat: (lon ^ (e & 1), lat ^ (2 * (e >> 1)))
    deep_move = lambda e: lambda lon, lat: (lon ^ (2 * e), lat)

    def one(rows):
        return [shape((rows, FF), bf16)]

    got = shift(sent, move=core_move)
    parts = [shape((CHUNK, FF), f32)] + one(CHUNK) * (QUADS - 1)
    own, *parts = small_call(core_add_kernel, parts, (keep, got), "core_add", after=after)
    gots = [shift(value, move=chip_move(e)) for e, value in zip(FAR_FIRST, parts)]
    full = [shape((FULL, 128), bf16)]
    (total,) = small_call(chip_add_kernel, full, (own, *gots, land), "chip_add")
    reach = 1
    while reach < lon_count // 2:
        got = shift(total, move=deep_move(reach))
        reach *= 2
        (total,) = small_call(add_kernel, full, (total, got), "deep_add")
    near = [total] + [shift(total, move=chip_move(e)) for e in range(1, QUADS)]
    (total,) = small_call(join_kernel, [shape((QUADS * FULL, 128), bf16)], near, "join")
    got = shift(total, move=core_move)
    return finish(got, finish(total))


AXES = ("deep", "x", "y", "core")


def send(value, lon_count, lat_count, move):
    pairs = []
    for lon in range(lon_count):
        for lat in range(lat_count):
            to_lon, to_lat = move(lon, lat)
            pairs.append((lon * lat_count + lat, (to_lon % lon_count) * lat_count + to_lat % lat_count))
    return lax.ppermute(value, AXES, pairs)


def body(
    lon_count, lat_count,
    tokens, cotangent, land_sea, land_vector, triple_weight, project_weight, up_weight, down_weight, earth_bias,
):
    levels, rows, cols, features = tokens.shape
    shift = functools.partial(send, lon_count=lon_count, lat_count=lat_count)
    lon_windows = cols // WW

    own, north, corner, side = pack(tokens, cotangent, land_sea, land_vector, rows, cols)
    north = shift(north, move=lambda lon, lat: (lon, lat + 1))
    corner = shift(corner, move=lambda lon, lat: (lon + 1, lat + 1))
    side = shift(side, move=lambda lon, lat: (lon + 1, lat))
    bias = expand_bias(earth_bias)

    sizes = [part.size for part in piece_rows(rows, cols)]
    pieces = (own, north, corner, side)
    near = near_block(own, north, bias, triple_weight, project_weight, lon_windows)
    own, north, side, corner, keep, sent = block(
        pieces, bias, triple_weight, project_weight, up_weight, down_weight.T, near, lon_windows, sizes
    )
    north = shift(north, move=lambda lon, lat: (lon, lat - 1))
    side = shift(side, move=lambda lon, lat: (lon - 1, lat))
    corner = shift(corner, move=lambda lon, lat: (lon - 1, lat - 1))
    after = (north, side, corner)
    grad_tokens, land = to_home((own, north, side, corner), land_sea, sizes, rows, cols)
    triple, project, up, down, land = reduce_all(keep, sent, land, shift, lon_count, after)
    return grad_tokens.reshape(tokens.shape), triple, project, up, down.T, land.reshape(features)


def solution(mesh):
    lon_count, lat_count = mesh.shape["lon"], mesh.shape["lat"]
    fine = jax.sharding.Mesh(mesh.devices.reshape(lon_count // 2, 2, lat_count // 2, 2), AXES)
    lon, lat = AXES[:2], AXES[2:]
    return jax.shard_map(
        functools.partial(body, lon_count, lat_count),
        mesh=fine,
        in_specs=(
            P(None, lat, lon, None),
            P(None, lat, lon, None),
            P(lat, lon),
            P(),
            P(),
            P(),
            P(),
            P(),
            P(lat, None, None, None, None),
        ),
        out_specs=(P(None, lat, lon, None), P(), P(), P(), P(), P()),
        check_vma=False,
    )
```

```python
import functools
import math

import jax
import jax.numpy as jnp
import numpy as np
from jax import lax
from jax.experimental import pallas as pl
from jax.experimental.pallas import tpu as pltpu
from jax.sharding import PartitionSpec as P

Z = 4
WZ = 2
WH = 6
WW = 12
C = 192
HEADS = 6
HEAD = 32
FF = 768
HZ, HH, HW = WZ // 2, WH // 2, WW // 2
TOK = WZ * WH * WW
PLACES = WZ * WH
RELW = 2 * WW - 1
SPOTS = PLACES // 2
STRIP = -(-RELW * SPOTS // 128) * 128
RUN, SHORT = WW * SPOTS, (WW - HW) * SPOTS

mask_fill = -10000.0
norm_eps = 1e-05
log2e = 1.4426950408889634
root_half = 0.7071067811865476
inv_root_tau = 0.3989422804014327
score_scale = HEAD**-0.5

f32 = jnp.float32
bf16 = jnp.bfloat16
MIB = 1 << 20

QUADS = 4
FAR_FIRST = range(QUADS - 1, 0, -1)
PART = C // (2 * QUADS)
CHUNK = 3 * PART
BLOCKS = FF // 128
EXTRA = 8
FULL = BLOCKS * CHUNK + EXTRA


def mm(a, b):
    return lax.dot_general(a, b, (((1,), (0,)), ((), ())), preferred_element_type=f32)


def mm_nt(a, b):
    return lax.dot_general(a, b, (((1,), (1,)), ((), ())), preferred_element_type=f32)


def mm_tn(a, b):
    return lax.dot_general(a, b, (((0,), (0,)), ((), ())), preferred_element_type=f32)


def unit_norm(values):
    average = jnp.mean(values, -1, keepdims=True)
    centred = values - average
    variance = jnp.mean(centred * centred, -1, keepdims=True)
    spread = lax.rsqrt(variance + norm_eps)
    return centred * spread, spread


def norm_back(upstream, unit, spread):
    first = jnp.mean(upstream, -1, keepdims=True)
    second = jnp.mean(upstream * unit, -1, keepdims=True)
    return spread * (upstream - first - unit * second)


def piece_rows(rows, cols):
    home = np.arange(Z * rows * cols).reshape(Z, rows, cols)

    def run(level, row, col, width):
        levels = [(level * WZ + z - HZ) % Z for z in range(WZ)]
        return home[levels, row : row + HH, col : col + width].transpose(2, 0, 1).reshape(-1)

    levels = range(Z // WZ)
    parts = []
    for row in (0, rows - HH):
        whole = [run(a, row, w * WW - HW, WW) for w in range(1, cols // WW) for a in levels]
        parts.append(np.concatenate(whole + [run(a, row, 0, WW - HW) for a in levels]))
    for row in (0, rows - HH):
        parts.append(np.concatenate([run(a, row, cols - HW, HW) for a in levels]))
    return parts


def window_runs(lon_windows):
    levels = Z // WZ
    whole = (lon_windows - 1) * levels
    runs = [[(1, n * RUN, RUN), (0, n * RUN, RUN)] for n in range(whole)]
    for a in range(levels):
        inner = whole * RUN + a * SHORT
        west = (a * (RUN - SHORT), RUN - SHORT)
        runs.append([(3, *west), (1, inner, SHORT), (2, *west), (0, inner, SHORT)])
    return runs


def spots(places):
    return jnp.asarray(np.argsort(places).astype(np.int32)[None])


def one_hot(spot_ref):
    count = spot_ref.shape[1]
    rows = lax.broadcasted_iota(jnp.int32, (count, count), 0)
    return (rows == spot_ref[...]).astype(f32).astype(bf16)


def vmem(count):
    return [pl.BlockSpec(memory_space=pltpu.VMEM)] * count


def shape(dims, dtype):
    return jax.ShapeDtypeStruct(dims, dtype)


def cost(flops, moved):
    return pl.CostEstimate(flops=flops, bytes_accessed=moved, transcendentals=0)


def land_column(land_ref, rows, cols):
    eye = (
        lax.broadcasted_iota(jnp.int32, (cols, cols), 0)
        == lax.broadcasted_iota(jnp.int32, (cols, cols), 1)
    ).astype(f32)
    land = land_ref[...].astype(f32)
    parts = [jnp.sum(eye * land[i : i + 1, :], -1, keepdims=True) for i in range(rows)]
    return jnp.concatenate(parts, axis=0)


def pack_kernel(rows, cols, *refs):
    sources, outs, (tokens_ref, cot_ref, land_ref, vec_ref, perm_ref, sems) = refs[:5], refs[5:-6], refs[-6:]
    copies = [
        pltpu.make_async_copy(source, target, sems.at[n])
        for n, (source, target) in enumerate(zip(sources, (tokens_ref, cot_ref, land_ref, vec_ref, perm_ref)))
    ]
    for copy in copies:
        copy.start()
    for copy in copies:
        copy.wait()
    column = land_column(land_ref, rows, cols)
    added = column * vec_ref[...]
    added = jnp.concatenate([added] * Z, axis=0)
    embedded = (tokens_ref[...].astype(f32) + added).astype(bf16)
    perm = one_hot(perm_ref)
    column = jnp.concatenate([column] * Z, axis=0)
    spare = jnp.broadcast_to(column, (column.shape[0], 2 * 128 - C)).astype(bf16)
    left = mm(perm, jnp.concatenate([embedded, spare], axis=1))
    left, flags = left[:, :C], left[:, C : C + 1]
    right = mm(perm, cot_ref[...])
    packed = jnp.concatenate([left, right], axis=1)
    start = 0
    for out in outs:
        count = out.shape[0] - EXTRA
        eye = lax.broadcasted_iota(jnp.int32, (count, count), 0) == lax.broadcasted_iota(jnp.int32, (count, count), 1)
        row = jnp.sum(jnp.where(eye, flags[start : start + count], 0.0), 0, keepdims=True)
        row = jnp.concatenate([row, jnp.zeros((1, 2 * C - count), f32)], axis=1)
        row = jnp.broadcast_to(row, (EXTRA, 2 * C))
        out[...] = jnp.concatenate([packed[start : start + count], row], axis=0).astype(bf16)
        start += count


def pack(tokens, cotangent, land_sea, vector, rows, cols):
    parts = piece_rows(rows, cols)
    perm = spots(np.concatenate(parts))
    count = Z * rows * cols
    return pl.pallas_call(
        functools.partial(pack_kernel, rows, cols),
        out_shape=[shape((part.size + EXTRA, 2 * C), bf16) for part in parts],
        in_specs=[pl.BlockSpec(memory_space=pltpu.HBM)] * 5,
        out_specs=vmem(4),
        scratch_shapes=[
            pltpu.VMEM((count, C), bf16),
            pltpu.VMEM((count, C), bf16),
            pltpu.VMEM((rows, cols), jnp.int32),
            pltpu.VMEM((1, C), f32),
            pltpu.VMEM((1, count), jnp.int32),
            pltpu.SemaphoreType.DMA((5,)),
        ],
        cost_estimate=cost(4 * count * count * C, 4 * MIB),
        name="pack",
    )(tokens.reshape(count, C), cotangent.reshape(count, C), land_sea, vector.reshape(1, C), perm)


def floor_div(values, divisor):
    return (values * (65536 // divisor + 1)) >> 16


def remainder(values, divisor):
    return values - floor_div(values, divisor) * divisor


def place_order(order):
    half = floor_div(order, SPOTS)
    spot = order - half * SPOTS
    level = floor_div(spot, HH)
    return level * WH + half * HH + (spot - level * HH)


def bias_kernel(levels, table_ref, out_ref, *wide_refs):
    groups = levels * HEADS
    pairs = PLACES * PLACES
    row = lax.broadcasted_iota(jnp.int32, (HEADS * RELW, HEADS * STRIP), 0)
    lane = lax.broadcasted_iota(jnp.int32, (HEADS * RELW, HEADS * STRIP), 1)
    head = floor_div(row, RELW)
    ahead = lane - (head * STRIP + (RELW - 1 - (row - head * RELW)) * SPOTS)
    onehot = ((ahead >= 0) & (ahead < SPOTS)).astype(f32).astype(bf16)
    row = lax.broadcasted_iota(jnp.int32, (pairs, pairs), 0)
    source = place_order(floor_div(row, PLACES)) * PLACES + remainder(row, PLACES)
    reorder = (lax.broadcasted_iota(jnp.int32, (pairs, pairs), 1) == source).astype(f32).astype(bf16)
    for level in range(levels):
        table = table_ref[:, level, :].T
        high = table.astype(bf16)
        rest = (table - high.astype(f32)).astype(bf16)
        wide = mm(mm(reorder, high).astype(bf16), onehot) + mm(mm(reorder, rest).astype(bf16), onehot)
        for head in range(HEADS):
            for n, wide_ref in enumerate(wide_refs):
                start = head * STRIP + n * 128
                wide_ref[(level * HEADS + head) * pairs : (level * HEADS + head + 1) * pairs, :] = wide[:, start : start + 128]
    strips = groups * PLACES
    row = lax.broadcasted_iota(jnp.int32, (strips, STRIP), 0)
    spot = remainder(lax.broadcasted_iota(jnp.int32, (strips, STRIP), 1), SPOTS)
    own = remainder(row, PLACES)
    first_level = (row < HEADS * PLACES).astype(jnp.int32)
    own_north = (own < SPOTS).astype(jnp.int32)
    own_low = (own - SPOTS * (1 - own_north) < HZ * HH).astype(jnp.int32)
    low = (spot < HZ * HH).astype(jnp.int32)
    pole = (lax.axis_index("y") + lax.axis_index("core") == 0).astype(jnp.int32)
    halves = []
    for half in range(2):
        parts = []
        for n, wide_ref in enumerate(wide_refs):
            here = spot[:, n * 128 : (n + 1) * 128]
            part = jnp.zeros((strips, 128), f32)
            for p in range(SPOTS):
                place = p // HH * WH + half * HH + p % HH
                part = jnp.where(here == p, wide_ref[pl.ds(place, strips, stride=PLACES), :], part)
            parts.append(part)
        strip = jnp.concatenate(parts, axis=1)
        differs = first_level * (own_low ^ low) + pole * (own_north ^ (1 - half))
        halves.append(jnp.where(differs > 0, strip + mask_fill, strip) * log2e)
    for w in range(WW):
        start = (WW - 1 - w) * SPOTS
        part = jnp.concatenate([strip[:, start : start + RUN] for strip in halves], axis=1)
        for g in range(groups):
            for half in range(2):
                rows = part[g * PLACES + half * SPOTS : g * PLACES + (half + 1) * SPOTS, :]
                out_ref[g, half * RUN + w * SPOTS : half * RUN + (w + 1) * SPOTS, :] = rows


def expand_bias(table):
    levels = table.shape[1]
    groups = levels * HEADS
    pairs = PLACES * PLACES
    flat = table[0].transpose(1, 3, 0, 2).reshape(HEADS * RELW, levels, pairs)
    return pl.pallas_call(
        functools.partial(bias_kernel, levels),
        out_shape=shape((groups, TOK, TOK), f32),
        in_specs=vmem(1),
        out_specs=vmem(1)[0],
        scratch_shapes=[pltpu.VMEM((groups * pairs, 128), f32)] * (STRIP // 128),
        compiler_params=pltpu.CompilerParams(vmem_limit_bytes=28 * MIB),
        cost_estimate=cost(10**9, 8 * MIB),
        name="bias",
    )(flat)


def head_masks(count):
    lane = lax.broadcasted_iota(jnp.int32, (count, C), 1)
    return [((lane >= h * HEAD) & (lane < (h + 1) * HEAD)).astype(f32) for h in range(HEADS)]


def stacked(values, masks):
    return jnp.concatenate([values * mask for mask in masks], axis=0)


def head_sum(values, masks):
    total = values[:TOK] * masks[0]
    for h in range(1, HEADS):
        total = total + values[h * TOK : (h + 1) * TOK] * masks[h]
    return total


def position():
    return lax.axis_index("core"), lax.axis_index("y") * 2 + lax.axis_index("x"), lax.axis_index("deep")


def chunk_rows(block):
    return pl.ds(pl.multiple_of(block * PART, PART), PART)


def split_parts(total_refs, keep_ref, send_ref):
    core, chip, _ = position()
    for out, side in ((keep_ref, core), (send_ref, 1 - core)):
        parts = []
        for g in range(QUADS):
            rows = chunk_rows(side * QUADS + jnp.bitwise_xor(chip, g))
            parts += [ref[rows, :] for ref in total_refs]
        out[...] = jnp.concatenate(parts, axis=0).astype(out.dtype)


def attend(first, runs, pieces, bias_ref, triple_ref, project_ref, *refs):
    q_ref, k_ref, v_ref, p_ref, mixed_ref, normed_ref, unit_ref, spread_ref, summed_ref, cot_ref = refs
    pieces = [piece.astype(f32) for piece in pieces]
    ordered = jnp.concatenate([pieces[n][start : start + count] for n, start, count in runs], axis=0)
    emb = ordered[:, :C]
    cot_ref[...] = ordered[:, C:].astype(bf16)
    unit, spread = unit_norm(emb)
    unit_ref[...] = unit
    spread_ref[...] = spread
    normed = unit.astype(bf16)
    normed_ref[...] = normed
    packed = mm(normed, triple_ref[...])
    q_ref[...] = packed[:, :C].astype(bf16)
    k_ref[...] = packed[:, C : 2 * C].astype(bf16)
    v_ref[...] = packed[:, 2 * C :].astype(bf16)
    masks = head_masks(TOK)
    masks_b = [mask.astype(bf16) for mask in masks]
    for w in range(emb.shape[0] // TOK):
        rows = slice(w * TOK, (w + 1) * TOK)
        heads = slice(w * HEADS, (w + 1) * HEADS)
        level = (first + w) % (Z // WZ)
        scores = mm_nt(stacked(q_ref[rows, :], masks_b), k_ref[rows, :])
        bias = bias_ref[level * HEADS : (level + 1) * HEADS].reshape(HEADS * TOK, TOK)
        raised = jnp.exp2(scores * (score_scale * log2e) + bias)
        probs = raised * (1.0 / jnp.sum(raised, -1, keepdims=True))
        probs_b = probs.astype(bf16)
        p_ref[heads] = probs_b.reshape(HEADS, TOK, TOK)
        mixed = head_sum(mm(probs_b, v_ref[rows, :]), masks).astype(bf16)
        mixed_ref[rows, :] = mixed
        summed_ref[rows, :] = emb[rows] + mm(mixed, project_ref[...]).astype(bf16).astype(f32)


def feed_back(summed, cot, up_ref, down_ref, gsum_ref, up_grad_ref, down_grad_ref):
    unit2, spread2 = unit_norm(summed)
    normed2 = unit2.astype(bf16)
    back = jnp.zeros(unit2.shape, f32)
    block = 256
    for start in range(0, FF, block):
        cols = slice(start, start + block)
        up_part = up_ref[:, cols]
        pre = mm(normed2, up_part)
        upstream = mm(cot, down_ref[:, cols])
        phi = 0.5 * (1.0 + lax.erf(pre * root_half))
        activated = (pre * phi).astype(bf16)
        slope = phi + pre * inv_root_tau * jnp.exp2(pre * pre * (-0.5 * log2e))
        hidden = (upstream * slope).astype(bf16)
        up_grad_ref[:, cols] = mm_tn(normed2, hidden)
        down_grad_ref[:, cols] = mm_tn(cot, activated)
        back = back + mm_nt(hidden, up_part)
    gsum_ref[...] = cot.astype(f32) + norm_back(back, unit2, spread2)


def attend_back(at, q_ref, k_ref, v_ref, p_ref, gsum_ref, project_ref, gq_ref, gk_ref, gv_ref):
    masks = head_masks(TOK)
    masks_b = [mask.astype(bf16) for mask in masks]
    for w in range(q_ref.shape[0] // TOK):
        rows = slice(w * TOK, (w + 1) * TOK)
        full_rows = slice(at + w * TOK, at + (w + 1) * TOK)
        grad = gsum_ref[full_rows, :].astype(bf16)
        grad_mixed_b = mm_nt(grad, project_ref[...]).astype(bf16)
        probs_b = p_ref[w * HEADS : (w + 1) * HEADS].reshape(HEADS * TOK, TOK)
        probs = probs_b.astype(f32)
        grad_probs = mm_nt(stacked(grad_mixed_b, masks_b), v_ref[rows, :])
        inner = jnp.sum(grad_probs * probs, -1, keepdims=True)
        scaled = (probs * (grad_probs - inner) * score_scale).astype(bf16)
        grad_q = head_sum(mm(scaled, k_ref[rows, :]), masks)
        grad_mixed_t = grad_mixed_b.astype(f32).T.astype(bf16)
        query_t = q_ref[rows, :].astype(f32).T.astype(bf16)
        grad_k, grad_v = [], []
        for h in range(HEADS):
            spot = slice(h * HEAD, (h + 1) * HEAD)
            span = slice(h * TOK, (h + 1) * TOK)
            grad_k.append(mm(query_t[spot], scaled[span]))
            grad_v.append(mm(grad_mixed_t[spot], probs_b[span]))
        gq_ref[full_rows, :] = grad_q.astype(bf16)
        gk_ref[full_rows, :] = jnp.concatenate(grad_k, axis=0).T.astype(bf16)
        gv_ref[full_rows, :] = jnp.concatenate(grad_v, axis=0).T.astype(bf16)


def halved(rows):
    return -(-rows // 16) * 8


def tokens_back(
    lon_windows, sizes, gq_ref, gk_ref, gv_ref, mixed, normed, unit, spread, gsum_ref, triple_ref, up_grad_ref, down_grad_ref,
    *rest,
):
    flag_refs, rest = rest[: len(sizes)], rest[len(sizes) :]
    outs, (land_ref, keep_ref, send_ref, total_ref) = rest[: len(sizes) - 1], rest[len(sizes) - 1 :]
    triple = triple_ref[...]
    grad_normed = jnp.zeros(unit.shape, f32)
    parts = []
    for n, ref in enumerate((gq_ref, gk_ref, gv_ref)):
        grad = ref[...]
        grad_normed = grad_normed + mm_nt(grad, triple[:, n * C : (n + 1) * C])
        parts.append(mm_tn(normed, grad))
    parts.append(mm_tn(mixed, gsum_ref[...].astype(bf16)))
    total_ref[...] = jnp.concatenate(parts, axis=1)
    grad_normed = grad_normed.astype(bf16).astype(f32)
    grad_tokens = gsum_ref[...] + norm_back(grad_normed, unit, spread)
    parts, at = [[] for _ in sizes], 0
    for n, start, count in [run for window in window_runs(lon_windows) for run in window]:
        parts[n].append((start, grad_tokens[at : at + count]))
        at += count
    land = jnp.zeros((EXTRA, C), f32)
    wide = []
    for size, flag_ref, part in zip(sizes, flag_refs, parts):
        piece = jnp.concatenate([value for _, value in sorted(part, key=lambda item: item[0])], axis=0)
        flags = flag_ref[size - 8 : size + 8, :].astype(f32)[8:, :size]
        land = land + mm(flags.astype(bf16), piece.astype(bf16))
        half = halved(size)
        second = jnp.concatenate([piece[half:], jnp.zeros((2 * half - size, C), f32)], axis=0)
        wide.append(jnp.concatenate([piece[:half], second], axis=1))
    land_ref[...] = land[0:1]
    own, north, side, corner = wide
    for out, value in zip(outs, (own, jnp.concatenate([north, corner], axis=0), side)):
        out[...] = value.astype(bf16)
    split_parts((up_grad_ref, down_grad_ref, total_ref), keep_ref, send_ref)


def saved_shapes(count):
    dims = [((count, C), bf16)] * 3 + [((count // TOK * HEADS, TOK, TOK), bf16)] + [((count, C), bf16)] * 2
    return dims + [((count, C), f32), ((count, 1), f32), ((count, C), f32), ((count, C), bf16)]


SAVED = len(saved_shapes(TOK))


def split_runs(lon_windows):
    windows = window_runs(lon_windows)
    whole = (lon_windows - 1) * (Z // WZ)
    return whole, *[[run for window in part for run in window] for part in (windows[:whole], windows[whole:])]


def near_kernel(lon_windows, own_ref, north_ref, *refs):
    runs = split_runs(lon_windows)[1]
    attend(0, runs, (own_ref[...], north_ref[...]), *refs)


def near_block(own, north, bias, triple, project, lon_windows):
    count = split_runs(lon_windows)[0] * TOK
    return pl.pallas_call(
        functools.partial(near_kernel, lon_windows),
        out_shape=[shape(*dims) for dims in saved_shapes(count)],
        in_specs=vmem(5),
        out_specs=vmem(SAVED),
        compiler_params=pltpu.CompilerParams(vmem_limit_bytes=24 * MIB),
        cost_estimate=cost(3 * 10**9, 8 * MIB),
        name="near_block",
    )(own, north, bias, triple, project)


def block_kernel(lon_windows, sizes, *refs):
    whole, _, runs = split_runs(lon_windows)
    pieces, refs = refs[:4], refs[4:]
    (bias_ref, triple_ref, project_ref, up_ref, down_ref), refs = refs[:5], refs[5:]
    near, refs = refs[:SAVED], refs[SAVED:]
    outs, refs = refs[: len(sizes) + 2], refs[len(sizes) + 2 :]
    far, (gsum, up_grad, down_grad, gq, gk, gv, total) = refs[:SAVED], refs[SAVED:]
    attend(whole, runs, [ref[...] for ref in pieces], bias_ref, triple_ref, project_ref, *far)
    mixed, normed, unit, spread, summed, cot = [
        jnp.concatenate([one[...], other[...]], axis=0) for one, other in zip(near[4:], far[4:])
    ]
    feed_back(summed, cot, up_ref, down_ref, gsum, up_grad, down_grad)
    attend_back(0, *near[:4], gsum, project_ref, gq, gk, gv)
    attend_back(whole * TOK, *far[:4], gsum, project_ref, gq, gk, gv)
    tokens_back(
        lon_windows, sizes, gq, gk, gv, mixed, normed, unit, spread, gsum, triple_ref, up_grad, down_grad,
        *pieces, *outs, total,
    )


def block(pieces, bias, triple, project, up, down, near, lon_windows, sizes):
    count = sum(sizes)
    own, north, side, corner = [halved(size) for size in sizes]
    out_shape = [shape((size, 2 * C), bf16) for size in (own, north + corner, side)] + [
        shape((1, C), f32),
        shape((QUADS * CHUNK, FF), f32),
        shape((QUADS * CHUNK, FF), bf16),
    ]
    return pl.pallas_call(
        functools.partial(block_kernel, lon_windows, sizes),
        out_shape=out_shape,
        in_specs=vmem(9 + SAVED),
        out_specs=vmem(len(out_shape)),
        scratch_shapes=[pltpu.VMEM(*dims) for dims in saved_shapes(count - near[0].shape[0])]
        + [pltpu.VMEM((count, C), f32)]
        + [pltpu.VMEM((C, FF), f32)] * 2
        + [pltpu.VMEM((count, C), bf16)] * 3
        + [pltpu.VMEM((C, FF), f32)],
        compiler_params=pltpu.CompilerParams(vmem_limit_bytes=28 * MIB),
        cost_estimate=cost(8 * 10**9, 16 * MIB),
        name="block",
    )(*pieces, bias, triple, project, up, down, *near)


def side_kernel(side_ref, north_ref, *refs):
    corner = north_ref[...].astype(f32)[-side_ref.shape[0] :]
    refs[-1][...] = jnp.concatenate([side_ref[...].astype(f32), corner], axis=0).astype(bf16)


def home_kernel(sizes, own_ref, north_ref, side_ref, perm_ref, out_ref):
    wide = [ref[...].astype(f32) for ref in (own_ref, north_ref, side_ref)]
    half = wide[2].shape[0] // 2
    wide = [wide[0], wide[1][:-half], wide[2][:half], wide[2][half:]]
    pieces = []
    for size, value in zip(sizes, wide):
        pieces += [value[:, :C], value[: size - value.shape[0], C:]]
    pieces = jnp.concatenate(pieces, axis=0).astype(bf16)
    out_ref[...] = mm(one_hot(perm_ref), pieces).astype(bf16)


def to_home(own, north, side, sizes, rows, cols):
    count = Z * rows * cols
    perm = spots(np.argsort(np.concatenate(piece_rows(rows, cols))))
    return pl.pallas_call(
        functools.partial(home_kernel, sizes),
        out_shape=shape((count, C), bf16),
        in_specs=vmem(4),
        out_specs=vmem(1)[0],
        compiler_params=pltpu.CompilerParams(vmem_limit_bytes=32 * MIB),
        cost_estimate=cost(2 * count * count * C, 4 * MIB),
        name="to_home",
    )(own, north, side, perm)


def core_add_kernel(keep_ref, got_ref, *refs):
    own_ref, outs = refs[-QUADS], refs[1 - QUADS :]
    total = keep_ref[...] + got_ref[...].astype(f32)
    own_ref[...] = total[:CHUNK]
    for e, out in zip(FAR_FIRST, outs):
        out[...] = total[e * CHUNK : (e + 1) * CHUNK].astype(bf16)


def chip_add_kernel(keep_ref, *refs):
    gots, (land_ref, out_ref) = refs[:-2], refs[-2:]
    total = keep_ref[...]
    for ref in gots:
        total = total + ref[...].astype(f32)
    land = land_ref[...]
    rest = jnp.concatenate([land[:, 128:], jnp.zeros((1, 2 * 128 - C), f32)], axis=1)
    parts = [total[:, n * 128 : (n + 1) * 128] for n in range(BLOCKS)]
    total = jnp.concatenate(parts + [land[:, :128], rest, jnp.zeros((EXTRA - 2, 128), f32)], axis=0)
    out_ref[...] = total.astype(bf16)


def add_kernel(one_ref, two_ref, *refs):
    refs[-1][...] = (one_ref[...].astype(f32) + two_ref[...].astype(f32)).astype(bf16)


def join_kernel(*refs):
    refs[-1][...] = jnp.concatenate([ref[...] for ref in refs[:-1]], axis=0)


def small_call(kernel, out_shape, args, name, after=(), scratch=()):
    return pl.pallas_call(
        kernel,
        out_shape=out_shape,
        in_specs=vmem(len(args)) + [pl.BlockSpec(memory_space=pl.ANY)] * len(after),
        out_specs=vmem(len(out_shape)),
        scratch_shapes=scratch,
        compiler_params=pltpu.CompilerParams(vmem_limit_bytes=16 * MIB),
        cost_estimate=cost(10**6, 2 * MIB),
        name=name,
    )(*args, *after)


def finish_kernel(far, chunks_ref, *refs):
    if far:
        before_ref, refs = refs[0], refs[5:]
    outs, land_ref, (up_ref, down_ref, triple_ref, project_ref, lands_ref, sum_ref, sems) = refs[:4], refs[4], refs[5:]
    core, chip, _ = position()
    side = 1 - core if far else core
    for g in range(QUADS):
        tiles = chunks_ref[g * FULL : (g + 1) * FULL, :].astype(f32)
        chunk = jnp.concatenate([tiles[n * CHUNK : (n + 1) * CHUNK] for n in range(BLOCKS)], axis=1)
        block = jnp.bitwise_xor(chip, g)
        rows = chunk_rows(block)
        up_ref[rows, :] = chunk[:PART]
        down_ref[rows, :] = chunk[PART : 2 * PART]
        triple_ref[rows, :] = chunk[2 * PART : CHUNK, : 3 * C]
        project_ref[rows, :] = chunk[2 * PART : CHUNK, 3 * C :]
        lands_ref[pl.ds(pl.multiple_of(block * EXTRA, EXTRA), EXTRA), :] = tiles[BLOCKS * CHUNK :]
    copies = []
    for n, (source, out) in enumerate(zip((triple_ref, project_ref, up_ref, down_ref), outs)):
        rows = pl.ds(pl.multiple_of(side * QUADS * PART, 8), QUADS * PART)
        copies.append(pltpu.make_async_copy(source, out.at[rows, :], sems.at[n]))
    for copy in copies:
        copy.start()
    lands = lands_ref[...]
    lands = [sum(lands[g * EXTRA + n : g * EXTRA + n + 1] for g in range(QUADS)) for n in range(2)]
    land = jnp.concatenate([lands[0], lands[1][:, : C - 128]], axis=1)
    if far:
        sum_ref[...] = land + before_ref[...]
        copies.append(pltpu.make_async_copy(sum_ref, land_ref, sems.at[4]))
        copies[-1].start()
    else:
        land_ref[...] = land
    for copy in copies:
        copy.wait()


def finish(chunks, before=()):
    rows = QUADS * PART
    widths = (3 * C, C, FF, FF)
    hbm = [pl.BlockSpec(memory_space=pltpu.HBM)] * 4
    land, weights = before[4:], before[:4]
    return pl.pallas_call(
        functools.partial(finish_kernel, bool(before)),
        out_shape=[shape((C, width), f32) for width in widths] + [shape((1, C), f32)],
        in_specs=vmem(1 + len(land)) + hbm[: len(weights)],
        out_specs=hbm + (hbm[:1] if before else vmem(1)),
        scratch_shapes=[
            pltpu.VMEM((rows, FF), f32),
            pltpu.VMEM((rows, FF), f32),
            pltpu.VMEM((rows, 3 * C), f32),
            pltpu.VMEM((rows, C), f32),
            pltpu.VMEM((QUADS * EXTRA, 128), f32),
            pltpu.VMEM((1, C), f32),
            pltpu.SemaphoreType.DMA((5,)),
        ],
        input_output_aliases={2 + n: n for n in range(len(weights))},
        compiler_params=pltpu.CompilerParams(vmem_limit_bytes=16 * MIB),
        cost_estimate=cost(10**6, 2 * MIB),
        name="finish_far" if before else "finish_own",
    )(chunks, *land, *weights)


def reduce_all(keep, sent, land, side, north, go_home, shift, lon_count):
    core_move = lambda lon, lat: (lon, lat ^ 1)
    chip_move = lambda e: lambda lon, lat: (lon ^ (e & 1), lat ^ (2 * (e >> 1)))
    deep_move = lambda e: lambda lon, lat: (lon ^ (2 * e), lat)

    def one(rows):
        return [shape((rows, FF), bf16)]

    got = shift(sent, move=core_move)
    parts = [shape((CHUNK, FF), f32)] + one(CHUNK) * (QUADS - 1)
    own, *parts = small_call(core_add_kernel, parts, (keep, got), "core_add", after=(north,))
    gots = [shift(value, move=chip_move(e)) for e, value in zip(FAR_FIRST, parts)]
    full = [shape((FULL, 128), bf16)]
    (total,) = small_call(chip_add_kernel, full, (own, *gots, land), "chip_add")
    (side,) = small_call(side_kernel, [shape((2 * side.shape[0], 2 * C), bf16)], (side, north), "side", after=(total,))
    side = shift(side, move=lambda lon, lat: (lon - 1, lat))
    grad_tokens = go_home(north, side)
    reach, waits = 1, [(side,), (grad_tokens,)]
    while reach < lon_count // 2:
        got = shift(total, move=deep_move(reach))
        reach *= 2
        (total,) = small_call(add_kernel, full, (total, got), "deep_add", after=waits.pop(0) if waits else ())
    near = [total] + [shift(total, move=chip_move(e)) for e in range(1, QUADS)]
    (total,) = small_call(join_kernel, [shape((QUADS * FULL, 128), bf16)], near, "join")
    got = shift(total, move=core_move)
    return finish(got, finish(total)), grad_tokens


AXES = ("deep", "x", "y", "core")


def send(value, lon_count, lat_count, move):
    pairs = []
    for lon in range(lon_count):
        for lat in range(lat_count):
            to_lon, to_lat = move(lon, lat)
            pairs.append((lon * lat_count + lat, (to_lon % lon_count) * lat_count + to_lat % lat_count))
    return lax.ppermute(value, AXES, pairs)


def body(
    lon_count, lat_count,
    tokens, cotangent, land_sea, land_vector, triple_weight, project_weight, up_weight, down_weight, earth_bias,
):
    levels, rows, cols, features = tokens.shape
    shift = functools.partial(send, lon_count=lon_count, lat_count=lat_count)
    lon_windows = cols // WW

    own, north, side, corner = pack(tokens, cotangent, land_sea, land_vector, rows, cols)
    north = shift(north, move=lambda lon, lat: (lon, lat + 1))
    side = shift(side, move=lambda lon, lat: (lon + 1, lat))
    corner = shift(corner, move=lambda lon, lat: (lon + 1, lat + 1))
    bias = expand_bias(earth_bias)

    sizes = [part.size for part in piece_rows(rows, cols)]
    pieces = (own, north, side, corner)
    near = near_block(own, north, bias, triple_weight, project_weight, lon_windows)
    own, north, side, land, keep, sent = block(
        pieces, bias, triple_weight, project_weight, up_weight, down_weight.T, near, lon_windows, sizes
    )
    north = shift(north, move=lambda lon, lat: (lon, lat - 1))
    go_home = lambda north, side: to_home(own, north, side, sizes, rows, cols)
    sums, grad_tokens = reduce_all(keep, sent, land, side, north, go_home, shift, lon_count)
    triple, project, up, down, land = sums
    return grad_tokens.reshape(tokens.shape), triple, project, up, down.T, land.reshape(features)


def solution(mesh):
    lon_count, lat_count = mesh.shape["lon"], mesh.shape["lat"]
    fine = jax.sharding.Mesh(mesh.devices.reshape(lon_count // 2, 2, lat_count // 2, 2), AXES)
    lon, lat = AXES[:2], AXES[2:]
    return jax.shard_map(
        functools.partial(body, lon_count, lat_count),
        mesh=fine,
        in_specs=(
            P(None, lat, lon, None),
            P(None, lat, lon, None),
            P(lat, lon),
            P(),
            P(),
            P(),
            P(),
            P(),
            P(lat, None, None, None, None),
        ),
        out_specs=(P(None, lat, lon, None), P(), P(), P(), P(), P()),
        check_vma=False,
    )
```

```python
import functools
import math

import jax
import jax.numpy as jnp
import numpy as np
from jax import lax
from jax.experimental import pallas as pl
from jax.experimental.pallas import tpu as pltpu
from jax.sharding import PartitionSpec as P

Z = 4
WZ = 2
WH = 6
WW = 12
C = 192
HEADS = 6
HEAD = 32
FF = 768
HZ, HH, HW = WZ // 2, WH // 2, WW // 2
TOK = WZ * WH * WW
PLACES = WZ * WH
RELW = 2 * WW - 1
SPOTS = PLACES // 2
STRIP = -(-RELW * SPOTS // 128) * 128
RUN, SHORT = WW * SPOTS, (WW - HW) * SPOTS

mask_fill = -10000.0
norm_eps = 1e-05
log2e = 1.4426950408889634
root_half = 0.7071067811865476
inv_root_tau = 0.3989422804014327
score_scale = HEAD**-0.5

f32 = jnp.float32
bf16 = jnp.bfloat16
MIB = 1 << 20

QUADS = 4
FAR_FIRST = range(QUADS - 1, 0, -1)
PART = C // (2 * QUADS)
CHUNK = 3 * PART
BLOCKS = FF // 128
EXTRA = 8
FULL = BLOCKS * CHUNK + EXTRA


def mm(a, b):
    return lax.dot_general(a, b, (((1,), (0,)), ((), ())), preferred_element_type=f32)


def mm_nt(a, b):
    return lax.dot_general(a, b, (((1,), (1,)), ((), ())), preferred_element_type=f32)


def mm_tn(a, b):
    return lax.dot_general(a, b, (((0,), (0,)), ((), ())), preferred_element_type=f32)


def unit_norm(values):
    average = jnp.mean(values, -1, keepdims=True)
    centred = values - average
    variance = jnp.mean(centred * centred, -1, keepdims=True)
    spread = lax.rsqrt(variance + norm_eps)
    return centred * spread, spread


def norm_back(upstream, unit, spread):
    first = jnp.mean(upstream, -1, keepdims=True)
    second = jnp.mean(upstream * unit, -1, keepdims=True)
    return spread * (upstream - first - unit * second)


def piece_rows(rows, cols):
    home = np.arange(Z * rows * cols).reshape(Z, rows, cols)

    def run(level, row, col, width):
        levels = [(level * WZ + z - HZ) % Z for z in range(WZ)]
        return home[levels, row : row + HH, col : col + width].transpose(2, 0, 1).reshape(-1)

    levels = range(Z // WZ)
    parts = []
    for row in (0, rows - HH):
        whole = [run(a, row, w * WW - HW, WW) for w in range(1, cols // WW) for a in levels]
        parts.append(np.concatenate(whole + [run(a, row, 0, WW - HW) for a in levels]))
    for row in (0, rows - HH):
        parts.append(np.concatenate([run(a, row, cols - HW, HW) for a in levels]))
    return parts


def window_runs(lon_windows):
    levels = Z // WZ
    whole = (lon_windows - 1) * levels
    runs = [[(1, n * RUN, RUN), (0, n * RUN, RUN)] for n in range(whole)]
    for a in range(levels):
        inner = whole * RUN + a * SHORT
        west = (a * (RUN - SHORT), RUN - SHORT)
        runs.append([(3, *west), (1, inner, SHORT), (2, *west), (0, inner, SHORT)])
    return runs


def spots(places):
    return jnp.asarray(np.argsort(places).astype(np.int32)[None])


def one_hot(spot_ref):
    count = spot_ref.shape[1]
    rows = lax.broadcasted_iota(jnp.int32, (count, count), 0)
    return (rows == spot_ref[...]).astype(f32).astype(bf16)


def vmem(count):
    return [pl.BlockSpec(memory_space=pltpu.VMEM)] * count


def shape(dims, dtype):
    return jax.ShapeDtypeStruct(dims, dtype)


def cost(flops, moved):
    return pl.CostEstimate(flops=flops, bytes_accessed=moved, transcendentals=0)


def land_column(land_ref, rows, cols):
    eye = (
        lax.broadcasted_iota(jnp.int32, (cols, cols), 0)
        == lax.broadcasted_iota(jnp.int32, (cols, cols), 1)
    ).astype(f32)
    land = land_ref[...].astype(f32)
    parts = [jnp.sum(eye * land[i : i + 1, :], -1, keepdims=True) for i in range(rows)]
    return jnp.concatenate(parts, axis=0)


def pack_kernel(rows, cols, *refs):
    sources, outs, (tokens_ref, cot_ref, land_ref, vec_ref, perm_ref, sems) = refs[:5], refs[5:-6], refs[-6:]
    copies = [
        pltpu.make_async_copy(source, target, sems.at[n])
        for n, (source, target) in enumerate(zip(sources, (tokens_ref, cot_ref, land_ref, vec_ref, perm_ref)))
    ]
    for copy in copies:
        copy.start()
    for copy in copies:
        copy.wait()
    column = land_column(land_ref, rows, cols)
    added = column * vec_ref[...]
    added = jnp.concatenate([added] * Z, axis=0)
    embedded = (tokens_ref[...].astype(f32) + added).astype(bf16)
    perm = one_hot(perm_ref)
    column = jnp.concatenate([column] * Z, axis=0)
    spare = jnp.broadcast_to(column, (column.shape[0], 2 * 128 - C)).astype(bf16)
    left = mm(perm, jnp.concatenate([embedded, spare], axis=1))
    left, flags = left[:, :C], left[:, C : C + 1]
    right = mm(perm, cot_ref[...])
    packed = jnp.concatenate([left, right], axis=1)
    start = 0
    for out in outs:
        count = out.shape[0] - EXTRA
        eye = lax.broadcasted_iota(jnp.int32, (count, count), 0) == lax.broadcasted_iota(jnp.int32, (count, count), 1)
        row = jnp.sum(jnp.where(eye, flags[start : start + count], 0.0), 0, keepdims=True)
        row = jnp.concatenate([row, jnp.zeros((1, 2 * C - count), f32)], axis=1)
        row = jnp.broadcast_to(row, (EXTRA, 2 * C))
        out[...] = jnp.concatenate([packed[start : start + count], row], axis=0).astype(bf16)
        start += count


def pack(tokens, cotangent, land_sea, vector, rows, cols):
    parts = piece_rows(rows, cols)
    perm = spots(np.concatenate(parts))
    count = Z * rows * cols
    return pl.pallas_call(
        functools.partial(pack_kernel, rows, cols),
        out_shape=[shape((part.size + EXTRA, 2 * C), bf16) for part in parts],
        in_specs=[pl.BlockSpec(memory_space=pltpu.HBM)] * 5,
        out_specs=vmem(4),
        scratch_shapes=[
            pltpu.VMEM((count, C), bf16),
            pltpu.VMEM((count, C), bf16),
            pltpu.VMEM((rows, cols), jnp.int32),
            pltpu.VMEM((1, C), f32),
            pltpu.VMEM((1, count), jnp.int32),
            pltpu.SemaphoreType.DMA((5,)),
        ],
        cost_estimate=cost(4 * count * count * C, 4 * MIB),
        name="pack",
    )(tokens.reshape(count, C), cotangent.reshape(count, C), land_sea, vector.reshape(1, C), perm)


def floor_div(values, divisor):
    return (values * (65536 // divisor + 1)) >> 16


def remainder(values, divisor):
    return values - floor_div(values, divisor) * divisor


def place_order(order):
    half = floor_div(order, SPOTS)
    spot = order - half * SPOTS
    level = floor_div(spot, HH)
    return level * WH + half * HH + (spot - level * HH)


def bias_kernel(levels, table_ref, out_ref, *wide_refs):
    groups = levels * HEADS
    pairs = PLACES * PLACES
    row = lax.broadcasted_iota(jnp.int32, (HEADS * RELW, HEADS * STRIP), 0)
    lane = lax.broadcasted_iota(jnp.int32, (HEADS * RELW, HEADS * STRIP), 1)
    head = floor_div(row, RELW)
    ahead = lane - (head * STRIP + (RELW - 1 - (row - head * RELW)) * SPOTS)
    onehot = ((ahead >= 0) & (ahead < SPOTS)).astype(f32).astype(bf16)
    row = lax.broadcasted_iota(jnp.int32, (pairs, pairs), 0)
    source = place_order(floor_div(row, PLACES)) * PLACES + remainder(row, PLACES)
    reorder = (lax.broadcasted_iota(jnp.int32, (pairs, pairs), 1) == source).astype(f32).astype(bf16)
    for level in range(levels):
        table = table_ref[:, level, :].T
        high = table.astype(bf16)
        rest = (table - high.astype(f32)).astype(bf16)
        wide = mm(mm(reorder, high).astype(bf16), onehot) + mm(mm(reorder, rest).astype(bf16), onehot)
        for head in range(HEADS):
            for n, wide_ref in enumerate(wide_refs):
                start = head * STRIP + n * 128
                wide_ref[(level * HEADS + head) * pairs : (level * HEADS + head + 1) * pairs, :] = wide[:, start : start + 128]
    strips = groups * PLACES
    row = lax.broadcasted_iota(jnp.int32, (strips, STRIP), 0)
    spot = remainder(lax.broadcasted_iota(jnp.int32, (strips, STRIP), 1), SPOTS)
    own = remainder(row, PLACES)
    first_level = (row < HEADS * PLACES).astype(jnp.int32)
    own_north = (own < SPOTS).astype(jnp.int32)
    own_low = (own - SPOTS * (1 - own_north) < HZ * HH).astype(jnp.int32)
    low = (spot < HZ * HH).astype(jnp.int32)
    pole = (lax.axis_index("y") + lax.axis_index("core") == 0).astype(jnp.int32)
    halves = []
    for half in range(2):
        parts = []
        for n, wide_ref in enumerate(wide_refs):
            here = spot[:, n * 128 : (n + 1) * 128]
            part = jnp.zeros((strips, 128), f32)
            for p in range(SPOTS):
                place = p // HH * WH + half * HH + p % HH
                part = jnp.where(here == p, wide_ref[pl.ds(place, strips, stride=PLACES), :], part)
            parts.append(part)
        strip = jnp.concatenate(parts, axis=1)
        differs = first_level * (own_low ^ low) + pole * (own_north ^ (1 - half))
        halves.append(jnp.where(differs > 0, strip + mask_fill, strip) * log2e)
    for w in range(WW):
        start = (WW - 1 - w) * SPOTS
        part = jnp.concatenate([strip[:, start : start + RUN] for strip in halves], axis=1)
        for g in range(groups):
            for half in range(2):
                rows = part[g * PLACES + half * SPOTS : g * PLACES + (half + 1) * SPOTS, :]
                out_ref[g, half * RUN + w * SPOTS : half * RUN + (w + 1) * SPOTS, :] = rows


def expand_bias(table):
    levels = table.shape[1]
    groups = levels * HEADS
    pairs = PLACES * PLACES
    flat = table[0].transpose(1, 3, 0, 2).reshape(HEADS * RELW, levels, pairs)
    return pl.pallas_call(
        functools.partial(bias_kernel, levels),
        out_shape=shape((groups, TOK, TOK), f32),
        in_specs=vmem(1),
        out_specs=vmem(1)[0],
        scratch_shapes=[pltpu.VMEM((groups * pairs, 128), f32)] * (STRIP // 128),
        compiler_params=pltpu.CompilerParams(vmem_limit_bytes=28 * MIB),
        cost_estimate=cost(10**9, 8 * MIB),
        name="bias",
    )(flat)


def head_masks(count):
    lane = lax.broadcasted_iota(jnp.int32, (count, C), 1)
    return [((lane >= h * HEAD) & (lane < (h + 1) * HEAD)).astype(f32) for h in range(HEADS)]


def stacked(values, masks):
    return jnp.concatenate([values * mask for mask in masks], axis=0)


def head_sum(values, masks):
    total = values[:TOK] * masks[0]
    for h in range(1, HEADS):
        total = total + values[h * TOK : (h + 1) * TOK] * masks[h]
    return total


def position():
    return lax.axis_index("core"), lax.axis_index("y") * 2 + lax.axis_index("x"), lax.axis_index("deep")


def chunk_rows(block):
    return pl.ds(pl.multiple_of(block * PART, PART), PART)


def split_parts(total_refs, keep_ref, send_ref):
    core, chip, _ = position()
    for out, side in ((keep_ref, core), (send_ref, 1 - core)):
        parts = []
        for g in range(QUADS):
            rows = chunk_rows(side * QUADS + jnp.bitwise_xor(chip, g))
            parts += [ref[rows, :] for ref in total_refs]
        out[...] = jnp.concatenate(parts, axis=0).astype(out.dtype)


def attend(first, runs, pieces, bias_ref, triple_ref, project_ref, *refs):
    q_ref, k_ref, v_ref, p_ref, mixed_ref, normed_ref, unit_ref, spread_ref, summed_ref, cot_ref = refs
    pieces = [piece.astype(f32) for piece in pieces]
    ordered = jnp.concatenate([pieces[n][start : start + count] for n, start, count in runs], axis=0)
    emb = ordered[:, :C]
    cot_ref[...] = ordered[:, C:].astype(bf16)
    unit, spread = unit_norm(emb)
    unit_ref[...] = unit
    spread_ref[...] = spread
    normed = unit.astype(bf16)
    normed_ref[...] = normed
    packed = mm(normed, triple_ref[...])
    q_ref[...] = packed[:, :C].astype(bf16)
    k_ref[...] = packed[:, C : 2 * C].astype(bf16)
    v_ref[...] = packed[:, 2 * C :].astype(bf16)
    masks = head_masks(TOK)
    masks_b = [mask.astype(bf16) for mask in masks]
    for w in range(emb.shape[0] // TOK):
        rows = slice(w * TOK, (w + 1) * TOK)
        heads = slice(w * HEADS, (w + 1) * HEADS)
        level = (first + w) % (Z // WZ)
        scores = mm_nt(stacked(q_ref[rows, :], masks_b), k_ref[rows, :])
        bias = bias_ref[level * HEADS : (level + 1) * HEADS].reshape(HEADS * TOK, TOK)
        raised = jnp.exp2(scores * (score_scale * log2e) + bias)
        probs = raised * (1.0 / jnp.sum(raised, -1, keepdims=True))
        probs_b = probs.astype(bf16)
        p_ref[heads] = probs_b.reshape(HEADS, TOK, TOK)
        mixed = head_sum(mm(probs_b, v_ref[rows, :]), masks).astype(bf16)
        mixed_ref[rows, :] = mixed
        summed_ref[rows, :] = emb[rows] + mm(mixed, project_ref[...]).astype(bf16).astype(f32)


def feed_back(summed, cot, up_ref, down_ref, gsum_ref, up_grad_ref, down_grad_ref):
    unit2, spread2 = unit_norm(summed)
    normed2 = unit2.astype(bf16)
    back = jnp.zeros(unit2.shape, f32)
    block = 256
    for start in range(0, FF, block):
        cols = slice(start, start + block)
        up_part = up_ref[:, cols]
        pre = mm(normed2, up_part)
        upstream = mm(cot, down_ref[:, cols])
        phi = 0.5 * (1.0 + lax.erf(pre * root_half))
        activated = (pre * phi).astype(bf16)
        slope = phi + pre * inv_root_tau * jnp.exp2(pre * pre * (-0.5 * log2e))
        hidden = (upstream * slope).astype(bf16)
        up_grad_ref[:, cols] = mm_tn(normed2, hidden)
        down_grad_ref[:, cols] = mm_tn(cot, activated)
        back = back + mm_nt(hidden, up_part)
    gsum_ref[...] = cot.astype(f32) + norm_back(back, unit2, spread2)


def attend_back(at, q_ref, k_ref, v_ref, p_ref, gsum_ref, project_ref, gq_ref, gk_ref, gv_ref):
    masks = head_masks(TOK)
    masks_b = [mask.astype(bf16) for mask in masks]
    for w in range(q_ref.shape[0] // TOK):
        rows = slice(w * TOK, (w + 1) * TOK)
        full_rows = slice(at + w * TOK, at + (w + 1) * TOK)
        grad = gsum_ref[full_rows, :].astype(bf16)
        grad_mixed_b = mm_nt(grad, project_ref[...]).astype(bf16)
        probs_b = p_ref[w * HEADS : (w + 1) * HEADS].reshape(HEADS * TOK, TOK)
        probs = probs_b.astype(f32)
        grad_probs = mm_nt(stacked(grad_mixed_b, masks_b), v_ref[rows, :])
        inner = jnp.sum(grad_probs * probs, -1, keepdims=True)
        scaled = (probs * (grad_probs - inner) * score_scale).astype(bf16)
        grad_q = head_sum(mm(scaled, k_ref[rows, :]), masks)
        grad_mixed_t = grad_mixed_b.astype(f32).T.astype(bf16)
        query_t = q_ref[rows, :].astype(f32).T.astype(bf16)
        grad_k, grad_v = [], []
        for h in range(HEADS):
            spot = slice(h * HEAD, (h + 1) * HEAD)
            span = slice(h * TOK, (h + 1) * TOK)
            grad_k.append(mm(query_t[spot], scaled[span]))
            grad_v.append(mm(grad_mixed_t[spot], probs_b[span]))
        gq_ref[full_rows, :] = grad_q.astype(bf16)
        gk_ref[full_rows, :] = jnp.concatenate(grad_k, axis=0).T.astype(bf16)
        gv_ref[full_rows, :] = jnp.concatenate(grad_v, axis=0).T.astype(bf16)


def halved(rows):
    return -(-rows // 16) * 8


def tokens_back(
    lon_windows, sizes, gq_ref, gk_ref, gv_ref, mixed, normed, unit, spread, gsum_ref, triple_ref, up_grad_ref, down_grad_ref,
    *rest,
):
    flag_refs, rest = rest[: len(sizes)], rest[len(sizes) :]
    outs, (land_ref, keep_ref, send_ref, total_ref) = rest[: len(sizes) - 1], rest[len(sizes) - 1 :]
    triple = triple_ref[...]
    grad_normed = jnp.zeros(unit.shape, f32)
    parts = []
    for n, ref in enumerate((gq_ref, gk_ref, gv_ref)):
        grad = ref[...]
        grad_normed = grad_normed + mm_nt(grad, triple[:, n * C : (n + 1) * C])
        parts.append(mm_tn(normed, grad))
    parts.append(mm_tn(mixed, gsum_ref[...].astype(bf16)))
    total_ref[...] = jnp.concatenate(parts, axis=1)
    grad_normed = grad_normed.astype(bf16).astype(f32)
    grad_tokens = gsum_ref[...] + norm_back(grad_normed, unit, spread)
    parts, at = [[] for _ in sizes], 0
    for n, start, count in [run for window in window_runs(lon_windows) for run in window]:
        parts[n].append((start, grad_tokens[at : at + count]))
        at += count
    land = jnp.zeros((EXTRA, C), f32)
    wide = []
    for size, flag_ref, part in zip(sizes, flag_refs, parts):
        piece = jnp.concatenate([value for _, value in sorted(part, key=lambda item: item[0])], axis=0)
        flags = flag_ref[size - 8 : size + 8, :].astype(f32)[8:, :size]
        land = land + mm(flags.astype(bf16), piece.astype(bf16))
        half = halved(size)
        second = jnp.concatenate([piece[half:], jnp.zeros((2 * half - size, C), f32)], axis=0)
        wide.append(jnp.concatenate([piece[:half], second], axis=1))
    land_ref[...] = land[0:1]
    own, north, side, corner = wide
    for out, value in zip(outs, (own, jnp.concatenate([north, corner], axis=0), side)):
        out[...] = value.astype(bf16)
    split_parts((up_grad_ref, down_grad_ref, total_ref), keep_ref, send_ref)


def saved_shapes(count):
    dims = [((count, C), bf16)] * 3 + [((count // TOK * HEADS, TOK, TOK), bf16)] + [((count, C), bf16)] * 2
    return dims + [((count, C), f32), ((count, 1), f32), ((count, C), f32), ((count, C), bf16)]


SAVED = len(saved_shapes(TOK))


def split_runs(lon_windows):
    windows = window_runs(lon_windows)
    whole = (lon_windows - 1) * (Z // WZ)
    return whole, *[[run for window in part for run in window] for part in (windows[:whole], windows[whole:])]


def near_kernel(lon_windows, own_ref, north_ref, *refs):
    runs = split_runs(lon_windows)[1]
    attend(0, runs, (own_ref[...], north_ref[...]), *refs)


def near_block(own, north, bias, triple, project, lon_windows):
    count = split_runs(lon_windows)[0] * TOK
    return pl.pallas_call(
        functools.partial(near_kernel, lon_windows),
        out_shape=[shape(*dims) for dims in saved_shapes(count)],
        in_specs=vmem(5),
        out_specs=vmem(SAVED),
        compiler_params=pltpu.CompilerParams(vmem_limit_bytes=24 * MIB),
        cost_estimate=cost(3 * 10**9, 8 * MIB),
        name="near_block",
    )(own, north, bias, triple, project)


def block_kernel(lon_windows, sizes, *refs):
    whole, _, runs = split_runs(lon_windows)
    pieces, refs = refs[:4], refs[4:]
    (bias_ref, triple_ref, project_ref, up_ref, down_ref), refs = refs[:5], refs[5:]
    near, refs = refs[:SAVED], refs[SAVED:]
    outs, refs = refs[: len(sizes) + 2], refs[len(sizes) + 2 :]
    far, (gsum, up_grad, down_grad, gq, gk, gv, total) = refs[:SAVED], refs[SAVED:]
    attend(whole, runs, [ref[...] for ref in pieces], bias_ref, triple_ref, project_ref, *far)
    mixed, normed, unit, spread, summed, cot = [
        jnp.concatenate([one[...], other[...]], axis=0) for one, other in zip(near[4:], far[4:])
    ]
    feed_back(summed, cot, up_ref, down_ref, gsum, up_grad, down_grad)
    attend_back(0, *near[:4], gsum, project_ref, gq, gk, gv)
    attend_back(whole * TOK, *far[:4], gsum, project_ref, gq, gk, gv)
    tokens_back(
        lon_windows, sizes, gq, gk, gv, mixed, normed, unit, spread, gsum, triple_ref, up_grad, down_grad,
        *pieces, *outs, total,
    )


def block(pieces, bias, triple, project, up, down, near, lon_windows, sizes):
    count = sum(sizes)
    own, north, side, corner = [halved(size) for size in sizes]
    out_shape = [shape((size, 2 * C), bf16) for size in (own, north + corner, side)] + [
        shape((1, C), f32),
        shape((QUADS * CHUNK, FF), f32),
        shape((QUADS * CHUNK, FF), bf16),
    ]
    return pl.pallas_call(
        functools.partial(block_kernel, lon_windows, sizes),
        out_shape=out_shape,
        in_specs=vmem(9 + SAVED),
        out_specs=vmem(len(out_shape)),
        scratch_shapes=[pltpu.VMEM(*dims) for dims in saved_shapes(count - near[0].shape[0])]
        + [pltpu.VMEM((count, C), f32)]
        + [pltpu.VMEM((C, FF), f32)] * 2
        + [pltpu.VMEM((count, C), bf16)] * 3
        + [pltpu.VMEM((C, FF), f32)],
        compiler_params=pltpu.CompilerParams(vmem_limit_bytes=28 * MIB),
        cost_estimate=cost(8 * 10**9, 16 * MIB),
        name="block",
    )(*pieces, bias, triple, project, up, down, *near)


def side_kernel(side_ref, north_ref, *refs):
    corner = north_ref[...].astype(f32)[-side_ref.shape[0] :]
    refs[-1][...] = jnp.concatenate([side_ref[...].astype(f32), corner], axis=0).astype(bf16)


def home_kernel(sizes, own_ref, north_ref, side_ref, perm_ref, out_ref, done_ref):
    wide = [ref[...].astype(f32) for ref in (own_ref, north_ref, side_ref)]
    half = wide[2].shape[0] // 2
    wide = [wide[0], wide[1][:-half], wide[2][:half], wide[2][half:]]
    pieces = []
    for size, value in zip(sizes, wide):
        pieces += [value[:, :C], value[: size - value.shape[0], C:]]
    pieces = jnp.concatenate(pieces, axis=0).astype(bf16)
    out_ref[...] = mm(one_hot(perm_ref), pieces).astype(bf16)
    done_ref[...] = jnp.zeros_like(done_ref)


def to_home(own, north, side, sizes, rows, cols):
    count = Z * rows * cols
    perm = spots(np.argsort(np.concatenate(piece_rows(rows, cols))))
    return pl.pallas_call(
        functools.partial(home_kernel, sizes),
        out_shape=[shape((count, C), bf16), shape((8, 128), f32)],
        in_specs=vmem(4),
        out_specs=vmem(2),
        compiler_params=pltpu.CompilerParams(vmem_limit_bytes=32 * MIB),
        cost_estimate=cost(2 * count * count * C, 4 * MIB),
        name="to_home",
    )(own, north, side, perm)


def core_add_kernel(keep_ref, got_ref, *refs):
    own_ref, outs = refs[-QUADS], refs[1 - QUADS :]
    total = keep_ref[...] + got_ref[...].astype(f32)
    own_ref[...] = total[:CHUNK]
    for e, out in zip(FAR_FIRST, outs):
        out[...] = total[e * CHUNK : (e + 1) * CHUNK].astype(bf16)


def chip_add_kernel(keep_ref, *refs):
    gots, (land_ref, out_ref) = refs[:-2], refs[-2:]
    total = keep_ref[...]
    for ref in gots:
        total = total + ref[...].astype(f32)
    land = land_ref[...]
    rest = jnp.concatenate([land[:, 128:], jnp.zeros((1, 2 * 128 - C), f32)], axis=1)
    parts = [total[:, n * 128 : (n + 1) * 128] for n in range(BLOCKS)]
    total = jnp.concatenate(parts + [land[:, :128], rest, jnp.zeros((EXTRA - 2, 128), f32)], axis=0)
    out_ref[...] = total.astype(bf16)


def add_kernel(one_ref, two_ref, *refs):
    refs[-1][...] = (one_ref[...].astype(f32) + two_ref[...].astype(f32)).astype(bf16)


def join_kernel(*refs):
    refs[-1][...] = jnp.concatenate([ref[...] for ref in refs[:-1]], axis=0)


def small_call(kernel, out_shape, args, name, after=(), scratch=()):
    return pl.pallas_call(
        kernel,
        out_shape=out_shape,
        in_specs=vmem(len(args)) + [pl.BlockSpec(memory_space=pl.ANY)] * len(after),
        out_specs=vmem(len(out_shape)),
        scratch_shapes=scratch,
        compiler_params=pltpu.CompilerParams(vmem_limit_bytes=16 * MIB),
        cost_estimate=cost(10**6, 2 * MIB),
        name=name,
    )(*args, *after)


def finish_kernel(far, chunks_ref, *refs):
    if far:
        before_ref, refs = refs[0], refs[5:]
    outs, land_ref, (up_ref, down_ref, triple_ref, project_ref, lands_ref, sum_ref, sems) = refs[:4], refs[4], refs[5:]
    core, chip, _ = position()
    side = 1 - core if far else core
    for g in range(QUADS):
        tiles = chunks_ref[g * FULL : (g + 1) * FULL, :].astype(f32)
        chunk = jnp.concatenate([tiles[n * CHUNK : (n + 1) * CHUNK] for n in range(BLOCKS)], axis=1)
        block = jnp.bitwise_xor(chip, g)
        rows = chunk_rows(block)
        up_ref[rows, :] = chunk[:PART]
        down_ref[rows, :] = chunk[PART : 2 * PART]
        triple_ref[rows, :] = chunk[2 * PART : CHUNK, : 3 * C]
        project_ref[rows, :] = chunk[2 * PART : CHUNK, 3 * C :]
        lands_ref[pl.ds(pl.multiple_of(block * EXTRA, EXTRA), EXTRA), :] = tiles[BLOCKS * CHUNK :]
    copies = []
    for n, (source, out) in enumerate(zip((triple_ref, project_ref, up_ref, down_ref), outs)):
        rows = pl.ds(pl.multiple_of(side * QUADS * PART, 8), QUADS * PART)
        copies.append(pltpu.make_async_copy(source, out.at[rows, :], sems.at[n]))
    for copy in copies:
        copy.start()
    lands = lands_ref[...]
    lands = [sum(lands[g * EXTRA + n : g * EXTRA + n + 1] for g in range(QUADS)) for n in range(2)]
    land = jnp.concatenate([lands[0], lands[1][:, : C - 128]], axis=1)
    if far:
        sum_ref[...] = land + before_ref[...]
        copies.append(pltpu.make_async_copy(sum_ref, land_ref, sems.at[4]))
        copies[-1].start()
    else:
        land_ref[...] = land
    for copy in copies:
        copy.wait()


def finish(chunks, before=()):
    rows = QUADS * PART
    widths = (3 * C, C, FF, FF)
    hbm = [pl.BlockSpec(memory_space=pltpu.HBM)] * 4
    land, weights = before[4:], before[:4]
    return pl.pallas_call(
        functools.partial(finish_kernel, bool(before)),
        out_shape=[shape((C, width), f32) for width in widths] + [shape((1, C), f32)],
        in_specs=vmem(1 + len(land)) + hbm[: len(weights)],
        out_specs=hbm + (hbm[:1] if before else vmem(1)),
        scratch_shapes=[
            pltpu.VMEM((rows, FF), f32),
            pltpu.VMEM((rows, FF), f32),
            pltpu.VMEM((rows, 3 * C), f32),
            pltpu.VMEM((rows, C), f32),
            pltpu.VMEM((QUADS * EXTRA, 128), f32),
            pltpu.VMEM((1, C), f32),
            pltpu.SemaphoreType.DMA((5,)),
        ],
        input_output_aliases={2 + n: n for n in range(len(weights))},
        compiler_params=pltpu.CompilerParams(vmem_limit_bytes=16 * MIB),
        cost_estimate=cost(10**6, 2 * MIB),
        name="finish_far" if before else "finish_own",
    )(chunks, *land, *weights)


def reduce_all(keep, sent, land, side, north, go_home, shift, lon_count):
    core_move = lambda lon, lat: (lon, lat ^ 1)
    chip_move = lambda e: lambda lon, lat: (lon ^ (e & 1), lat ^ (2 * (e >> 1)))
    deep_move = lambda e: lambda lon, lat: (lon ^ (2 * e), lat)

    def one(rows):
        return [shape((rows, FF), bf16)]

    got = shift(sent, move=core_move)
    parts = [shape((CHUNK, FF), f32)] + one(CHUNK) * (QUADS - 1)
    own, *parts = small_call(core_add_kernel, parts, (keep, got), "core_add", after=(north,))
    gots = [shift(value, move=chip_move(e)) for e, value in zip(FAR_FIRST, parts)]
    full = [shape((FULL, 128), bf16)]
    (total,) = small_call(chip_add_kernel, full, (own, *gots, land), "chip_add")
    (side,) = small_call(side_kernel, [shape((2 * side.shape[0], 2 * C), bf16)], (side, north), "side", after=(total,))
    side = shift(side, move=lambda lon, lat: (lon - 1, lat))
    grad_tokens, done = go_home(north, side)
    reach, waits = 1, [(side,), (done,)]
    while reach < lon_count // 2:
        got = shift(total, move=deep_move(reach))
        reach *= 2
        (total,) = small_call(add_kernel, full, (total, got), "deep_add", after=waits.pop(0) if waits else ())
    near = [total] + [shift(total, move=chip_move(e)) for e in range(1, QUADS)]
    (total,) = small_call(join_kernel, [shape((QUADS * FULL, 128), bf16)], near, "join")
    got = shift(total, move=core_move)
    return finish(got, finish(total)), grad_tokens


AXES = ("deep", "x", "y", "core")


def send(value, lon_count, lat_count, move):
    pairs = []
    for lon in range(lon_count):
        for lat in range(lat_count):
            to_lon, to_lat = move(lon, lat)
            pairs.append((lon * lat_count + lat, (to_lon % lon_count) * lat_count + to_lat % lat_count))
    return lax.ppermute(value, AXES, pairs)


def body(
    lon_count, lat_count,
    tokens, cotangent, land_sea, land_vector, triple_weight, project_weight, up_weight, down_weight, earth_bias,
):
    levels, rows, cols, features = tokens.shape
    shift = functools.partial(send, lon_count=lon_count, lat_count=lat_count)
    lon_windows = cols // WW

    own, north, side, corner = pack(tokens, cotangent, land_sea, land_vector, rows, cols)
    north = shift(north, move=lambda lon, lat: (lon, lat + 1))
    side = shift(side, move=lambda lon, lat: (lon + 1, lat))
    corner = shift(corner, move=lambda lon, lat: (lon + 1, lat + 1))
    bias = expand_bias(earth_bias)

    sizes = [part.size for part in piece_rows(rows, cols)]
    pieces = (own, north, side, corner)
    near = near_block(own, north, bias, triple_weight, project_weight, lon_windows)
    own, north, side, land, keep, sent = block(
        pieces, bias, triple_weight, project_weight, up_weight, down_weight.T, near, lon_windows, sizes
    )
    north = shift(north, move=lambda lon, lat: (lon, lat - 1))
    go_home = lambda north, side: to_home(own, north, side, sizes, rows, cols)
    sums, grad_tokens = reduce_all(keep, sent, land, side, north, go_home, shift, lon_count)
    triple, project, up, down, land = sums
    return grad_tokens.reshape(tokens.shape), triple, project, up, down.T, land.reshape(features)


def solution(mesh):
    lon_count, lat_count = mesh.shape["lon"], mesh.shape["lat"]
    fine = jax.sharding.Mesh(mesh.devices.reshape(lon_count // 2, 2, lat_count // 2, 2), AXES)
    lon, lat = AXES[:2], AXES[2:]
    return jax.shard_map(
        functools.partial(body, lon_count, lat_count),
        mesh=fine,
        in_specs=(
            P(None, lat, lon, None),
            P(None, lat, lon, None),
            P(lat, lon),
            P(),
            P(),
            P(),
            P(),
            P(),
            P(lat, None, None, None, None),
        ),
        out_specs=(P(None, lat, lon, None), P(), P(), P(), P(), P()),
        check_vma=False,
    )
```

```python
import functools
import math

import jax
import jax.numpy as jnp
import numpy as np
from jax import lax
from jax.experimental import pallas as pl
from jax.experimental.pallas import tpu as pltpu
from jax.sharding import PartitionSpec as P

Z = 4
WZ = 2
WH = 6
WW = 12
C = 192
HEADS = 6
HEAD = 32
FF = 768
HZ, HH, HW = WZ // 2, WH // 2, WW // 2
TOK = WZ * WH * WW
PLACES = WZ * WH
RELW = 2 * WW - 1
SPOTS = PLACES // 2
STRIP = -(-RELW * SPOTS // 128) * 128
RUN, SHORT = WW * SPOTS, (WW - HW) * SPOTS

mask_fill = -10000.0
norm_eps = 1e-05
log2e = 1.4426950408889634
root_half = 0.7071067811865476
inv_root_tau = 0.3989422804014327
score_scale = HEAD**-0.5

f32 = jnp.float32
bf16 = jnp.bfloat16
MIB = 1 << 20

QUADS = 4
FAR_FIRST = range(QUADS - 1, 0, -1)
PART = C // (2 * QUADS)
CHUNK = 3 * PART
BLOCKS = FF // 128
EXTRA = 8
FULL = BLOCKS * CHUNK + EXTRA


def mm(a, b):
    return lax.dot_general(a, b, (((1,), (0,)), ((), ())), preferred_element_type=f32)


def mm_nt(a, b):
    return lax.dot_general(a, b, (((1,), (1,)), ((), ())), preferred_element_type=f32)


def mm_tn(a, b):
    return lax.dot_general(a, b, (((0,), (0,)), ((), ())), preferred_element_type=f32)


def unit_norm(values):
    average = jnp.mean(values, -1, keepdims=True)
    centred = values - average
    variance = jnp.mean(centred * centred, -1, keepdims=True)
    spread = lax.rsqrt(variance + norm_eps)
    return centred * spread, spread


def norm_back(upstream, unit, spread):
    first = jnp.mean(upstream, -1, keepdims=True)
    second = jnp.mean(upstream * unit, -1, keepdims=True)
    return spread * (upstream - first - unit * second)


def piece_rows(rows, cols):
    home = np.arange(Z * rows * cols).reshape(Z, rows, cols)

    def run(level, row, col, width):
        levels = [(level * WZ + z - HZ) % Z for z in range(WZ)]
        return home[levels, row : row + HH, col : col + width].transpose(2, 0, 1).reshape(-1)

    levels = range(Z // WZ)
    parts = []
    for row in (0, rows - HH):
        whole = [run(a, row, w * WW - HW, WW) for w in range(1, cols // WW) for a in levels]
        parts.append(np.concatenate(whole + [run(a, row, 0, WW - HW) for a in levels]))
    for row in (0, rows - HH):
        parts.append(np.concatenate([run(a, row, cols - HW, HW) for a in levels]))
    return parts


def window_runs(lon_windows):
    levels = Z // WZ
    whole = (lon_windows - 1) * levels
    runs = [[(1, n * RUN, RUN), (0, n * RUN, RUN)] for n in range(whole)]
    for a in range(levels):
        inner = whole * RUN + a * SHORT
        west = (a * (RUN - SHORT), RUN - SHORT)
        runs.append([(3, *west), (1, inner, SHORT), (2, *west), (0, inner, SHORT)])
    return runs


def spots(places):
    return jnp.asarray(np.argsort(places).astype(np.int32)[None])


def one_hot(spot_ref):
    count = spot_ref.shape[1]
    rows = lax.broadcasted_iota(jnp.int32, (count, count), 0)
    return (rows == spot_ref[...]).astype(f32).astype(bf16)


def vmem(count):
    return [pl.BlockSpec(memory_space=pltpu.VMEM)] * count


def shape(dims, dtype):
    return jax.ShapeDtypeStruct(dims, dtype)


def cost(flops, moved):
    return pl.CostEstimate(flops=flops, bytes_accessed=moved, transcendentals=0)


def land_column(land_ref, rows, cols):
    eye = (
        lax.broadcasted_iota(jnp.int32, (cols, cols), 0)
        == lax.broadcasted_iota(jnp.int32, (cols, cols), 1)
    ).astype(f32)
    land = land_ref[...].astype(f32)
    parts = [jnp.sum(eye * land[i : i + 1, :], -1, keepdims=True) for i in range(rows)]
    return jnp.concatenate(parts, axis=0)


def pack_kernel(rows, cols, *refs):
    sources, outs, (tokens_ref, cot_ref, land_ref, vec_ref, perm_ref, sems) = refs[:5], refs[5:-6], refs[-6:]
    copies = [
        pltpu.make_async_copy(source, target, sems.at[n])
        for n, (source, target) in enumerate(zip(sources, (tokens_ref, cot_ref, land_ref, vec_ref, perm_ref)))
    ]
    for copy in copies:
        copy.start()
    for copy in copies:
        copy.wait()
    column = land_column(land_ref, rows, cols)
    added = column * vec_ref[...]
    added = jnp.concatenate([added] * Z, axis=0)
    embedded = (tokens_ref[...].astype(f32) + added).astype(bf16)
    perm = one_hot(perm_ref)
    column = jnp.concatenate([column] * Z, axis=0)
    spare = jnp.broadcast_to(column, (column.shape[0], 2 * 128 - C)).astype(bf16)
    left = mm(perm, jnp.concatenate([embedded, spare], axis=1))
    left, flags = left[:, :C], left[:, C : C + 1]
    right = mm(perm, cot_ref[...])
    packed = jnp.concatenate([left, right], axis=1)
    start = 0
    for out in outs:
        count = out.shape[0] - EXTRA
        eye = lax.broadcasted_iota(jnp.int32, (count, count), 0) == lax.broadcasted_iota(jnp.int32, (count, count), 1)
        row = jnp.sum(jnp.where(eye, flags[start : start + count], 0.0), 0, keepdims=True)
        row = jnp.concatenate([row, jnp.zeros((1, 2 * C - count), f32)], axis=1)
        row = jnp.broadcast_to(row, (EXTRA, 2 * C))
        out[...] = jnp.concatenate([packed[start : start + count], row], axis=0).astype(bf16)
        start += count


def pack(tokens, cotangent, land_sea, vector, rows, cols):
    parts = piece_rows(rows, cols)
    perm = spots(np.concatenate(parts))
    count = Z * rows * cols
    return pl.pallas_call(
        functools.partial(pack_kernel, rows, cols),
        out_shape=[shape((part.size + EXTRA, 2 * C), bf16) for part in parts],
        in_specs=[pl.BlockSpec(memory_space=pltpu.HBM)] * 5,
        out_specs=vmem(4),
        scratch_shapes=[
            pltpu.VMEM((count, C), bf16),
            pltpu.VMEM((count, C), bf16),
            pltpu.VMEM((rows, cols), jnp.int32),
            pltpu.VMEM((1, C), f32),
            pltpu.VMEM((1, count), jnp.int32),
            pltpu.SemaphoreType.DMA((5,)),
        ],
        cost_estimate=cost(4 * count * count * C, 4 * MIB),
        name="pack",
    )(tokens.reshape(count, C), cotangent.reshape(count, C), land_sea, vector.reshape(1, C), perm)


def floor_div(values, divisor):
    return (values * (65536 // divisor + 1)) >> 16


def remainder(values, divisor):
    return values - floor_div(values, divisor) * divisor


def place_order(order):
    half = floor_div(order, SPOTS)
    spot = order - half * SPOTS
    level = floor_div(spot, HH)
    return level * WH + half * HH + (spot - level * HH)


def bias_kernel(levels, table_ref, out_ref, *wide_refs):
    groups = levels * HEADS
    pairs = PLACES * PLACES
    row = lax.broadcasted_iota(jnp.int32, (HEADS * RELW, HEADS * STRIP), 0)
    lane = lax.broadcasted_iota(jnp.int32, (HEADS * RELW, HEADS * STRIP), 1)
    head = floor_div(row, RELW)
    ahead = lane - (head * STRIP + (RELW - 1 - (row - head * RELW)) * SPOTS)
    onehot = ((ahead >= 0) & (ahead < SPOTS)).astype(f32).astype(bf16)
    row = lax.broadcasted_iota(jnp.int32, (pairs, pairs), 0)
    source = place_order(floor_div(row, PLACES)) * PLACES + remainder(row, PLACES)
    reorder = (lax.broadcasted_iota(jnp.int32, (pairs, pairs), 1) == source).astype(f32).astype(bf16)
    for level in range(levels):
        table = table_ref[:, level, :].T
        high = table.astype(bf16)
        rest = (table - high.astype(f32)).astype(bf16)
        wide = mm(mm(reorder, high).astype(bf16), onehot) + mm(mm(reorder, rest).astype(bf16), onehot)
        for head in range(HEADS):
            for n, wide_ref in enumerate(wide_refs):
                start = head * STRIP + n * 128
                wide_ref[(level * HEADS + head) * pairs : (level * HEADS + head + 1) * pairs, :] = wide[:, start : start + 128]
    strips = groups * PLACES
    row = lax.broadcasted_iota(jnp.int32, (strips, STRIP), 0)
    spot = remainder(lax.broadcasted_iota(jnp.int32, (strips, STRIP), 1), SPOTS)
    own = remainder(row, PLACES)
    first_level = (row < HEADS * PLACES).astype(jnp.int32)
    own_north = (own < SPOTS).astype(jnp.int32)
    own_low = (own - SPOTS * (1 - own_north) < HZ * HH).astype(jnp.int32)
    low = (spot < HZ * HH).astype(jnp.int32)
    pole = (lax.axis_index("y") + lax.axis_index("core") == 0).astype(jnp.int32)
    halves = []
    for half in range(2):
        parts = []
        for n, wide_ref in enumerate(wide_refs):
            here = spot[:, n * 128 : (n + 1) * 128]
            part = jnp.zeros((strips, 128), f32)
            for p in range(SPOTS):
                place = p // HH * WH + half * HH + p % HH
                part = jnp.where(here == p, wide_ref[pl.ds(place, strips, stride=PLACES), :], part)
            parts.append(part)
        strip = jnp.concatenate(parts, axis=1)
        differs = first_level * (own_low ^ low) + pole * (own_north ^ (1 - half))
        halves.append(jnp.where(differs > 0, strip + mask_fill, strip) * log2e)
    for w in range(WW):
        start = (WW - 1 - w) * SPOTS
        part = jnp.concatenate([strip[:, start : start + RUN] for strip in halves], axis=1)
        for g in range(groups):
            for half in range(2):
                rows = part[g * PLACES + half * SPOTS : g * PLACES + (half + 1) * SPOTS, :]
                out_ref[g, half * RUN + w * SPOTS : half * RUN + (w + 1) * SPOTS, :] = rows


def expand_bias(table):
    levels = table.shape[1]
    groups = levels * HEADS
    pairs = PLACES * PLACES
    flat = table[0].transpose(1, 3, 0, 2).reshape(HEADS * RELW, levels, pairs)
    return pl.pallas_call(
        functools.partial(bias_kernel, levels),
        out_shape=shape((groups, TOK, TOK), f32),
        in_specs=vmem(1),
        out_specs=vmem(1)[0],
        scratch_shapes=[pltpu.VMEM((groups * pairs, 128), f32)] * (STRIP // 128),
        compiler_params=pltpu.CompilerParams(vmem_limit_bytes=28 * MIB),
        cost_estimate=cost(10**9, 8 * MIB),
        name="bias",
    )(flat)


def head_masks(count):
    lane = lax.broadcasted_iota(jnp.int32, (count, C), 1)
    return [((lane >= h * HEAD) & (lane < (h + 1) * HEAD)).astype(f32) for h in range(HEADS)]


def stacked(values, masks):
    return jnp.concatenate([values * mask for mask in masks], axis=0)


def head_sum(values, masks):
    total = values[:TOK] * masks[0]
    for h in range(1, HEADS):
        total = total + values[h * TOK : (h + 1) * TOK] * masks[h]
    return total


def position():
    return lax.axis_index("core"), lax.axis_index("y") * 2 + lax.axis_index("x"), lax.axis_index("deep")


def chunk_rows(block):
    return pl.ds(pl.multiple_of(block * PART, PART), PART)


def split_parts(total_refs, keep_ref, send_ref):
    core, chip, _ = position()
    for out, side in ((keep_ref, core), (send_ref, 1 - core)):
        parts = []
        for g in range(QUADS):
            rows = chunk_rows(side * QUADS + jnp.bitwise_xor(chip, g))
            parts += [ref[rows, :] for ref in total_refs]
        out[...] = jnp.concatenate(parts, axis=0).astype(out.dtype)


def attend(first, runs, pieces, bias_ref, triple_ref, project_ref, *refs):
    q_ref, k_ref, v_ref, p_ref, mixed_ref, normed_ref, unit_ref, spread_ref, summed_ref, cot_ref = refs
    pieces = [piece.astype(f32) for piece in pieces]
    ordered = jnp.concatenate([pieces[n][start : start + count] for n, start, count in runs], axis=0)
    emb = ordered[:, :C]
    cot_ref[...] = ordered[:, C:].astype(bf16)
    unit, spread = unit_norm(emb)
    unit_ref[...] = unit
    spread_ref[...] = spread
    normed = unit.astype(bf16)
    normed_ref[...] = normed
    packed = mm(normed, triple_ref[...])
    q_ref[...] = packed[:, :C].astype(bf16)
    k_ref[...] = packed[:, C : 2 * C].astype(bf16)
    v_ref[...] = packed[:, 2 * C :].astype(bf16)
    masks = head_masks(TOK)
    masks_b = [mask.astype(bf16) for mask in masks]
    for w in range(emb.shape[0] // TOK):
        rows = slice(w * TOK, (w + 1) * TOK)
        heads = slice(w * HEADS, (w + 1) * HEADS)
        level = (first + w) % (Z // WZ)
        scores = mm_nt(stacked(q_ref[rows, :], masks_b), k_ref[rows, :])
        bias = bias_ref[level * HEADS : (level + 1) * HEADS].reshape(HEADS * TOK, TOK)
        raised = jnp.exp2(scores * (score_scale * log2e) + bias)
        probs = raised * (1.0 / jnp.sum(raised, -1, keepdims=True))
        probs_b = probs.astype(bf16)
        p_ref[heads] = probs_b.reshape(HEADS, TOK, TOK)
        mixed = head_sum(mm(probs_b, v_ref[rows, :]), masks).astype(bf16)
        mixed_ref[rows, :] = mixed
        summed_ref[rows, :] = emb[rows] + mm(mixed, project_ref[...]).astype(bf16).astype(f32)


def feed_back(summed, cot, up_ref, down_ref, gsum_ref, up_grad_ref, down_grad_ref, before=()):
    unit2, spread2 = unit_norm(summed)
    normed2 = unit2.astype(bf16)
    back = jnp.zeros(unit2.shape, f32)
    block = 256
    for start in range(0, FF, block):
        cols = slice(start, start + block)
        up_part = up_ref[:, cols]
        pre = mm(normed2, up_part)
        upstream = mm(cot, down_ref[:, cols])
        phi = 0.5 * (1.0 + lax.erf(pre * root_half))
        activated = (pre * phi).astype(bf16)
        slope = phi + pre * inv_root_tau * jnp.exp2(pre * pre * (-0.5 * log2e))
        hidden = (upstream * slope).astype(bf16)
        grads = [mm_tn(normed2, hidden), mm_tn(cot, activated)]
        grads = [grad + ref[:, cols] for grad, ref in zip(grads, before)] or grads
        up_grad_ref[:, cols], down_grad_ref[:, cols] = grads
        back = back + mm_nt(hidden, up_part)
    gsum_ref[...] = cot.astype(f32) + norm_back(back, unit2, spread2)


def attend_back(at, q_ref, k_ref, v_ref, p_ref, gsum_ref, project_ref, gq_ref, gk_ref, gv_ref):
    masks = head_masks(TOK)
    masks_b = [mask.astype(bf16) for mask in masks]
    for w in range(q_ref.shape[0] // TOK):
        rows = slice(w * TOK, (w + 1) * TOK)
        full_rows = slice(at + w * TOK, at + (w + 1) * TOK)
        grad = gsum_ref[rows, :].astype(bf16)
        grad_mixed_b = mm_nt(grad, project_ref[...]).astype(bf16)
        probs_b = p_ref[w * HEADS : (w + 1) * HEADS].reshape(HEADS * TOK, TOK)
        probs = probs_b.astype(f32)
        grad_probs = mm_nt(stacked(grad_mixed_b, masks_b), v_ref[rows, :])
        inner = jnp.sum(grad_probs * probs, -1, keepdims=True)
        scaled = (probs * (grad_probs - inner) * score_scale).astype(bf16)
        grad_q = head_sum(mm(scaled, k_ref[rows, :]), masks)
        grad_mixed_t = grad_mixed_b.astype(f32).T.astype(bf16)
        query_t = q_ref[rows, :].astype(f32).T.astype(bf16)
        grad_k, grad_v = [], []
        for h in range(HEADS):
            spot = slice(h * HEAD, (h + 1) * HEAD)
            span = slice(h * TOK, (h + 1) * TOK)
            grad_k.append(mm(query_t[spot], scaled[span]))
            grad_v.append(mm(grad_mixed_t[spot], probs_b[span]))
        gq_ref[full_rows, :] = grad_q.astype(bf16)
        gk_ref[full_rows, :] = jnp.concatenate(grad_k, axis=0).T.astype(bf16)
        gv_ref[full_rows, :] = jnp.concatenate(grad_v, axis=0).T.astype(bf16)


def halved(rows):
    return -(-rows // 16) * 8


def tokens_back(
    lon_windows, sizes, gq_ref, gk_ref, gv_ref, mixed, normed, unit, spread, gsum, triple_ref, up_grad_ref, down_grad_ref,
    *rest,
):
    flag_refs, rest = rest[: len(sizes)], rest[len(sizes) :]
    outs, (land_ref, keep_ref, send_ref, total_ref) = rest[: len(sizes) - 1], rest[len(sizes) - 1 :]
    triple = triple_ref[...]
    grad_normed = jnp.zeros(unit.shape, f32)
    parts = []
    for n, ref in enumerate((gq_ref, gk_ref, gv_ref)):
        grad = ref[...]
        grad_normed = grad_normed + mm_nt(grad, triple[:, n * C : (n + 1) * C])
        parts.append(mm_tn(normed, grad))
    parts.append(mm_tn(mixed, gsum.astype(bf16)))
    total_ref[...] = jnp.concatenate(parts, axis=1)
    grad_normed = grad_normed.astype(bf16).astype(f32)
    grad_tokens = gsum + norm_back(grad_normed, unit, spread)
    parts, at = [[] for _ in sizes], 0
    for n, start, count in [run for window in window_runs(lon_windows) for run in window]:
        parts[n].append((start, grad_tokens[at : at + count]))
        at += count
    land = jnp.zeros((EXTRA, C), f32)
    wide = []
    for size, flag_ref, part in zip(sizes, flag_refs, parts):
        piece = jnp.concatenate([value for _, value in sorted(part, key=lambda item: item[0])], axis=0)
        flags = flag_ref[size - 8 : size + 8, :].astype(f32)[8:, :size]
        land = land + mm(flags.astype(bf16), piece.astype(bf16))
        half = halved(size)
        second = jnp.concatenate([piece[half:], jnp.zeros((2 * half - size, C), f32)], axis=0)
        wide.append(jnp.concatenate([piece[:half], second], axis=1))
    land_ref[...] = land[0:1]
    own, north, side, corner = wide
    for out, value in zip(outs, (own, jnp.concatenate([north, corner], axis=0), side)):
        out[...] = value.astype(bf16)
    split_parts((up_grad_ref, down_grad_ref, total_ref), keep_ref, send_ref)


def saved_shapes(count):
    dims = [((count, C), bf16)] * 3 + [((count // TOK * HEADS, TOK, TOK), bf16)] + [((count, C), bf16)] * 2
    return dims + [((count, C), f32), ((count, 1), f32), ((count, C), f32), ((count, C), bf16)]


SAVED = len(saved_shapes(TOK))


def split_runs(lon_windows):
    windows = window_runs(lon_windows)
    whole = (lon_windows - 1) * (Z // WZ)
    return whole, *[[run for window in part for run in window] for part in (windows[:whole], windows[whole:])]


def near_kernel(lon_windows, own_ref, north_ref, bias_ref, triple_ref, project_ref, up_ref, down_ref, *refs):
    runs = split_runs(lon_windows)[1]
    saved, (gsum, up_grad, down_grad, summed, cot) = refs[: SAVED - 2], refs[SAVED - 2 :]
    attend(0, runs, (own_ref[...], north_ref[...]), bias_ref, triple_ref, project_ref, *saved, summed, cot)
    feed_back(summed[...], cot[...], up_ref, down_ref, gsum, up_grad, down_grad)


def near_block(own, north, bias, triple, project, up, down, lon_windows):
    count = split_runs(lon_windows)[0] * TOK
    dims = saved_shapes(count)
    outs = dims[:-2] + [((count, C), f32)] + [((C, FF), f32)] * 2
    return pl.pallas_call(
        functools.partial(near_kernel, lon_windows),
        out_shape=[shape(*out) for out in outs],
        in_specs=vmem(7),
        out_specs=vmem(len(outs)),
        scratch_shapes=[pltpu.VMEM(*dim) for dim in dims[-2:]],
        compiler_params=pltpu.CompilerParams(vmem_limit_bytes=24 * MIB),
        cost_estimate=cost(3 * 10**9, 8 * MIB),
        name="near_block",
    )(own, north, bias, triple, project, up, down)


def block_kernel(lon_windows, sizes, *refs):
    whole, _, runs = split_runs(lon_windows)
    pieces, refs = refs[:4], refs[4:]
    (bias_ref, triple_ref, project_ref, up_ref, down_ref), refs = refs[:5], refs[5:]
    near, refs = refs[: SAVED + 1], refs[SAVED + 1 :]
    outs, refs = refs[: len(sizes) + 2], refs[len(sizes) + 2 :]
    far, (gsum, up_grad, down_grad, gq, gk, gv, total) = refs[:SAVED], refs[SAVED:]
    attend(whole, runs, [ref[...] for ref in pieces], bias_ref, triple_ref, project_ref, *far)
    near, near_gsum, near_grads = near[: SAVED - 2], near[SAVED - 2], near[SAVED - 1 :]
    far, (summed, cot) = far[:-2], far[-2:]
    feed_back(summed[...], cot[...], up_ref, down_ref, gsum, up_grad, down_grad, near_grads)
    attend_back(0, *near[:4], near_gsum, project_ref, gq, gk, gv)
    attend_back(whole * TOK, *far[:4], gsum, project_ref, gq, gk, gv)
    pairs = zip((*near[4:], near_gsum), (*far[4:], gsum))
    mixed, normed, unit, spread, gsum = [jnp.concatenate([one[...], other[...]], axis=0) for one, other in pairs]
    tokens_back(
        lon_windows, sizes, gq, gk, gv, mixed, normed, unit, spread, gsum, triple_ref, up_grad, down_grad,
        *pieces, *outs, total,
    )


def block(pieces, bias, triple, project, up, down, near, lon_windows, sizes):
    count = sum(sizes)
    own, north, side, corner = [halved(size) for size in sizes]
    out_shape = [shape((size, 2 * C), bf16) for size in (own, north + corner, side)] + [
        shape((1, C), f32),
        shape((QUADS * CHUNK, FF), f32),
        shape((QUADS * CHUNK, FF), bf16),
    ]
    return pl.pallas_call(
        functools.partial(block_kernel, lon_windows, sizes),
        out_shape=out_shape,
        in_specs=vmem(9 + len(near)),
        out_specs=vmem(len(out_shape)),
        scratch_shapes=[pltpu.VMEM(*dims) for dims in saved_shapes(count - near[0].shape[0])]
        + [pltpu.VMEM((count - near[0].shape[0], C), f32)]
        + [pltpu.VMEM((C, FF), f32)] * 2
        + [pltpu.VMEM((count, C), bf16)] * 3
        + [pltpu.VMEM((C, FF), f32)],
        compiler_params=pltpu.CompilerParams(vmem_limit_bytes=28 * MIB),
        cost_estimate=cost(8 * 10**9, 16 * MIB),
        name="block",
    )(*pieces, bias, triple, project, up, down, *near)


def side_kernel(side_ref, north_ref, *refs):
    corner = north_ref[...].astype(f32)[-side_ref.shape[0] :]
    refs[-1][...] = jnp.concatenate([side_ref[...].astype(f32), corner], axis=0).astype(bf16)


def home_kernel(sizes, own_ref, north_ref, side_ref, perm_ref, out_ref, done_ref):
    wide = [ref[...].astype(f32) for ref in (own_ref, north_ref, side_ref)]
    half = wide[2].shape[0] // 2
    wide = [wide[0], wide[1][:-half], wide[2][:half], wide[2][half:]]
    pieces = []
    for size, value in zip(sizes, wide):
        pieces += [value[:, :C], value[: size - value.shape[0], C:]]
    pieces = jnp.concatenate(pieces, axis=0).astype(bf16)
    out_ref[...] = mm(one_hot(perm_ref), pieces).astype(bf16)
    done_ref[...] = jnp.zeros_like(done_ref)


def to_home(own, north, side, sizes, rows, cols):
    count = Z * rows * cols
    perm = spots(np.argsort(np.concatenate(piece_rows(rows, cols))))
    return pl.pallas_call(
        functools.partial(home_kernel, sizes),
        out_shape=[shape((count, C), bf16), shape((8, 128), f32)],
        in_specs=vmem(4),
        out_specs=vmem(2),
        compiler_params=pltpu.CompilerParams(vmem_limit_bytes=32 * MIB),
        cost_estimate=cost(2 * count * count * C, 4 * MIB),
        name="to_home",
    )(own, north, side, perm)


def core_add_kernel(keep_ref, got_ref, *refs):
    own_ref, outs = refs[-QUADS], refs[1 - QUADS :]
    total = keep_ref[...] + got_ref[...].astype(f32)
    own_ref[...] = total[:CHUNK]
    for e, out in zip(FAR_FIRST, outs):
        out[...] = total[e * CHUNK : (e + 1) * CHUNK].astype(bf16)


def chip_add_kernel(keep_ref, *refs):
    gots, (land_ref, out_ref) = refs[:-2], refs[-2:]
    total = keep_ref[...]
    for ref in gots:
        total = total + ref[...].astype(f32)
    land = land_ref[...]
    rest = jnp.concatenate([land[:, 128:], jnp.zeros((1, 2 * 128 - C), f32)], axis=1)
    parts = [total[:, n * 128 : (n + 1) * 128] for n in range(BLOCKS)]
    total = jnp.concatenate(parts + [land[:, :128], rest, jnp.zeros((EXTRA - 2, 128), f32)], axis=0)
    out_ref[...] = total.astype(bf16)


def add_kernel(one_ref, two_ref, *refs):
    refs[-1][...] = (one_ref[...].astype(f32) + two_ref[...].astype(f32)).astype(bf16)


def join_kernel(*refs):
    refs[-1][...] = jnp.concatenate([ref[...] for ref in refs[:-1]], axis=0)


def small_call(kernel, out_shape, args, name, after=(), scratch=()):
    return pl.pallas_call(
        kernel,
        out_shape=out_shape,
        in_specs=vmem(len(args)) + [pl.BlockSpec(memory_space=pl.ANY)] * len(after),
        out_specs=vmem(len(out_shape)),
        scratch_shapes=scratch,
        compiler_params=pltpu.CompilerParams(vmem_limit_bytes=16 * MIB),
        cost_estimate=cost(10**6, 2 * MIB),
        name=name,
    )(*args, *after)


def finish_kernel(far, chunks_ref, *refs):
    if far:
        before_ref, refs = refs[0], refs[5:]
    outs, land_ref, (up_ref, down_ref, triple_ref, project_ref, lands_ref, sum_ref, sems) = refs[:4], refs[4], refs[5:]
    core, chip, _ = position()
    side = 1 - core if far else core
    for g in range(QUADS):
        tiles = chunks_ref[g * FULL : (g + 1) * FULL, :].astype(f32)
        chunk = jnp.concatenate([tiles[n * CHUNK : (n + 1) * CHUNK] for n in range(BLOCKS)], axis=1)
        block = jnp.bitwise_xor(chip, g)
        rows = chunk_rows(block)
        up_ref[rows, :] = chunk[:PART]
        down_ref[rows, :] = chunk[PART : 2 * PART]
        triple_ref[rows, :] = chunk[2 * PART : CHUNK, : 3 * C]
        project_ref[rows, :] = chunk[2 * PART : CHUNK, 3 * C :]
        lands_ref[pl.ds(pl.multiple_of(block * EXTRA, EXTRA), EXTRA), :] = tiles[BLOCKS * CHUNK :]
    copies = []
    for n, (source, out) in enumerate(zip((triple_ref, project_ref, up_ref, down_ref), outs)):
        rows = pl.ds(pl.multiple_of(side * QUADS * PART, 8), QUADS * PART)
        copies.append(pltpu.make_async_copy(source, out.at[rows, :], sems.at[n]))
    for copy in copies:
        copy.start()
    lands = lands_ref[...]
    lands = [sum(lands[g * EXTRA + n : g * EXTRA + n + 1] for g in range(QUADS)) for n in range(2)]
    land = jnp.concatenate([lands[0], lands[1][:, : C - 128]], axis=1)
    if far:
        sum_ref[...] = land + before_ref[...]
        copies.append(pltpu.make_async_copy(sum_ref, land_ref, sems.at[4]))
        copies[-1].start()
    else:
        land_ref[...] = land
    for copy in copies:
        copy.wait()


def finish(chunks, before=()):
    rows = QUADS * PART
    widths = (3 * C, C, FF, FF)
    hbm = [pl.BlockSpec(memory_space=pltpu.HBM)] * 4
    land, weights = before[4:], before[:4]
    return pl.pallas_call(
        functools.partial(finish_kernel, bool(before)),
        out_shape=[shape((C, width), f32) for width in widths] + [shape((1, C), f32)],
        in_specs=vmem(1 + len(land)) + hbm[: len(weights)],
        out_specs=hbm + (hbm[:1] if before else vmem(1)),
        scratch_shapes=[
            pltpu.VMEM((rows, FF), f32),
            pltpu.VMEM((rows, FF), f32),
            pltpu.VMEM((rows, 3 * C), f32),
            pltpu.VMEM((rows, C), f32),
            pltpu.VMEM((QUADS * EXTRA, 128), f32),
            pltpu.VMEM((1, C), f32),
            pltpu.SemaphoreType.DMA((5,)),
        ],
        input_output_aliases={2 + n: n for n in range(len(weights))},
        compiler_params=pltpu.CompilerParams(vmem_limit_bytes=16 * MIB),
        cost_estimate=cost(10**6, 2 * MIB),
        name="finish_far" if before else "finish_own",
    )(chunks, *land, *weights)


def reduce_all(keep, sent, land, side, north, go_home, shift, lon_count):
    core_move = lambda lon, lat: (lon, lat ^ 1)
    chip_move = lambda e: lambda lon, lat: (lon ^ (e & 1), lat ^ (2 * (e >> 1)))
    deep_move = lambda e: lambda lon, lat: (lon ^ (2 * e), lat)

    def one(rows):
        return [shape((rows, FF), bf16)]

    got = shift(sent, move=core_move)
    parts = [shape((CHUNK, FF), f32)] + one(CHUNK) * (QUADS - 1)
    own, *parts = small_call(core_add_kernel, parts, (keep, got), "core_add", after=(north,))
    gots = [shift(value, move=chip_move(e)) for e, value in zip(FAR_FIRST, parts)]
    full = [shape((FULL, 128), bf16)]
    (total,) = small_call(chip_add_kernel, full, (own, *gots, land), "chip_add")
    (side,) = small_call(side_kernel, [shape((2 * side.shape[0], 2 * C), bf16)], (side, north), "side", after=(total,))
    side = shift(side, move=lambda lon, lat: (lon - 1, lat))
    grad_tokens, done = go_home(north, side)
    reach, waits = 1, [(side,), (done,)]
    while reach < lon_count // 2:
        got = shift(total, move=deep_move(reach))
        reach *= 2
        (total,) = small_call(add_kernel, full, (total, got), "deep_add", after=waits.pop(0) if waits else ())
    near = [total] + [shift(total, move=chip_move(e)) for e in range(1, QUADS)]
    (total,) = small_call(join_kernel, [shape((QUADS * FULL, 128), bf16)], near, "join")
    got = shift(total, move=core_move)
    return finish(got, finish(total)), grad_tokens


AXES = ("deep", "x", "y", "core")


def send(value, lon_count, lat_count, move):
    pairs = []
    for lon in range(lon_count):
        for lat in range(lat_count):
            to_lon, to_lat = move(lon, lat)
            pairs.append((lon * lat_count + lat, (to_lon % lon_count) * lat_count + to_lat % lat_count))
    return lax.ppermute(value, AXES, pairs)


def body(
    lon_count, lat_count,
    tokens, cotangent, land_sea, land_vector, triple_weight, project_weight, up_weight, down_weight, earth_bias,
):
    levels, rows, cols, features = tokens.shape
    shift = functools.partial(send, lon_count=lon_count, lat_count=lat_count)
    lon_windows = cols // WW

    own, north, side, corner = pack(tokens, cotangent, land_sea, land_vector, rows, cols)
    north = shift(north, move=lambda lon, lat: (lon, lat + 1))
    side = shift(side, move=lambda lon, lat: (lon + 1, lat))
    corner = shift(corner, move=lambda lon, lat: (lon + 1, lat + 1))
    bias = expand_bias(earth_bias)

    sizes = [part.size for part in piece_rows(rows, cols)]
    pieces = (own, north, side, corner)
    near = near_block(own, north, bias, triple_weight, project_weight, up_weight, down_weight.T, lon_windows)
    own, north, side, land, keep, sent = block(
        pieces, bias, triple_weight, project_weight, up_weight, down_weight.T, near, lon_windows, sizes
    )
    north = shift(north, move=lambda lon, lat: (lon, lat - 1))
    go_home = lambda north, side: to_home(own, north, side, sizes, rows, cols)
    sums, grad_tokens = reduce_all(keep, sent, land, side, north, go_home, shift, lon_count)
    triple, project, up, down, land = sums
    return grad_tokens.reshape(tokens.shape), triple, project, up, down.T, land.reshape(features)


def solution(mesh):
    lon_count, lat_count = mesh.shape["lon"], mesh.shape["lat"]
    fine = jax.sharding.Mesh(mesh.devices.reshape(lon_count // 2, 2, lat_count // 2, 2), AXES)
    lon, lat = AXES[:2], AXES[2:]
    return jax.shard_map(
        functools.partial(body, lon_count, lat_count),
        mesh=fine,
        in_specs=(
            P(None, lat, lon, None),
            P(None, lat, lon, None),
            P(lat, lon),
            P(),
            P(),
            P(),
            P(),
            P(),
            P(lat, None, None, None, None),
        ),
        out_specs=(P(None, lat, lon, None), P(), P(), P(), P(), P()),
        check_vma=False,
    )
```

```python
import functools
import math

import jax
import jax.numpy as jnp
import numpy as np
from jax import lax
from jax.experimental import pallas as pl
from jax.experimental.pallas import tpu as pltpu
from jax.sharding import PartitionSpec as P

Z = 4
WZ = 2
WH = 6
WW = 12
C = 192
HEADS = 6
HEAD = 32
FF = 768
HZ, HH, HW = WZ // 2, WH // 2, WW // 2
TOK = WZ * WH * WW
PLACES = WZ * WH
RELW = 2 * WW - 1
SPOTS = PLACES // 2
STRIP = -(-RELW * SPOTS // 128) * 128
RUN, SHORT = WW * SPOTS, (WW - HW) * SPOTS

mask_fill = -10000.0
norm_eps = 1e-05
log2e = 1.4426950408889634
root_half = 0.7071067811865476
inv_root_tau = 0.3989422804014327
score_scale = HEAD**-0.5

f32 = jnp.float32
bf16 = jnp.bfloat16
MIB = 1 << 20

QUADS = 4
FAR_FIRST = range(QUADS - 1, 0, -1)
PART = C // (2 * QUADS)
CHUNK = 3 * PART
BLOCKS = FF // 128
EXTRA = 8
FULL = BLOCKS * CHUNK + EXTRA


def mm(a, b):
    return lax.dot_general(a, b, (((1,), (0,)), ((), ())), preferred_element_type=f32)


def mm_nt(a, b):
    return lax.dot_general(a, b, (((1,), (1,)), ((), ())), preferred_element_type=f32)


def mm_tn(a, b):
    return lax.dot_general(a, b, (((0,), (0,)), ((), ())), preferred_element_type=f32)


def unit_norm(values):
    average = jnp.mean(values, -1, keepdims=True)
    centred = values - average
    variance = jnp.mean(centred * centred, -1, keepdims=True)
    spread = lax.rsqrt(variance + norm_eps)
    return centred * spread, spread


def norm_back(upstream, unit, spread):
    first = jnp.mean(upstream, -1, keepdims=True)
    second = jnp.mean(upstream * unit, -1, keepdims=True)
    return spread * (upstream - first - unit * second)


def piece_rows(rows, cols):
    home = np.arange(Z * rows * cols).reshape(Z, rows, cols)

    def run(level, row, col, width):
        levels = [(level * WZ + z - HZ) % Z for z in range(WZ)]
        return home[levels, row : row + HH, col : col + width].transpose(2, 0, 1).reshape(-1)

    levels = range(Z // WZ)
    parts = []
    for row in (0, rows - HH):
        whole = [run(a, row, w * WW - HW, WW) for w in range(1, cols // WW) for a in levels]
        parts.append(np.concatenate(whole + [run(a, row, 0, WW - HW) for a in levels]))
    for row in (0, rows - HH):
        parts.append(np.concatenate([run(a, row, cols - HW, HW) for a in levels]))
    return parts


def window_runs(lon_windows):
    levels = Z // WZ
    whole = (lon_windows - 1) * levels
    runs = [[(1, n * RUN, RUN), (0, n * RUN, RUN)] for n in range(whole)]
    for a in range(levels):
        inner = whole * RUN + a * SHORT
        west = (a * (RUN - SHORT), RUN - SHORT)
        runs.append([(3, *west), (1, inner, SHORT), (2, *west), (0, inner, SHORT)])
    return runs


def spots(places):
    return jnp.asarray(np.argsort(places).astype(np.int32)[None])


def one_hot(spot_ref):
    count = spot_ref.shape[1]
    rows = lax.broadcasted_iota(jnp.int32, (count, count), 0)
    return (rows == spot_ref[...]).astype(f32).astype(bf16)


def vmem(count):
    return [pl.BlockSpec(memory_space=pltpu.VMEM)] * count


def shape(dims, dtype):
    return jax.ShapeDtypeStruct(dims, dtype)


def cost(flops, moved):
    return pl.CostEstimate(flops=flops, bytes_accessed=moved, transcendentals=0)


def land_column(land_ref, rows, cols):
    eye = (
        lax.broadcasted_iota(jnp.int32, (cols, cols), 0)
        == lax.broadcasted_iota(jnp.int32, (cols, cols), 1)
    ).astype(f32)
    land = land_ref[...].astype(f32)
    parts = [jnp.sum(eye * land[i : i + 1, :], -1, keepdims=True) for i in range(rows)]
    return jnp.concatenate(parts, axis=0)


def pack_kernel(rows, cols, *refs):
    sources, outs, (tokens_ref, cot_ref, land_ref, vec_ref, perm_ref, sems) = refs[:5], refs[5:-6], refs[-6:]
    copies = [
        pltpu.make_async_copy(source, target, sems.at[n])
        for n, (source, target) in enumerate(zip(sources, (tokens_ref, cot_ref, land_ref, vec_ref, perm_ref)))
    ]
    for copy in copies:
        copy.start()
    for copy in copies:
        copy.wait()
    column = land_column(land_ref, rows, cols)
    added = column * vec_ref[...]
    added = jnp.concatenate([added] * Z, axis=0)
    embedded = (tokens_ref[...].astype(f32) + added).astype(bf16)
    perm = one_hot(perm_ref)
    column = jnp.concatenate([column] * Z, axis=0)
    spare = jnp.broadcast_to(column, (column.shape[0], 2 * 128 - C)).astype(bf16)
    left = mm(perm, jnp.concatenate([embedded, spare], axis=1))
    left, flags = left[:, :C], left[:, C : C + 1]
    right = mm(perm, cot_ref[...])
    packed = jnp.concatenate([left, right], axis=1)
    start = 0
    for out in outs:
        count = out.shape[0] - EXTRA
        eye = lax.broadcasted_iota(jnp.int32, (count, count), 0) == lax.broadcasted_iota(jnp.int32, (count, count), 1)
        row = jnp.sum(jnp.where(eye, flags[start : start + count], 0.0), 0, keepdims=True)
        row = jnp.concatenate([row, jnp.zeros((1, 2 * C - count), f32)], axis=1)
        row = jnp.broadcast_to(row, (EXTRA, 2 * C))
        out[...] = jnp.concatenate([packed[start : start + count], row], axis=0).astype(bf16)
        start += count


def pack(tokens, cotangent, land_sea, vector, rows, cols):
    parts = piece_rows(rows, cols)
    perm = spots(np.concatenate(parts))
    count = Z * rows * cols
    return pl.pallas_call(
        functools.partial(pack_kernel, rows, cols),
        out_shape=[shape((part.size + EXTRA, 2 * C), bf16) for part in parts],
        in_specs=[pl.BlockSpec(memory_space=pltpu.HBM)] * 5,
        out_specs=vmem(4),
        scratch_shapes=[
            pltpu.VMEM((count, C), bf16),
            pltpu.VMEM((count, C), bf16),
            pltpu.VMEM((rows, cols), jnp.int32),
            pltpu.VMEM((1, C), f32),
            pltpu.VMEM((1, count), jnp.int32),
            pltpu.SemaphoreType.DMA((5,)),
        ],
        compiler_params=pltpu.CompilerParams(vmem_limit_bytes=24 * MIB),
        cost_estimate=cost(4 * count * count * C, 4 * MIB),
        name="pack",
    )(*[
        pltpu.with_memory_space_constraint(value, pltpu.HBM)
        for value in (tokens.reshape(count, C), cotangent.reshape(count, C), land_sea, vector.reshape(1, C), perm)
    ])


def floor_div(values, divisor):
    return (values * (65536 // divisor + 1)) >> 16


def remainder(values, divisor):
    return values - floor_div(values, divisor) * divisor


def place_order(order):
    half = floor_div(order, SPOTS)
    spot = order - half * SPOTS
    level = floor_div(spot, HH)
    return level * WH + half * HH + (spot - level * HH)


def bias_kernel(levels, source_ref, out_ref, table_ref, sem, *wide_refs):
    copy = pltpu.make_async_copy(source_ref, table_ref, sem)
    copy.start()
    groups = levels * HEADS
    pairs = PLACES * PLACES
    row = lax.broadcasted_iota(jnp.int32, (HEADS * RELW, HEADS * STRIP), 0)
    lane = lax.broadcasted_iota(jnp.int32, (HEADS * RELW, HEADS * STRIP), 1)
    head = floor_div(row, RELW)
    ahead = lane - (head * STRIP + (RELW - 1 - (row - head * RELW)) * SPOTS)
    onehot = ((ahead >= 0) & (ahead < SPOTS)).astype(f32).astype(bf16)
    row = lax.broadcasted_iota(jnp.int32, (pairs, pairs), 0)
    source = place_order(floor_div(row, PLACES)) * PLACES + remainder(row, PLACES)
    reorder = (lax.broadcasted_iota(jnp.int32, (pairs, pairs), 1) == source).astype(f32).astype(bf16)
    copy.wait()
    for level in range(levels):
        table = table_ref[:, level, :].T
        high = table.astype(bf16)
        rest = (table - high.astype(f32)).astype(bf16)
        wide = mm(mm(reorder, high).astype(bf16), onehot) + mm(mm(reorder, rest).astype(bf16), onehot)
        for head in range(HEADS):
            for n, wide_ref in enumerate(wide_refs):
                start = head * STRIP + n * 128
                wide_ref[(level * HEADS + head) * pairs : (level * HEADS + head + 1) * pairs, :] = wide[:, start : start + 128]
    strips = groups * PLACES
    row = lax.broadcasted_iota(jnp.int32, (strips, STRIP), 0)
    spot = remainder(lax.broadcasted_iota(jnp.int32, (strips, STRIP), 1), SPOTS)
    own = remainder(row, PLACES)
    first_level = (row < HEADS * PLACES).astype(jnp.int32)
    own_north = (own < SPOTS).astype(jnp.int32)
    own_low = (own - SPOTS * (1 - own_north) < HZ * HH).astype(jnp.int32)
    low = (spot < HZ * HH).astype(jnp.int32)
    pole = (lax.axis_index("y") + lax.axis_index("core") == 0).astype(jnp.int32)
    halves = []
    for half in range(2):
        parts = []
        for n, wide_ref in enumerate(wide_refs):
            here = spot[:, n * 128 : (n + 1) * 128]
            part = jnp.zeros((strips, 128), f32)
            for p in range(SPOTS):
                place = p // HH * WH + half * HH + p % HH
                part = jnp.where(here == p, wide_ref[pl.ds(place, strips, stride=PLACES), :], part)
            parts.append(part)
        strip = jnp.concatenate(parts, axis=1)
        differs = first_level * (own_low ^ low) + pole * (own_north ^ (1 - half))
        halves.append(jnp.where(differs > 0, strip + mask_fill, strip) * log2e)
    for w in range(WW):
        start = (WW - 1 - w) * SPOTS
        part = jnp.concatenate([strip[:, start : start + RUN] for strip in halves], axis=1)
        for g in range(groups):
            for half in range(2):
                rows = part[g * PLACES + half * SPOTS : g * PLACES + (half + 1) * SPOTS, :]
                out_ref[g, half * RUN + w * SPOTS : half * RUN + (w + 1) * SPOTS, :] = rows


def expand_bias(table):
    levels = table.shape[1]
    groups = levels * HEADS
    pairs = PLACES * PLACES
    flat = table[0].transpose(1, 3, 0, 2).reshape(HEADS * RELW, levels, pairs)
    return pl.pallas_call(
        functools.partial(bias_kernel, levels),
        out_shape=shape((groups, TOK, TOK), f32),
        in_specs=[pl.BlockSpec(memory_space=pltpu.HBM)],
        out_specs=vmem(1)[0],
        scratch_shapes=[pltpu.VMEM(flat.shape, f32), pltpu.SemaphoreType.DMA]
        + [pltpu.VMEM((groups * pairs, 128), f32)] * (STRIP // 128),
        compiler_params=pltpu.CompilerParams(vmem_limit_bytes=28 * MIB),
        cost_estimate=cost(10**9, 8 * MIB),
        name="bias",
    )(pltpu.with_memory_space_constraint(flat, pltpu.HBM))


def head_masks(count):
    lane = lax.broadcasted_iota(jnp.int32, (count, C), 1)
    return [((lane >= h * HEAD) & (lane < (h + 1) * HEAD)).astype(f32) for h in range(HEADS)]


def stacked(values, masks):
    return jnp.concatenate([values * mask for mask in masks], axis=0)


def head_sum(values, masks):
    total = values[:TOK] * masks[0]
    for h in range(1, HEADS):
        total = total + values[h * TOK : (h + 1) * TOK] * masks[h]
    return total


def position():
    return lax.axis_index("core"), lax.axis_index("y") * 2 + lax.axis_index("x"), lax.axis_index("deep")


def chunk_rows(block):
    return pl.ds(pl.multiple_of(block * PART, PART), PART)


def split_parts(total_refs, keep_ref, send_ref):
    core, chip, _ = position()
    for out, side in ((keep_ref, core), (send_ref, 1 - core)):
        parts = []
        for g in range(QUADS):
            rows = chunk_rows(side * QUADS + jnp.bitwise_xor(chip, g))
            parts += [ref[rows, :] for ref in total_refs]
        out[...] = jnp.concatenate(parts, axis=0).astype(out.dtype)


def attend(first, runs, pieces, bias_ref, triple_ref, project_ref, *refs):
    q_ref, k_ref, v_ref, p_ref, mixed_ref, normed_ref, unit_ref, spread_ref, summed_ref, cot_ref = refs
    pieces = [piece.astype(f32) for piece in pieces]
    ordered = jnp.concatenate([pieces[n][start : start + count] for n, start, count in runs], axis=0)
    emb = ordered[:, :C]
    cot_ref[...] = ordered[:, C:].astype(bf16)
    unit, spread = unit_norm(emb)
    unit_ref[...] = unit
    spread_ref[...] = spread
    normed = unit.astype(bf16)
    normed_ref[...] = normed
    packed = mm(normed, triple_ref[...])
    q_ref[...] = packed[:, :C].astype(bf16)
    k_ref[...] = packed[:, C : 2 * C].astype(bf16)
    v_ref[...] = packed[:, 2 * C :].astype(bf16)
    masks = head_masks(TOK)
    masks_b = [mask.astype(bf16) for mask in masks]
    for w in range(emb.shape[0] // TOK):
        rows = slice(w * TOK, (w + 1) * TOK)
        heads = slice(w * HEADS, (w + 1) * HEADS)
        level = (first + w) % (Z // WZ)
        scores = mm_nt(stacked(q_ref[rows, :], masks_b), k_ref[rows, :])
        bias = bias_ref[level * HEADS : (level + 1) * HEADS].reshape(HEADS * TOK, TOK)
        raised = jnp.exp2(scores * (score_scale * log2e) + bias)
        probs = raised * (1.0 / jnp.sum(raised, -1, keepdims=True))
        probs_b = probs.astype(bf16)
        p_ref[heads] = probs_b.reshape(HEADS, TOK, TOK)
        mixed = head_sum(mm(probs_b, v_ref[rows, :]), masks).astype(bf16)
        mixed_ref[rows, :] = mixed
        summed_ref[rows, :] = emb[rows] + mm(mixed, project_ref[...]).astype(bf16).astype(f32)


def feed_back(summed, cot, up_ref, down_ref, gsum_ref, up_grad_ref, down_grad_ref):
    unit2, spread2 = unit_norm(summed)
    normed2 = unit2.astype(bf16)
    back = jnp.zeros(unit2.shape, f32)
    block = 256
    for start in range(0, FF, block):
        cols = slice(start, start + block)
        up_part = up_ref[:, cols]
        pre = mm(normed2, up_part)
        upstream = mm(cot, down_ref[:, cols])
        phi = 0.5 * (1.0 + lax.erf(pre * root_half))
        activated = (pre * phi).astype(bf16)
        slope = phi + pre * inv_root_tau * jnp.exp2(pre * pre * (-0.5 * log2e))
        hidden = (upstream * slope).astype(bf16)
        up_grad_ref[:, cols] = mm_tn(normed2, hidden)
        down_grad_ref[:, cols] = mm_tn(cot, activated)
        back = back + mm_nt(hidden, up_part)
    gsum_ref[...] = cot.astype(f32) + norm_back(back, unit2, spread2)


def attend_back(at, q_ref, k_ref, v_ref, p_ref, gsum_ref, project_ref, gq_ref, gk_ref, gv_ref):
    masks = head_masks(TOK)
    masks_b = [mask.astype(bf16) for mask in masks]
    for w in range(q_ref.shape[0] // TOK):
        rows = slice(w * TOK, (w + 1) * TOK)
        full_rows = slice(at + w * TOK, at + (w + 1) * TOK)
        grad = gsum_ref[full_rows, :].astype(bf16)
        grad_mixed_b = mm_nt(grad, project_ref[...]).astype(bf16)
        probs_b = p_ref[w * HEADS : (w + 1) * HEADS].reshape(HEADS * TOK, TOK)
        probs = probs_b.astype(f32)
        grad_probs = mm_nt(stacked(grad_mixed_b, masks_b), v_ref[rows, :])
        inner = jnp.sum(grad_probs * probs, -1, keepdims=True)
        scaled = (probs * (grad_probs - inner) * score_scale).astype(bf16)
        grad_q = head_sum(mm(scaled, k_ref[rows, :]), masks)
        grad_mixed_t = grad_mixed_b.astype(f32).T.astype(bf16)
        query_t = q_ref[rows, :].astype(f32).T.astype(bf16)
        grad_k, grad_v = [], []
        for h in range(HEADS):
            spot = slice(h * HEAD, (h + 1) * HEAD)
            span = slice(h * TOK, (h + 1) * TOK)
            grad_k.append(mm(query_t[spot], scaled[span]))
            grad_v.append(mm(grad_mixed_t[spot], probs_b[span]))
        gq_ref[full_rows, :] = grad_q.astype(bf16)
        gk_ref[full_rows, :] = jnp.concatenate(grad_k, axis=0).T.astype(bf16)
        gv_ref[full_rows, :] = jnp.concatenate(grad_v, axis=0).T.astype(bf16)


def halved(rows):
    return -(-rows // 16) * 8


def tokens_back(
    lon_windows, sizes, gq_ref, gk_ref, gv_ref, mixed, normed, unit, spread, gsum_ref, triple_ref, up_grad_ref, down_grad_ref,
    *rest,
):
    flag_refs, rest = rest[: len(sizes)], rest[len(sizes) :]
    outs, (land_ref, keep_ref, send_ref, total_ref) = rest[: len(sizes) - 1], rest[len(sizes) - 1 :]
    triple = triple_ref[...]
    grad_normed = jnp.zeros(unit.shape, f32)
    parts = []
    for n, ref in enumerate((gq_ref, gk_ref, gv_ref)):
        grad = ref[...]
        grad_normed = grad_normed + mm_nt(grad, triple[:, n * C : (n + 1) * C])
        parts.append(mm_tn(normed, grad))
    parts.append(mm_tn(mixed, gsum_ref[...].astype(bf16)))
    total_ref[...] = jnp.concatenate(parts, axis=1)
    grad_normed = grad_normed.astype(bf16).astype(f32)
    grad_tokens = gsum_ref[...] + norm_back(grad_normed, unit, spread)
    parts, at = [[] for _ in sizes], 0
    for n, start, count in [run for window in window_runs(lon_windows) for run in window]:
        parts[n].append((start, grad_tokens[at : at + count]))
        at += count
    land = jnp.zeros((EXTRA, C), f32)
    wide = []
    for size, flag_ref, part in zip(sizes, flag_refs, parts):
        piece = jnp.concatenate([value for _, value in sorted(part, key=lambda item: item[0])], axis=0)
        flags = flag_ref[size - 8 : size + 8, :].astype(f32)[8:, :size]
        land = land + mm(flags.astype(bf16), piece.astype(bf16))
        half = halved(size)
        second = jnp.concatenate([piece[half:], jnp.zeros((2 * half - size, C), f32)], axis=0)
        wide.append(jnp.concatenate([piece[:half], second], axis=1))
    land_ref[...] = land[0:1]
    own, north, side, corner = wide
    for out, value in zip(outs, (own, jnp.concatenate([north, corner], axis=0), side)):
        out[...] = value.astype(bf16)
    split_parts((up_grad_ref, down_grad_ref, total_ref), keep_ref, send_ref)


def saved_shapes(count):
    dims = [((count, C), bf16)] * 3 + [((count // TOK * HEADS, TOK, TOK), bf16)] + [((count, C), bf16)] * 2
    return dims + [((count, C), f32), ((count, 1), f32), ((count, C), f32), ((count, C), bf16)]


SAVED = len(saved_shapes(TOK))


def split_runs(lon_windows):
    windows = window_runs(lon_windows)
    whole = (lon_windows - 1) * (Z // WZ)
    return whole, *[[run for window in part for run in window] for part in (windows[:whole], windows[whole:])]


def near_kernel(lon_windows, own_ref, north_ref, *refs):
    runs = split_runs(lon_windows)[1]
    attend(0, runs, (own_ref[...], north_ref[...]), *refs)


def near_block(own, north, bias, triple, project, lon_windows):
    count = split_runs(lon_windows)[0] * TOK
    return pl.pallas_call(
        functools.partial(near_kernel, lon_windows),
        out_shape=[shape(*dims) for dims in saved_shapes(count)],
        in_specs=vmem(5),
        out_specs=vmem(SAVED),
        compiler_params=pltpu.CompilerParams(vmem_limit_bytes=24 * MIB),
        cost_estimate=cost(3 * 10**9, 8 * MIB),
        name="near_block",
    )(own, north, bias, triple, project)


def block_kernel(lon_windows, sizes, *refs):
    whole, _, runs = split_runs(lon_windows)
    pieces, refs = refs[:4], refs[4:]
    (bias_ref, triple_ref, project_ref, up_ref, down_ref), refs = refs[:5], refs[5:]
    near, refs = refs[:SAVED], refs[SAVED:]
    outs, refs = refs[: len(sizes) + 2], refs[len(sizes) + 2 :]
    far, (gsum, up_grad, down_grad, gq, gk, gv, total) = refs[:SAVED], refs[SAVED:]
    attend(whole, runs, [ref[...] for ref in pieces], bias_ref, triple_ref, project_ref, *far)
    mixed, normed, unit, spread, summed, cot = [
        jnp.concatenate([one[...], other[...]], axis=0) for one, other in zip(near[4:], far[4:])
    ]
    feed_back(summed, cot, up_ref, down_ref, gsum, up_grad, down_grad)
    attend_back(0, *near[:4], gsum, project_ref, gq, gk, gv)
    attend_back(whole * TOK, *far[:4], gsum, project_ref, gq, gk, gv)
    tokens_back(
        lon_windows, sizes, gq, gk, gv, mixed, normed, unit, spread, gsum, triple_ref, up_grad, down_grad,
        *pieces, *outs, total,
    )


def block(pieces, bias, triple, project, up, down, near, lon_windows, sizes):
    count = sum(sizes)
    own, north, side, corner = [halved(size) for size in sizes]
    out_shape = [shape((size, 2 * C), bf16) for size in (own, north + corner, side)] + [
        shape((1, C), f32),
        shape((QUADS * CHUNK, FF), f32),
        shape((QUADS * CHUNK, FF), bf16),
    ]
    return pl.pallas_call(
        functools.partial(block_kernel, lon_windows, sizes),
        out_shape=out_shape,
        in_specs=vmem(9 + SAVED),
        out_specs=vmem(len(out_shape)),
        scratch_shapes=[pltpu.VMEM(*dims) for dims in saved_shapes(count - near[0].shape[0])]
        + [pltpu.VMEM((count, C), f32)]
        + [pltpu.VMEM((C, FF), f32)] * 2
        + [pltpu.VMEM((count, C), bf16)] * 3
        + [pltpu.VMEM((C, FF), f32)],
        compiler_params=pltpu.CompilerParams(vmem_limit_bytes=28 * MIB),
        cost_estimate=cost(8 * 10**9, 16 * MIB),
        name="block",
    )(*pieces, bias, triple, project, up, down, *near)


def side_kernel(side_ref, north_ref, *refs):
    corner = north_ref[...].astype(f32)[-side_ref.shape[0] :]
    refs[-1][...] = jnp.concatenate([side_ref[...].astype(f32), corner], axis=0).astype(bf16)


def home_kernel(sizes, own_ref, north_ref, side_ref, perm_ref, out_ref, done_ref):
    wide = [ref[...].astype(f32) for ref in (own_ref, north_ref, side_ref)]
    half = wide[2].shape[0] // 2
    wide = [wide[0], wide[1][:-half], wide[2][:half], wide[2][half:]]
    pieces = []
    for size, value in zip(sizes, wide):
        pieces += [value[:, :C], value[: size - value.shape[0], C:]]
    pieces = jnp.concatenate(pieces, axis=0).astype(bf16)
    out_ref[...] = mm(one_hot(perm_ref), pieces).astype(bf16)
    done_ref[...] = jnp.zeros_like(done_ref)


def to_home(own, north, side, sizes, rows, cols):
    count = Z * rows * cols
    perm = spots(np.argsort(np.concatenate(piece_rows(rows, cols))))
    return pl.pallas_call(
        functools.partial(home_kernel, sizes),
        out_shape=[shape((count, C), bf16), shape((8, 128), f32)],
        in_specs=vmem(4),
        out_specs=vmem(2),
        compiler_params=pltpu.CompilerParams(vmem_limit_bytes=32 * MIB),
        cost_estimate=cost(2 * count * count * C, 4 * MIB),
        name="to_home",
    )(own, north, side, perm)


def core_add_kernel(keep_ref, got_ref, *refs):
    own_ref, outs = refs[-QUADS], refs[1 - QUADS :]
    total = keep_ref[...] + got_ref[...].astype(f32)
    own_ref[...] = total[:CHUNK]
    for e, out in zip(FAR_FIRST, outs):
        out[...] = total[e * CHUNK : (e + 1) * CHUNK].astype(bf16)


def chip_add_kernel(keep_ref, *refs):
    gots, (land_ref, out_ref) = refs[:-2], refs[-2:]
    total = keep_ref[...]
    for ref in gots:
        total = total + ref[...].astype(f32)
    land = land_ref[...]
    rest = jnp.concatenate([land[:, 128:], jnp.zeros((1, 2 * 128 - C), f32)], axis=1)
    parts = [total[:, n * 128 : (n + 1) * 128] for n in range(BLOCKS)]
    total = jnp.concatenate(parts + [land[:, :128], rest, jnp.zeros((EXTRA - 2, 128), f32)], axis=0)
    out_ref[...] = total.astype(bf16)


def add_kernel(one_ref, two_ref, *refs):
    refs[-1][...] = (one_ref[...].astype(f32) + two_ref[...].astype(f32)).astype(bf16)


def join_kernel(*refs):
    refs[-1][...] = jnp.concatenate([ref[...] for ref in refs[:-1]], axis=0)


def small_call(kernel, out_shape, args, name, after=(), scratch=()):
    return pl.pallas_call(
        kernel,
        out_shape=out_shape,
        in_specs=vmem(len(args)) + [pl.BlockSpec(memory_space=pl.ANY)] * len(after),
        out_specs=vmem(len(out_shape)),
        scratch_shapes=scratch,
        compiler_params=pltpu.CompilerParams(vmem_limit_bytes=16 * MIB),
        cost_estimate=cost(10**6, 2 * MIB),
        name=name,
    )(*args, *after)


def finish_kernel(far, chunks_ref, *refs):
    if far:
        before_ref, refs = refs[0], refs[5:]
    outs, land_ref, (up_ref, down_ref, triple_ref, project_ref, lands_ref, sum_ref, sems) = refs[:4], refs[4], refs[5:]
    core, chip, _ = position()
    side = 1 - core if far else core
    for g in range(QUADS):
        tiles = chunks_ref[g * FULL : (g + 1) * FULL, :].astype(f32)
        chunk = jnp.concatenate([tiles[n * CHUNK : (n + 1) * CHUNK] for n in range(BLOCKS)], axis=1)
        block = jnp.bitwise_xor(chip, g)
        rows = chunk_rows(block)
        up_ref[rows, :] = chunk[:PART]
        down_ref[rows, :] = chunk[PART : 2 * PART]
        triple_ref[rows, :] = chunk[2 * PART : CHUNK, : 3 * C]
        project_ref[rows, :] = chunk[2 * PART : CHUNK, 3 * C :]
        lands_ref[pl.ds(pl.multiple_of(block * EXTRA, EXTRA), EXTRA), :] = tiles[BLOCKS * CHUNK :]
    copies = []
    for n, (source, out) in enumerate(zip((triple_ref, project_ref, up_ref, down_ref), outs)):
        rows = pl.ds(pl.multiple_of(side * QUADS * PART, 8), QUADS * PART)
        copies.append(pltpu.make_async_copy(source, out.at[rows, :], sems.at[n]))
    for copy in copies:
        copy.start()
    lands = lands_ref[...]
    lands = [sum(lands[g * EXTRA + n : g * EXTRA + n + 1] for g in range(QUADS)) for n in range(2)]
    land = jnp.concatenate([lands[0], lands[1][:, : C - 128]], axis=1)
    if far:
        sum_ref[...] = land + before_ref[...]
        copies.append(pltpu.make_async_copy(sum_ref, land_ref, sems.at[4]))
        copies[-1].start()
    else:
        land_ref[...] = land
    for copy in copies:
        copy.wait()


def finish(chunks, before=()):
    rows = QUADS * PART
    widths = (3 * C, C, FF, FF)
    hbm = [pl.BlockSpec(memory_space=pltpu.HBM)] * 4
    land, weights = before[4:], before[:4]
    return pl.pallas_call(
        functools.partial(finish_kernel, bool(before)),
        out_shape=[shape((C, width), f32) for width in widths] + [shape((1, C), f32)],
        in_specs=vmem(1 + len(land)) + hbm[: len(weights)],
        out_specs=hbm + (hbm[:1] if before else vmem(1)),
        scratch_shapes=[
            pltpu.VMEM((rows, FF), f32),
            pltpu.VMEM((rows, FF), f32),
            pltpu.VMEM((rows, 3 * C), f32),
            pltpu.VMEM((rows, C), f32),
            pltpu.VMEM((QUADS * EXTRA, 128), f32),
            pltpu.VMEM((1, C), f32),
            pltpu.SemaphoreType.DMA((5,)),
        ],
        input_output_aliases={2 + n: n for n in range(len(weights))},
        compiler_params=pltpu.CompilerParams(vmem_limit_bytes=16 * MIB),
        cost_estimate=cost(10**6, 2 * MIB),
        name="finish_far" if before else "finish_own",
    )(chunks, *land, *weights)


def reduce_all(keep, sent, land, side, north, go_home, shift, lon_count):
    core_move = lambda lon, lat: (lon, lat ^ 1)
    chip_move = lambda e: lambda lon, lat: (lon ^ (e & 1), lat ^ (2 * (e >> 1)))
    deep_move = lambda e: lambda lon, lat: (lon ^ (2 * e), lat)

    def one(rows):
        return [shape((rows, FF), bf16)]

    got = shift(sent, move=core_move)
    parts = [shape((CHUNK, FF), f32)] + one(CHUNK) * (QUADS - 1)
    own, *parts = small_call(core_add_kernel, parts, (keep, got), "core_add", after=(north,))
    gots = [shift(value, move=chip_move(e)) for e, value in zip(FAR_FIRST, parts)]
    full = [shape((FULL, 128), bf16)]
    (total,) = small_call(chip_add_kernel, full, (own, *gots, land), "chip_add")
    (side,) = small_call(side_kernel, [shape((2 * side.shape[0], 2 * C), bf16)], (side, north), "side", after=(total,))
    side = shift(side, move=lambda lon, lat: (lon - 1, lat))
    grad_tokens, done = go_home(north, side)
    reach, waits = 1, [(side,), (done,)]
    while reach < lon_count // 2:
        got = shift(total, move=deep_move(reach))
        reach *= 2
        (total,) = small_call(add_kernel, full, (total, got), "deep_add", after=waits.pop(0) if waits else ())
    near = [total] + [shift(total, move=chip_move(e)) for e in range(1, QUADS)]
    (total,) = small_call(join_kernel, [shape((QUADS * FULL, 128), bf16)], near, "join")
    got = shift(total, move=core_move)
    return finish(got, finish(total)), grad_tokens


AXES = ("deep", "x", "y", "core")


def send(value, lon_count, lat_count, move):
    pairs = []
    for lon in range(lon_count):
        for lat in range(lat_count):
            to_lon, to_lat = move(lon, lat)
            pairs.append((lon * lat_count + lat, (to_lon % lon_count) * lat_count + to_lat % lat_count))
    return lax.ppermute(value, AXES, pairs)


def body(
    lon_count, lat_count,
    tokens, cotangent, land_sea, land_vector, triple_weight, project_weight, up_weight, down_weight, earth_bias,
):
    levels, rows, cols, features = tokens.shape
    shift = functools.partial(send, lon_count=lon_count, lat_count=lat_count)
    lon_windows = cols // WW

    own, north, side, corner = pack(tokens, cotangent, land_sea, land_vector, rows, cols)
    north = shift(north, move=lambda lon, lat: (lon, lat + 1))
    side = shift(side, move=lambda lon, lat: (lon + 1, lat))
    corner = shift(corner, move=lambda lon, lat: (lon + 1, lat + 1))
    bias = expand_bias(earth_bias)

    sizes = [part.size for part in piece_rows(rows, cols)]
    pieces = (own, north, side, corner)
    near = near_block(own, north, bias, triple_weight, project_weight, lon_windows)
    own, north, side, land, keep, sent = block(
        pieces, bias, triple_weight, project_weight, up_weight, down_weight.T, near, lon_windows, sizes
    )
    north = shift(north, move=lambda lon, lat: (lon, lat - 1))
    go_home = lambda north, side: to_home(own, north, side, sizes, rows, cols)
    sums, grad_tokens = reduce_all(keep, sent, land, side, north, go_home, shift, lon_count)
    triple, project, up, down, land = sums
    return grad_tokens.reshape(tokens.shape), triple, project, up, down.T, land.reshape(features)


def solution(mesh):
    lon_count, lat_count = mesh.shape["lon"], mesh.shape["lat"]
    fine = jax.sharding.Mesh(mesh.devices.reshape(lon_count // 2, 2, lat_count // 2, 2), AXES)
    lon, lat = AXES[:2], AXES[2:]
    return jax.shard_map(
        functools.partial(body, lon_count, lat_count),
        mesh=fine,
        in_specs=(
            P(None, lat, lon, None),
            P(None, lat, lon, None),
            P(lat, lon),
            P(),
            P(),
            P(),
            P(),
            P(),
            P(lat, None, None, None, None),
        ),
        out_specs=(P(None, lat, lon, None), P(), P(), P(), P(), P()),
        check_vma=False,
    )
```

```python
import functools
import math

import jax
import jax.numpy as jnp
import numpy as np
from jax import lax
from jax.experimental import pallas as pl
from jax.experimental.pallas import tpu as pltpu
from jax.sharding import PartitionSpec as P

Z = 4
WZ = 2
WH = 6
WW = 12
C = 192
HEADS = 6
HEAD = 32
FF = 768
HZ, HH, HW = WZ // 2, WH // 2, WW // 2
TOK = WZ * WH * WW
PLACES = WZ * WH
RELW = 2 * WW - 1
SPOTS = PLACES // 2
STRIP = -(-RELW * SPOTS // 128) * 128
RUN, SHORT = WW * SPOTS, (WW - HW) * SPOTS

mask_fill = -10000.0
norm_eps = 1e-05
log2e = 1.4426950408889634
root_half = 0.7071067811865476
inv_root_tau = 0.3989422804014327
score_scale = HEAD**-0.5

f32 = jnp.float32
bf16 = jnp.bfloat16
MIB = 1 << 20

QUADS = 4
FAR_FIRST = range(QUADS - 1, 0, -1)
PART = C // (2 * QUADS)
CHUNK = 3 * PART
BLOCKS = FF // 128
EXTRA = 8
FULL = BLOCKS * CHUNK + EXTRA


def mm(a, b):
    return lax.dot_general(a, b, (((1,), (0,)), ((), ())), preferred_element_type=f32)


def mm_nt(a, b):
    return lax.dot_general(a, b, (((1,), (1,)), ((), ())), preferred_element_type=f32)


def mm_tn(a, b):
    return lax.dot_general(a, b, (((0,), (0,)), ((), ())), preferred_element_type=f32)


def unit_norm(values):
    average = jnp.mean(values, -1, keepdims=True)
    centred = values - average
    variance = jnp.mean(centred * centred, -1, keepdims=True)
    spread = lax.rsqrt(variance + norm_eps)
    return centred * spread, spread


def norm_back(upstream, unit, spread):
    first = jnp.mean(upstream, -1, keepdims=True)
    second = jnp.mean(upstream * unit, -1, keepdims=True)
    return spread * (upstream - first - unit * second)


def piece_rows(rows, cols):
    home = np.arange(Z * rows * cols).reshape(Z, rows, cols)

    def run(level, row, col, width):
        levels = [(level * WZ + z - HZ) % Z for z in range(WZ)]
        return home[levels, row : row + HH, col : col + width].transpose(2, 0, 1).reshape(-1)

    levels = range(Z // WZ)
    parts = []
    for row in (0, rows - HH):
        whole = [run(a, row, w * WW - HW, WW) for w in range(1, cols // WW) for a in levels]
        parts.append(np.concatenate(whole + [run(a, row, 0, WW - HW) for a in levels]))
    for row in (0, rows - HH):
        parts.append(np.concatenate([run(a, row, cols - HW, HW) for a in levels]))
    return parts


def window_runs(lon_windows):
    levels = Z // WZ
    whole = (lon_windows - 1) * levels
    runs = [[(1, n * RUN, RUN), (0, n * RUN, RUN)] for n in range(whole)]
    for a in range(levels):
        inner = whole * RUN + a * SHORT
        west = (a * (RUN - SHORT), RUN - SHORT)
        runs.append([(3, *west), (1, inner, SHORT), (2, *west), (0, inner, SHORT)])
    return runs


def spots(places):
    return jnp.asarray(np.argsort(places).astype(np.int32)[None])


def one_hot(spot_ref):
    count = spot_ref.shape[1]
    rows = lax.broadcasted_iota(jnp.int32, (count, count), 0)
    return (rows == spot_ref[...]).astype(f32).astype(bf16)


def vmem(count):
    return [pl.BlockSpec(memory_space=pltpu.VMEM)] * count


def shape(dims, dtype):
    return jax.ShapeDtypeStruct(dims, dtype)


def cost(flops, moved):
    return pl.CostEstimate(flops=flops, bytes_accessed=moved, transcendentals=0)


def land_column(land_ref, rows, cols):
    eye = (
        lax.broadcasted_iota(jnp.int32, (cols, cols), 0)
        == lax.broadcasted_iota(jnp.int32, (cols, cols), 1)
    ).astype(f32)
    land = land_ref[...].astype(f32)
    parts = [jnp.sum(eye * land[i : i + 1, :], -1, keepdims=True) for i in range(rows)]
    return jnp.concatenate(parts, axis=0)


def pack_kernel(rows, cols, *refs):
    sources, outs, (tokens_ref, cot_ref, land_ref, vec_ref, perm_ref, sems) = refs[:6], refs[6:-7], refs[-6:]
    targets = (tokens_ref, cot_ref, land_ref, vec_ref, perm_ref, refs[-7])
    copies = [
        pltpu.make_async_copy(source, target, sems.at[n])
        for n, (source, target) in enumerate(zip(sources, targets))
    ]
    for copy in copies:
        copy.start()
    for copy in copies[:5]:
        copy.wait()
    column = land_column(land_ref, rows, cols)
    added = column * vec_ref[...]
    added = jnp.concatenate([added] * Z, axis=0)
    embedded = (tokens_ref[...].astype(f32) + added).astype(bf16)
    perm = one_hot(perm_ref)
    column = jnp.concatenate([column] * Z, axis=0)
    spare = jnp.broadcast_to(column, (column.shape[0], 2 * 128 - C)).astype(bf16)
    left = mm(perm, jnp.concatenate([embedded, spare], axis=1))
    left, flags = left[:, :C], left[:, C : C + 1]
    right = mm(perm, cot_ref[...])
    packed = jnp.concatenate([left, right], axis=1)
    start = 0
    for out in outs:
        count = out.shape[0] - EXTRA
        eye = lax.broadcasted_iota(jnp.int32, (count, count), 0) == lax.broadcasted_iota(jnp.int32, (count, count), 1)
        row = jnp.sum(jnp.where(eye, flags[start : start + count], 0.0), 0, keepdims=True)
        row = jnp.concatenate([row, jnp.zeros((1, 2 * C - count), f32)], axis=1)
        row = jnp.broadcast_to(row, (EXTRA, 2 * C))
        out[...] = jnp.concatenate([packed[start : start + count], row], axis=0).astype(bf16)
        start += count
    copies[5].wait()


def pack(tokens, cotangent, land_sea, vector, table, rows, cols):
    flat = table[0].transpose(1, 3, 0, 2).reshape(HEADS * RELW, table.shape[1], PLACES * PLACES)
    parts = piece_rows(rows, cols)
    perm = spots(np.concatenate(parts))
    count = Z * rows * cols
    return pl.pallas_call(
        functools.partial(pack_kernel, rows, cols),
        out_shape=[shape((part.size + EXTRA, 2 * C), bf16) for part in parts] + [shape(flat.shape, f32)],
        in_specs=[pl.BlockSpec(memory_space=pltpu.HBM)] * 6,
        out_specs=vmem(5),
        scratch_shapes=[
            pltpu.VMEM((count, C), bf16),
            pltpu.VMEM((count, C), bf16),
            pltpu.VMEM((rows, cols), jnp.int32),
            pltpu.VMEM((1, C), f32),
            pltpu.VMEM((1, count), jnp.int32),
            pltpu.SemaphoreType.DMA((6,)),
        ],
        compiler_params=pltpu.CompilerParams(vmem_limit_bytes=24 * MIB),
        cost_estimate=cost(4 * count * count * C, 4 * MIB),
        name="pack",
    )(*[
        pltpu.with_memory_space_constraint(value, pltpu.HBM)
        for value in (tokens.reshape(count, C), cotangent.reshape(count, C), land_sea, vector.reshape(1, C), perm, flat)
    ])


def floor_div(values, divisor):
    return (values * (65536 // divisor + 1)) >> 16


def remainder(values, divisor):
    return values - floor_div(values, divisor) * divisor


def place_order(order):
    half = floor_div(order, SPOTS)
    spot = order - half * SPOTS
    level = floor_div(spot, HH)
    return level * WH + half * HH + (spot - level * HH)


def bias_kernel(levels, table_ref, out_ref, *wide_refs):
    groups = levels * HEADS
    pairs = PLACES * PLACES
    row = lax.broadcasted_iota(jnp.int32, (HEADS * RELW, HEADS * STRIP), 0)
    lane = lax.broadcasted_iota(jnp.int32, (HEADS * RELW, HEADS * STRIP), 1)
    head = floor_div(row, RELW)
    ahead = lane - (head * STRIP + (RELW - 1 - (row - head * RELW)) * SPOTS)
    onehot = ((ahead >= 0) & (ahead < SPOTS)).astype(f32).astype(bf16)
    row = lax.broadcasted_iota(jnp.int32, (pairs, pairs), 0)
    source = place_order(floor_div(row, PLACES)) * PLACES + remainder(row, PLACES)
    reorder = (lax.broadcasted_iota(jnp.int32, (pairs, pairs), 1) == source).astype(f32).astype(bf16)
    for level in range(levels):
        table = table_ref[:, level, :].T
        high = table.astype(bf16)
        rest = (table - high.astype(f32)).astype(bf16)
        wide = mm(mm(reorder, high).astype(bf16), onehot) + mm(mm(reorder, rest).astype(bf16), onehot)
        for head in range(HEADS):
            for n, wide_ref in enumerate(wide_refs):
                start = head * STRIP + n * 128
                wide_ref[(level * HEADS + head) * pairs : (level * HEADS + head + 1) * pairs, :] = wide[:, start : start + 128]
    strips = groups * PLACES
    row = lax.broadcasted_iota(jnp.int32, (strips, STRIP), 0)
    spot = remainder(lax.broadcasted_iota(jnp.int32, (strips, STRIP), 1), SPOTS)
    own = remainder(row, PLACES)
    first_level = (row < HEADS * PLACES).astype(jnp.int32)
    own_north = (own < SPOTS).astype(jnp.int32)
    own_low = (own - SPOTS * (1 - own_north) < HZ * HH).astype(jnp.int32)
    low = (spot < HZ * HH).astype(jnp.int32)
    pole = (lax.axis_index("y") + lax.axis_index("core") == 0).astype(jnp.int32)
    halves = []
    for half in range(2):
        parts = []
        for n, wide_ref in enumerate(wide_refs):
            here = spot[:, n * 128 : (n + 1) * 128]
            part = jnp.zeros((strips, 128), f32)
            for p in range(SPOTS):
                place = p // HH * WH + half * HH + p % HH
                part = jnp.where(here == p, wide_ref[pl.ds(place, strips, stride=PLACES), :], part)
            parts.append(part)
        strip = jnp.concatenate(parts, axis=1)
        differs = first_level * (own_low ^ low) + pole * (own_north ^ (1 - half))
        halves.append(jnp.where(differs > 0, strip + mask_fill, strip) * log2e)
    for w in range(WW):
        start = (WW - 1 - w) * SPOTS
        part = jnp.concatenate([strip[:, start : start + RUN] for strip in halves], axis=1)
        for g in range(groups):
            for half in range(2):
                rows = part[g * PLACES + half * SPOTS : g * PLACES + (half + 1) * SPOTS, :]
                out_ref[g, half * RUN + w * SPOTS : half * RUN + (w + 1) * SPOTS, :] = rows


def expand_bias(flat):
    levels = flat.shape[1]
    groups = levels * HEADS
    pairs = PLACES * PLACES
    return pl.pallas_call(
        functools.partial(bias_kernel, levels),
        out_shape=shape((groups, TOK, TOK), f32),
        in_specs=vmem(1),
        out_specs=vmem(1)[0],
        scratch_shapes=[pltpu.VMEM((groups * pairs, 128), f32)] * (STRIP // 128),
        compiler_params=pltpu.CompilerParams(vmem_limit_bytes=28 * MIB),
        cost_estimate=cost(10**9, 8 * MIB),
        name="bias",
    )(flat)


def head_masks(count):
    lane = lax.broadcasted_iota(jnp.int32, (count, C), 1)
    return [((lane >= h * HEAD) & (lane < (h + 1) * HEAD)).astype(f32) for h in range(HEADS)]


def stacked(values, masks):
    return jnp.concatenate([values * mask for mask in masks], axis=0)


def head_sum(values, masks):
    total = values[:TOK] * masks[0]
    for h in range(1, HEADS):
        total = total + values[h * TOK : (h + 1) * TOK] * masks[h]
    return total


def position():
    return lax.axis_index("core"), lax.axis_index("y") * 2 + lax.axis_index("x"), lax.axis_index("deep")


def chunk_rows(block):
    return pl.ds(pl.multiple_of(block * PART, PART), PART)


def split_parts(total_refs, keep_ref, send_ref):
    core, chip, _ = position()
    for out, side in ((keep_ref, core), (send_ref, 1 - core)):
        parts = []
        for g in range(QUADS):
            rows = chunk_rows(side * QUADS + jnp.bitwise_xor(chip, g))
            parts += [ref[rows, :] for ref in total_refs]
        out[...] = jnp.concatenate(parts, axis=0).astype(out.dtype)


def attend(first, runs, pieces, bias_ref, triple_ref, project_ref, *refs):
    q_ref, k_ref, v_ref, p_ref, mixed_ref, normed_ref, unit_ref, spread_ref, summed_ref, cot_ref = refs
    pieces = [piece.astype(f32) for piece in pieces]
    ordered = jnp.concatenate([pieces[n][start : start + count] for n, start, count in runs], axis=0)
    emb = ordered[:, :C]
    cot_ref[...] = ordered[:, C:].astype(bf16)
    unit, spread = unit_norm(emb)
    unit_ref[...] = unit
    spread_ref[...] = spread
    normed = unit.astype(bf16)
    normed_ref[...] = normed
    packed = mm(normed, triple_ref[...])
    q_ref[...] = packed[:, :C].astype(bf16)
    k_ref[...] = packed[:, C : 2 * C].astype(bf16)
    v_ref[...] = packed[:, 2 * C :].astype(bf16)
    masks = head_masks(TOK)
    masks_b = [mask.astype(bf16) for mask in masks]
    for w in range(emb.shape[0] // TOK):
        rows = slice(w * TOK, (w + 1) * TOK)
        heads = slice(w * HEADS, (w + 1) * HEADS)
        level = (first + w) % (Z // WZ)
        scores = mm_nt(stacked(q_ref[rows, :], masks_b), k_ref[rows, :])
        bias = bias_ref[level * HEADS : (level + 1) * HEADS].reshape(HEADS * TOK, TOK)
        raised = jnp.exp2(scores * (score_scale * log2e) + bias)
        probs = raised * (1.0 / jnp.sum(raised, -1, keepdims=True))
        probs_b = probs.astype(bf16)
        p_ref[heads] = probs_b.reshape(HEADS, TOK, TOK)
        mixed = head_sum(mm(probs_b, v_ref[rows, :]), masks).astype(bf16)
        mixed_ref[rows, :] = mixed
        summed_ref[rows, :] = emb[rows] + mm(mixed, project_ref[...]).astype(bf16).astype(f32)


def feed_back(summed, cot, up_ref, down_ref, gsum_ref, up_grad_ref, down_grad_ref):
    unit2, spread2 = unit_norm(summed)
    normed2 = unit2.astype(bf16)
    back = jnp.zeros(unit2.shape, f32)
    block = 256
    for start in range(0, FF, block):
        cols = slice(start, start + block)
        up_part = up_ref[:, cols]
        pre = mm(normed2, up_part)
        upstream = mm(cot, down_ref[:, cols])
        phi = 0.5 * (1.0 + lax.erf(pre * root_half))
        activated = (pre * phi).astype(bf16)
        slope = phi + pre * inv_root_tau * jnp.exp2(pre * pre * (-0.5 * log2e))
        hidden = (upstream * slope).astype(bf16)
        up_grad_ref[:, cols] = mm_tn(normed2, hidden)
        down_grad_ref[:, cols] = mm_tn(cot, activated)
        back = back + mm_nt(hidden, up_part)
    gsum_ref[...] = cot.astype(f32) + norm_back(back, unit2, spread2)


def attend_back(at, q_ref, k_ref, v_ref, p_ref, gsum_ref, project_ref, gq_ref, gk_ref, gv_ref):
    masks = head_masks(TOK)
    masks_b = [mask.astype(bf16) for mask in masks]
    for w in range(q_ref.shape[0] // TOK):
        rows = slice(w * TOK, (w + 1) * TOK)
        full_rows = slice(at + w * TOK, at + (w + 1) * TOK)
        grad = gsum_ref[full_rows, :].astype(bf16)
        grad_mixed_b = mm_nt(grad, project_ref[...]).astype(bf16)
        probs_b = p_ref[w * HEADS : (w + 1) * HEADS].reshape(HEADS * TOK, TOK)
        probs = probs_b.astype(f32)
        grad_probs = mm_nt(stacked(grad_mixed_b, masks_b), v_ref[rows, :])
        inner = jnp.sum(grad_probs * probs, -1, keepdims=True)
        scaled = (probs * (grad_probs - inner) * score_scale).astype(bf16)
        grad_q = head_sum(mm(scaled, k_ref[rows, :]), masks)
        grad_mixed_t = grad_mixed_b.astype(f32).T.astype(bf16)
        query_t = q_ref[rows, :].astype(f32).T.astype(bf16)
        grad_k, grad_v = [], []
        for h in range(HEADS):
            spot = slice(h * HEAD, (h + 1) * HEAD)
            span = slice(h * TOK, (h + 1) * TOK)
            grad_k.append(mm(query_t[spot], scaled[span]))
            grad_v.append(mm(grad_mixed_t[spot], probs_b[span]))
        gq_ref[full_rows, :] = grad_q.astype(bf16)
        gk_ref[full_rows, :] = jnp.concatenate(grad_k, axis=0).T.astype(bf16)
        gv_ref[full_rows, :] = jnp.concatenate(grad_v, axis=0).T.astype(bf16)


def halved(rows):
    return -(-rows // 16) * 8


def tokens_back(
    lon_windows, sizes, gq_ref, gk_ref, gv_ref, mixed, normed, unit, spread, gsum_ref, triple_ref, up_grad_ref, down_grad_ref,
    *rest,
):
    flag_refs, rest = rest[: len(sizes)], rest[len(sizes) :]
    outs, (land_ref, keep_ref, send_ref, total_ref) = rest[: len(sizes) - 1], rest[len(sizes) - 1 :]
    triple = triple_ref[...]
    grad_normed = jnp.zeros(unit.shape, f32)
    parts = []
    for n, ref in enumerate((gq_ref, gk_ref, gv_ref)):
        grad = ref[...]
        grad_normed = grad_normed + mm_nt(grad, triple[:, n * C : (n + 1) * C])
        parts.append(mm_tn(normed, grad))
    parts.append(mm_tn(mixed, gsum_ref[...].astype(bf16)))
    total_ref[...] = jnp.concatenate(parts, axis=1)
    grad_normed = grad_normed.astype(bf16).astype(f32)
    grad_tokens = gsum_ref[...] + norm_back(grad_normed, unit, spread)
    parts, at = [[] for _ in sizes], 0
    for n, start, count in [run for window in window_runs(lon_windows) for run in window]:
        parts[n].append((start, grad_tokens[at : at + count]))
        at += count
    land = jnp.zeros((EXTRA, C), f32)
    wide = []
    for size, flag_ref, part in zip(sizes, flag_refs, parts):
        piece = jnp.concatenate([value for _, value in sorted(part, key=lambda item: item[0])], axis=0)
        flags = flag_ref[size - 8 : size + 8, :].astype(f32)[8:, :size]
        land = land + mm(flags.astype(bf16), piece.astype(bf16))
        half = halved(size)
        second = jnp.concatenate([piece[half:], jnp.zeros((2 * half - size, C), f32)], axis=0)
        wide.append(jnp.concatenate([piece[:half], second], axis=1))
    land_ref[...] = land[0:1]
    own, north, side, corner = wide
    for out, value in zip(outs, (own, jnp.concatenate([north, corner], axis=0), side)):
        out[...] = value.astype(bf16)
    split_parts((up_grad_ref, down_grad_ref, total_ref), keep_ref, send_ref)


def saved_shapes(count):
    dims = [((count, C), bf16)] * 3 + [((count // TOK * HEADS, TOK, TOK), bf16)] + [((count, C), bf16)] * 2
    return dims + [((count, C), f32), ((count, 1), f32), ((count, C), f32), ((count, C), bf16)]


SAVED = len(saved_shapes(TOK))


def split_runs(lon_windows):
    windows = window_runs(lon_windows)
    whole = (lon_windows - 1) * (Z // WZ)
    return whole, *[[run for window in part for run in window] for part in (windows[:whole], windows[whole:])]


def near_kernel(lon_windows, own_ref, north_ref, *refs):
    runs = split_runs(lon_windows)[1]
    attend(0, runs, (own_ref[...], north_ref[...]), *refs)


def near_block(own, north, bias, triple, project, lon_windows):
    count = split_runs(lon_windows)[0] * TOK
    return pl.pallas_call(
        functools.partial(near_kernel, lon_windows),
        out_shape=[shape(*dims) for dims in saved_shapes(count)],
        in_specs=vmem(5),
        out_specs=vmem(SAVED),
        compiler_params=pltpu.CompilerParams(vmem_limit_bytes=24 * MIB),
        cost_estimate=cost(3 * 10**9, 8 * MIB),
        name="near_block",
    )(own, north, bias, triple, project)


def block_kernel(lon_windows, sizes, *refs):
    whole, _, runs = split_runs(lon_windows)
    pieces, refs = refs[:4], refs[4:]
    (bias_ref, triple_ref, project_ref, up_ref, down_ref), refs = refs[:5], refs[5:]
    near, refs = refs[:SAVED], refs[SAVED:]
    outs, refs = refs[: len(sizes) + 2], refs[len(sizes) + 2 :]
    far, (gsum, up_grad, down_grad, gq, gk, gv, total) = refs[:SAVED], refs[SAVED:]
    attend(whole, runs, [ref[...] for ref in pieces], bias_ref, triple_ref, project_ref, *far)
    mixed, normed, unit, spread, summed, cot = [
        jnp.concatenate([one[...], other[...]], axis=0) for one, other in zip(near[4:], far[4:])
    ]
    feed_back(summed, cot, up_ref, down_ref, gsum, up_grad, down_grad)
    attend_back(0, *near[:4], gsum, project_ref, gq, gk, gv)
    attend_back(whole * TOK, *far[:4], gsum, project_ref, gq, gk, gv)
    tokens_back(
        lon_windows, sizes, gq, gk, gv, mixed, normed, unit, spread, gsum, triple_ref, up_grad, down_grad,
        *pieces, *outs, total,
    )


def block(pieces, bias, triple, project, up, down, near, lon_windows, sizes):
    count = sum(sizes)
    own, north, side, corner = [halved(size) for size in sizes]
    out_shape = [shape((size, 2 * C), bf16) for size in (own, north + corner, side)] + [
        shape((1, C), f32),
        shape((QUADS * CHUNK, FF), f32),
        shape((QUADS * CHUNK, FF), bf16),
    ]
    return pl.pallas_call(
        functools.partial(block_kernel, lon_windows, sizes),
        out_shape=out_shape,
        in_specs=vmem(9 + SAVED),
        out_specs=vmem(len(out_shape)),
        scratch_shapes=[pltpu.VMEM(*dims) for dims in saved_shapes(count - near[0].shape[0])]
        + [pltpu.VMEM((count, C), f32)]
        + [pltpu.VMEM((C, FF), f32)] * 2
        + [pltpu.VMEM((count, C), bf16)] * 3
        + [pltpu.VMEM((C, FF), f32)],
        compiler_params=pltpu.CompilerParams(vmem_limit_bytes=28 * MIB),
        cost_estimate=cost(8 * 10**9, 16 * MIB),
        name="block",
    )(*pieces, bias, triple, project, up, down, *near)


def side_kernel(side_ref, north_ref, *refs):
    corner = north_ref[...].astype(f32)[-side_ref.shape[0] :]
    refs[-1][...] = jnp.concatenate([side_ref[...].astype(f32), corner], axis=0).astype(bf16)


def home_kernel(sizes, own_ref, north_ref, side_ref, perm_ref, out_ref, done_ref):
    wide = [ref[...].astype(f32) for ref in (own_ref, north_ref, side_ref)]
    half = wide[2].shape[0] // 2
    wide = [wide[0], wide[1][:-half], wide[2][:half], wide[2][half:]]
    pieces = []
    for size, value in zip(sizes, wide):
        pieces += [value[:, :C], value[: size - value.shape[0], C:]]
    pieces = jnp.concatenate(pieces, axis=0).astype(bf16)
    out_ref[...] = mm(one_hot(perm_ref), pieces).astype(bf16)
    done_ref[...] = jnp.zeros_like(done_ref)


def to_home(own, north, side, sizes, rows, cols):
    count = Z * rows * cols
    perm = spots(np.argsort(np.concatenate(piece_rows(rows, cols))))
    return pl.pallas_call(
        functools.partial(home_kernel, sizes),
        out_shape=[shape((count, C), bf16), shape((8, 128), f32)],
        in_specs=vmem(4),
        out_specs=vmem(2),
        compiler_params=pltpu.CompilerParams(vmem_limit_bytes=32 * MIB),
        cost_estimate=cost(2 * count * count * C, 4 * MIB),
        name="to_home",
    )(own, north, side, perm)


def core_add_kernel(keep_ref, got_ref, *refs):
    own_ref, outs = refs[-QUADS], refs[1 - QUADS :]
    total = keep_ref[...] + got_ref[...].astype(f32)
    own_ref[...] = total[:CHUNK]
    for e, out in zip(FAR_FIRST, outs):
        out[...] = total[e * CHUNK : (e + 1) * CHUNK].astype(bf16)


def chip_add_kernel(keep_ref, *refs):
    gots, (land_ref, out_ref) = refs[:-2], refs[-2:]
    total = keep_ref[...]
    for ref in gots:
        total = total + ref[...].astype(f32)
    land = land_ref[...]
    rest = jnp.concatenate([land[:, 128:], jnp.zeros((1, 2 * 128 - C), f32)], axis=1)
    parts = [total[:, n * 128 : (n + 1) * 128] for n in range(BLOCKS)]
    total = jnp.concatenate(parts + [land[:, :128], rest, jnp.zeros((EXTRA - 2, 128), f32)], axis=0)
    out_ref[...] = total.astype(bf16)


def add_kernel(one_ref, two_ref, *refs):
    refs[-1][...] = (one_ref[...].astype(f32) + two_ref[...].astype(f32)).astype(bf16)


def join_kernel(*refs):
    refs[-1][...] = jnp.concatenate([ref[...] for ref in refs[:-1]], axis=0)


def small_call(kernel, out_shape, args, name, after=(), scratch=()):
    return pl.pallas_call(
        kernel,
        out_shape=out_shape,
        in_specs=vmem(len(args)) + [pl.BlockSpec(memory_space=pl.ANY)] * len(after),
        out_specs=vmem(len(out_shape)),
        scratch_shapes=scratch,
        compiler_params=pltpu.CompilerParams(vmem_limit_bytes=16 * MIB),
        cost_estimate=cost(10**6, 2 * MIB),
        name=name,
    )(*args, *after)


def finish_kernel(far, chunks_ref, *refs):
    if far:
        before_ref, refs = refs[0], refs[5:]
    outs, land_ref, (up_ref, down_ref, triple_ref, project_ref, lands_ref, sum_ref, sems) = refs[:4], refs[4], refs[5:]
    core, chip, _ = position()
    side = 1 - core if far else core
    for g in range(QUADS):
        tiles = chunks_ref[g * FULL : (g + 1) * FULL, :].astype(f32)
        chunk = jnp.concatenate([tiles[n * CHUNK : (n + 1) * CHUNK] for n in range(BLOCKS)], axis=1)
        block = jnp.bitwise_xor(chip, g)
        rows = chunk_rows(block)
        up_ref[rows, :] = chunk[:PART]
        down_ref[rows, :] = chunk[PART : 2 * PART]
        triple_ref[rows, :] = chunk[2 * PART : CHUNK, : 3 * C]
        project_ref[rows, :] = chunk[2 * PART : CHUNK, 3 * C :]
        lands_ref[pl.ds(pl.multiple_of(block * EXTRA, EXTRA), EXTRA), :] = tiles[BLOCKS * CHUNK :]
    copies = []
    for n, (source, out) in enumerate(zip((triple_ref, project_ref, up_ref, down_ref), outs)):
        rows = pl.ds(pl.multiple_of(side * QUADS * PART, 8), QUADS * PART)
        copies.append(pltpu.make_async_copy(source, out.at[rows, :], sems.at[n]))
    for copy in copies:
        copy.start()
    lands = lands_ref[...]
    lands = [sum(lands[g * EXTRA + n : g * EXTRA + n + 1] for g in range(QUADS)) for n in range(2)]
    land = jnp.concatenate([lands[0], lands[1][:, : C - 128]], axis=1)
    if far:
        sum_ref[...] = land + before_ref[...]
        copies.append(pltpu.make_async_copy(sum_ref, land_ref, sems.at[4]))
        copies[-1].start()
    else:
        land_ref[...] = land
    for copy in copies:
        copy.wait()


def finish(chunks, before=()):
    rows = QUADS * PART
    widths = (3 * C, C, FF, FF)
    hbm = [pl.BlockSpec(memory_space=pltpu.HBM)] * 4
    land, weights = before[4:], before[:4]
    return pl.pallas_call(
        functools.partial(finish_kernel, bool(before)),
        out_shape=[shape((C, width), f32) for width in widths] + [shape((1, C), f32)],
        in_specs=vmem(1 + len(land)) + hbm[: len(weights)],
        out_specs=hbm + (hbm[:1] if before else vmem(1)),
        scratch_shapes=[
            pltpu.VMEM((rows, FF), f32),
            pltpu.VMEM((rows, FF), f32),
            pltpu.VMEM((rows, 3 * C), f32),
            pltpu.VMEM((rows, C), f32),
            pltpu.VMEM((QUADS * EXTRA, 128), f32),
            pltpu.VMEM((1, C), f32),
            pltpu.SemaphoreType.DMA((5,)),
        ],
        input_output_aliases={2 + n: n for n in range(len(weights))},
        compiler_params=pltpu.CompilerParams(vmem_limit_bytes=16 * MIB),
        cost_estimate=cost(10**6, 2 * MIB),
        name="finish_far" if before else "finish_own",
    )(chunks, *land, *weights)


def reduce_all(keep, sent, land, side, north, go_home, shift, lon_count):
    core_move = lambda lon, lat: (lon, lat ^ 1)
    chip_move = lambda e: lambda lon, lat: (lon ^ (e & 1), lat ^ (2 * (e >> 1)))
    deep_move = lambda e: lambda lon, lat: (lon ^ (2 * e), lat)

    def one(rows):
        return [shape((rows, FF), bf16)]

    got = shift(sent, move=core_move)
    parts = [shape((CHUNK, FF), f32)] + one(CHUNK) * (QUADS - 1)
    own, *parts = small_call(core_add_kernel, parts, (keep, got), "core_add", after=(north,))
    gots = [shift(value, move=chip_move(e)) for e, value in zip(FAR_FIRST, parts)]
    full = [shape((FULL, 128), bf16)]
    (total,) = small_call(chip_add_kernel, full, (own, *gots, land), "chip_add")
    (side,) = small_call(side_kernel, [shape((2 * side.shape[0], 2 * C), bf16)], (side, north), "side", after=(total,))
    side = shift(side, move=lambda lon, lat: (lon - 1, lat))
    grad_tokens, done = go_home(north, side)
    reach, waits = 1, [(side,), (done,)]
    while reach < lon_count // 2:
        got = shift(total, move=deep_move(reach))
        reach *= 2
        (total,) = small_call(add_kernel, full, (total, got), "deep_add", after=waits.pop(0) if waits else ())
    near = [total] + [shift(total, move=chip_move(e)) for e in range(1, QUADS)]
    (total,) = small_call(join_kernel, [shape((QUADS * FULL, 128), bf16)], near, "join")
    got = shift(total, move=core_move)
    return finish(got, finish(total)), grad_tokens


AXES = ("deep", "x", "y", "core")


def send(value, lon_count, lat_count, move):
    pairs = []
    for lon in range(lon_count):
        for lat in range(lat_count):
            to_lon, to_lat = move(lon, lat)
            pairs.append((lon * lat_count + lat, (to_lon % lon_count) * lat_count + to_lat % lat_count))
    return lax.ppermute(value, AXES, pairs)


def body(
    lon_count, lat_count,
    tokens, cotangent, land_sea, land_vector, triple_weight, project_weight, up_weight, down_weight, earth_bias,
):
    levels, rows, cols, features = tokens.shape
    shift = functools.partial(send, lon_count=lon_count, lat_count=lat_count)
    lon_windows = cols // WW

    own, north, side, corner, table = pack(tokens, cotangent, land_sea, land_vector, earth_bias, rows, cols)
    north = shift(north, move=lambda lon, lat: (lon, lat + 1))
    side = shift(side, move=lambda lon, lat: (lon + 1, lat))
    corner = shift(corner, move=lambda lon, lat: (lon + 1, lat + 1))
    bias = expand_bias(table)

    sizes = [part.size for part in piece_rows(rows, cols)]
    pieces = (own, north, side, corner)
    near = near_block(own, north, bias, triple_weight, project_weight, lon_windows)
    own, north, side, land, keep, sent = block(
        pieces, bias, triple_weight, project_weight, up_weight, down_weight.T, near, lon_windows, sizes
    )
    north = shift(north, move=lambda lon, lat: (lon, lat - 1))
    go_home = lambda north, side: to_home(own, north, side, sizes, rows, cols)
    sums, grad_tokens = reduce_all(keep, sent, land, side, north, go_home, shift, lon_count)
    triple, project, up, down, land = sums
    return grad_tokens.reshape(tokens.shape), triple, project, up, down.T, land.reshape(features)


def solution(mesh):
    lon_count, lat_count = mesh.shape["lon"], mesh.shape["lat"]
    fine = jax.sharding.Mesh(mesh.devices.reshape(lon_count // 2, 2, lat_count // 2, 2), AXES)
    lon, lat = AXES[:2], AXES[2:]
    return jax.shard_map(
        functools.partial(body, lon_count, lat_count),
        mesh=fine,
        in_specs=(
            P(None, lat, lon, None),
            P(None, lat, lon, None),
            P(lat, lon),
            P(),
            P(),
            P(),
            P(),
            P(),
            P(lat, None, None, None, None),
        ),
        out_specs=(P(None, lat, lon, None), P(), P(), P(), P(), P()),
        check_vma=False,
    )
```
